32 devices in a mesh: ctx: 8 (over y, x, core), tp: 4 (over z).
Axes of the slice: x: 2, y: 2, z: 4, core: 2. Of those that a mesh axis runs over, the one named last changes fastest.
Arguments:
- hidden_in: bfloat16 [6144, 1024], P('ctx'), may hold values from -6 to 6
- doc_lengths: int32 [8], replicated, may hold values from 1 to 5760, as said below
- cotangent: bfloat16 [6144, 1024], P('ctx'), may hold values from -6 to 6
- attn_gain: float32 [2, 1024], replicated, may hold values from 0.5 to 1.5
- ffn_gain: float32 [2, 1024], replicated, may hold values from 0.5 to 1.5
- qk_gain: float32 [2, 2, 128], replicated, may hold values from 0.5 to 1.5
- w_query: bfloat16 [2, 1024, 2048], P(None, None, 'tp'), may hold values from -0.1875 to 0.1875
- key_weight: bfloat16 [2, 1024, 1024], P(None, None, 'tp'), may hold values from -0.1875 to 0.1875
- value_weight: bfloat16 [2, 1024, 1024], P(None, None, 'tp'), may hold values from -0.1875 to 0.1875
- w_out: bfloat16 [2, 2048, 1024], P(None, 'tp'), may hold values from -2 to 2
- w_gate: bfloat16 [2, 1024, 3072], P(None, None, 'tp'), may hold values from -0.1875 to 0.1875
- w_up: bfloat16 [2, 1024, 3072], P(None, None, 'tp'), may hold values from -0.1875 to 0.1875
- w_down: bfloat16 [2, 3072, 1024], P(None, 'tp'), may hold values from -0.109375 to 0.109375
Outputs:
- hidden_out: bfloat16 [6144, 1024], P('ctx')
- hidden_grad: float32 [6144, 1024], P('ctx')
- attn_gain_grad: float32 [2, 1024], P(None, 'ctx')
- ffn_gain_grad: float32 [2, 1024], P(None, 'ctx')
- qk_gain_grad: float32 [2, 2, 128], replicated
- query_grad: float32 [2, 1024, 2048], P(None, 'ctx', 'tp')
- key_grad: float32 [2, 1024, 1024], P(None, 'ctx', 'tp')
- value_grad: float32 [2, 1024, 1024], P(None, 'ctx', 'tp')
- out_grad: float32 [2, 2048, 1024], P(None, ('tp', 'ctx'))
- gate_grad: float32 [2, 1024, 3072], P(None, 'ctx', 'tp')
- up_grad: float32 [2, 1024, 3072], P(None, 'ctx', 'tp')
- down_grad: float32 [2, 3072, 1024], P(None, ('tp', 'ctx'))
The draws below stay inside these ranges and needn't reach their ends.
Inputs may be any that keep to these rules, and one draw needn't show every extreme that they name: `doc_lengths`: lengths of 8 packed documents in order, summing to 6144; exactly one of them, at a place drawn from the seed, has 5760 tokens.
All inputs are finite; a program needn't handle non-finite values.
Results may differ from the reference program's by a relative error of at most 0.03.
Values may be sent and summed in bfloat16 or wider, within the bound.
A program may use at most 256 MiB of HBM per device.

```python
import jax
import jax.numpy as jnp
from jax import lax

MODEL_WIDTH = 1024
QUERY_HEADS = 16
KEY_VALUE_HEADS = 8
HEAD_SIZE = 128
FF = 3072
ATTENTION_WINDOW = 1024
DECODER_LAYERS = 2
DOCS = 8
TOK_DEV = 768
PACKED_TOKENS = 6144


def draw_doc_lengths(key, part):
    key = jax.random.fold_in(key, 7)
    place_key, cut_key = jax.random.split(key)
    short_total = TOK_DEV // 2
    longest = jax.random.randint(place_key, (), 0, DOCS)
    cuts = jnp.sort(jax.random.permutation(cut_key, short_total - 1)[:DOCS - 2] + 1).astype(jnp.int32)
    edges = jnp.concatenate([jnp.zeros((1,), jnp.int32), cuts, jnp.full((1,), short_total, jnp.int32)])
    shorts = edges[1:] - edges[:-1]
    slot = jnp.arange(DOCS, dtype=jnp.int32)
    source = jnp.clip(jnp.where(slot < longest, slot, slot - 1), 0, DOCS - 2)
    return jnp.where(slot == longest, PACKED_TOKENS - short_total, shorts[source]).astype(jnp.int32)


def raised(drawn, stream_key, source, target, shards_of, factor):
    def block_of(dim):
        return (jnp.arange(drawn.shape[dim]) // (drawn.shape[dim] // shards_of)).reshape((-1,) + (1,) * (drawn.ndim - 1 - dim))

    one_side = jax.random.permutation(stream_key, shards_of)[block_of(target)]
    far = (block_of(target) + shards_of // 2) % shards_of
    return jnp.where((block_of(source) == one_side) | (block_of(source) == far), factor * drawn, drawn)


def level_of(key, shape, pieces, low, high):
    loudness, own = 1.0, jax.random.fold_in(key, 6)
    for dim, parts in pieces:
        draws = jnp.exp(jax.random.uniform(jax.random.fold_in(own, dim), (parts,), jnp.float32, low / len(pieces), high / len(pieces)))
        loudness = loudness * jnp.repeat(draws, shape[dim] // parts).reshape([-1 if axis == dim else 1 for axis in range(len(shape))])
    return loudness


def noise(rng, dims, width, reach, cuts=(), kind=jnp.bfloat16):
    values = jax.random.normal(rng, dims, jnp.float32) * width
    if len(cuts) > 0:
        values = level_of(rng, dims, cuts, -0.22, 0.18) * values
    return jnp.clip(values, min=-reach, max=reach).astype(kind)


def noise_with(own_key, dims, spread, most, shards, heavy, held_as=jnp.bfloat16):
    values = spread * jax.random.normal(own_key, dims, jnp.float32)
    if shards:
        values = values * level_of(own_key, dims, shards, -0.22, 0.18)
    return jnp.clip(raised(values, jax.random.fold_in(own_key, 3), *heavy), -most, most).astype(held_as)


def setup_inputs(seed: int = 0) -> dict:
    key_of = jax.random.split(jax.random.key(seed), 14)
    hidden_in = noise(key_of[0], (PACKED_TOKENS, MODEL_WIDTH), 1.0, 6.0, ((0, 8),))
    doc_lengths = draw_doc_lengths(jax.random.fold_in(key_of[13], 71), 0)
    cotangent = noise_with(key_of[2], (PACKED_TOKENS, MODEL_WIDTH), 1.0, 6.0, ((0, 8),), (0, 1, 8, 2.0))
    attn_gain = jnp.clip(1.0 + 0.1 * jax.random.normal(key_of[3], (DECODER_LAYERS, MODEL_WIDTH), jnp.float32), 0.5, 1.5)
    ffn_gain = jnp.clip(1.0 + 0.1 * jax.random.normal(key_of[4], (DECODER_LAYERS, MODEL_WIDTH), jnp.float32), 0.5, 1.5)
    qk_gain = jnp.clip(1.0 + 0.1 * jax.random.normal(key_of[5], (DECODER_LAYERS, 2, HEAD_SIZE), jnp.float32), 0.5, 1.5)
    w_query = noise(key_of[6], (DECODER_LAYERS, MODEL_WIDTH, QUERY_HEADS * HEAD_SIZE), MODEL_WIDTH ** -0.5, 0.1875, ((2, 4),))
    key_weight = noise(key_of[7], (DECODER_LAYERS, MODEL_WIDTH, KEY_VALUE_HEADS * HEAD_SIZE), MODEL_WIDTH ** -0.5, 0.1875, ((2, 4),))
    value_weight = noise(key_of[8], (DECODER_LAYERS, MODEL_WIDTH, KEY_VALUE_HEADS * HEAD_SIZE), MODEL_WIDTH ** -0.5, 0.1875, ((2, 4),))
    w_out = noise(key_of[9], (DECODER_LAYERS, QUERY_HEADS * HEAD_SIZE, MODEL_WIDTH), (max(QUERY_HEADS * HEAD_SIZE // 256, 4)) ** -0.5, 2.0, ((1, 4),))
    w_gate = noise(key_of[10], (DECODER_LAYERS, MODEL_WIDTH, FF), MODEL_WIDTH ** -0.5, 0.1875, ((2, 4),))
    w_up = noise(key_of[11], (DECODER_LAYERS, MODEL_WIDTH, FF), MODEL_WIDTH ** -0.5, 0.1875, ((2, 4),))
    w_down = noise(key_of[12], (DECODER_LAYERS, FF, MODEL_WIDTH), FF ** -0.5, 0.109375, ((1, 4),))
    return {"hidden_in": hidden_in, "doc_lengths": doc_lengths, "cotangent": cotangent, "attn_gain": attn_gain, "ffn_gain": ffn_gain, "qk_gain": qk_gain, "w_query": w_query, "key_weight": key_weight, "value_weight": value_weight, "w_out": w_out, "w_gate": w_gate, "w_up": w_up, "w_down": w_down}


EPS = 1e-06
THETA = 1000000.0

@jax.custom_vjp
def lower_bound(v):
    return lax.optimization_barrier(v.astype(jnp.bfloat16)).astype(jnp.float32)

@jax.custom_vjp
def lower_bound_backward(v):
    return v

def low_keep(v):
    return (lower_bound(v), None)

def low_pass(kept, grad):
    return (grad,)

def back_keep(v):
    return (v, None)

def back_low(kept, grad):
    return (lower_bound(grad),)
lower_bound.defvjp(low_keep, low_pass)
lower_bound_backward.defvjp(back_keep, back_low)

def matrix_product(left, right):
    return jnp.dot(left, right, precision=lax.Precision.HIGHEST)

def doc_info(lengths, place):
    ends = jnp.cumsum(lengths)
    passed = ends[None, :] <= place[:, None]
    segment = lax.optimization_barrier(jnp.sum(passed.astype(jnp.int32), axis=1))
    begin = lax.optimization_barrier(jnp.sum(jnp.where(passed, lengths[None, :], 0), axis=1))
    return (segment, place - begin)

def rope_tables(positions):
    half = HEAD_SIZE // 2
    freq = THETA ** (-(jnp.arange(half, dtype=jnp.float32) * 2.0) / HEAD_SIZE)
    angle = positions.astype(jnp.float32)[:, None] * freq[None, :]
    return (jnp.cos(angle), jnp.sin(angle))

def rotate(value_rows, cosine, sine):
    half = value_rows.shape[-1] // 2
    first = value_rows[..., :half]
    second = value_rows[..., half:]
    cosine = cosine[:, None, :]
    sine = sine[:, None, :]
    return jnp.concatenate([first * cosine - second * sine, second * cosine + first * sine], axis=-1)

def rms_norm(value_rows, gain):
    return value_rows * lax.rsqrt(lax.optimization_barrier(jnp.mean(value_rows * value_rows, axis=-1, keepdims=True)) + EPS) * gain

def attend(query_rows, key_rows, value_rows, segment, key_segment, key_place):
    scale = HEAD_SIZE ** (-0.5)
    key_rows_padded = jnp.concatenate([jnp.zeros((ATTENTION_WINDOW, KEY_VALUE_HEADS, HEAD_SIZE), jnp.float32), key_rows])
    value_rows_padded = jnp.concatenate([jnp.zeros((ATTENTION_WINDOW, KEY_VALUE_HEADS, HEAD_SIZE), jnp.float32), value_rows])
    grouped_heads = query_rows.reshape(PACKED_TOKENS, KEY_VALUE_HEADS, QUERY_HEADS // KEY_VALUE_HEADS, HEAD_SIZE)
    place = jnp.arange(PACKED_TOKENS, dtype=jnp.int32)

    def block(start):
        query_block = lax.dynamic_slice_in_dim(grouped_heads, start, TOK_DEV, 0)
        key_block = lax.dynamic_slice_in_dim(key_rows_padded, start, ATTENTION_WINDOW + TOK_DEV, 0)
        value_block = lax.dynamic_slice_in_dim(value_rows_padded, start, ATTENTION_WINDOW + TOK_DEV, 0)
        query_segment = lax.dynamic_slice_in_dim(segment, start, TOK_DEV, 0)
        query_place = lax.dynamic_slice_in_dim(place, start, TOK_DEV, 0)
        block_segment = lax.dynamic_slice_in_dim(key_segment, start, ATTENTION_WINDOW + TOK_DEV, 0)
        block_place = lax.dynamic_slice_in_dim(key_place, start, ATTENTION_WINDOW + TOK_DEV, 0)
        scores = lower_bound_backward(jnp.einsum('qgrd,kgd->grqk', query_block, key_block, precision=lax.Precision.HIGHEST) * scale)
        gap = query_place[:, None] - block_place[None, :]
        visible = (query_segment[:, None] == block_segment[None, :]) & (gap >= 0) & (gap < ATTENTION_WINDOW)
        scores = jnp.where(visible[None, None], scores, -1e+30)
        top = lax.optimization_barrier(jnp.max(scores, axis=-1, keepdims=True))
        weights = jnp.exp(scores - top)
        probs = weights / lax.optimization_barrier(jnp.sum(weights, axis=-1, keepdims=True))
        mixed = jnp.einsum('grqk,kgd->qgrd', lower_bound(probs), value_block, precision=lax.Precision.HIGHEST)
        return mixed.reshape(TOK_DEV, QUERY_HEADS * HEAD_SIZE)
    starts = jnp.arange(PACKED_TOKENS // TOK_DEV, dtype=jnp.int32) * TOK_DEV
    return lax.map(jax.checkpoint(block), starts).reshape(PACKED_TOKENS, QUERY_HEADS * HEAD_SIZE)

def layer_pass(stream, layer_index, params, tables):
    attn_gain, ffn_gain, qk_gain, w_query, key_weight, value_weight, w_out, w_gate, w_up, w_down = params
    cosine, sine, segment, key_segment, key_place = tables
    first_input = lower_bound(rms_norm(stream, attn_gain[layer_index]))
    query_proj = lower_bound_backward(matrix_product(first_input, w_query[layer_index])).reshape(PACKED_TOKENS, QUERY_HEADS, HEAD_SIZE)
    key_projected = lower_bound_backward(matrix_product(first_input, key_weight[layer_index])).reshape(PACKED_TOKENS, KEY_VALUE_HEADS, HEAD_SIZE)
    value_projected = lower_bound(lower_bound_backward(matrix_product(first_input, value_weight[layer_index]))).reshape(PACKED_TOKENS, KEY_VALUE_HEADS, HEAD_SIZE)
    query_rows = lower_bound(rotate(rms_norm(query_proj, qk_gain[layer_index, 0]), cosine, sine))
    key_rows = lower_bound(rotate(rms_norm(key_projected, qk_gain[layer_index, 1]), cosine, sine))
    attended = lower_bound(lower_bound_backward(attend(query_rows, key_rows, value_projected, segment, key_segment, key_place)))
    middle = stream + lower_bound_backward(matrix_product(attended, w_out[layer_index]))
    second_in = lower_bound(rms_norm(middle, ffn_gain[layer_index]))
    gate_act = lower_bound_backward(matrix_product(second_in, w_gate[layer_index]))
    up_act = lower_bound_backward(matrix_product(second_in, w_up[layer_index]))
    hidden = lower_bound(gate_act * jax.nn.sigmoid(gate_act) * up_act)
    return middle + lower_bound_backward(matrix_product(hidden, w_down[layer_index]))

def reference(hidden_in, doc_lengths, cotangent, attn_gain, ffn_gain, qk_gain, w_query, key_weight, value_weight, w_out, w_gate, w_up, w_down):
    place = jnp.arange(PACKED_TOKENS, dtype=jnp.int32)
    segment, position = doc_info(doc_lengths, place)
    cosine, sine = rope_tables(position)
    key_place = jnp.arange(PACKED_TOKENS + ATTENTION_WINDOW, dtype=jnp.int32) - ATTENTION_WINDOW
    key_segment = jnp.concatenate([jnp.full((ATTENTION_WINDOW,), -1, jnp.int32), segment])
    tables = (cosine, sine, segment, key_segment, key_place)

    def forward(stream, gain_a, gain_f, gain_qk, wq_all, wk_all, wv_all, wo_all, wg_all, wu_all, wd_all):
        params = (gain_a, gain_f, gain_qk, wq_all, wk_all, wv_all, wo_all, wg_all, wu_all, wd_all)
        for layer_index in range(DECODER_LAYERS):
            stream = layer_pass(stream, layer_index, params, tables)
        return stream
    primals = (hidden_in.astype(jnp.float32), attn_gain, ffn_gain, qk_gain, w_query.astype(jnp.float32), key_weight.astype(jnp.float32), value_weight.astype(jnp.float32), w_out.astype(jnp.float32), w_gate.astype(jnp.float32), w_up.astype(jnp.float32), w_down.astype(jnp.float32))
    result, pull = jax.vjp(forward, *primals)
    grads = pull(cotangent.astype(jnp.float32))
    return (result.astype(jnp.bfloat16), grads[0], grads[1], grads[2], grads[3], grads[4], grads[5], grads[6], grads[7], grads[8], grads[9], grads[10])
```

```python
import types

import jax
import jax.numpy as jnp
from jax import lax
from jax.experimental import pallas as pl
from jax.experimental.pallas import tpu as pltpu
from jax.sharding import PartitionSpec as P

HEAD_SIZE = 128
ATTENTION_WINDOW = 1024
EPS = 1e-06
THETA = 1000000.0

UNIT = 64
WIDE = 128
KEY_BLOCK = 384
HOP = 2
CTX = "ctx"
TP = "tp"
MESH = pl.DeviceIdType.MESH
F32 = jnp.float32
BF16 = jnp.bfloat16
SCALE = HEAD_SIZE ** (-0.5)
EXP2_SCALE = SCALE * 1.4426950408889634
ANY = pl.ANY
VMEM = pltpu.VMEM
DMA = pltpu.SemaphoreType.DMA


def dot_nn(left, right):
    return jnp.dot(left, right, preferred_element_type=F32)


def dot_nt(left, right):
    return lax.dot_general(left, right, (((1,), (1,)), ((), ())), preferred_element_type=F32)


def dot_tn(left, right):
    return lax.dot_general(left, right, (((0,), (0,)), ((), ())), preferred_element_type=F32)


def rms_inverse(value_rows):
    return lax.rsqrt(jnp.mean(value_rows * value_rows, axis=-1, keepdims=True) + EPS)


def rotate(value_rows, cosine, sine):
    return value_rows * cosine + pltpu.roll(value_rows, HEAD_SIZE // 2, 1) * sine


def unrotate(grad, cosine, sine):
    return grad * cosine + pltpu.roll(grad * sine, HEAD_SIZE // 2, 1)


def norm_back(grad, unit, inverse, gain):
    scaled = grad * gain
    inner = jnp.mean(scaled * unit, axis=-1, keepdims=True)
    return inverse * (scaled - unit * inner)


def column_sum(value_rows):
    return jnp.sum(value_rows, axis=0, keepdims=True)


def make_tables(lengths, rows):
    start = lax.axis_index(CTX) * rows
    spot = start + jnp.arange(rows, dtype=jnp.int32)
    passed = jnp.cumsum(lengths)[None, :] <= spot[:, None]
    begin = jnp.sum(jnp.where(passed, lengths[None, :], 0), axis=1)
    half = HEAD_SIZE // 2
    freq = THETA ** (-(jnp.arange(half, dtype=F32) * 2.0) / HEAD_SIZE)
    angle = (spot - begin).astype(F32)[:, None] * freq[None, :]
    cosine, sine = jnp.cos(angle), jnp.sin(angle)
    lowest = jnp.maximum(begin, spot - (ATTENTION_WINDOW - 1)) - (start - ATTENTION_WINDOW)
    return types.SimpleNamespace(
        cosine=jnp.concatenate([cosine, cosine], axis=1),
        sine=jnp.concatenate([-sine, sine], axis=1),
        lowest=lowest[:, None],
    )


def halo_plan(rows):
    reach = -(-ATTENTION_WINDOW // rows)
    plan = []
    for hop in range(1, reach + 1):
        need = min(rows, ATTENTION_WINDOW - (hop - 1) * rows)
        plan.append((hop, need, ATTENTION_WINDOW - (hop - 1) * rows - need))
    return plan


def unit_rows(u):
    return pl.ds(pl.multiple_of(u * UNIT, UNIT), UNIT)


def wide_rows(w):
    return pl.ds(pl.multiple_of(w * WIDE, WIDE), WIDE)


def subs(w):
    return [w * (WIDE // UNIT) + i for i in range(WIDE // UNIT)]


def shaped(*shape, kind=BF16):
    return jax.ShapeDtypeStruct(shape, kind)


def listed(value):
    return list(value) if isinstance(value, list) else [value]


def run_kernel(body, ins, outs, scratch, collective_id):
    groups = [ins, outs, scratch]
    flat = [[x for value in group.values() for x in listed(value)] for group in groups]

    def named(values, chosen):
        values = list(values)
        found = {}
        for group in chosen:
            for name, value in group.items():
                if isinstance(value, list):
                    found[name] = [values.pop(0) for unused in value]
                else:
                    found[name] = values.pop(0)
        return types.SimpleNamespace(**found)

    results = pl.pallas_call(
        lambda *refs: body(named(refs, groups)),
        out_shape=[shape for shape, unused in flat[1]],
        in_specs=[pl.BlockSpec(memory_space=space) for unused, space in flat[0]],
        out_specs=[pl.BlockSpec(memory_space=space) for unused, space in flat[1]],
        scratch_shapes=flat[2],
        compiler_params=pltpu.CompilerParams(
            collective_id=collective_id, has_side_effects=True, vmem_limit_bytes=62 * 2**20
        ),
    )(*[array for array, unused in flat[0]])
    return named(results, [outs])


def place():
    return lax.axis_index(CTX), lax.axis_index(TP)


def remote(source, target, send, receive, device):
    return pltpu.make_async_remote_copy(
        src_ref=source,
        dst_ref=target,
        send_sem=send,
        recv_sem=receive,
        device_id=device,
        device_id_type=MESH,
    )


def greet(partners):
    barrier = pltpu.get_barrier_semaphore()
    total = 0
    for exists, device in partners:
        total = total + jnp.where(exists, 1, 0)

        @pl.when(exists)
        def _():
            pl.semaphore_signal(barrier, inc=1, device_id=device, device_id_type=MESH)

    pl.semaphore_wait(barrier, total)


def line_partners():
    c, t = place()
    outer = (t == 0) | (t == 3)
    return [
        (outer, (c, jnp.where(t == 0, 1, 2))),
        (jnp.logical_not(outer), (c, jnp.where(t == 1, 0, 3))),
        (jnp.logical_not(outer), (c, jnp.clip(3 - t, 1, 2))),
    ]


def halo_partners(rows, count):
    c, t = place()
    partners = []
    for hop, unused, unused_too in halo_plan(rows):
        partners.append((c + hop < count, (jnp.minimum(c + hop, count - 1), t)))
        partners.append((c >= hop, (jnp.maximum(c - hop, 0), t)))
    return partners


class LineSum:
    def __init__(self, refs):
        self.part, self.total, self.inner, self.sems = refs
        self.c, self.t = place()
        self.outer = (self.t == 0) | (self.t == 3)
        self.is_inner = jnp.logical_not(self.outer)

    def copy(self, source, target, u, send, receive, to):
        return remote(
            source.at[u],
            target.at[u],
            self.sems.at[send, u],
            self.sems.at[receive, u],
            (self.c, to),
        )

    def inwards(self, u):
        return self.copy(self.part, self.total, u, 0, 1, jnp.where(self.t < 2, 1, 2))

    def across(self, u):
        return self.copy(self.part, self.inner, u, 0, 2, jnp.clip(3 - self.t, 1, 2))

    def outwards(self, u):
        return self.copy(self.total, self.total, u, 3, 4, jnp.where(self.t < 2, 0, 3))

    def push(self, w, value):
        for i, u in enumerate(subs(w)):
            self.part[u] = value[i * UNIT : (i + 1) * UNIT].astype(BF16)

        @pl.when(self.outer)
        def _():
            for u in subs(w):
                self.inwards(u).start()

    def meet(self, u):
        @pl.when(self.is_inner)
        def _():
            self.inwards(u).wait_recv()
            self.part[u] = (self.part[u].astype(F32) + self.total[u].astype(F32)).astype(BF16)
            self.across(u).start()

    def spread(self, u):
        @pl.when(self.is_inner)
        def _():
            self.across(u).wait_recv()
            self.total[u] = (self.part[u].astype(F32) + self.inner[u].astype(F32)).astype(BF16)
            self.outwards(u).start()

    def take(self, u):
        @pl.when(self.outer)
        def _():
            self.outwards(u).wait_recv()

        return self.total[u].astype(F32)

    def take_wide(self, w):
        return jnp.concatenate([self.take(u) for u in subs(w)], axis=0)

    def finish(self, u):
        @pl.when(self.outer)
        def _():
            self.inwards(u).wait_send()

        @pl.when(self.is_inner)
        def _():
            self.across(u).wait_send()
            self.outwards(u).wait_send()

    def stages(self, begin, hop=HOP):
        return [(begin + 2 * hop, self.spread, 1), (begin + hop, self.meet, 1)]


def line_scratch(units, width):
    block = VMEM((units, UNIT, width), BF16)
    return [block, block, block, DMA((5, units))]


def pipeline(units, stages, tasks=()):
    steps = units + max(delay + 1 - taken for delay, unused, taken in stages)

    def step(s, carry):
        for delay, function, taken in stages:
            ready = (s >= delay) & (s < units + delay)
            if taken > 1:
                ready = ready & ((s - delay) % taken == 0)

            @pl.when(ready)
            def _():
                function((s - delay) // taken if taken > 1 else s - delay)

        for at, task in tasks:
            if at < steps:

                @pl.when(s == at)
                def _():
                    task()

        return carry

    lax.fori_loop(0, steps, step, 0)
    for at, task in tasks:
        if at >= steps:
            task()


def each_of(number, function):
    def step(u, carry):
        function(u)
        return carry

    lax.fori_loop(0, number, step, 0)


class Loads:
    def __init__(self, sems):
        self.sems, self.number = sems, 0

    def __call__(self, source, target):
        copy = pltpu.make_async_copy(source, target, self.sems.at[self.number])
        copy.start()
        self.number += 1
        return copy


def wait_all(*copies):
    for copy in copies:
        copy.wait()


class Stores:
    def __init__(self, sems):
        self.sems, self.copies = sems, []

    def __call__(self, source, target):
        index = len(self.copies)

        def copy(u):
            rows = unit_rows(u)
            return pltpu.make_async_copy(source.at[rows], target.at[rows], self.sems.at[index, u])

        self.copies.append(copy)
        return copy

    def finish(self, u):
        for copy in self.copies:
            copy(u).wait()


def send_out(units, *copies):
    for u in units:
        for copy in copies:
            copy(u).start()


class Halo:
    def __init__(self, keys, sems, rows, count):
        self.keys, self.sems, self.rows, self.count = keys, sems, rows, count
        self.plan = halo_plan(rows)
        self.c, self.t = place()

    def copy(self, index, u, hop, need, offset):
        target = pl.multiple_of(offset + u * UNIT - (self.rows - need), UNIT)
        return remote(
            self.keys.at[pl.ds(pl.multiple_of(ATTENTION_WINDOW + u * UNIT, UNIT), UNIT)],
            self.keys.at[pl.ds(target, UNIT)],
            self.sems.at[2 * index, u],
            self.sems.at[2 * index + 1, u],
            (jnp.minimum(self.c + hop, self.count - 1), self.t),
        )

    def each(self, u, function, receives):
        for index, (hop, need, offset) in enumerate(self.plan):
            exists = self.c >= hop if receives else self.c + hop < self.count

            @pl.when(exists & (u >= (self.rows - need) // UNIT))
            def _():
                function(self.copy(index, u, hop, need, offset))

    def blank(self):
        width = self.keys.shape[1]
        for hop, need, offset in self.plan:

            @pl.when(self.c < hop)
            def _():
                self.keys[offset : offset + need] = jnp.zeros((need, width), BF16)

    def send(self, u):
        self.each(u, lambda copy: copy.start(), False)

    def finish(self, u):
        self.each(u, lambda copy: copy.wait_recv(), True)
        self.each(u, lambda copy: copy.wait_send(), False)


def project(n, first, number, stream, layer):
    rows = pl.ds(pl.multiple_of(first, number), number)
    own = pl.ds(pl.multiple_of(ATTENTION_WINDOW + first, number), number)
    normed = (stream * rms_inverse(stream) * n.attn_gain[layer : layer + 1]).astype(BF16)
    n.a1_v[rows] = normed
    key = dot_nn(normed, n.wk_v[...])
    query = dot_nn(normed, n.wq_v[...])
    n.qraw_v[rows] = query
    n.kraw_v[rows] = key
    cosine, sine = n.cosine[rows], n.sine[rows]
    for raw, out, out_rows, which in ((key, n.kv_v, own, 1), (query, n.q_v, rows, 0)):
        gain = n.qk_gain[layer, which : which + 1]
        for head in range(raw.shape[1] // HEAD_SIZE):
            cols = slice(head * HEAD_SIZE, (head + 1) * HEAD_SIZE)
            part = raw[:, cols]
            part = part * rms_inverse(part) * gain
            out[out_rows, cols] = rotate(part, cosine, sine).astype(BF16)
    n.kv_v[own, key.shape[1] :] = dot_nn(normed, n.wv_v[...]).astype(BF16)


def project_shapes(s):
    return dict(
        a1=((s.rows, s.model), BF16),
        qraw=((s.rows, s.queries), F32),
        kraw=((s.rows, s.keys), F32),
        q=((s.rows, s.queries), BF16),
        kv=((ATTENTION_WINDOW + s.rows, 2 * s.keys), BF16),
    )


def outputs(shapes):
    return {x: (shaped(*shape, kind=kind), ANY) for x, (shape, kind) in shapes.items()}


def buffers(shapes):
    return {x + "_v": VMEM(shape, kind) for x, (shape, kind) in shapes.items()}


def project_ins(w, tables):
    return dict(
        attn_gain=(w.attn_gain, VMEM),
        qk_gain=(w.qk_gain, VMEM),
        cosine=(tables.cosine, VMEM),
        sine=(tables.sine, VMEM),
        wq=(w.w_query, ANY),
        wk=(w.key_weight, ANY),
        wv=(w.value_weight, ANY),
    )


def project_scratch(s):
    return buffers(project_shapes(s)) | dict(
        wq_v=VMEM((s.model, s.queries), BF16),
        wk_v=VMEM((s.model, s.keys), BF16),
        wv_v=VMEM((s.model, s.keys), BF16),
        halo_sems=DMA((2 * len(halo_plan(s.rows)), s.units)),
    )


def first_projection(stream, w, tables, s):
    def body(n):
        loads = Loads(n.load_sems)
        weights = (
            loads(n.wk.at[0], n.wk_v),
            loads(n.wv.at[0], n.wv_v),
            loads(n.wq.at[0], n.wq_v),
        )
        stores = Stores(n.store_sems)
        made = (
            stores(n.a1_v, n.a1),
            stores(n.qraw_v, n.qraw),
            stores(n.kraw_v, n.kraw),
            stores(n.q_v, n.q),
        )
        halo = Halo(n.kv_v, n.halo_sems, s.rows, s.count)
        greet(halo_partners(s.rows, s.count))
        halo.blank()
        wait_all(*weights)

        def each(i):
            project(n, i * WIDE, WIDE, n.x[wide_rows(i)].astype(F32), 0)
            for u in subs(i):
                halo.send(u)
            send_out(subs(i), *made)

        each_of(s.rows // WIDE, each)
        each_of(s.units, halo.finish)
        keys = loads(n.kv_v, n.kv)
        each_of(s.units, stores.finish)
        keys.wait()

    return run_kernel(
        body,
        dict(x=(stream, VMEM)) | project_ins(w, tables),
        outputs(project_shapes(s)),
        project_scratch(s) | dict(load_sems=DMA((4,)), store_sems=DMA((4, s.units))),
        1,
    )


def key_block(i, block):
    return pl.ds(pl.multiple_of(i * WIDE + block * KEY_BLOCK, HEAD_SIZE), KEY_BLOCK)


def visible(i, lowest, block, repeat):
    shape = (WIDE, KEY_BLOCK)
    col = block * KEY_BLOCK + lax.broadcasted_iota(jnp.int32, shape, 1)
    seen = col >= lowest - i * WIDE
    if (block + 1) * KEY_BLOCK > ATTENTION_WINDOW:
        row = ATTENTION_WINDOW + lax.broadcasted_iota(jnp.int32, shape, 0)
        seen = seen & (col <= row)
    keep = jnp.where(seen, 1.0, 0.0)
    return jnp.concatenate([keep] * repeat, axis=0)


def key_blocks():
    return (ATTENTION_WINDOW + WIDE) // KEY_BLOCK


def stacked(value, group, repeat):
    first = group * repeat
    return jnp.concatenate(
        [value[:, (first + r) * HEAD_SIZE : (first + r + 1) * HEAD_SIZE] for r in range(repeat)],
        axis=0,
    )


def head_cols(index):
    return slice(index * HEAD_SIZE, (index + 1) * HEAD_SIZE)


def attend(n, i, s):
    rows = wide_rows(i)
    lowest = n.lowest[rows]
    lane = lax.broadcasted_iota(jnp.int32, (WIDE, HEAD_SIZE), 1)
    query_rows = n.qin_v[rows]
    queries = [stacked(query_rows, g, s.repeat) for g in range(s.groups)]
    mixed = [jnp.zeros((s.repeat * WIDE, HEAD_SIZE), F32) for unused in queries]
    total = [jnp.zeros((s.repeat * WIDE, 1), F32) for unused in queries]
    for block in range(key_blocks()):
        keys = key_block(i, block)
        keep = visible(i, lowest, block, s.repeat)
        for g in range(s.groups):
            scores = dot_nt(queries[g], n.kvin_v[keys, head_cols(g)])
            weights = jnp.exp2(scores * EXP2_SCALE) * keep
            total[g] = total[g] + jnp.sum(weights, axis=-1, keepdims=True)
            values = n.kvin_v[keys, head_cols(s.groups + g)]
            mixed[g] = mixed[g] + dot_nn(weights.astype(BF16), values)
    inverses = jnp.zeros((WIDE, HEAD_SIZE), F32)
    for g in range(s.groups):
        inverse = 1.0 / total[g]
        result = (mixed[g] * inverse).astype(BF16)
        for r in range(s.repeat):
            head = g * s.repeat + r
            part = slice(r * WIDE, (r + 1) * WIDE)
            n.o_v[rows, head_cols(head)] = result[part]
            inverses = jnp.where(lane == head, inverse[part], inverses)
    n.inv_v[rows] = inverses


def attend_back(n, i, grad_out, keys_ref, query_ref, s):
    rows = wide_rows(i)
    lowest = n.lowest[rows]
    query_rows, mixed_rows, inverses = query_ref[rows], n.o_v[rows], n.inv_v[rows]
    queries, grads, inners, scales, found = [], [], [], [], []
    for g in range(s.groups):
        queries.append(stacked(query_rows, g, s.repeat))
        grads.append(stacked(grad_out, g, s.repeat))
        mixed = stacked(mixed_rows, g, s.repeat)
        inners.append(
            jnp.sum(grads[g].astype(F32) * mixed.astype(F32), axis=-1, keepdims=True)
        )
        heads = [g * s.repeat + r for r in range(s.repeat)]
        scales.append(jnp.concatenate([inverses[:, h : h + 1] for h in heads], axis=0))
        found.append(jnp.zeros((s.repeat * WIDE, HEAD_SIZE), F32))
    for block in range(key_blocks()):
        keys = key_block(i, block)
        keep = visible(i, lowest, block, s.repeat)
        for g in range(s.groups):
            key_rows = keys_ref[keys, head_cols(g)]
            scores = dot_nt(queries[g], key_rows)
            probs = jnp.exp2(scores * EXP2_SCALE) * (keep * scales[g])
            grad_probs = dot_nt(grads[g], keys_ref[keys, head_cols(s.groups + g)])
            grad_scores = (probs * (grad_probs - inners[g])).astype(BF16)
            found[g] = found[g] + dot_nn(grad_scores, key_rows)
            n.dkv_v[keys, head_cols(g)] += dot_tn(grad_scores, queries[g])
            n.dkv_v[keys, head_cols(s.groups + g)] += dot_tn(probs.astype(BF16), grads[g])
    return [
        found[g][r * WIDE : (r + 1) * WIDE] for g in range(s.groups) for r in range(s.repeat)
    ]


def head_back(n, rows, grad, raw, which, layer):
    gain = n.qk_gain[layer, which : which + 1]
    turned = unrotate(grad, n.cosine[rows], n.sine[rows])
    inverse = rms_inverse(raw)
    unit = raw * inverse
    n.qk_sum[which : which + 1] += column_sum(turned * unit)
    return norm_back(turned, unit, inverse, gain).astype(BF16)


class Returns:
    def __init__(self, n, s):
        self.grads, self.low, self.back, self.sems = n.dkv_v, n.low_v, n.back_v, n.return_sems
        self.s, self.plan = s, halo_plan(s.rows)
        self.c, self.t = place()
        self.blocks = []
        for index, (hop, need, offset) in enumerate(self.plan):
            for b in range(need // WIDE):
                self.blocks.append((index, hop, offset + b * WIDE, b * WIDE))
        self.blocks.sort(key=lambda item: item[2])

    def copy(self, number):
        index, hop, source, target = self.blocks[number]
        return remote(
            self.low.at[pl.ds(source, WIDE)],
            self.back[index].at[pl.ds(target, WIDE)],
            self.sems.at[0, number],
            self.sems.at[1, number],
            (jnp.maximum(self.c - hop, 0), self.t),
        )

    def blank(self):
        for index, (hop, need, unused) in enumerate(self.plan):

            @pl.when(self.c + hop >= self.s.count)
            def _():
                self.back[index][...] = jnp.zeros((need, self.low.shape[1]), BF16)

    def send(self, number):
        rows = pl.ds(self.blocks[number][2], WIDE)

        @pl.when(self.c >= self.blocks[number][1])
        def _():
            self.low[rows] = self.grads[rows].astype(BF16)
            self.copy(number).start()

    def send_complete(self, i):
        for number, block in enumerate(self.blocks):
            if block[2] // WIDE < self.s.rows // WIDE - 1:

                @pl.when(i == block[2] // WIDE)
                def _():
                    self.send(number)

    def send_rest(self):
        for number, block in enumerate(self.blocks):
            if block[2] // WIDE >= self.s.rows // WIDE - 1:
                self.send(number)

    def receive(self):
        for number, block in enumerate(self.blocks):

            @pl.when(self.c + block[1] < self.s.count)
            def _():
                self.copy(number).wait_recv()

    def finish(self):
        for number, block in enumerate(self.blocks):

            @pl.when(self.c >= block[1])
            def _():
                self.copy(number).wait_send()


def attention_back_scratch(s):
    plan = halo_plan(s.rows)
    return dict(
        dkv_v=VMEM((ATTENTION_WINDOW + s.rows, 2 * s.keys), F32),
        low_v=VMEM((ATTENTION_WINDOW, 2 * s.keys), BF16),
        back_v=[VMEM((need, 2 * s.keys), BF16) for unused, need, unused_too in plan],
        total_v=VMEM((WIDE, 2 * s.keys), F32),
        return_sems=DMA((2, ATTENTION_WINDOW // WIDE)),
    )


def attention_back_shapes(s):
    return dict(
        dyb=((s.rows, s.model), BF16),
        dgate=((s.rows, s.hidden), BF16),
        dup=((s.rows, s.hidden), BF16),
        dhb=((s.rows, s.model), BF16),
        dq=((s.rows, s.queries), BF16),
        dk=((s.rows, s.keys), BF16),
        dv=((s.rows, s.keys), BF16),
    )


def attention_back_outs(s):
    return outputs(attention_back_shapes(s)) | dict(
        dres=(shaped(s.rows, s.model, kind=F32), ANY),
        ffn_sum=(shaped(1, s.model, kind=F32), VMEM),
        qk_sum=(shaped(2, HEAD_SIZE, kind=F32), VMEM),
    )


def back_start(n, returns):
    returns.blank()
    n.dkv_v[...] = jnp.zeros_like(n.dkv_v)
    n.ffn_sum[...] = jnp.zeros_like(n.ffn_sum)
    n.qk_sum[...] = jnp.zeros_like(n.qk_sum)


def feed_back(n, i, gate, up, lower, made):
    here = wide_rows(i)
    low = n.g_v[here].astype(BF16)
    n.dyb_v[here] = low
    grad_hidden = dot_nt(low, n.wd_v[...])
    sigma = jax.nn.sigmoid(gate)
    dgate = (grad_hidden * up * (sigma * (1.0 + gate * (1.0 - sigma)))).astype(BF16)
    dup = (grad_hidden * gate * sigma).astype(BF16)
    n.dgate_v[here] = dgate
    n.dup_v[here] = dup
    lower.push(i, dot_nt(dgate, n.wg_v[...]) + dot_nt(dup, n.wu_v[...]))
    send_out(subs(i), *made)


def attention_back(n, i, middle, keys_ref, query_ref, layer, lower, returns, made, s):
    here = wide_rows(i)
    grad_in = lower.take_wide(i)
    inverse = rms_inverse(middle)
    unit = middle * inverse
    n.ffn_sum[...] += column_sum(grad_in * unit)
    total = n.g_v[here] + norm_back(grad_in, unit, inverse, n.ffn_gain[layer : layer + 1])
    n.g_v[here] = total
    low = total.astype(BF16)
    n.dhb_v[here] = low
    grad_out = dot_nt(low, n.wo_v[...]).astype(BF16)
    pieces = attend_back(n, i, grad_out, keys_ref, query_ref, s)
    returns.send_complete(i)
    for head, piece in enumerate(pieces):
        n.dq_v[here, head_cols(head)] = head_back(
            n, here, piece * SCALE, n.qraw_v[here, head_cols(head)], 0, layer
        )
    send_out(subs(i), *made)


def keys_back(n, layer, returns, made, s):
    def each(i):
        here = wide_rows(i)
        own = pl.ds(pl.multiple_of(ATTENTION_WINDOW + i * WIDE, WIDE), WIDE)
        n.total_v[...] = n.dkv_v[own]
        for index, (hop, need, unused) in enumerate(returns.plan):
            skipped = s.rows - need

            @pl.when(i >= skipped // WIDE)
            def _():
                part = pl.ds(pl.multiple_of(i * WIDE - skipped, WIDE), WIDE)
                n.total_v[...] += n.back_v[index][part].astype(F32)

        for g in range(s.groups):
            n.dk_v[here, head_cols(g)] = head_back(
                n, here, n.total_v[:, head_cols(g)] * SCALE, n.kraw_v[here, head_cols(g)], 1, layer
            )
        n.dv_v[here] = n.total_v[:, s.keys :].astype(BF16)
        send_out(subs(i), *made)

    each_of(s.rows // WIDE, each)


def feed(n, i, middle, layer):
    here = wide_rows(i)
    normed = (middle * rms_inverse(middle) * n.ffn_gain[layer : layer + 1]).astype(BF16)
    n.a2_v[here] = normed
    gate = dot_nn(normed, n.wg_v[...])
    up = dot_nn(normed, n.wu_v[...])
    inside = (gate * jax.nn.sigmoid(gate) * up).astype(BF16)
    n.hidden_v[here] = inside
    return gate, up, dot_nn(inside, n.wd_v[...])


def layer_ins(stream, saved, w, tables):
    return dict(
        x=(stream, ANY),
        qin=(saved.q, ANY),
        kvin=(saved.kv, ANY),
        ffn_gain=(w.ffn_gain, VMEM),
        lowest=(tables.lowest, VMEM),
        wo=(w.w_out, ANY),
        wg=(w.w_gate, ANY),
        wu=(w.w_up, ANY),
        wd=(w.w_down, ANY),
    )


def weight_scratch(s):
    return dict(
        wo_v=VMEM((s.queries, s.model), BF16),
        wg_v=VMEM((s.model, s.hidden), BF16),
        wu_v=VMEM((s.model, s.hidden), BF16),
        wd_v=VMEM((s.hidden, s.model), BF16),
    )


def layer_scratch(stream, s):
    return weight_scratch(s) | dict(
        x_v=VMEM((s.rows, s.model), stream.dtype),
        qin_v=VMEM((s.rows, s.queries), BF16),
        kvin_v=VMEM((ATTENTION_WINDOW + s.rows, 2 * s.keys), BF16),
        load_sems=DMA((16,)),
        store_sems=DMA((16, s.units)),
        first=line_scratch(s.units, s.model),
        second=line_scratch(s.units, s.model),
    )


def layer_loads(n, loads, layer):
    early = (
        loads(n.qin, n.qin_v),
        loads(n.kvin, n.kvin_v),
        loads(n.wo.at[layer], n.wo_v),
    )
    late = (
        loads(n.x, n.x_v),
        loads(n.wg.at[layer], n.wg_v),
        loads(n.wu.at[layer], n.wu_v),
        loads(n.wd.at[layer], n.wd_v),
    )
    return early, late


def kept_shapes(s):
    return dict(
        o=((s.rows, s.queries), BF16),
        a2=((s.rows, s.model), BF16),
        hidden=((s.rows, s.hidden), BF16),
    )


def forward_shapes(s):
    return kept_shapes(s) | dict(
        inv=((s.rows, HEAD_SIZE), F32),
        h=((s.rows, s.model), F32),
        gate=((s.rows, s.hidden), BF16),
        up=((s.rows, s.hidden), BF16),
        y=((s.rows, s.model), F32),
    )


def forward_layer(layer, stream, saved, w, tables, s):
    def body(n):
        loads = Loads(n.load_sems)
        early, late = layer_loads(n, loads, layer)
        above = (
            loads(n.wq.at[layer + 1], n.wq_v),
            loads(n.wk.at[layer + 1], n.wk_v),
            loads(n.wv.at[layer + 1], n.wv_v),
        )
        stores = Stores(n.store_sems)
        mixed = (stores(n.o_v, n.o), stores(n.inv_v, n.inv))
        fed = (
            stores(n.h_v, n.h),
            stores(n.a2_v, n.a2),
            stores(n.hidden_v, n.hidden),
            stores(n.gate_v, n.gate),
            stores(n.up_v, n.up),
        )
        closed = (
            stores(n.y_v, n.y),
            stores(n.a1_v, n.a1),
            stores(n.qraw_v, n.qraw),
            stores(n.kraw_v, n.kraw),
            stores(n.q_v, n.q),
        )
        first, second = LineSum(n.first), LineSum(n.second)
        halo = Halo(n.kv_v, n.halo_sems, s.rows, s.count)
        greet(line_partners() + halo_partners(s.rows, s.count))
        halo.blank()
        wait_all(*early)

        def mix(i):
            attend(n, i, s)
            first.push(i, dot_nn(n.o_v[wide_rows(i)], n.wo_v[...]))
            send_out(subs(i), *mixed)

        def feed_wide(i):
            pl.when(i == 0)(lambda: wait_all(*late))
            here = wide_rows(i)
            middle = n.x_v[here].astype(F32) + first.take_wide(i)
            n.h_v[here] = middle
            gate, up, part = feed(n, i, middle, layer)
            second.push(i, part)
            n.gate_v[here] = gate.astype(BF16)
            n.up_v[here] = up.astype(BF16)
            send_out(subs(i), *fed)

        def close(u):
            pl.when(u == 0)(lambda: wait_all(*above))
            here = unit_rows(u)
            result = n.h_v[here] + second.take(u)
            n.y_v[here] = result
            project(n, u * UNIT, UNIT, result, layer + 1)
            halo.send(u)
            send_out([u], *closed)

        at = 3 * HOP + 1
        pipeline(
            s.units,
            second.stages(at)
            + first.stages(0)
            + [(at + 3 * HOP, close, 1), (at, feed_wide, WIDE // UNIT), (0, mix, WIDE // UNIT)],
        )
        each_of(s.units, halo.finish)
        keys = loads(n.kv_v, n.kv)

        def finish(u):
            first.finish(u)
            second.finish(u)
            stores.finish(u)

        each_of(s.units, finish)
        keys.wait()

    return run_kernel(
        body,
        layer_ins(stream, saved, w, tables) | project_ins(w, tables),
        outputs(forward_shapes(s)) | outputs(project_shapes(s)),
        layer_scratch(stream, s) | buffers(forward_shapes(s)) | project_scratch(s),
        2 + layer,
    )


def turn_layer(layer, stream, saved, cotangent, w, tables, s):
    def body(n):
        loads = Loads(n.load_sems)
        early, late = layer_loads(n, loads, layer)
        late = late + (loads(n.grad, n.grad_v),)
        raws = (loads(n.qraw, n.qraw_v), loads(n.kraw, n.kraw_v))
        stores = Stores(n.store_sems)
        mixed = (stores(n.o_v, n.o),)
        fed = (stores(n.a2_v, n.a2), stores(n.hidden_v, n.hidden))
        fed_back = (stores(n.dyb_v, n.dyb), stores(n.dgate_v, n.dgate), stores(n.dup_v, n.dup))
        closed = (stores(n.y_v, n.y),)
        turned = (stores(n.g_v, n.dres), stores(n.dhb_v, n.dhb), stores(n.dq_v, n.dq))
        keyed = (stores(n.dk_v, n.dk), stores(n.dv_v, n.dv))
        first, second, lower = LineSum(n.first), LineSum(n.second), LineSum(n.lower)
        returns = Returns(n, s)
        greet(line_partners() + halo_partners(s.rows, s.count))
        back_start(n, returns)
        wait_all(*early)

        def mix(i):
            attend(n, i, s)
            first.push(i, dot_nn(n.o_v[wide_rows(i)], n.wo_v[...]))
            send_out(subs(i), *mixed)

        def feed_both(i):
            pl.when(i == 0)(lambda: wait_all(*late))
            here = wide_rows(i)
            middle = n.x_v[here] + first.take_wide(i)
            n.x_v[here] = middle
            n.g_v[here] = n.grad_v[here].astype(F32)
            gate, up, part = feed(n, i, middle, layer)
            feed_back(n, i, gate, up, lower, fed_back)
            second.push(i, part)
            send_out(subs(i), *fed)

        def close(u):
            here = unit_rows(u)
            n.y_v[here] = (n.x_v[here] + second.take(u)).astype(BF16)
            send_out([u], *closed)

        def attention(i):
            pl.when(i == 0)(lambda: wait_all(*raws))
            middle = n.x_v[wide_rows(i)]
            attention_back(
                n, i, middle, n.kvin_v, n.qin_v, layer, lower, returns, turned, s
            )

        at = 3 * HOP + 1
        pipeline(
            s.units,
            lower.stages(at)
            + second.stages(at, HOP + 1)
            + first.stages(0)
            + [
                (at + 3 * HOP + 3, close, 1),
                (at + 3 * HOP + 1, attention, WIDE // UNIT),
                (at, feed_both, WIDE // UNIT),
                (0, mix, WIDE // UNIT),
            ],
        )
        returns.send_rest()
        returns.receive()
        keys_back(n, layer, returns, keyed, s)
        returns.finish()

        def finish(u):
            first.finish(u)
            second.finish(u)
            lower.finish(u)
            stores.finish(u)

        each_of(s.units, finish)

    shapes = kept_shapes(s) | dict(y=((s.rows, s.model), BF16))
    return run_kernel(
        body,
        layer_ins(stream, saved, w, tables)
        | dict(
            grad=(cotangent, ANY),
            qraw=(saved.qraw, ANY),
            kraw=(saved.kraw, ANY),
            qk_gain=(w.qk_gain, VMEM),
            cosine=(tables.cosine, VMEM),
            sine=(tables.sine, VMEM),
        ),
        outputs(shapes) | attention_back_outs(s),
        layer_scratch(stream, s)
        | buffers(shapes)
        | buffers(attention_back_shapes(s))
        | attention_back_scratch(s)
        | dict(
            inv_v=VMEM((s.rows, HEAD_SIZE), F32),
            grad_v=VMEM((s.rows, s.model), BF16),
            g_v=VMEM((s.rows, s.model), F32),
            qraw_v=VMEM((s.rows, s.queries), F32),
            kraw_v=VMEM((s.rows, s.keys), F32),
            lower=line_scratch(s.units, s.model),
        ),
        2 + layer,
    )


def halving_partners(count):
    c, t = place()
    return [(c >= 0, (c ^ (1 << b), t)) for b in range(count.bit_length() - 1)]


class Scatter:
    def __init__(self, n, s, sizes, factors=None):
        self.n, self.s, self.sizes, self.factors = n, s, sizes, factors
        self.bits = s.count.bit_length() - 1
        self.c, self.t = place()
        self.loads = []

    def bit(self, b):
        return (self.c >> b) & 1

    def order(self, index):
        rest = list(range(1, self.bits))
        return [0] + (rest if index % 2 == 0 else rest[::-1])

    def spot(self, picks):
        low = 0 if self.factors else 1
        return tuple(picks.get(b, slice(None)) for b in range(self.bits - 1, low - 1, -1))

    def own(self, index):
        return (self.n.whole_v if self.factors else self.n.own)[index]

    def copy(self, index, step):
        order = self.order(index)
        picks = {b: self.bit(b) for b in order[:step]}
        picks[order[step]] = 1 - self.bit(order[step])
        if step == 0 and not self.factors:
            source = self.n.whole[index].at[
                (slice(None),) * (self.bits - 1) + (1 - self.bit(0),)
            ]
        else:
            source = self.own(index).at[self.spot(picks)]
        sems = self.n.scatter_sems
        return remote(
            source,
            self.n.got[index * self.bits + step],
            sems.at[0, index, step],
            sems.at[1, index, step],
            (self.c ^ (1 << order[step]), self.t),
        )

    def load(self, index):
        return pltpu.make_async_copy(
            self.n.whole[index].at[(slice(None),) * (self.bits - 1) + (self.bit(0),)],
            self.n.own[index],
            self.n.scatter_load_sems.at[index],
        )

    def start(self, index):
        if self.factors:
            left, right, needed = self.factors[index]
            wait_all(*needed)
            line = self.sizes[index][0]
            half = self.s.count // 2
            for part in range(2):
                product = dot_tn(left[:, part * half * line : (part + 1) * half * line], right[...])
                for k in range(half):
                    block = part * half + k
                    at = tuple((block >> b) & 1 for b in range(self.bits - 1, -1, -1))
                    self.own(index)[at + (slice(0, line),)] = product[
                        k * line : (k + 1) * line
                    ].astype(BF16)
        else:
            self.load(index).start()
        self.copy(index, 0).start()

    def add(self, index, step):
        order = self.order(index)
        if step == 0 and not self.factors:
            self.load(index).wait()
        self.copy(index, step).wait_recv()
        free = [b for b in range(self.bits - 1, 0, -1) if b not in order[: step + 1]]
        own, got = self.own(index), self.n.got[index * self.bits + step]
        line = self.sizes[index][0]

        def one(k, carry):
            picks = {b: (k >> (len(free) - 1 - i)) & 1 for i, b in enumerate(free)}
            here = self.spot({b: self.bit(b) for b in order[: step + 1]} | picks)
            total = own[here].astype(F32) + got[tuple(picks[b] for b in free)].astype(F32)
            if step == self.bits - 1:
                self.n.sums_v[index][...] = total[:line]
            else:
                own[here] = total.astype(BF16)
            return carry

        if free:
            lax.fori_loop(0, 1 << len(free), one, 0)
        else:
            one(0, 0)
        if step < self.bits - 1:
            self.copy(index, step + 1).start()
        else:
            self.store(index).start()

    def store(self, index):
        target = self.n.sums[index].at[0] if self.factors else self.n.sums[index]
        return pltpu.make_async_copy(
            self.n.sums_v[index], target, self.n.scatter_store_sems.at[index]
        )

    def tasks(self, every, bases):
        found = []
        for index in range(len(self.sizes)):
            found.append((bases[0] + index * every, lambda index=index: self.start(index)))
            for step in range(self.bits):
                at = bases[min(step + 1, len(bases) - 1)] + index * every
                at += 100 * max(0, step + 2 - len(bases))
                found.append((at, lambda index=index, step=step: self.add(index, step)))
        found.sort(key=lambda item: item[0])
        return found

    def finish(self):
        for index in range(len(self.sizes)):
            self.store(index).wait()
            for step in range(self.bits):
                self.copy(index, step).wait_send()


def scatter_scratch(s, sizes, computed):
    bits = s.count.bit_length() - 1
    tails = [(line + -line % 16, width) for line, width in sizes]
    found = dict(
        sums_v=[VMEM(size, F32) for size in sizes],
        got=[
            VMEM((2,) * (bits - 1 - step) + tail, BF16) for tail in tails for step in range(bits)
        ],
        scatter_sems=DMA((2, len(sizes), bits)),
        scatter_load_sems=DMA((len(sizes),)),
        scatter_store_sems=DMA((len(sizes),)),
    )
    if computed:
        return found | dict(whole_v=[VMEM((2,) * bits + tail, BF16) for tail in tails])
    return found | dict(own=[VMEM((2,) * (bits - 1) + tail, BF16) for tail in tails])


def block_view(array, s):
    bits = s.count.bit_length() - 1
    line = array.shape[0] // s.count
    view = array.reshape((2,) * bits + (line, array.shape[1]))
    if line % 16:
        view = jnp.pad(view, [(0, 0)] * bits + [(0, -line % 16), (0, 0)])
    return view


def factor_pairs(k):
    return [
        (k.a2, k.dup),
        (k.a2, k.dgate),
        (k.a1, k.dq),
        (k.hidden, k.dyb),
        (k.o, k.dhb),
        (k.a1, k.dk),
        (k.a1, k.dv),
    ]


def grad_sizes(s):
    return [
        (s.model // s.count, s.hidden),
        (s.model // s.count, s.hidden),
        (s.model // s.count, s.queries),
        (s.hidden // s.count, s.model),
        (s.queries // s.count, s.model),
        (s.model // s.count, s.keys),
        (s.model // s.count, s.keys),
    ]


def head_ins(k, w):
    return dict(
        hq=(k.dq, ANY),
        hk=(k.dk, ANY),
        hv=(k.dv, ANY),
        wq=(w.w_query, ANY),
        wk=(w.key_weight, ANY),
        wv=(w.value_weight, ANY),
        x=(k.x, ANY),
        attn_gain=(w.attn_gain, VMEM),
        grad=(k.dres, ANY),
    )


def head_scratch(k, s):
    return dict(
        hq_v=VMEM((s.rows, s.queries), BF16),
        hk_v=VMEM((s.rows, s.keys), BF16),
        hv_v=VMEM((s.rows, s.keys), BF16),
        wq_v=VMEM((s.model, s.queries), BF16),
        wk_v=VMEM((s.model, s.keys), BF16),
        wv_v=VMEM((s.model, s.keys), BF16),
        x_v=VMEM((s.rows, s.model), k.x.dtype),
        g_v=VMEM((s.rows, s.model), F32),
        upper=line_scratch(s.units, s.model),
        load_sems=DMA((32,)),
        store_sems=DMA((10, s.units)),
    )


def head_loads(n, loads, layer):
    early = (
        loads(n.hq, n.hq_v),
        loads(n.wq.at[layer], n.wq_v),
        loads(n.hk, n.hk_v),
        loads(n.wk.at[layer], n.wk_v),
        loads(n.hv, n.hv_v),
        loads(n.wv.at[layer], n.wv_v),
    )
    return early, (loads(n.x, n.x_v), loads(n.grad, n.g_v))


def head_inputs(n, i, upper):
    here = wide_rows(i)
    upper.push(
        i,
        dot_nt(n.hq_v[here], n.wq_v[...])
        + dot_nt(n.hk_v[here], n.wk_v[...])
        + dot_nt(n.hv_v[here], n.wv_v[...]),
    )


def head_norm(n, here, grad_in, layer):
    stream = n.x_v[here].astype(F32)
    inverse = rms_inverse(stream)
    unit = stream * inverse
    n.attn_sum[...] += column_sum(grad_in * unit)
    n.g_v[here] += norm_back(grad_in, unit, inverse, n.attn_gain[layer : layer + 1])


def backward_layer(layer, kept, w, tables, s):
    above, here_kept = kept[layer + 1], kept[layer]
    sizes = grad_sizes(s)

    def body(n):
        loads = Loads(n.load_sems)
        early, middle_loads = head_loads(n, loads, layer + 1)
        scatter = Scatter(n, s, sizes)
        feeds = (
            loads(n.wd.at[layer], n.wd_v),
            loads(n.gate, n.gate_v),
            loads(n.up, n.up_v),
            loads(n.wg.at[layer], n.wg_v),
            loads(n.wu.at[layer], n.wu_v),
        )
        lates = (
            loads(n.wo.at[layer], n.wo_v),
            loads(n.q, n.q_v),
            loads(n.kv, n.kv_v),
            loads(n.o, n.o_v),
            loads(n.inv, n.inv_v),
            loads(n.qraw, n.qraw_v),
            loads(n.kraw, n.kraw_v),
        )
        stores = Stores(n.store_sems)
        fed_back = (stores(n.dyb_v, n.dyb), stores(n.dgate_v, n.dgate), stores(n.dup_v, n.dup))
        turned = (stores(n.g_v, n.dres), stores(n.dhb_v, n.dhb), stores(n.dq_v, n.dq))
        keyed = (stores(n.dk_v, n.dk), stores(n.dv_v, n.dv))
        upper, lower = LineSum(n.upper), LineSum(n.lower)
        returns = Returns(n, s)
        greet(line_partners() + halo_partners(s.rows, s.count) + halving_partners(s.count))
        n.attn_sum[...] = jnp.zeros_like(n.attn_sum)
        back_start(n, returns)
        wait_all(*early)

        def middle_copy(i):
            rows = wide_rows(i)
            return pltpu.make_async_copy(n.h.at[rows], n.x_v.at[rows], n.middle_sems.at[i])

        def inputs(i):
            head_inputs(n, i, upper)

        def pass_norm(i):
            pl.when(i == 0)(lambda: wait_all(*middle_loads, *feeds))
            here = wide_rows(i)
            head_norm(n, here, upper.take_wide(i), layer + 1)
            middle_copy(i).start()
            gate, up = n.gate_v[here].astype(F32), n.up_v[here].astype(F32)
            feed_back(n, i, gate, up, lower, fed_back)

        def attention(i):
            pl.when(i == 0)(lambda: wait_all(*lates))
            middle_copy(i).wait()
            attention_back(
                n, i, n.x_v[wide_rows(i)], n.kv_v, n.q_v, layer, lower, returns, turned, s
            )

        at = 3 * HOP + 1
        pipeline(
            s.units,
            lower.stages(at)
            + upper.stages(0)
            + [
                (at + 3 * HOP + 1, attention, WIDE // UNIT),
                (at, pass_norm, WIDE // UNIT),
                (0, inputs, WIDE // UNIT),
            ],
            scatter.tasks(1, SCATTER_MIDDLE),
        )
        returns.send_rest()
        returns.receive()
        keys_back(n, layer, returns, keyed, s)
        returns.finish()
        scatter.finish()

        def finish(u):
            upper.finish(u)
            lower.finish(u)
            stores.finish(u)

        each_of(s.units, finish)

    whole = [
        block_view(dot_tn(left, right).astype(BF16), s) for left, right in factor_pairs(above)
    ]
    held = dict(
        gate=here_kept.gate,
        up=here_kept.up,
        q=here_kept.q,
        kv=here_kept.kv,
        o=here_kept.o,
        inv=here_kept.inv,
        qraw=here_kept.qraw,
        kraw=here_kept.kraw,
    )
    return run_kernel(
        body,
        head_ins(above, w)
        | {x: (array, ANY) for x, array in held.items()}
        | dict(
            h=(here_kept.h, ANY),
            wd=(w.w_down, ANY),
            wg=(w.w_gate, ANY),
            wu=(w.w_up, ANY),
            wo=(w.w_out, ANY),
            ffn_gain=(w.ffn_gain, VMEM),
            qk_gain=(w.qk_gain, VMEM),
            cosine=(tables.cosine, VMEM),
            sine=(tables.sine, VMEM),
            lowest=(tables.lowest, VMEM),
            whole=[(array, ANY) for array in whole],
        ),
        attention_back_outs(s)
        | dict(
            attn_sum=(shaped(1, s.model, kind=F32), VMEM),
            sums=[(shaped(*size, kind=F32), ANY) for size in sizes],
        ),
        head_scratch(above, s)
        | weight_scratch(s)
        | {x + "_v": VMEM(array.shape, array.dtype) for x, array in held.items()}
        | buffers(attention_back_shapes(s))
        | attention_back_scratch(s)
        | scatter_scratch(s, sizes, False)
        | dict(
            lower=line_scratch(s.units, s.model),
            middle_sems=DMA((s.rows // WIDE,)),
        ),
        20 + layer,
    )


def backward_end(kept, w, s):
    bottom = kept[0]
    sizes = grad_sizes(s)
    layers = len(kept)
    width = s.model // s.count
    bits = s.count.bit_length() - 1
    tp_bits = s.line.bit_length() - 1
    rounds = [(1 << b, 0) for b in range(bits)] + [(0, 1 << b) for b in range(tp_bits)]

    def body(n):
        c, t = place()
        loads = Loads(n.load_sems)
        early, lates = head_loads(n, loads, 0)
        a2, dup, dgate = loads(n.a2, n.a2_v), loads(n.dup, n.dup_v), loads(n.dgate, n.dgate_v)
        a1, hidden, dyb = loads(n.a1, n.a1_v), loads(n.hidden, n.hidden_v), loads(n.dyb, n.dyb_v)
        o, dhb = loads(n.o, n.o_v), loads(n.dhb, n.dhb_v)
        factors = [
            (n.a2_v, n.dup_v, (a2, dup)),
            (n.a2_v, n.dgate_v, (dgate,)),
            (n.a1_v, n.hq_v, (a1,)),
            (n.hidden_v, n.dyb_v, (hidden, dyb)),
            (n.o_v, n.dhb_v, (o, dhb)),
            (n.a1_v, n.hk_v, ()),
            (n.a1_v, n.hv_v, ()),
        ]
        scatter = Scatter(n, s, sizes, factors)
        stores = Stores(n.store_sems)
        out = stores(n.g_v, n.dres)
        upper = LineSum(n.upper)
        others = [(c >= 0, ((c + k) % s.count, t)) for k in range(1, s.count)]
        lines = [(c >= 0, (c, t ^ (1 << b))) for b in range(tp_bits)]
        greet(line_partners() + halving_partners(s.count) + others + lines)
        n.attn_sum[...] = jnp.zeros_like(n.attn_sum)
        n.acc[...] = jnp.zeros_like(n.acc)
        n.gains[...] = jnp.zeros_like(n.gains)
        for layer in range(layers):
            n.acc[0, 2 * layer : 2 * layer + 2] = n.qk_in[layer][...]
        wait_all(*early)
        above = [
            loads(n.done[(layer - 1) * len(sizes) + index], n.sums[index].at[layer])
            for layer in range(1, layers)
            for index in range(len(sizes))
        ]

        def head_copy(k):
            return remote(
                n.acc.at[k],
                n.other.at[k],
                n.small_sems.at[0, k],
                n.small_sems.at[1, k],
                (c ^ rounds[k][0], t ^ rounds[k][1]),
            )

        def head_step(k):
            if k > 0:
                head_copy(k - 1).wait_recv()
                n.acc[k] = n.acc[k - 1] + n.other[k - 1]
            if k < len(rounds):
                head_copy(k).start()

        def pass_norm(u):
            pl.when(u == 0)(lambda: wait_all(*lates))
            head_norm(n, unit_rows(u), upper.take(u), 0)
            send_out([u], out)

        tasks = scatter.tasks(1, SCATTER_END)
        tasks += [(2 * k + 1, lambda k=k: head_step(k)) for k in range(len(rounds) + 1)]
        tasks.sort(key=lambda item: item[0])
        pipeline(
            s.units,
            upper.stages(0)
            + [
                (3 * HOP, pass_norm, 1),
                (0, lambda i: head_inputs(n, i, upper), WIDE // UNIT),
            ],
            tasks,
        )
        gains = [n.attn_sum] + n.attn_in + n.ffn_in
        for d in range(s.count):
            for row, gain in enumerate(gains):
                n.gains[d, row : row + 1] = gain[:, d * width : (d + 1) * width]

        def gain_copy(k):
            to = (c + k) % s.count
            return remote(
                n.gains.at[to],
                n.gains_got.at[k],
                n.gain_sems.at[0, k],
                n.gain_sems.at[1, k],
                (to, t),
            )

        for k in range(1, s.count):
            gain_copy(k).start()
        for layer in range(layers):
            n.qk_total[layer] = n.acc[len(rounds), 2 * layer : 2 * layer + 2]
        total = n.gains[c]
        for k in range(1, s.count):
            gain_copy(k).wait_recv()
            total = total + n.gains_got[k]
        n.attn_total[...] = total[:layers]
        n.ffn_total[...] = total[layers : 2 * layers]
        for k in range(1, s.count):
            gain_copy(k).wait_send()
        for k in range(len(rounds)):
            head_copy(k).wait_send()
        scatter.finish()
        wait_all(*above)

        def finish(u):
            upper.finish(u)
            stores.finish(u)

        each_of(s.units, finish)

    held = dict(
        a1=bottom.a1,
        a2=bottom.a2,
        o=bottom.o,
        hidden=bottom.hidden,
        dyb=bottom.dyb,
        dgate=bottom.dgate,
        dup=bottom.dup,
        dhb=bottom.dhb,
    )
    small = (len(rounds) + 1, 2 * layers + -2 * layers % 8, HEAD_SIZE)
    slabs = (s.count, 2 * layers + -2 * layers % 8, width)
    return run_kernel(
        body,
        head_ins(bottom, w)
        | {x: (array, ANY) for x, array in held.items()}
        | dict(
            qk_in=[(k.qk_sum, VMEM) for k in kept],
            attn_in=[(k.attn_sum, VMEM) for k in kept[1:]],
            ffn_in=[(k.ffn_sum, VMEM) for k in kept],
            done=[(array, ANY) for k in kept[1:] for array in k.sums],
        ),
        dict(
            dres=(shaped(s.rows, s.model, kind=F32), ANY),
            attn_total=(shaped(layers, width, kind=F32), VMEM),
            ffn_total=(shaped(layers, width, kind=F32), VMEM),
            qk_total=(shaped(layers, 2, HEAD_SIZE, kind=F32), VMEM),
            sums=[(shaped(layers, *size, kind=F32), ANY) for size in sizes],
        ),
        head_scratch(bottom, s)
        | {x + "_v": VMEM(array.shape, array.dtype) for x, array in held.items()}
        | scatter_scratch(s, sizes, True)
        | dict(
            attn_sum=VMEM((1, s.model), F32),
            acc=VMEM(small, F32),
            other=VMEM(small, F32),
            gains=VMEM(slabs, F32),
            gains_got=VMEM(slabs, F32),
            small_sems=DMA((2, len(rounds))),
            gain_sems=DMA((2, s.count)),
        ),
        19,
    )


SCATTER_MIDDLE = (0, 3, 9, 16)
SCATTER_END = (0, 2, 7, 11)


def body(hidden_in, doc_lengths, cotangent, attn_gain, ffn_gain, qk_gain, w_query, *others):
    key_weight, value_weight, w_out, w_gate, w_up, w_down = others
    w = types.SimpleNamespace(
        attn_gain=attn_gain,
        ffn_gain=ffn_gain,
        qk_gain=qk_gain,
        w_query=w_query,
        key_weight=key_weight,
        value_weight=value_weight,
        w_out=w_out,
        w_gate=w_gate,
        w_up=w_up,
        w_down=w_down,
    )
    rows, model = hidden_in.shape
    layers, unused, queries = w_query.shape
    keys = key_weight.shape[2]
    s = types.SimpleNamespace(
        rows=rows,
        model=model,
        queries=queries,
        keys=keys,
        hidden=w_gate.shape[2],
        units=rows // UNIT,
        groups=keys // HEAD_SIZE,
        repeat=queries // keys,
        count=lax.axis_size(CTX),
        line=lax.axis_size(TP),
    )
    tables = make_tables(doc_lengths, rows)

    kept = []
    stream = hidden_in
    saved = first_projection(stream, w, tables, s)
    for layer in range(layers):
        if layer < layers - 1:
            result = forward_layer(layer, stream, saved, w, tables, s)
        else:
            result = turn_layer(layer, stream, saved, cotangent, w, tables, s)
        own = dict(a1=saved.a1, qraw=saved.qraw, kraw=saved.kraw, q=saved.q, kv=saved.kv)
        kept.append(types.SimpleNamespace(**(vars(result) | own | dict(x=stream))))
        stream = result.y
        saved = result

    for layer in range(layers - 2, -1, -1):
        result = backward_layer(layer, kept, w, tables, s)
        kept[layer + 1].attn_sum = result.attn_sum
        kept[layer + 1].sums = result.sums
        vars(kept[layer]).update(
            dyb=result.dyb,
            dgate=result.dgate,
            dup=result.dup,
            dhb=result.dhb,
            dq=result.dq,
            dk=result.dk,
            dv=result.dv,
            dres=result.dres,
            ffn_sum=result.ffn_sum,
            qk_sum=result.qk_sum,
        )
    end = backward_end(kept, w, s)
    up, gate, query, down, out, key, value = end.sums
    return (
        stream,
        end.dres,
        end.attn_total,
        end.ffn_total,
        end.qk_total,
        query,
        key,
        value,
        out,
        gate,
        up,
        down,
    )


def solution(mesh):
    by_rows = P(CTX, None)
    by_columns = P(None, None, TP)
    by_hidden = P(None, TP, None)
    grad_columns = P(None, CTX, TP)
    grad_rows = P(None, (TP, CTX), None)
    return jax.shard_map(
        body,
        mesh=mesh,
        in_specs=(by_rows, P(), by_rows, P(), P(), P())
        + (by_columns,) * 3
        + (by_hidden,)
        + (by_columns,) * 2
        + (by_hidden,),
        out_specs=(by_rows, by_rows, P(None, CTX), P(None, CTX), P())
        + (grad_columns,) * 3
        + (grad_rows,)
        + (grad_columns,) * 2
        + (grad_rows,),
        check_vma=False,
    )
```

```python
import types

import jax
import jax.numpy as jnp
from jax import lax
from jax.experimental import pallas as pl
from jax.experimental.pallas import tpu as pltpu
from jax.sharding import PartitionSpec as P

HEAD_SIZE = 128
ATTENTION_WINDOW = 1024
EPS = 1e-06
THETA = 1000000.0

UNIT = 64
WIDE = 128
KEY_BLOCK = 384
HOP = 2
ARRIVED = 3 * HOP + WIDE // UNIT - 1
CTX = "ctx"
TP = "tp"
MESH = pl.DeviceIdType.MESH
F32 = jnp.float32
BF16 = jnp.bfloat16
SCALE = HEAD_SIZE ** (-0.5)
EXP2_SCALE = SCALE * 1.4426950408889634
ANY = pl.ANY
VMEM = pltpu.VMEM
DMA = pltpu.SemaphoreType.DMA


def dot_nn(left, right):
    return jnp.dot(left, right, preferred_element_type=F32)


def dot_nt(left, right):
    return lax.dot_general(left, right, (((1,), (1,)), ((), ())), preferred_element_type=F32)


def dot_tn(left, right):
    return lax.dot_general(left, right, (((0,), (0,)), ((), ())), preferred_element_type=F32)


def rms_inverse(value_rows):
    return lax.rsqrt(jnp.mean(value_rows * value_rows, axis=-1, keepdims=True) + EPS)


def rotate(value_rows, cosine, sine):
    return value_rows * cosine + pltpu.roll(value_rows, HEAD_SIZE // 2, 1) * sine


def unrotate(grad, cosine, sine):
    return grad * cosine + pltpu.roll(grad * sine, HEAD_SIZE // 2, 1)


def norm_back(grad, unit, inverse, gain):
    scaled = grad * gain
    inner = jnp.mean(scaled * unit, axis=-1, keepdims=True)
    return inverse * (scaled - unit * inner)


def column_sum(value_rows):
    return jnp.sum(value_rows, axis=0, keepdims=True)


def make_tables(lengths, rows):
    start = lax.axis_index(CTX) * rows
    spot = start + jnp.arange(rows, dtype=jnp.int32)
    order = jnp.arange(lengths.shape[0])
    ends = jnp.sum(jnp.where(order[None, :] <= order[:, None], lengths[None, :], 0), axis=1)
    passed = ends[None, :] <= spot[:, None]
    begin = jnp.sum(jnp.where(passed, lengths[None, :], 0), axis=1)
    lane = jnp.arange(HEAD_SIZE)
    half = HEAD_SIZE // 2
    freq = THETA ** (-((lane % half).astype(F32) * 2.0) / HEAD_SIZE)
    angle = (spot - begin).astype(F32)[:, None] * freq[None, :]
    lowest = jnp.maximum(begin, spot - (ATTENTION_WINDOW - 1)) - (start - ATTENTION_WINDOW)
    return types.SimpleNamespace(
        cosine=jnp.cos(angle),
        sine=jnp.sin(angle) * jnp.where(lane < half, -1.0, 1.0)[None, :],
        lowest=lowest[:, None],
    )


def halo_plan(rows):
    reach = -(-ATTENTION_WINDOW // rows)
    plan = []
    for hop in range(1, reach + 1):
        need = min(rows, ATTENTION_WINDOW - (hop - 1) * rows)
        plan.append((hop, need, ATTENTION_WINDOW - (hop - 1) * rows - need))
    return plan


def unit_rows(u):
    return pl.ds(pl.multiple_of(u * UNIT, UNIT), UNIT)


def wide_rows(w):
    return pl.ds(pl.multiple_of(w * WIDE, WIDE), WIDE)


def subs(w):
    return [w * (WIDE // UNIT) + i for i in range(WIDE // UNIT)]


def shaped(*shape, kind=BF16):
    return jax.ShapeDtypeStruct(shape, kind)


def listed(value):
    return list(value) if isinstance(value, list) else [value]


def run_kernel(body, ins, outs, scratch, collective_id):
    groups = [ins, outs, scratch]
    flat = [[x for value in group.values() for x in listed(value)] for group in groups]

    def named(values, chosen):
        values = list(values)
        found = {}
        for group in chosen:
            for name, value in group.items():
                if isinstance(value, list):
                    found[name] = [values.pop(0) for unused in value]
                else:
                    found[name] = values.pop(0)
        return types.SimpleNamespace(**found)

    results = pl.pallas_call(
        lambda *refs: body(named(refs, groups)),
        out_shape=[shape for shape, unused in flat[1]],
        in_specs=[pl.BlockSpec(memory_space=space) for unused, space in flat[0]],
        out_specs=[pl.BlockSpec(memory_space=space) for unused, space in flat[1]],
        scratch_shapes=flat[2],
        compiler_params=pltpu.CompilerParams(
            collective_id=collective_id,
            has_side_effects=collective_id is not None,
            vmem_limit_bytes=62 * 2**20,
        ),
    )(*[array for array, unused in flat[0]])
    return named(results, [outs])


def place():
    return lax.axis_index(CTX), lax.axis_index(TP)


def remote(source, target, send, receive, device):
    return pltpu.make_async_remote_copy(
        src_ref=source,
        dst_ref=target,
        send_sem=send,
        recv_sem=receive,
        device_id=device,
        device_id_type=MESH,
    )


def greet(partners):
    barrier = pltpu.get_barrier_semaphore()
    total = 0
    for exists, device in partners:
        total = total + jnp.where(exists, 1, 0)

        @pl.when(exists)
        def _():
            pl.semaphore_signal(barrier, inc=1, device_id=device, device_id_type=MESH)

    pl.semaphore_wait(barrier, total)


def line_partners():
    c, t = place()
    outer = (t == 0) | (t == 3)
    return [
        (outer, (c, jnp.where(t == 0, 1, 2))),
        (jnp.logical_not(outer), (c, jnp.where(t == 1, 0, 3))),
        (jnp.logical_not(outer), (c, jnp.clip(3 - t, 1, 2))),
    ]


def halo_partners(rows, count):
    c, t = place()
    partners = []
    for hop, unused, unused_too in halo_plan(rows):
        partners.append((c + hop < count, (jnp.minimum(c + hop, count - 1), t)))
        partners.append((c >= hop, (jnp.maximum(c - hop, 0), t)))
    return partners


class LineSum:
    def __init__(self, refs):
        self.part, self.total, self.inner, self.sems = refs
        self.c, self.t = place()
        self.outer = (self.t == 0) | (self.t == 3)
        self.is_inner = jnp.logical_not(self.outer)

    def copy(self, source, target, u, send, receive, to):
        return remote(
            source.at[u],
            target.at[u],
            self.sems.at[send, u],
            self.sems.at[receive, u],
            (self.c, to),
        )

    def inwards(self, u):
        return self.copy(self.part, self.total, u, 0, 1, jnp.where(self.t < 2, 1, 2))

    def across(self, u):
        return self.copy(self.part, self.inner, u, 0, 2, jnp.clip(3 - self.t, 1, 2))

    def outwards(self, u):
        return self.copy(self.total, self.total, u, 3, 4, jnp.where(self.t < 2, 0, 3))

    def hold(self, w, value):
        for i, u in enumerate(subs(w)):
            self.part[u] = value[i * UNIT : (i + 1) * UNIT].astype(BF16)

    def send(self, u):
        @pl.when(self.outer)
        def _():
            self.inwards(u).start()

    def push(self, w, value):
        self.hold(w, value)
        for u in subs(w):
            self.send(u)

    def meet(self, u):
        @pl.when(self.is_inner)
        def _():
            self.inwards(u).wait_recv()
            self.part[u] = (self.part[u].astype(F32) + self.total[u].astype(F32)).astype(BF16)
            self.across(u).start()

    def spread(self, u):
        @pl.when(self.is_inner)
        def _():
            self.across(u).wait_recv()
            self.total[u] = (self.part[u].astype(F32) + self.inner[u].astype(F32)).astype(BF16)
            self.outwards(u).start()

    def take(self, u):
        @pl.when(self.outer)
        def _():
            self.outwards(u).wait_recv()

        return self.total[u].astype(F32)

    def take_wide(self, w):
        return jnp.concatenate([self.take(u) for u in subs(w)], axis=0)

    def finish(self, u):
        @pl.when(self.outer)
        def _():
            self.inwards(u).wait_send()

        @pl.when(self.is_inner)
        def _():
            self.across(u).wait_send()
            self.outwards(u).wait_send()

    def stages(self, begin, hop=HOP):
        return [(begin + 2 * hop, self.spread, 1), (begin + hop, self.meet, 1)]


def line_scratch(units, width):
    block = VMEM((units, UNIT, width), BF16)
    return [block, block, block, DMA((5, units))]


def pipeline(units, stages, tasks=()):
    steps = units + max(delay + 1 - taken for delay, unused, taken in stages)

    def step(s, carry):
        for delay, function, taken in stages:
            ready = (s >= delay) & (s < units + delay)
            if taken > 1:
                ready = ready & ((s - delay) % taken == 0)

            @pl.when(ready)
            def _():
                function((s - delay) // taken if taken > 1 else s - delay)

        for at, task in tasks:
            if at < steps:

                @pl.when(s == at)
                def _():
                    task()

        return carry

    lax.fori_loop(0, steps, step, 0)
    for at, task in tasks:
        if at >= steps:
            task()


def each_of(number, function):
    def step(u, carry):
        function(u)
        return carry

    lax.fori_loop(0, number, step, 0)


class Loads:
    def __init__(self, sems):
        self.sems, self.number = sems, 0

    def __call__(self, source, target):
        copy = pltpu.make_async_copy(source, target, self.sems.at[self.number])
        copy.start()
        self.number += 1
        return copy


def wait_all(*copies):
    for copy in copies:
        copy.wait()


class Stores:
    def __init__(self, sems):
        self.sems, self.copies = sems, []

    def __call__(self, source, target):
        index = len(self.copies)

        def copy(u):
            rows = unit_rows(u)
            return pltpu.make_async_copy(source.at[rows], target.at[rows], self.sems.at[index, u])

        self.copies.append(copy)
        return copy

    def finish(self, u):
        for copy in self.copies:
            copy(u).wait()


def send_out(units, *copies):
    for u in units:
        for copy in copies:
            copy(u).start()


class Halo:
    def __init__(self, keys, sems, rows, count):
        self.keys, self.sems, self.rows, self.count = keys, sems, rows, count
        self.plan = halo_plan(rows)
        self.c, self.t = place()

    def copy(self, index, u, hop, need, offset):
        target = pl.multiple_of(offset + u * UNIT - (self.rows - need), UNIT)
        return remote(
            self.keys.at[pl.ds(pl.multiple_of(ATTENTION_WINDOW + u * UNIT, UNIT), UNIT)],
            self.keys.at[pl.ds(target, UNIT)],
            self.sems.at[2 * index, u],
            self.sems.at[2 * index + 1, u],
            (jnp.minimum(self.c + hop, self.count - 1), self.t),
        )

    def each(self, u, function, receives):
        for index, (hop, need, offset) in enumerate(self.plan):
            exists = self.c >= hop if receives else self.c + hop < self.count

            @pl.when(exists & (u >= (self.rows - need) // UNIT))
            def _():
                function(self.copy(index, u, hop, need, offset))

    def blank(self):
        width = self.keys.shape[1]
        for hop, need, offset in self.plan:

            @pl.when(self.c < hop)
            def _():
                self.keys[offset : offset + need] = jnp.zeros((need, width), BF16)

    def send(self, u):
        self.each(u, lambda copy: copy.start(), False)

    def finish(self, u):
        self.each(u, lambda copy: copy.wait_recv(), True)
        self.each(u, lambda copy: copy.wait_send(), False)


def project_heads(n, raw, out, out_rows, rows, which, layer):
    cosine, sine = n.cosine[rows], n.sine[rows]
    gain = n.qk_gain[layer, which : which + 1]
    for head in range(raw.shape[1] // HEAD_SIZE):
        part = raw[:, head_cols(head)]
        part = part * rms_inverse(part) * gain
        out[out_rows, head_cols(head)] = rotate(part, cosine, sine).astype(BF16)


def project_keys(n, first, number, stream, layer):
    rows = pl.ds(pl.multiple_of(first, number), number)
    own = pl.ds(pl.multiple_of(ATTENTION_WINDOW + first, number), number)
    normed = (stream * rms_inverse(stream) * n.attn_gain[layer : layer + 1]).astype(BF16)
    n.a1_v[rows] = normed
    key = dot_nn(normed, n.wk_v[...])
    n.kraw_v[rows] = key
    n.kv_v[own, key.shape[1] :] = dot_nn(normed, n.wv_v[...]).astype(BF16)
    project_heads(n, key, n.kv_v, own, rows, 1, layer)


def project_queries(n, first, number, layer):
    rows = pl.ds(pl.multiple_of(first, number), number)
    query = dot_nn(n.a1_v[rows], n.wq_v[...])
    n.qraw_v[rows] = query
    project_heads(n, query, n.q_v, rows, rows, 0, layer)


def project_shapes(s):
    return dict(
        a1=((s.rows, s.model), BF16),
        qraw=((s.rows, s.queries), F32),
        kraw=((s.rows, s.keys), F32),
        q=((s.rows, s.queries), BF16),
        kv=((ATTENTION_WINDOW + s.rows, 2 * s.keys), BF16),
    )


def outputs(shapes):
    return {x: (shaped(*shape, kind=kind), ANY) for x, (shape, kind) in shapes.items()}


def buffers(shapes):
    return {x + "_v": VMEM(shape, kind) for x, (shape, kind) in shapes.items()}


def project_ins(w, tables):
    return dict(
        attn_gain=(w.attn_gain, VMEM),
        qk_gain=(w.qk_gain, VMEM),
        cosine=(tables.cosine, VMEM),
        sine=(tables.sine, VMEM),
        wq=(w.w_query, ANY),
        wk=(w.key_weight, ANY),
        wv=(w.value_weight, ANY),
    )


def project_scratch(s):
    return buffers(project_shapes(s)) | dict(
        wq_v=VMEM((s.model, s.queries), BF16),
        wk_v=VMEM((s.model, s.keys), BF16),
        wv_v=VMEM((s.model, s.keys), BF16),
        halo_sems=DMA((2 * len(halo_plan(s.rows)), s.units)),
    )


def first_projection(stream, w, tables, s):
    def body(n):
        loads = Loads(n.load_sems)
        weights = (
            loads(n.wk.at[0], n.wk_v),
            loads(n.wv.at[0], n.wv_v),
            loads(n.wq.at[0], n.wq_v),
        )
        stores = Stores(n.store_sems)
        made = (
            stores(n.a1_v, n.a1),
            stores(n.qraw_v, n.qraw),
            stores(n.kraw_v, n.kraw),
            stores(n.q_v, n.q),
        )
        halo = Halo(n.kv_v, n.halo_sems, s.rows, s.count)
        greet(halo_partners(s.rows, s.count))
        halo.blank()
        wait_all(*weights)

        def each_keys(i):
            project_keys(n, i * WIDE, WIDE, n.x[wide_rows(i)].astype(F32), 0)
            for u in subs(i):
                halo.send(u)

        def each_queries(i):
            project_queries(n, i * WIDE, WIDE, 0)
            send_out(subs(i), *made)

        each_of(s.rows // WIDE, each_keys)
        each_of(s.rows // WIDE, each_queries)
        each_of(s.units, halo.finish)
        keys = loads(n.kv_v, n.kv)
        each_of(s.units, stores.finish)
        keys.wait()

    return run_kernel(
        body,
        dict(x=(stream, VMEM)) | project_ins(w, tables),
        outputs(project_shapes(s)),
        project_scratch(s) | dict(load_sems=DMA((4,)), store_sems=DMA((4, s.units))),
        1,
    )


def key_block(i, block):
    return pl.ds(pl.multiple_of(i * WIDE + block * KEY_BLOCK, HEAD_SIZE), KEY_BLOCK)


def visible(i, lowest, block, repeat):
    shape = (WIDE, KEY_BLOCK)
    col = block * KEY_BLOCK + lax.broadcasted_iota(jnp.int32, shape, 1)
    seen = col >= lowest - i * WIDE
    if (block + 1) * KEY_BLOCK > ATTENTION_WINDOW:
        row = ATTENTION_WINDOW + lax.broadcasted_iota(jnp.int32, shape, 0)
        seen = seen & (col <= row)
    keep = jnp.where(seen, 1.0, 0.0)
    return jnp.concatenate([keep] * repeat, axis=0)


def key_blocks():
    return (ATTENTION_WINDOW + WIDE) // KEY_BLOCK


def stacked(value, group, repeat):
    first = group * repeat
    return jnp.concatenate(
        [value[:, (first + r) * HEAD_SIZE : (first + r + 1) * HEAD_SIZE] for r in range(repeat)],
        axis=0,
    )


def head_cols(index):
    return slice(index * HEAD_SIZE, (index + 1) * HEAD_SIZE)


def attend(n, i, s):
    rows = wide_rows(i)
    lowest = n.lowest[rows]
    lane = lax.broadcasted_iota(jnp.int32, (WIDE, HEAD_SIZE), 1)
    query_rows = n.qin_v[rows]
    queries = [stacked(query_rows, g, s.repeat) for g in range(s.groups)]
    mixed = [jnp.zeros((s.repeat * WIDE, HEAD_SIZE), F32) for unused in queries]
    total = [jnp.zeros((s.repeat * WIDE, 1), F32) for unused in queries]
    for block in range(key_blocks()):
        keys = key_block(i, block)
        keep = visible(i, lowest, block, s.repeat)
        for g in range(s.groups):
            scores = dot_nt(queries[g], n.kvin_v[keys, head_cols(g)])
            weights = jnp.exp2(scores * EXP2_SCALE) * keep
            total[g] = total[g] + jnp.sum(weights, axis=-1, keepdims=True)
            values = n.kvin_v[keys, head_cols(s.groups + g)]
            mixed[g] = mixed[g] + dot_nn(weights.astype(BF16), values)
    inverses = jnp.zeros((WIDE, HEAD_SIZE), F32)
    for g in range(s.groups):
        inverse = 1.0 / total[g]
        result = (mixed[g] * inverse).astype(BF16)
        for r in range(s.repeat):
            head = g * s.repeat + r
            part = slice(r * WIDE, (r + 1) * WIDE)
            n.o_v[rows, head_cols(head)] = result[part]
            inverses = jnp.where(lane == head, inverse[part], inverses)
    n.inv_v[rows] = inverses


def attend_back(n, i, grad_out, keys_ref, query_ref, s):
    rows = wide_rows(i)
    lowest = n.lowest[rows]
    query_rows, mixed_rows, inverses = query_ref[rows], n.o_v[rows], n.inv_v[rows]
    queries, grads, inners, scales, found = [], [], [], [], []
    for g in range(s.groups):
        queries.append(stacked(query_rows, g, s.repeat))
        grads.append(stacked(grad_out, g, s.repeat))
        mixed = stacked(mixed_rows, g, s.repeat)
        inners.append(
            jnp.sum(grads[g].astype(F32) * mixed.astype(F32), axis=-1, keepdims=True)
        )
        heads = [g * s.repeat + r for r in range(s.repeat)]
        scales.append(jnp.concatenate([inverses[:, h : h + 1] for h in heads], axis=0))
        found.append(jnp.zeros((s.repeat * WIDE, HEAD_SIZE), F32))
    for block in range(key_blocks()):
        keys = key_block(i, block)
        keep = visible(i, lowest, block, s.repeat)
        for g in range(s.groups):
            key_rows = keys_ref[keys, head_cols(g)]
            scores = dot_nt(queries[g], key_rows)
            probs = jnp.exp2(scores * EXP2_SCALE) * (keep * scales[g])
            grad_probs = dot_nt(grads[g], keys_ref[keys, head_cols(s.groups + g)])
            grad_scores = (probs * (grad_probs - inners[g])).astype(BF16)
            found[g] = found[g] + dot_nn(grad_scores, key_rows)
            n.dkv_v[keys, head_cols(g)] += dot_tn(grad_scores, queries[g])
            n.dkv_v[keys, head_cols(s.groups + g)] += dot_tn(probs.astype(BF16), grads[g])
    return [
        found[g][r * WIDE : (r + 1) * WIDE] for g in range(s.groups) for r in range(s.repeat)
    ]


def head_back(n, rows, grad, raw, which, layer):
    gain = n.qk_gain[layer, which : which + 1]
    turned = unrotate(grad, n.cosine[rows], n.sine[rows])
    inverse = rms_inverse(raw)
    unit = raw * inverse
    n.qk_sum[which : which + 1] += column_sum(turned * unit)
    return norm_back(turned, unit, inverse, gain).astype(BF16)


class Returns:
    def __init__(self, n, s):
        self.grads, self.low, self.back, self.sems = n.dkv_v, n.low_v, n.back_v, n.return_sems
        self.s, self.plan = s, halo_plan(s.rows)
        self.c, self.t = place()
        self.blocks = []
        for index, (hop, need, offset) in enumerate(self.plan):
            for b in range(need // WIDE):
                self.blocks.append((index, hop, offset + b * WIDE, b * WIDE))
        self.blocks.sort(key=lambda item: item[2])

    def copy(self, number):
        index, hop, source, target = self.blocks[number]
        return remote(
            self.low.at[pl.ds(source, WIDE)],
            self.back[index].at[pl.ds(target, WIDE)],
            self.sems.at[0, number],
            self.sems.at[1, number],
            (jnp.maximum(self.c - hop, 0), self.t),
        )

    def blank(self):
        for index, (hop, need, unused) in enumerate(self.plan):

            @pl.when(self.c + hop >= self.s.count)
            def _():
                self.back[index][...] = jnp.zeros((need, self.low.shape[1]), BF16)

    def send(self, number):
        rows = pl.ds(self.blocks[number][2], WIDE)

        @pl.when(self.c >= self.blocks[number][1])
        def _():
            self.low[rows] = self.grads[rows].astype(BF16)
            self.copy(number).start()

    def send_complete(self, i):
        for number, block in enumerate(self.blocks):
            if block[2] // WIDE < self.s.rows // WIDE - 1:

                @pl.when(i == block[2] // WIDE)
                def _():
                    self.send(number)

    def send_rest(self):
        for number, block in enumerate(self.blocks):
            if block[2] // WIDE >= self.s.rows // WIDE - 1:
                self.send(number)

    def receive(self):
        for number, block in enumerate(self.blocks):

            @pl.when(self.c + block[1] < self.s.count)
            def _():
                self.copy(number).wait_recv()

    def finish(self):
        for number, block in enumerate(self.blocks):

            @pl.when(self.c >= block[1])
            def _():
                self.copy(number).wait_send()


def attention_back_scratch(s):
    plan = halo_plan(s.rows)
    return dict(
        dkv_v=VMEM((ATTENTION_WINDOW + s.rows, 2 * s.keys), F32),
        low_v=VMEM((ATTENTION_WINDOW, 2 * s.keys), BF16),
        back_v=[VMEM((need, 2 * s.keys), BF16) for unused, need, unused_too in plan],
        total_v=VMEM((WIDE, 2 * s.keys), F32),
        return_sems=DMA((2, ATTENTION_WINDOW // WIDE)),
    )


def attention_back_shapes(s):
    return dict(
        dyb=((s.rows, s.model), BF16),
        dgate=((s.rows, s.hidden), BF16),
        dup=((s.rows, s.hidden), BF16),
        dhb=((s.rows, s.model), BF16),
        dq=((s.rows, s.queries), BF16),
        dk=((s.rows, s.keys), BF16),
        dv=((s.rows, s.keys), BF16),
    )


def attention_back_sums(s):
    return dict(
        dres=(shaped(s.rows, s.model, kind=F32), ANY),
        ffn_sum=(shaped(1, s.model, kind=F32), VMEM),
        qk_sum=(shaped(2, HEAD_SIZE, kind=F32), VMEM),
    )


def back_start(n, returns):
    returns.blank()
    n.dkv_v[...] = jnp.zeros_like(n.dkv_v)
    n.ffn_sum[...] = jnp.zeros_like(n.ffn_sum)
    n.qk_sum[...] = jnp.zeros_like(n.qk_sum)


def feed_back(n, i, gate, up, lower, made):
    here = wide_rows(i)
    low = n.g_v[here].astype(BF16)
    n.dyb_v[here] = low
    grad_hidden = dot_nt(low, n.wd_v[...])
    sigma = jax.nn.sigmoid(gate)
    dgate = (grad_hidden * up * (sigma * (1.0 + gate * (1.0 - sigma)))).astype(BF16)
    dup = (grad_hidden * gate * sigma).astype(BF16)
    n.dgate_v[here] = dgate
    n.dup_v[here] = dup
    lower.push(i, dot_nt(dgate, n.wg_v[...]) + dot_nt(dup, n.wu_v[...]))
    send_out(subs(i), *made)


def attention_back(n, i, middle, keys_ref, query_ref, layer, lower, returns, made, s):
    here = wide_rows(i)
    grad_in = lower.take_wide(i)
    inverse = rms_inverse(middle)
    unit = middle * inverse
    n.ffn_sum[...] += column_sum(grad_in * unit)
    total = n.g_v[here] + norm_back(grad_in, unit, inverse, n.ffn_gain[layer : layer + 1])
    n.g_v[here] = total
    low = total.astype(BF16)
    n.dhb_v[here] = low
    grad_out = dot_nt(low, n.wo_v[...]).astype(BF16)
    pieces = attend_back(n, i, grad_out, keys_ref, query_ref, s)
    returns.send_complete(i)
    for head, piece in enumerate(pieces):
        n.dq_v[here, head_cols(head)] = head_back(
            n, here, piece * SCALE, n.qraw_v[here, head_cols(head)], 0, layer
        )
    send_out(subs(i), *made)


def keys_back(n, layer, returns, made, s):
    def each(i):
        here = wide_rows(i)
        own = pl.ds(pl.multiple_of(ATTENTION_WINDOW + i * WIDE, WIDE), WIDE)
        n.total_v[...] = n.dkv_v[own]
        for index, (hop, need, unused) in enumerate(returns.plan):
            skipped = s.rows - need

            @pl.when(i >= skipped // WIDE)
            def _():
                part = pl.ds(pl.multiple_of(i * WIDE - skipped, WIDE), WIDE)
                n.total_v[...] += n.back_v[index][part].astype(F32)

        for g in range(s.groups):
            n.dk_v[here, head_cols(g)] = head_back(
                n, here, n.total_v[:, head_cols(g)] * SCALE, n.kraw_v[here, head_cols(g)], 1, layer
            )
        n.dv_v[here] = n.total_v[:, s.keys :].astype(BF16)
        send_out(subs(i), *made)

    each_of(s.rows // WIDE, each)


def feed(n, i, middle, layer):
    here = wide_rows(i)
    normed = (middle * rms_inverse(middle) * n.ffn_gain[layer : layer + 1]).astype(BF16)
    n.a2_v[here] = normed
    gate = dot_nn(normed, n.wg_v[...])
    up = dot_nn(normed, n.wu_v[...])
    inside = (gate * jax.nn.sigmoid(gate) * up).astype(BF16)
    n.hidden_v[here] = inside
    return gate, up, dot_nn(inside, n.wd_v[...])


def layer_ins(stream, saved, w, tables):
    return dict(
        x=(stream, ANY),
        qin=(saved.q, ANY),
        kvin=(saved.kv, ANY),
        ffn_gain=(w.ffn_gain, VMEM),
        lowest=(tables.lowest, VMEM),
        wo=(w.w_out, ANY),
        wg=(w.w_gate, ANY),
        wu=(w.w_up, ANY),
        wd=(w.w_down, ANY),
    )


def weight_scratch(s):
    return dict(
        wo_v=VMEM((s.queries, s.model), BF16),
        wg_v=VMEM((s.model, s.hidden), BF16),
        wu_v=VMEM((s.model, s.hidden), BF16),
        wd_v=VMEM((s.hidden, s.model), BF16),
    )


def layer_scratch(stream, s):
    return weight_scratch(s) | dict(
        x_v=VMEM((s.rows, s.model), stream.dtype),
        qin_v=VMEM((s.rows, s.queries), BF16),
        kvin_v=VMEM((ATTENTION_WINDOW + s.rows, 2 * s.keys), BF16),
        load_sems=DMA((16,)),
        store_sems=DMA((16, s.units)),
        first=line_scratch(s.units, s.model),
        second=line_scratch(s.units, s.model),
    )


def layer_loads(n, loads, layer):
    early = (
        loads(n.qin, n.qin_v),
        loads(n.kvin, n.kvin_v),
        loads(n.wo.at[layer], n.wo_v),
    )
    late = (
        loads(n.x, n.x_v),
        loads(n.wg.at[layer], n.wg_v),
        loads(n.wu.at[layer], n.wu_v),
        loads(n.wd.at[layer], n.wd_v),
    )
    return early, late


def kept_shapes(s):
    return dict(
        o=((s.rows, s.queries), BF16),
        a2=((s.rows, s.model), BF16),
        hidden=((s.rows, s.hidden), BF16),
    )


def forward_shapes(s):
    return kept_shapes(s) | dict(
        inv=((s.rows, HEAD_SIZE), F32),
        h=((s.rows, s.model), F32),
        gate=((s.rows, s.hidden), BF16),
        up=((s.rows, s.hidden), BF16),
        y=((s.rows, s.model), F32),
    )


def forward_layer(layer, stream, saved, w, tables, s):
    def body(n):
        loads = Loads(n.load_sems)
        early, late = layer_loads(n, loads, layer)
        above = (
            loads(n.wq.at[layer + 1], n.wq_v),
            loads(n.wk.at[layer + 1], n.wk_v),
            loads(n.wv.at[layer + 1], n.wv_v),
        )
        stores = Stores(n.store_sems)
        mixed = (stores(n.o_v, n.o), stores(n.inv_v, n.inv))
        fed = (
            stores(n.h_v, n.h),
            stores(n.a2_v, n.a2),
            stores(n.hidden_v, n.hidden),
            stores(n.gate_v, n.gate),
            stores(n.up_v, n.up),
        )
        closed = (
            stores(n.y_v, n.y),
            stores(n.a1_v, n.a1),
            stores(n.qraw_v, n.qraw),
            stores(n.kraw_v, n.kraw),
            stores(n.q_v, n.q),
        )
        first, second = LineSum(n.first), LineSum(n.second)
        halo = Halo(n.kv_v, n.halo_sems, s.rows, s.count)
        greet(line_partners() + halo_partners(s.rows, s.count))
        halo.blank()
        wait_all(*early)

        def mix(i):
            attend(n, i, s)
            first.push(i, dot_nn(n.o_v[wide_rows(i)], n.wo_v[...]))
            send_out(subs(i), *mixed)

        def feed_wide(i):
            pl.when(i == 0)(lambda: wait_all(*late))
            here = wide_rows(i)
            middle = n.x_v[here].astype(F32) + first.take_wide(i)
            n.h_v[here] = middle
            gate, up, part = feed(n, i, middle, layer)
            second.push(i, part)
            n.gate_v[here] = gate.astype(BF16)
            n.up_v[here] = up.astype(BF16)
            send_out(subs(i), *fed)

        def close(u):
            pl.when(u == 0)(lambda: wait_all(*above))
            here = unit_rows(u)
            result = n.h_v[here] + second.take(u)
            n.y_v[here] = result
            project_keys(n, u * UNIT, UNIT, result, layer + 1)
            halo.send(u)
            project_queries(n, u * UNIT, UNIT, layer + 1)
            send_out([u], *closed)

        at = ARRIVED
        pipeline(
            s.units,
            second.stages(at)
            + first.stages(0)
            + [(at + 3 * HOP, close, 1), (at, feed_wide, WIDE // UNIT), (0, mix, WIDE // UNIT)],
        )
        each_of(s.units, halo.finish)
        keys = loads(n.kv_v, n.kv)

        def finish(u):
            first.finish(u)
            second.finish(u)
            stores.finish(u)

        each_of(s.units, finish)
        keys.wait()

    return run_kernel(
        body,
        layer_ins(stream, saved, w, tables) | project_ins(w, tables),
        outputs(forward_shapes(s)) | outputs(project_shapes(s)),
        layer_scratch(stream, s) | buffers(forward_shapes(s)) | project_scratch(s),
        2 + layer,
    )


def turn_layer(layer, stream, saved, cotangent, w, tables, s):
    def body(n):
        loads = Loads(n.load_sems)
        early, late = layer_loads(n, loads, layer)
        late = late + (loads(n.grad, n.grad_v),)
        raws = (loads(n.qraw, n.qraw_v), loads(n.kraw, n.kraw_v))
        a1 = loads(n.a1, n.a1_v)
        stores = Stores(n.store_sems)
        closed = (stores(n.y_v, n.y),)
        turned = (stores(n.g_v, n.dres), stores(n.dq_v, n.dq))
        keyed = (stores(n.dk_v, n.dk), stores(n.dv_v, n.dv))
        first, second, lower = LineSum(n.first), LineSum(n.second), LineSum(n.lower)
        returns = Returns(n, s)
        greet(line_partners() + halo_partners(s.rows, s.count))
        back_start(n, returns)
        wait_all(*early)

        def mix(i):
            attend(n, i, s)
            first.push(i, dot_nn(n.o_v[wide_rows(i)], n.wo_v[...]))

        def feed_both(i):
            pl.when(i == 0)(lambda: wait_all(*late))
            here = wide_rows(i)
            middle = n.x_v[here] + first.take_wide(i)
            n.x_v[here] = middle
            n.g_v[here] = n.grad_v[here].astype(F32)
            gate, up, part = feed(n, i, middle, layer)
            feed_back(n, i, gate, up, lower, ())
            second.hold(i, part)

        def close(u):
            here = unit_rows(u)
            n.y_v[here] = (n.x_v[here] + second.take(u)).astype(BF16)
            send_out([u], *closed)

        def attention(i):
            pl.when(i == 0)(lambda: wait_all(*raws))
            middle = n.x_v[wide_rows(i)]
            attention_back(
                n, i, middle, n.kvin_v, n.qin_v, layer, lower, returns, turned, s
            )

        at = ARRIVED
        def gradient(index):
            left, right = factors[index]
            block_products(n.grads_v[index], left, right, sizes[index][0], s)
            gradient_store(index).start()

        def gradient_store(index):
            return pltpu.make_async_copy(n.grads_v[index], n.grads[index], n.grad_sems.at[index])

        def end_keys():
            returns.receive()
            keys_back(n, layer, returns, keyed, s)
            a1.wait()

        factors = [
            (n.a2_v, n.dup_v),
            (n.a2_v, n.dgate_v),
            (n.a1_v, n.dq_v),
            (n.hidden_v, n.dyb_v),
            (n.o_v, n.dhb_v),
            (n.a1_v, n.dk_v),
            (n.a1_v, n.dv_v),
        ]
        after = at + ARRIVED + s.units
        tasks = [(after, returns.send_rest), (after + 4, end_keys)]
        for index, step in enumerate((1, 2, 5, 3, 4, 6, 6)):
            tasks.append((after + step, lambda index=index: gradient(index)))
        tasks.sort(key=lambda item: item[0])
        pipeline(
            s.units,
            lower.stages(at)
            + second.stages(OUTPUT_AT, HOP + 1)
            + first.stages(0)
            + [
                (OUTPUT_AT, second.send, 1),
                (OUTPUT_AT + 3 * HOP + 3, close, 1),
                (at + ARRIVED, attention, WIDE // UNIT),
                (at, feed_both, WIDE // UNIT),
                (0, mix, WIDE // UNIT),
            ],
            tasks,
        )
        returns.finish()
        for index in range(len(sizes)):
            gradient_store(index).wait()

        def finish(u):
            first.finish(u)
            second.finish(u)
            lower.finish(u)
            stores.finish(u)

        each_of(s.units, finish)

    sizes = grad_sizes(s)
    backs = attention_back_shapes(s)
    blocks = block_shapes(s, sizes)
    return run_kernel(
        body,
        layer_ins(stream, saved, w, tables)
        | dict(
            grad=(cotangent, ANY),
            a1=(saved.a1, ANY),
            qraw=(saved.qraw, ANY),
            kraw=(saved.kraw, ANY),
            qk_gain=(w.qk_gain, VMEM),
            cosine=(tables.cosine, VMEM),
            sine=(tables.sine, VMEM),
        ),
        outputs({x: backs[x] for x in dict(dq=0, dk=0, dv=0)})
        | attention_back_sums(s)
        | dict(
            y=(shaped(s.rows, s.model), ANY),
            grads=[(shaped(*block), ANY) for block in blocks],
        ),
        layer_scratch(stream, s)
        | buffers(kept_shapes(s))
        | buffers(backs)
        | attention_back_scratch(s)
        | dict(
            y_v=VMEM((s.rows, s.model), BF16),
            a1_v=VMEM((s.rows, s.model), BF16),
            grads_v=[VMEM(block, BF16) for block in blocks],
            grad_sems=DMA((len(sizes),)),
            inv_v=VMEM((s.rows, HEAD_SIZE), F32),
            grad_v=VMEM((s.rows, s.model), BF16),
            g_v=VMEM((s.rows, s.model), F32),
            qraw_v=VMEM((s.rows, s.queries), F32),
            kraw_v=VMEM((s.rows, s.keys), F32),
            lower=line_scratch(s.units, s.model),
        ),
        2 + layer,
    )


def halving_partners(count):
    c, t = place()
    return [(c >= 0, (c ^ (1 << b), t)) for b in range(count.bit_length() - 1)]


def block_products(target, left, right, line, s):
    bits = s.count.bit_length() - 1
    half = s.count // 2
    for part in range(2):
        product = dot_tn(left[:, part * half * line : (part + 1) * half * line], right[...])
        for k in range(half):
            block = part * half + k
            at = tuple((block >> b) & 1 for b in range(bits - 1, -1, -1))
            target[at + (slice(0, line),)] = product[k * line : (k + 1) * line].astype(BF16)


def block_shapes(s, sizes):
    bits = s.count.bit_length() - 1
    return [(2,) * bits + (line + -line % 16, width) for line, width in sizes]


class Scatter:
    def __init__(self, n, s, sizes, factors=None):
        self.n, self.s, self.sizes, self.factors = n, s, sizes, factors
        self.bits = s.count.bit_length() - 1
        self.c, self.t = place()
        self.beside = []

    def bit(self, b):
        return (self.c >> b) & 1

    def order(self, index):
        rest = list(range(1, self.bits))
        return [0] + (rest if index % 2 == 0 else rest[::-1])

    def spot(self, picks):
        low = 0 if self.factors else 1
        return tuple(picks.get(b, slice(None)) for b in range(self.bits - 1, low - 1, -1))

    def own(self, index):
        return (self.n.whole_v if self.factors else self.n.own)[index]

    def copy(self, index, step):
        order = self.order(index)
        picks = {b: self.bit(b) for b in order[:step]}
        picks[order[step]] = 1 - self.bit(order[step])
        if step == 0 and not self.factors:
            source = self.n.whole[index].at[
                (slice(None),) * (self.bits - 1) + (1 - self.bit(0),)
            ]
        else:
            source = self.own(index).at[self.spot(picks)]
        sems = self.n.scatter_sems
        return remote(
            source,
            self.n.got[index * self.bits + step],
            sems.at[0, index, step],
            sems.at[1, index, step],
            (self.c ^ (1 << order[step]), self.t),
        )

    def load(self, index):
        return pltpu.make_async_copy(
            self.n.whole[index].at[(slice(None),) * (self.bits - 1) + (self.bit(0),)],
            self.n.own[index],
            self.n.scatter_load_sems.at[index],
        )

    def start(self, index):
        if self.factors:
            left, right, needed = self.factors[index]
            wait_all(*needed)
            block_products(self.own(index), left, right, self.sizes[index][0], self.s)
        else:
            self.load(index).start()
        self.copy(index, 0).start()

    def add(self, index, step):
        order = self.order(index)
        if step == 0 and not self.factors:
            self.load(index).wait()
        self.copy(index, step).wait_recv()
        free = [b for b in range(self.bits - 1, 0, -1) if b not in order[: step + 1]]
        own, got = self.own(index), self.n.got[index * self.bits + step]
        line = self.sizes[index][0]

        def one(k, carry):
            picks = {b: (k >> (len(free) - 1 - i)) & 1 for i, b in enumerate(free)}
            here = self.spot({b: self.bit(b) for b in order[: step + 1]} | picks)
            total = own[here].astype(F32) + got[tuple(picks[b] for b in free)].astype(F32)
            if step == self.bits - 1:
                self.sum_of(index)[...] = total[:line]
            else:
                own[here] = total.astype(BF16)
            return carry

        if free:
            lax.fori_loop(0, 1 << len(free), one, 0)
        else:
            one(0, 0)
        if step < self.bits - 1:
            self.copy(index, step + 1).start()
        else:
            for other in self.beside:
                other[index].wait()
            self.store(index).start()

    def sum_of(self, index):
        return self.n.sums_v[index].at[0] if self.factors else self.n.sums_v[index]

    def store(self, index):
        return pltpu.make_async_copy(
            self.n.sums_v[index], self.n.sums[index], self.n.scatter_store_sems.at[index]
        )

    def tasks(self, every, bases):
        found = []
        for index in range(len(self.sizes)):
            found.append(((bases[0] + index) * every, lambda index=index: self.start(index)))
            for step in range(self.bits):
                at = (bases[min(step + 1, len(bases) - 1)] + index) * every
                at += 100 * max(0, step + 2 - len(bases))
                found.append((at, lambda index=index, step=step: self.add(index, step)))
        found.sort(key=lambda item: item[0])
        return found

    def finish(self):
        for index in range(len(self.sizes)):
            self.store(index).wait()
            for step in range(self.bits):
                self.copy(index, step).wait_send()


def scatter_scratch(s, sizes, computed, layers):
    bits = s.count.bit_length() - 1
    tails = [(line + -line % 16, width) for line, width in sizes]
    found = dict(
        sums_v=[VMEM(((layers,) if computed else ()) + size, F32) for size in sizes],
        got=[
            VMEM((2,) * (bits - 1 - step) + tail, BF16) for tail in tails for step in range(bits)
        ],
        scatter_sems=DMA((2, len(sizes), bits)),
        scatter_load_sems=DMA((len(sizes),)),
        scatter_store_sems=DMA((len(sizes),)),
    )
    if computed:
        return found | dict(whole_v=[VMEM((2,) * bits + tail, BF16) for tail in tails])
    return found | dict(own=[VMEM((2,) * (bits - 1) + tail, BF16) for tail in tails])


def block_view(array, s):
    bits = s.count.bit_length() - 1
    line = array.shape[0] // s.count
    view = array.reshape((2,) * bits + (line, array.shape[1]))
    if line % 16:
        view = jnp.pad(view, [(0, 0)] * bits + [(0, -line % 16), (0, 0)])
    return view


def factor_pairs(k):
    return [
        (k.a2, k.dup),
        (k.a2, k.dgate),
        (k.a1, k.dq),
        (k.hidden, k.dyb),
        (k.o, k.dhb),
        (k.a1, k.dk),
        (k.a1, k.dv),
    ]


def grad_sizes(s):
    return [
        (s.model // s.count, s.hidden),
        (s.model // s.count, s.hidden),
        (s.model // s.count, s.queries),
        (s.hidden // s.count, s.model),
        (s.queries // s.count, s.model),
        (s.model // s.count, s.keys),
        (s.model // s.count, s.keys),
    ]


def head_ins(k, w):
    return dict(
        hq=(k.dq, ANY),
        hk=(k.dk, ANY),
        hv=(k.dv, ANY),
        wq=(w.w_query, ANY),
        wk=(w.key_weight, ANY),
        wv=(w.value_weight, ANY),
        x=(k.x, ANY),
        attn_gain=(w.attn_gain, VMEM),
        grad=(k.dres, ANY),
    )


def head_scratch(k, s):
    return dict(
        hq_v=VMEM((s.rows, s.queries), BF16),
        hk_v=VMEM((s.rows, s.keys), BF16),
        hv_v=VMEM((s.rows, s.keys), BF16),
        wq_v=VMEM((s.model, s.queries), BF16),
        wk_v=VMEM((s.model, s.keys), BF16),
        wv_v=VMEM((s.model, s.keys), BF16),
        x_v=VMEM((s.rows, s.model), k.x.dtype),
        g_v=VMEM((s.rows, s.model), F32),
        upper=line_scratch(s.units, s.model),
        load_sems=DMA((32,)),
        store_sems=DMA((10, s.units)),
    )


def head_loads(n, loads, layer):
    early = (
        loads(n.hq, n.hq_v),
        loads(n.wq.at[layer], n.wq_v),
        loads(n.hk, n.hk_v),
        loads(n.wk.at[layer], n.wk_v),
        loads(n.hv, n.hv_v),
        loads(n.wv.at[layer], n.wv_v),
    )
    return early, (loads(n.x, n.x_v), loads(n.grad, n.g_v))


def head_inputs(n, i, upper):
    here = wide_rows(i)
    upper.push(
        i,
        dot_nt(n.hq_v[here], n.wq_v[...])
        + dot_nt(n.hk_v[here], n.wk_v[...])
        + dot_nt(n.hv_v[here], n.wv_v[...]),
    )


def head_norm(n, here, grad_in, layer):
    stream = n.x_v[here].astype(F32)
    inverse = rms_inverse(stream)
    unit = stream * inverse
    n.attn_sum[...] += column_sum(grad_in * unit)
    n.g_v[here] += norm_back(grad_in, unit, inverse, n.attn_gain[layer : layer + 1])


def backward_layer(layer, kept, w, tables, s):
    above, here_kept = kept[layer + 1], kept[layer]
    sizes = grad_sizes(s)

    def body(n):
        loads = Loads(n.load_sems)
        early, middle_loads = head_loads(n, loads, layer + 1)
        scatter = Scatter(n, s, sizes)
        feeds = (
            loads(n.wd.at[layer], n.wd_v),
            loads(n.gate, n.gate_v),
            loads(n.up, n.up_v),
            loads(n.wg.at[layer], n.wg_v),
            loads(n.wu.at[layer], n.wu_v),
        )
        lates = (
            loads(n.wo.at[layer], n.wo_v),
            loads(n.q, n.q_v),
            loads(n.kv, n.kv_v),
            loads(n.o, n.o_v),
            loads(n.inv, n.inv_v),
            loads(n.qraw, n.qraw_v),
            loads(n.kraw, n.kraw_v),
        )
        stores = Stores(n.store_sems)
        fed_back = (stores(n.dyb_v, n.dyb), stores(n.dgate_v, n.dgate), stores(n.dup_v, n.dup))
        turned = (stores(n.g_v, n.dres), stores(n.dhb_v, n.dhb), stores(n.dq_v, n.dq))
        keyed = (stores(n.dk_v, n.dk), stores(n.dv_v, n.dv))
        upper, lower = LineSum(n.upper), LineSum(n.lower)
        returns = Returns(n, s)
        greet(line_partners() + halo_partners(s.rows, s.count) + halving_partners(s.count))
        n.attn_sum[...] = jnp.zeros_like(n.attn_sum)
        back_start(n, returns)
        wait_all(*early)

        def middle_copy(i):
            rows = wide_rows(i)
            return pltpu.make_async_copy(n.h.at[rows], n.x_v.at[rows], n.middle_sems.at[i])

        def inputs(i):
            head_inputs(n, i, upper)

        def pass_norm(i):
            pl.when(i == 0)(lambda: wait_all(*middle_loads, *feeds))
            here = wide_rows(i)
            head_norm(n, here, upper.take_wide(i), layer + 1)
            middle_copy(i).start()
            gate, up = n.gate_v[here].astype(F32), n.up_v[here].astype(F32)
            feed_back(n, i, gate, up, lower, fed_back)

        def attention(i):
            pl.when(i == 0)(lambda: wait_all(*lates))
            middle_copy(i).wait()
            attention_back(
                n, i, n.x_v[wide_rows(i)], n.kv_v, n.q_v, layer, lower, returns, turned, s
            )

        at = ARRIVED
        pipeline(
            s.units,
            lower.stages(at)
            + upper.stages(0)
            + [
                (at + ARRIVED, attention, WIDE // UNIT),
                (at, pass_norm, WIDE // UNIT),
                (0, inputs, WIDE // UNIT),
            ],
            scatter.tasks(64 // UNIT, SCATTER_MIDDLE),
        )
        returns.send_rest()
        returns.receive()
        keys_back(n, layer, returns, keyed, s)
        returns.finish()
        scatter.finish()

        def finish(u):
            upper.finish(u)
            lower.finish(u)
            stores.finish(u)

        each_of(s.units, finish)

    whole = above.grads or [
        block_view(dot_tn(left, right).astype(BF16), s) for left, right in factor_pairs(above)
    ]
    held = dict(
        gate=here_kept.gate,
        up=here_kept.up,
        q=here_kept.q,
        kv=here_kept.kv,
        o=here_kept.o,
        inv=here_kept.inv,
        qraw=here_kept.qraw,
        kraw=here_kept.kraw,
    )
    return run_kernel(
        body,
        head_ins(above, w)
        | {x: (array, ANY) for x, array in held.items()}
        | dict(
            h=(here_kept.h, ANY),
            wd=(w.w_down, ANY),
            wg=(w.w_gate, ANY),
            wu=(w.w_up, ANY),
            wo=(w.w_out, ANY),
            ffn_gain=(w.ffn_gain, VMEM),
            qk_gain=(w.qk_gain, VMEM),
            cosine=(tables.cosine, VMEM),
            sine=(tables.sine, VMEM),
            lowest=(tables.lowest, VMEM),
            whole=[(array, ANY) for array in whole],
        ),
        outputs(attention_back_shapes(s))
        | attention_back_sums(s)
        | dict(
            attn_sum=(shaped(1, s.model, kind=F32), VMEM),
            sums=[(shaped(*size, kind=F32), ANY) for size in sizes],
        ),
        head_scratch(above, s)
        | weight_scratch(s)
        | {x + "_v": VMEM(array.shape, array.dtype) for x, array in held.items()}
        | buffers(attention_back_shapes(s))
        | attention_back_scratch(s)
        | scatter_scratch(s, sizes, False, 1)
        | dict(
            lower=line_scratch(s.units, s.model),
            middle_sems=DMA((s.rows // WIDE,)),
        ),
        20 + layer,
    )


def backward_end(kept, w, s):
    bottom = kept[0]
    sizes = grad_sizes(s)
    layers = len(kept)
    width = s.model // s.count
    bits = s.count.bit_length() - 1
    tp_bits = s.line.bit_length() - 1
    rounds = [(1 << b, 0) for b in range(bits)] + [(0, 1 << b) for b in range(tp_bits)]

    def body(n):
        c, t = place()
        loads = Loads(n.load_sems)
        early, lates = head_loads(n, loads, 0)
        a2, dup, dgate = loads(n.a2, n.a2_v), loads(n.dup, n.dup_v), loads(n.dgate, n.dgate_v)
        a1, hidden, dyb = loads(n.a1, n.a1_v), loads(n.hidden, n.hidden_v), loads(n.dyb, n.dyb_v)
        o, dhb = loads(n.o, n.o_v), loads(n.dhb, n.dhb_v)
        factors = [
            (n.a2_v, n.dup_v, (a2, dup)),
            (n.a2_v, n.dgate_v, (dgate,)),
            (n.a1_v, n.hq_v, (a1,)),
            (n.hidden_v, n.dyb_v, (hidden, dyb)),
            (n.o_v, n.dhb_v, (o, dhb)),
            (n.a1_v, n.hk_v, ()),
            (n.a1_v, n.hv_v, ()),
        ]
        scatter = Scatter(n, s, sizes, factors)
        stores = Stores(n.store_sems)
        out = stores(n.g_v, n.dres)
        upper = LineSum(n.upper)
        others = [(c >= 0, ((c + k) % s.count, t)) for k in range(1, s.count)]
        lines = [(c >= 0, (c, t ^ (1 << b))) for b in range(tp_bits)]
        greet(line_partners() + halving_partners(s.count) + others + lines)
        n.attn_sum[...] = jnp.zeros_like(n.attn_sum)
        n.acc[...] = jnp.zeros_like(n.acc)
        n.gains[...] = jnp.zeros_like(n.gains)
        for layer in range(layers):
            n.acc[0, 2 * layer : 2 * layer + 2] = n.qk_in[layer][...]
        wait_all(*early)
        scatter.beside = [
            [
                loads(n.done[(layer - 1) * len(sizes) + index], n.sums_v[index].at[layer])
                for index in range(len(sizes))
            ]
            for layer in range(1, layers)
        ]

        def head_copy(k):
            return remote(
                n.acc.at[k],
                n.other.at[k],
                n.small_sems.at[0, k],
                n.small_sems.at[1, k],
                (c ^ rounds[k][0], t ^ rounds[k][1]),
            )

        def head_step(k):
            if k > 0:
                head_copy(k - 1).wait_recv()
                n.acc[k] = n.acc[k - 1] + n.other[k - 1]
            if k < len(rounds):
                head_copy(k).start()

        def pass_norm(u):
            pl.when(u == 0)(lambda: wait_all(*lates))
            head_norm(n, unit_rows(u), upper.take(u), 0)
            send_out([u], out)

        tasks = scatter.tasks(64 // UNIT, SCATTER_END)
        tasks += [(2 * k + 1, lambda k=k: head_step(k)) for k in range(len(rounds) + 1)]
        tasks.sort(key=lambda item: item[0])
        pipeline(
            s.units,
            upper.stages(0)
            + [
                (3 * HOP, pass_norm, 1),
                (0, lambda i: head_inputs(n, i, upper), WIDE // UNIT),
            ],
            tasks,
        )
        gains = [n.attn_sum] + n.attn_in + n.ffn_in
        for d in range(s.count):
            for row, gain in enumerate(gains):
                n.gains[d, row : row + 1] = gain[:, d * width : (d + 1) * width]

        def gain_copy(k):
            to = (c + k) % s.count
            return remote(
                n.gains.at[to],
                n.gains_got.at[k],
                n.gain_sems.at[0, k],
                n.gain_sems.at[1, k],
                (to, t),
            )

        for k in range(1, s.count):
            gain_copy(k).start()
        for layer in range(layers):
            n.qk_total[layer] = n.acc[len(rounds), 2 * layer : 2 * layer + 2]
        total = n.gains[c]
        for k in range(1, s.count):
            gain_copy(k).wait_recv()
            total = total + n.gains_got[k]
        n.attn_total[...] = total[:layers]
        n.ffn_total[...] = total[layers : 2 * layers]
        for k in range(1, s.count):
            gain_copy(k).wait_send()
        for k in range(len(rounds)):
            head_copy(k).wait_send()
        scatter.finish()

        def finish(u):
            upper.finish(u)
            stores.finish(u)

        each_of(s.units, finish)

    held = dict(
        a1=bottom.a1,
        a2=bottom.a2,
        o=bottom.o,
        hidden=bottom.hidden,
        dyb=bottom.dyb,
        dgate=bottom.dgate,
        dup=bottom.dup,
        dhb=bottom.dhb,
    )
    small = (len(rounds) + 1, 2 * layers + -2 * layers % 8, HEAD_SIZE)
    slabs = (s.count, 2 * layers + -2 * layers % 8, width)
    return run_kernel(
        body,
        head_ins(bottom, w)
        | {x: (array, ANY) for x, array in held.items()}
        | dict(
            qk_in=[(k.qk_sum, VMEM) for k in kept],
            attn_in=[(k.attn_sum, VMEM) for k in kept[1:]],
            ffn_in=[(k.ffn_sum, VMEM) for k in kept],
            done=[(array, ANY) for k in kept[1:] for array in k.sums],
        ),
        dict(
            dres=(shaped(s.rows, s.model, kind=F32), ANY),
            attn_total=(shaped(layers, width, kind=F32), VMEM),
            ffn_total=(shaped(layers, width, kind=F32), VMEM),
            qk_total=(shaped(layers, 2, HEAD_SIZE, kind=F32), VMEM),
            sums=[(shaped(layers, *size, kind=F32), ANY) for size in sizes],
        ),
        head_scratch(bottom, s)
        | {x + "_v": VMEM(array.shape, array.dtype) for x, array in held.items()}
        | scatter_scratch(s, sizes, True, layers)
        | dict(
            attn_sum=VMEM((1, s.model), F32),
            acc=VMEM(small, F32),
            other=VMEM(small, F32),
            gains=VMEM(slabs, F32),
            gains_got=VMEM(slabs, F32),
            small_sems=DMA((2, len(rounds))),
            gain_sems=DMA((2, s.count)),
        ),
        19,
    )


OUTPUT_AT = 12
def deliver(arrays):
    def body(n):
        copies = []
        for index, (source, target, held) in enumerate(zip(n.given, n.result, n.held)):
            copies.append(
                (
                    pltpu.make_async_copy(source, held, n.sems.at[0, index]),
                    pltpu.make_async_copy(held, target, n.sems.at[1, index]),
                )
            )
            copies[-1][0].start()
        for fetch, put in copies:
            fetch.wait()
            put.start()
        for fetch, put in copies:
            put.wait()

    return run_kernel(
        body,
        dict(given=[(array, ANY) for array in arrays]),
        dict(result=[(shaped(*array.shape, kind=array.dtype), ANY) for array in arrays]),
        dict(
            held=[VMEM(array.shape, array.dtype) for array in arrays],
            sems=DMA((2, len(arrays))),
        ),
        None,
    ).result


SCATTER_MIDDLE = (0, 3, 9, 16)
SCATTER_END = (0, 2, 7, 11)


def body(hidden_in, doc_lengths, cotangent, attn_gain, ffn_gain, qk_gain, w_query, *others):
    key_weight, value_weight, w_out, w_gate, w_up, w_down = others
    w = types.SimpleNamespace(
        attn_gain=attn_gain,
        ffn_gain=ffn_gain,
        qk_gain=qk_gain,
        w_query=w_query,
        key_weight=key_weight,
        value_weight=value_weight,
        w_out=w_out,
        w_gate=w_gate,
        w_up=w_up,
        w_down=w_down,
    )
    rows, model = hidden_in.shape
    layers, unused, queries = w_query.shape
    keys = key_weight.shape[2]
    s = types.SimpleNamespace(
        rows=rows,
        model=model,
        queries=queries,
        keys=keys,
        hidden=w_gate.shape[2],
        units=rows // UNIT,
        groups=keys // HEAD_SIZE,
        repeat=queries // keys,
        count=lax.axis_size(CTX),
        line=lax.axis_size(TP),
    )
    tables = make_tables(doc_lengths, rows)

    kept = []
    stream = hidden_in
    saved = first_projection(stream, w, tables, s)
    for layer in range(layers):
        if layer < layers - 1:
            result = forward_layer(layer, stream, saved, w, tables, s)
        else:
            result = turn_layer(layer, stream, saved, cotangent, w, tables, s)
        own = dict(a1=saved.a1, qraw=saved.qraw, kraw=saved.kraw, q=saved.q, kv=saved.kv)
        kept.append(types.SimpleNamespace(**(dict(grads=None) | vars(result) | own | dict(x=stream))))
        stream = result.y
        saved = result

    for layer in range(layers - 2, -1, -1):
        result = backward_layer(layer, kept, w, tables, s)
        kept[layer + 1].attn_sum = result.attn_sum
        kept[layer + 1].sums = result.sums
        vars(kept[layer]).update(
            dyb=result.dyb,
            dgate=result.dgate,
            dup=result.dup,
            dhb=result.dhb,
            dq=result.dq,
            dk=result.dk,
            dv=result.dv,
            dres=result.dres,
            ffn_sum=result.ffn_sum,
            qk_sum=result.qk_sum,
        )
    end = backward_end(kept, w, s)
    small = [end.attn_total, end.ffn_total, end.qk_total]
    stream, grad, *gains, up, gate, query, down, out, key, value = deliver(
        [stream, end.dres] + small + end.sums
    )
    return (
        stream,
        grad,
        *gains,
        query,
        key,
        value,
        out,
        gate,
        up,
        down,
    )


def solution(mesh):
    by_rows = P(CTX, None)
    by_columns = P(None, None, TP)
    by_hidden = P(None, TP, None)
    grad_columns = P(None, CTX, TP)
    grad_rows = P(None, (TP, CTX), None)
    return jax.shard_map(
        body,
        mesh=mesh,
        in_specs=(by_rows, P(), by_rows, P(), P(), P())
        + (by_columns,) * 3
        + (by_hidden,)
        + (by_columns,) * 2
        + (by_hidden,),
        out_specs=(by_rows, by_rows, P(None, CTX), P(None, CTX), P())
        + (grad_columns,) * 3
        + (grad_rows,)
        + (grad_columns,) * 2
        + (grad_rows,),
        check_vma=False,
    )
```

```python
import types

import jax
import jax.numpy as jnp
from jax import lax
from jax.experimental import pallas as pl
from jax.experimental.pallas import tpu as pltpu
from jax.sharding import PartitionSpec as P

HEAD_SIZE = 128
ATTENTION_WINDOW = 1024
EPS = 1e-06
THETA = 1000000.0

UNIT = 64
WIDE = 128
KEY_BLOCK = 384
HOP = 2
ARRIVED = 3 * HOP + WIDE // UNIT - 1
CTX = "ctx"
TP = "tp"
MESH = pl.DeviceIdType.MESH
F32 = jnp.float32
BF16 = jnp.bfloat16
SCALE = HEAD_SIZE ** (-0.5)
EXP2_SCALE = SCALE * 1.4426950408889634
ANY = pl.ANY
VMEM = pltpu.VMEM
DMA = pltpu.SemaphoreType.DMA


def dot_nn(left, right):
    return jnp.dot(left, right, preferred_element_type=F32)


def dot_nt(left, right):
    return lax.dot_general(left, right, (((1,), (1,)), ((), ())), preferred_element_type=F32)


def dot_tn(left, right):
    return lax.dot_general(left, right, (((0,), (0,)), ((), ())), preferred_element_type=F32)


def rms_inverse(value_rows):
    return lax.rsqrt(jnp.mean(value_rows * value_rows, axis=-1, keepdims=True) + EPS)


def rotate(value_rows, cosine, sine):
    return value_rows * cosine + pltpu.roll(value_rows, HEAD_SIZE // 2, 1) * sine


def unrotate(grad, cosine, sine):
    return grad * cosine + pltpu.roll(grad * sine, HEAD_SIZE // 2, 1)


def norm_back(grad, unit, inverse, gain):
    scaled = grad * gain
    inner = jnp.mean(scaled * unit, axis=-1, keepdims=True)
    return inverse * (scaled - unit * inner)


def column_sum(value_rows):
    return jnp.sum(value_rows, axis=0, keepdims=True)


def make_tables(lengths, rows):
    start = lax.axis_index(CTX) * rows
    spot = start + jnp.arange(rows, dtype=jnp.int32)
    order = jnp.arange(lengths.shape[0])
    ends = jnp.sum(jnp.where(order[None, :] <= order[:, None], lengths[None, :], 0), axis=1)
    passed = ends[None, :] <= spot[:, None]
    begin = jnp.sum(jnp.where(passed, lengths[None, :], 0), axis=1)
    lane = jnp.arange(HEAD_SIZE)
    half = HEAD_SIZE // 2
    freq = THETA ** (-((lane % half).astype(F32) * 2.0) / HEAD_SIZE)
    angle = (spot - begin).astype(F32)[:, None] * freq[None, :]
    lowest = jnp.maximum(begin, spot - (ATTENTION_WINDOW - 1)) - (start - ATTENTION_WINDOW)
    return types.SimpleNamespace(
        cosine=jnp.cos(angle),
        sine=jnp.sin(angle) * jnp.where(lane < half, -1.0, 1.0)[None, :],
        lowest=lowest[:, None],
    )


def halo_plan(rows):
    reach = -(-ATTENTION_WINDOW // rows)
    plan = []
    for hop in range(1, reach + 1):
        need = min(rows, ATTENTION_WINDOW - (hop - 1) * rows)
        plan.append((hop, need, ATTENTION_WINDOW - (hop - 1) * rows - need))
    return plan


def unit_rows(u):
    return pl.ds(pl.multiple_of(u * UNIT, UNIT), UNIT)


def wide_rows(w):
    return pl.ds(pl.multiple_of(w * WIDE, WIDE), WIDE)


def subs(w):
    return [w * (WIDE // UNIT) + i for i in range(WIDE // UNIT)]


def shaped(*shape, kind=BF16):
    return jax.ShapeDtypeStruct(shape, kind)


def listed(value):
    return list(value) if isinstance(value, list) else [value]


def run_kernel(body, ins, outs, scratch, collective_id):
    groups = [ins, outs, scratch]
    flat = [[x for value in group.values() for x in listed(value)] for group in groups]

    def named(values, chosen):
        values = list(values)
        found = {}
        for group in chosen:
            for name, value in group.items():
                if isinstance(value, list):
                    found[name] = [values.pop(0) for unused in value]
                else:
                    found[name] = values.pop(0)
        return types.SimpleNamespace(**found)

    results = pl.pallas_call(
        lambda *refs: body(named(refs, groups)),
        out_shape=[shape for shape, unused in flat[1]],
        in_specs=[pl.BlockSpec(memory_space=space) for unused, space in flat[0]],
        out_specs=[pl.BlockSpec(memory_space=space) for unused, space in flat[1]],
        scratch_shapes=flat[2],
        compiler_params=pltpu.CompilerParams(
            collective_id=collective_id,
            has_side_effects=collective_id is not None,
            vmem_limit_bytes=62 * 2**20,
        ),
    )(*[array for array, unused in flat[0]])
    return named(results, [outs])


def place():
    return lax.axis_index(CTX), lax.axis_index(TP)


def remote(source, target, send, receive, device):
    return pltpu.make_async_remote_copy(
        src_ref=source,
        dst_ref=target,
        send_sem=send,
        recv_sem=receive,
        device_id=device,
        device_id_type=MESH,
    )


def greet(partners):
    barrier = pltpu.get_barrier_semaphore()
    total = 0
    for exists, device in partners:
        total = total + jnp.where(exists, 1, 0)

        @pl.when(exists)
        def _():
            pl.semaphore_signal(barrier, inc=1, device_id=device, device_id_type=MESH)

    pl.semaphore_wait(barrier, total)


def line_partners():
    c, t = place()
    outer = (t == 0) | (t == 3)
    return [
        (outer, (c, jnp.where(t == 0, 1, 2))),
        (jnp.logical_not(outer), (c, jnp.where(t == 1, 0, 3))),
        (jnp.logical_not(outer), (c, jnp.clip(3 - t, 1, 2))),
    ]


def halo_partners(rows, count):
    c, t = place()
    partners = []
    for hop, unused, unused_too in halo_plan(rows):
        partners.append((c + hop < count, (jnp.minimum(c + hop, count - 1), t)))
        partners.append((c >= hop, (jnp.maximum(c - hop, 0), t)))
    return partners


class LineSum:
    def __init__(self, refs):
        self.part, self.total, self.inner, self.sems = refs
        self.c, self.t = place()
        self.outer = (self.t == 0) | (self.t == 3)
        self.is_inner = jnp.logical_not(self.outer)

    def copy(self, source, target, u, send, receive, to):
        return remote(
            source.at[u],
            target.at[u],
            self.sems.at[send, u],
            self.sems.at[receive, u],
            (self.c, to),
        )

    def inwards(self, u):
        return self.copy(self.part, self.total, u, 0, 1, jnp.where(self.t < 2, 1, 2))

    def across(self, u):
        return self.copy(self.part, self.inner, u, 0, 2, jnp.clip(3 - self.t, 1, 2))

    def outwards(self, u):
        return self.copy(self.total, self.total, u, 3, 4, jnp.where(self.t < 2, 0, 3))

    def hold(self, w, value):
        for i, u in enumerate(subs(w)):
            self.part[u] = value[i * UNIT : (i + 1) * UNIT].astype(BF16)

    def send(self, u):
        @pl.when(self.outer)
        def _():
            self.inwards(u).start()

    def push(self, w, value):
        self.hold(w, value)
        for u in subs(w):
            self.send(u)

    def meet(self, u):
        @pl.when(self.is_inner)
        def _():
            self.inwards(u).wait_recv()
            self.part[u] = (self.part[u].astype(F32) + self.total[u].astype(F32)).astype(BF16)
            self.across(u).start()

    def spread(self, u):
        @pl.when(self.is_inner)
        def _():
            self.across(u).wait_recv()
            self.total[u] = (self.part[u].astype(F32) + self.inner[u].astype(F32)).astype(BF16)
            self.outwards(u).start()

    def take(self, u):
        @pl.when(self.outer)
        def _():
            self.outwards(u).wait_recv()

        return self.total[u].astype(F32)

    def take_wide(self, w):
        return jnp.concatenate([self.take(u) for u in subs(w)], axis=0)

    def finish(self, u):
        @pl.when(self.outer)
        def _():
            self.inwards(u).wait_send()

        @pl.when(self.is_inner)
        def _():
            self.across(u).wait_send()
            self.outwards(u).wait_send()

    def stages(self, begin, hop=HOP):
        return [(begin + 2 * hop, self.spread, 1), (begin + hop, self.meet, 1)]


def line_scratch(units, width):
    block = VMEM((units, UNIT, width), BF16)
    return [block, block, block, DMA((5, units))]


def pipeline(units, stages, tasks=()):
    steps = units + max(delay + 1 - taken for delay, unused, taken in stages)

    def step(s, carry):
        for delay, function, taken in stages:
            ready = (s >= delay) & (s < units + delay)
            if taken > 1:
                ready = ready & ((s - delay) % taken == 0)

            @pl.when(ready)
            def _():
                function((s - delay) // taken if taken > 1 else s - delay)

        for at, task in tasks:
            if at < steps:

                @pl.when(s == at)
                def _():
                    task()

        return carry

    lax.fori_loop(0, steps, step, 0)
    for at, task in tasks:
        if at >= steps:
            task()


def each_of(number, function):
    def step(u, carry):
        function(u)
        return carry

    lax.fori_loop(0, number, step, 0)


class Loads:
    def __init__(self, sems):
        self.sems, self.number = sems, 0

    def __call__(self, source, target):
        copy = pltpu.make_async_copy(source, target, self.sems.at[self.number])
        copy.start()
        self.number += 1
        return copy


def wait_all(*copies):
    for copy in copies:
        copy.wait()


class Stores:
    def __init__(self, sems):
        self.sems, self.copies = sems, []

    def __call__(self, source, target):
        index = len(self.copies)

        def copy(u):
            rows = unit_rows(u)
            return pltpu.make_async_copy(source.at[rows], target.at[rows], self.sems.at[index, u])

        self.copies.append(copy)
        return copy

    def finish(self, u):
        for copy in self.copies:
            copy(u).wait()


def send_out(units, *copies):
    for u in units:
        for copy in copies:
            copy(u).start()


class Halo:
    def __init__(self, keys, sems, rows, count):
        self.keys, self.sems, self.rows, self.count = keys, sems, rows, count
        self.plan = halo_plan(rows)
        self.c, self.t = place()

    def copy(self, index, u, hop, need, offset):
        target = pl.multiple_of(offset + u * UNIT - (self.rows - need), UNIT)
        return remote(
            self.keys.at[pl.ds(pl.multiple_of(ATTENTION_WINDOW + u * UNIT, UNIT), UNIT)],
            self.keys.at[pl.ds(target, UNIT)],
            self.sems.at[2 * index, u],
            self.sems.at[2 * index + 1, u],
            (jnp.minimum(self.c + hop, self.count - 1), self.t),
        )

    def each(self, u, function, receives):
        for index, (hop, need, offset) in enumerate(self.plan):
            exists = self.c >= hop if receives else self.c + hop < self.count

            @pl.when(exists & (u >= (self.rows - need) // UNIT))
            def _():
                function(self.copy(index, u, hop, need, offset))

    def blank(self):
        width = self.keys.shape[1]
        for hop, need, offset in self.plan:

            @pl.when(self.c < hop)
            def _():
                self.keys[offset : offset + need] = jnp.zeros((need, width), BF16)

    def send(self, u):
        self.each(u, lambda copy: copy.start(), False)

    def finish(self, u):
        self.each(u, lambda copy: copy.wait_recv(), True)
        self.each(u, lambda copy: copy.wait_send(), False)


def project_heads(n, raw, out, out_rows, rows, which, layer):
    cosine, sine = n.cosine[rows], n.sine[rows]
    gain = n.qk_gain[layer, which : which + 1]
    for head in range(raw.shape[1] // HEAD_SIZE):
        part = raw[:, head_cols(head)]
        part = part * rms_inverse(part) * gain
        out[out_rows, head_cols(head)] = rotate(part, cosine, sine).astype(BF16)


def project_keys(n, first, number, stream, layer):
    rows = pl.ds(pl.multiple_of(first, number), number)
    own = pl.ds(pl.multiple_of(ATTENTION_WINDOW + first, number), number)
    normed = (stream * rms_inverse(stream) * n.attn_gain[layer : layer + 1]).astype(BF16)
    n.a1_v[rows] = normed
    key = dot_nn(normed, n.wk_v[...])
    n.kraw_v[rows] = key
    n.kv_v[own, key.shape[1] :] = dot_nn(normed, n.wv_v[...]).astype(BF16)
    project_heads(n, key, n.kv_v, own, rows, 1, layer)


def project_queries(n, first, number, layer):
    rows = pl.ds(pl.multiple_of(first, number), number)
    query = dot_nn(n.a1_v[rows], n.wq_v[...])
    n.qraw_v[rows] = query
    project_heads(n, query, n.q_v, rows, rows, 0, layer)


def project_shapes(s):
    return dict(
        a1=((s.rows, s.model), BF16),
        qraw=((s.rows, s.queries), F32),
        kraw=((s.rows, s.keys), F32),
        q=((s.rows, s.queries), BF16),
        kv=((ATTENTION_WINDOW + s.rows, 2 * s.keys), BF16),
    )


def outputs(shapes):
    return {x: (shaped(*shape, kind=kind), ANY) for x, (shape, kind) in shapes.items()}


def buffers(shapes):
    return {x + "_v": VMEM(shape, kind) for x, (shape, kind) in shapes.items()}


def project_ins(w, tables):
    return dict(
        attn_gain=(w.attn_gain, VMEM),
        qk_gain=(w.qk_gain, VMEM),
        cosine=(tables.cosine, VMEM),
        sine=(tables.sine, VMEM),
        wq=(w.w_query, ANY),
        wk=(w.key_weight, ANY),
        wv=(w.value_weight, ANY),
    )


def project_scratch(s):
    return buffers(project_shapes(s)) | dict(
        wq_v=VMEM((s.model, s.queries), BF16),
        wk_v=VMEM((s.model, s.keys), BF16),
        wv_v=VMEM((s.model, s.keys), BF16),
        halo_sems=DMA((2 * len(halo_plan(s.rows)), s.units)),
    )


def first_scratch(s):
    return dict(
        first_a1=VMEM((s.rows, s.model), BF16),
        first_qraw=VMEM((s.rows, s.queries), F32),
        first_kraw=VMEM((s.rows, s.keys), F32),
        first_wq=VMEM((s.model, s.queries), BF16),
        first_wk=VMEM((s.model, s.keys), BF16),
        first_wv=VMEM((s.model, s.keys), BF16),
        first_sems=DMA((2 * len(halo_plan(s.rows)), s.units)),
    )


def first_outs(s):
    return outputs({"own_" + x: shape for x, shape in project_shapes(s).items()})


def first_view(n):
    return types.SimpleNamespace(
        attn_gain=n.attn_gain,
        qk_gain=n.qk_gain,
        cosine=n.cosine,
        sine=n.sine,
        a1_v=n.first_a1,
        qraw_v=n.first_qraw,
        kraw_v=n.first_kraw,
        q_v=n.qin_v,
        kv_v=n.kvin_v,
        wq_v=n.first_wq,
        wk_v=n.first_wk,
        wv_v=n.first_wv,
    )


def key_block(i, block):
    return pl.ds(pl.multiple_of(i * WIDE + block * KEY_BLOCK, HEAD_SIZE), KEY_BLOCK)


def visible(i, lowest, block, repeat):
    shape = (WIDE, KEY_BLOCK)
    col = block * KEY_BLOCK + lax.broadcasted_iota(jnp.int32, shape, 1)
    seen = col >= lowest - i * WIDE
    if (block + 1) * KEY_BLOCK > ATTENTION_WINDOW:
        row = ATTENTION_WINDOW + lax.broadcasted_iota(jnp.int32, shape, 0)
        seen = seen & (col <= row)
    keep = jnp.where(seen, 1.0, 0.0)
    return jnp.concatenate([keep] * repeat, axis=0)


def key_blocks():
    return (ATTENTION_WINDOW + WIDE) // KEY_BLOCK


def stacked(value, group, repeat):
    first = group * repeat
    return jnp.concatenate(
        [value[:, (first + r) * HEAD_SIZE : (first + r + 1) * HEAD_SIZE] for r in range(repeat)],
        axis=0,
    )


def head_cols(index):
    return slice(index * HEAD_SIZE, (index + 1) * HEAD_SIZE)


def attend(n, i, s):
    rows = wide_rows(i)
    lowest = n.lowest[rows]
    lane = lax.broadcasted_iota(jnp.int32, (WIDE, HEAD_SIZE), 1)
    query_rows = n.qin_v[rows]
    queries = [stacked(query_rows, g, s.repeat) for g in range(s.groups)]
    mixed = [jnp.zeros((s.repeat * WIDE, HEAD_SIZE), F32) for unused in queries]
    total = [jnp.zeros((s.repeat * WIDE, 1), F32) for unused in queries]
    for block in range(key_blocks()):
        keys = key_block(i, block)
        keep = visible(i, lowest, block, s.repeat)
        for g in range(s.groups):
            scores = dot_nt(queries[g], n.kvin_v[keys, head_cols(g)])
            weights = jnp.exp2(scores * EXP2_SCALE) * keep
            total[g] = total[g] + jnp.sum(weights, axis=-1, keepdims=True)
            values = n.kvin_v[keys, head_cols(s.groups + g)]
            mixed[g] = mixed[g] + dot_nn(weights.astype(BF16), values)
    inverses = jnp.zeros((WIDE, HEAD_SIZE), F32)
    for g in range(s.groups):
        inverse = 1.0 / total[g]
        result = (mixed[g] * inverse).astype(BF16)
        for r in range(s.repeat):
            head = g * s.repeat + r
            part = slice(r * WIDE, (r + 1) * WIDE)
            n.o_v[rows, head_cols(head)] = result[part]
            inverses = jnp.where(lane == head, inverse[part], inverses)
    n.inv_v[rows] = inverses


def attend_back(n, i, grad_out, keys_ref, query_ref, s):
    rows = wide_rows(i)
    lowest = n.lowest[rows]
    query_rows, mixed_rows, inverses = query_ref[rows], n.o_v[rows], n.inv_v[rows]
    queries, grads, inners, scales, found = [], [], [], [], []
    for g in range(s.groups):
        queries.append(stacked(query_rows, g, s.repeat))
        grads.append(stacked(grad_out, g, s.repeat))
        mixed = stacked(mixed_rows, g, s.repeat)
        inners.append(
            jnp.sum(grads[g].astype(F32) * mixed.astype(F32), axis=-1, keepdims=True)
        )
        heads = [g * s.repeat + r for r in range(s.repeat)]
        scales.append(jnp.concatenate([inverses[:, h : h + 1] for h in heads], axis=0))
        found.append(jnp.zeros((s.repeat * WIDE, HEAD_SIZE), F32))
    for block in range(key_blocks()):
        keys = key_block(i, block)
        keep = visible(i, lowest, block, s.repeat)
        for g in range(s.groups):
            key_rows = keys_ref[keys, head_cols(g)]
            scores = dot_nt(queries[g], key_rows)
            probs = jnp.exp2(scores * EXP2_SCALE) * (keep * scales[g])
            grad_probs = dot_nt(grads[g], keys_ref[keys, head_cols(s.groups + g)])
            grad_scores = (probs * (grad_probs - inners[g])).astype(BF16)
            found[g] = found[g] + dot_nn(grad_scores, key_rows)
            n.dkv_v[keys, head_cols(g)] += dot_tn(grad_scores, queries[g])
            n.dkv_v[keys, head_cols(s.groups + g)] += dot_tn(probs.astype(BF16), grads[g])
    return [
        found[g][r * WIDE : (r + 1) * WIDE] for g in range(s.groups) for r in range(s.repeat)
    ]


def head_back(n, rows, grad, raw, which, layer):
    gain = n.qk_gain[layer, which : which + 1]
    turned = unrotate(grad, n.cosine[rows], n.sine[rows])
    inverse = rms_inverse(raw)
    unit = raw * inverse
    n.qk_sum[which : which + 1] += column_sum(turned * unit)
    return norm_back(turned, unit, inverse, gain).astype(BF16)


class Returns:
    def __init__(self, n, s):
        self.grads, self.low, self.back, self.sems = n.dkv_v, n.low_v, n.back_v, n.return_sems
        self.s, self.plan = s, halo_plan(s.rows)
        self.c, self.t = place()
        self.blocks = []
        for index, (hop, need, offset) in enumerate(self.plan):
            for b in range(need // WIDE):
                self.blocks.append((index, hop, offset + b * WIDE, b * WIDE))
        self.blocks.sort(key=lambda item: item[2])

    def copy(self, number):
        index, hop, source, target = self.blocks[number]
        return remote(
            self.low.at[pl.ds(source, WIDE)],
            self.back[index].at[pl.ds(target, WIDE)],
            self.sems.at[0, number],
            self.sems.at[1, number],
            (jnp.maximum(self.c - hop, 0), self.t),
        )

    def blank(self):
        for index, (hop, need, unused) in enumerate(self.plan):

            @pl.when(self.c + hop >= self.s.count)
            def _():
                self.back[index][...] = jnp.zeros((need, self.low.shape[1]), BF16)

    def send(self, number):
        rows = pl.ds(self.blocks[number][2], WIDE)

        @pl.when(self.c >= self.blocks[number][1])
        def _():
            self.low[rows] = self.grads[rows].astype(BF16)
            self.copy(number).start()

    def send_complete(self, i):
        for number, block in enumerate(self.blocks):
            if block[2] // WIDE < self.s.rows // WIDE - 1:

                @pl.when(i == block[2] // WIDE)
                def _():
                    self.send(number)

    def send_rest(self):
        for number, block in enumerate(self.blocks):
            if block[2] // WIDE >= self.s.rows // WIDE - 1:
                self.send(number)

    def receive(self):
        for number, block in enumerate(self.blocks):

            @pl.when(self.c + block[1] < self.s.count)
            def _():
                self.copy(number).wait_recv()

    def finish(self):
        for number, block in enumerate(self.blocks):

            @pl.when(self.c >= block[1])
            def _():
                self.copy(number).wait_send()


def attention_back_scratch(s):
    plan = halo_plan(s.rows)
    return dict(
        dkv_v=VMEM((ATTENTION_WINDOW + s.rows, 2 * s.keys), F32),
        low_v=VMEM((ATTENTION_WINDOW, 2 * s.keys), BF16),
        back_v=[VMEM((need, 2 * s.keys), BF16) for unused, need, unused_too in plan],
        total_v=VMEM((WIDE, 2 * s.keys), F32),
        return_sems=DMA((2, ATTENTION_WINDOW // WIDE)),
    )


def attention_back_shapes(s):
    return dict(
        dyb=((s.rows, s.model), BF16),
        dgate=((s.rows, s.hidden), BF16),
        dup=((s.rows, s.hidden), BF16),
        dhb=((s.rows, s.model), BF16),
        dq=((s.rows, s.queries), BF16),
        dk=((s.rows, s.keys), BF16),
        dv=((s.rows, s.keys), BF16),
    )


def attention_back_sums(s):
    return dict(
        dres=(shaped(s.rows, s.model, kind=F32), ANY),
        ffn_sum=(shaped(1, s.model, kind=F32), VMEM),
        qk_sum=(shaped(2, HEAD_SIZE, kind=F32), VMEM),
    )


def back_start(n, returns):
    returns.blank()
    n.dkv_v[...] = jnp.zeros_like(n.dkv_v)
    n.ffn_sum[...] = jnp.zeros_like(n.ffn_sum)
    n.qk_sum[...] = jnp.zeros_like(n.qk_sum)


def feed_back(n, i, gate, up, lower, made):
    here = wide_rows(i)
    low = n.g_v[here].astype(BF16)
    n.dyb_v[here] = low
    grad_hidden = dot_nt(low, n.wd_v[...])
    sigma = jax.nn.sigmoid(gate)
    dgate = (grad_hidden * up * (sigma * (1.0 + gate * (1.0 - sigma)))).astype(BF16)
    dup = (grad_hidden * gate * sigma).astype(BF16)
    n.dgate_v[here] = dgate
    n.dup_v[here] = dup
    lower.push(i, dot_nt(dgate, n.wg_v[...]) + dot_nt(dup, n.wu_v[...]))
    send_out(subs(i), *made)


def attention_back(n, i, middle, keys_ref, query_ref, layer, lower, returns, made, s):
    here = wide_rows(i)
    grad_in = lower.take_wide(i)
    inverse = rms_inverse(middle)
    unit = middle * inverse
    n.ffn_sum[...] += column_sum(grad_in * unit)
    total = n.g_v[here] + norm_back(grad_in, unit, inverse, n.ffn_gain[layer : layer + 1])
    n.g_v[here] = total
    low = total.astype(BF16)
    n.dhb_v[here] = low
    grad_out = dot_nt(low, n.wo_v[...]).astype(BF16)
    pieces = attend_back(n, i, grad_out, keys_ref, query_ref, s)
    returns.send_complete(i)
    for head, piece in enumerate(pieces):
        n.dq_v[here, head_cols(head)] = head_back(
            n, here, piece * SCALE, n.qraw_v[here, head_cols(head)], 0, layer
        )
    send_out(subs(i), *made)


def keys_back(n, layer, returns, made, s):
    def each(i):
        here = wide_rows(i)
        own = pl.ds(pl.multiple_of(ATTENTION_WINDOW + i * WIDE, WIDE), WIDE)
        n.total_v[...] = n.dkv_v[own]
        for index, (hop, need, unused) in enumerate(returns.plan):
            skipped = s.rows - need

            @pl.when(i >= skipped // WIDE)
            def _():
                part = pl.ds(pl.multiple_of(i * WIDE - skipped, WIDE), WIDE)
                n.total_v[...] += n.back_v[index][part].astype(F32)

        for g in range(s.groups):
            n.dk_v[here, head_cols(g)] = head_back(
                n, here, n.total_v[:, head_cols(g)] * SCALE, n.kraw_v[here, head_cols(g)], 1, layer
            )
        n.dv_v[here] = n.total_v[:, s.keys :].astype(BF16)
        send_out(subs(i), *made)

    each_of(s.rows // WIDE, each)


def feed(n, i, middle, layer):
    here = wide_rows(i)
    normed = (middle * rms_inverse(middle) * n.ffn_gain[layer : layer + 1]).astype(BF16)
    n.a2_v[here] = normed
    gate = dot_nn(normed, n.wg_v[...])
    up = dot_nn(normed, n.wu_v[...])
    inside = (gate * jax.nn.sigmoid(gate) * up).astype(BF16)
    n.hidden_v[here] = inside
    return gate, up, dot_nn(inside, n.wd_v[...])


def layer_ins(stream, saved, w, tables):
    before = dict(qin=(saved.q, ANY), kvin=(saved.kv, ANY)) if saved else {}
    return before | dict(
        x=(stream, ANY),
        ffn_gain=(w.ffn_gain, VMEM),
        lowest=(tables.lowest, VMEM),
        wo=(w.w_out, ANY),
        wg=(w.w_gate, ANY),
        wu=(w.w_up, ANY),
        wd=(w.w_down, ANY),
    )


def weight_scratch(s):
    return dict(
        wo_v=VMEM((s.queries, s.model), BF16),
        wg_v=VMEM((s.model, s.hidden), BF16),
        wu_v=VMEM((s.model, s.hidden), BF16),
        wd_v=VMEM((s.hidden, s.model), BF16),
    )


def layer_scratch(stream, s, stores):
    return weight_scratch(s) | dict(
        x_v=VMEM((s.rows, s.model), stream.dtype),
        qin_v=VMEM((s.rows, s.queries), BF16),
        kvin_v=VMEM((ATTENTION_WINDOW + s.rows, 2 * s.keys), BF16),
        load_sems=DMA((20,)),
        store_sems=DMA((stores, s.units)),
        first=line_scratch(s.units, s.model),
        second=line_scratch(s.units, s.model),
    )


def layer_loads(n, loads, layer, projected):
    if projected:
        early = (loads(n.qin, n.qin_v), loads(n.kvin, n.kvin_v))
    else:
        early = (loads(n.x, n.x_v),)
    early += (loads(n.wo.at[layer], n.wo_v),)
    late = () if not projected else (loads(n.x, n.x_v),)
    late += (
        loads(n.wg.at[layer], n.wg_v),
        loads(n.wu.at[layer], n.wu_v),
        loads(n.wd.at[layer], n.wd_v),
    )
    return early, late


def kept_shapes(s):
    return dict(
        o=((s.rows, s.queries), BF16),
        a2=((s.rows, s.model), BF16),
        hidden=((s.rows, s.hidden), BF16),
    )


def forward_shapes(s):
    return kept_shapes(s) | dict(
        inv=((s.rows, HEAD_SIZE), F32),
        h=((s.rows, s.model), F32),
        gate=((s.rows, s.hidden), BF16),
        up=((s.rows, s.hidden), BF16),
        y=((s.rows, s.model), F32),
    )


def forward_layer(layer, stream, saved, w, tables, s):
    def body(n):
        loads = Loads(n.load_sems)
        if not saved:
            own_weights = (
                loads(n.wk.at[layer], n.first_wk),
                loads(n.wv.at[layer], n.first_wv),
                loads(n.wq.at[layer], n.first_wq),
            )
        early, late = layer_loads(n, loads, layer, saved is not None)
        above = (
            loads(n.wq.at[layer + 1], n.wq_v),
            loads(n.wk.at[layer + 1], n.wk_v),
            loads(n.wv.at[layer + 1], n.wv_v),
        )
        stores = Stores(n.store_sems)
        mixed = (stores(n.o_v, n.o), stores(n.inv_v, n.inv))
        fed = (
            stores(n.h_v, n.h),
            stores(n.a2_v, n.a2),
            stores(n.hidden_v, n.hidden),
            stores(n.gate_v, n.gate),
            stores(n.up_v, n.up),
        )
        closed = (
            stores(n.y_v, n.y),
            stores(n.a1_v, n.a1),
            stores(n.qraw_v, n.qraw),
            stores(n.kraw_v, n.kraw),
            stores(n.q_v, n.q),
        )
        first, second = LineSum(n.first), LineSum(n.second)
        halo = Halo(n.kv_v, n.halo_sems, s.rows, s.count)
        greet(line_partners() + halo_partners(s.rows, s.count))
        halo.blank()
        wait_all(*early)
        if not saved:
            wait_all(*own_weights)
            own = first_view(n)
            own_halo = Halo(n.kvin_v, n.first_sems, s.rows, s.count)
            own_halo.blank()

            def own_keys(i):
                project_keys(own, i * WIDE, WIDE, n.x_v[wide_rows(i)].astype(F32), layer)
                for u in subs(i):
                    own_halo.send(u)

            def own_queries(i):
                project_queries(own, i * WIDE, WIDE, layer)

            each_of(s.rows // WIDE, own_keys)
            each_of(s.rows // WIDE, own_queries)
            each_of(s.units, own_halo.finish)
            own_out = (
                loads(n.kvin_v, n.own_kv),
                loads(n.first_a1, n.own_a1),
                loads(n.first_qraw, n.own_qraw),
                loads(n.first_kraw, n.own_kraw),
                loads(n.qin_v, n.own_q),
            )

        def mix(i):
            attend(n, i, s)
            first.push(i, dot_nn(n.o_v[wide_rows(i)], n.wo_v[...]))
            send_out(subs(i), *mixed)

        def feed_wide(i):
            pl.when(i == 0)(lambda: wait_all(*late))
            here = wide_rows(i)
            middle = n.x_v[here].astype(F32) + first.take_wide(i)
            n.h_v[here] = middle
            gate, up, part = feed(n, i, middle, layer)
            second.push(i, part)
            n.gate_v[here] = gate.astype(BF16)
            n.up_v[here] = up.astype(BF16)
            send_out(subs(i), *fed)

        def close(u):
            pl.when(u == 0)(lambda: wait_all(*above))
            here = unit_rows(u)
            result = n.h_v[here] + second.take(u)
            n.y_v[here] = result
            project_keys(n, u * UNIT, UNIT, result, layer + 1)
            halo.send(u)
            project_queries(n, u * UNIT, UNIT, layer + 1)
            send_out([u], *closed)

        at = ARRIVED
        pipeline(
            s.units,
            second.stages(at)
            + first.stages(0)
            + [(at + 3 * HOP, close, 1), (at, feed_wide, WIDE // UNIT), (0, mix, WIDE // UNIT)],
        )
        each_of(s.units, halo.finish)
        keys = loads(n.kv_v, n.kv)

        def finish(u):
            first.finish(u)
            second.finish(u)
            stores.finish(u)

        each_of(s.units, finish)
        keys.wait()
        if not saved:
            wait_all(*own_out)

    return run_kernel(
        body,
        layer_ins(stream, saved, w, tables) | project_ins(w, tables),
        outputs(forward_shapes(s))
        | outputs(project_shapes(s))
        | ({} if saved else first_outs(s)),
        layer_scratch(stream, s, 12)
        | buffers(forward_shapes(s))
        | project_scratch(s)
        | ({} if saved else first_scratch(s)),
        2 + layer,
    )


def turn_layer(layer, stream, saved, cotangent, w, tables, s):
    def body(n):
        loads = Loads(n.load_sems)
        early, late = layer_loads(n, loads, layer, True)
        late = late + (loads(n.grad, n.grad_v),)
        raws = (loads(n.qraw, n.qraw_v), loads(n.kraw, n.kraw_v))
        a1 = loads(n.a1, n.a1_v)
        stores = Stores(n.store_sems)
        closed = (stores(n.y_v, n.y),)
        turned = (stores(n.g_v, n.dres), stores(n.dq_v, n.dq))
        keyed = (stores(n.dk_v, n.dk), stores(n.dv_v, n.dv))
        first, second, lower = LineSum(n.first), LineSum(n.second), LineSum(n.lower)
        returns = Returns(n, s)
        greet(line_partners() + halo_partners(s.rows, s.count))
        wait_all(*early)

        def mix(i):
            attend(n, i, s)
            first.push(i, dot_nn(n.o_v[wide_rows(i)], n.wo_v[...]))

        def feed_both(i):
            pl.when(i == 0)(lambda: wait_all(*late))
            here = wide_rows(i)
            middle = n.x_v[here] + first.take_wide(i)
            n.x_v[here] = middle
            n.g_v[here] = n.grad_v[here].astype(F32)
            gate, up, part = feed(n, i, middle, layer)
            feed_back(n, i, gate, up, lower, ())
            second.hold(i, part)

        def close(u):
            here = unit_rows(u)
            n.y_v[here] = (n.x_v[here] + second.take(u)).astype(BF16)
            send_out([u], *closed)

        def attention(i):
            pl.when(i == 0)(lambda: wait_all(*raws))
            middle = n.x_v[wide_rows(i)]
            attention_back(
                n, i, middle, n.kvin_v, n.qin_v, layer, lower, returns, turned, s
            )

        at = ARRIVED
        def gradient(index):
            left, right = factors[index]
            block_products(n.grads_v[index], left, right, sizes[index][0], s)
            gradient_store(index).start()

        def gradient_store(index):
            return pltpu.make_async_copy(n.grads_v[index], n.grads[index], n.grad_sems.at[index])

        def end_keys():
            returns.receive()
            keys_back(n, layer, returns, keyed, s)
            a1.wait()

        factors = [
            (n.a2_v, n.dup_v),
            (n.a2_v, n.dgate_v),
            (n.a1_v, n.dq_v),
            (n.hidden_v, n.dyb_v),
            (n.o_v, n.dhb_v),
            (n.a1_v, n.dk_v),
            (n.a1_v, n.dv_v),
        ]
        after = at + ARRIVED + s.units
        tasks = [(1, lambda: back_start(n, returns)), (after, returns.send_rest), (after + 4, end_keys)]
        for index, step in enumerate((1, 2, 5, 3, 4, 6, 6)):
            tasks.append((after + step, lambda index=index: gradient(index)))
        tasks.sort(key=lambda item: item[0])
        pipeline(
            s.units,
            lower.stages(at)
            + second.stages(OUTPUT_AT, HOP + 1)
            + first.stages(0)
            + [
                (OUTPUT_AT, second.send, 1),
                (OUTPUT_AT + 3 * HOP + 3, close, 1),
                (at + ARRIVED, attention, WIDE // UNIT),
                (at, feed_both, WIDE // UNIT),
                (0, mix, WIDE // UNIT),
            ],
            tasks,
        )
        returns.finish()
        for index in range(len(sizes)):
            gradient_store(index).wait()

        def finish(u):
            first.finish(u)
            second.finish(u)
            lower.finish(u)
            stores.finish(u)

        each_of(s.units, finish)

    sizes = grad_sizes(s)
    backs = attention_back_shapes(s)
    blocks = block_shapes(s, sizes)
    return run_kernel(
        body,
        layer_ins(stream, saved, w, tables)
        | dict(
            grad=(cotangent, ANY),
            a1=(saved.a1, ANY),
            qraw=(saved.qraw, ANY),
            kraw=(saved.kraw, ANY),
            qk_gain=(w.qk_gain, VMEM),
            cosine=(tables.cosine, VMEM),
            sine=(tables.sine, VMEM),
        ),
        outputs({x: backs[x] for x in dict(dq=0, dk=0, dv=0)})
        | attention_back_sums(s)
        | dict(
            y=(shaped(s.rows, s.model), ANY),
            grads=[(shaped(*block), ANY) for block in blocks],
        ),
        layer_scratch(stream, s, 5)
        | buffers(kept_shapes(s))
        | buffers(backs)
        | attention_back_scratch(s)
        | dict(
            y_v=VMEM((s.rows, s.model), BF16),
            a1_v=VMEM((s.rows, s.model), BF16),
            grads_v=[VMEM(block, BF16) for block in blocks],
            grad_sems=DMA((len(sizes),)),
            inv_v=VMEM((s.rows, HEAD_SIZE), F32),
            grad_v=VMEM((s.rows, s.model), BF16),
            g_v=VMEM((s.rows, s.model), F32),
            qraw_v=VMEM((s.rows, s.queries), F32),
            kraw_v=VMEM((s.rows, s.keys), F32),
            lower=line_scratch(s.units, s.model),
        ),
        2 + layer,
    )


def halving_partners(count):
    c, t = place()
    return [(c >= 0, (c ^ (1 << b), t)) for b in range(count.bit_length() - 1)]


def block_products(target, left, right, line, s):
    bits = s.count.bit_length() - 1
    half = s.count // 2
    for part in range(2):
        product = dot_tn(left[:, part * half * line : (part + 1) * half * line], right[...])
        for k in range(half):
            block = part * half + k
            at = tuple((block >> b) & 1 for b in range(bits - 1, -1, -1))
            target[at + (slice(0, line),)] = product[k * line : (k + 1) * line].astype(BF16)


def block_shapes(s, sizes):
    bits = s.count.bit_length() - 1
    return [(2,) * bits + (line + -line % 16, width) for line, width in sizes]


class Scatter:
    def __init__(self, n, s, sizes, factors=None):
        self.n, self.s, self.sizes, self.factors = n, s, sizes, factors
        self.bits = s.count.bit_length() - 1
        self.c, self.t = place()
        self.beside = []

    def bit(self, b):
        return (self.c >> b) & 1

    def order(self, index):
        rest = list(range(1, self.bits))
        return [0] + (rest if index % 2 == 0 else rest[::-1])

    def spot(self, picks):
        low = 0 if self.factors else 1
        return tuple(picks.get(b, slice(None)) for b in range(self.bits - 1, low - 1, -1))

    def own(self, index):
        return (self.n.whole_v if self.factors else self.n.own)[index]

    def copy(self, index, step):
        order = self.order(index)
        picks = {b: self.bit(b) for b in order[:step]}
        picks[order[step]] = 1 - self.bit(order[step])
        if step == 0 and not self.factors:
            source = self.n.whole[index].at[
                (slice(None),) * (self.bits - 1) + (1 - self.bit(0),)
            ]
        else:
            source = self.own(index).at[self.spot(picks)]
        sems = self.n.scatter_sems
        return remote(
            source,
            self.n.got[index * self.bits + step],
            sems.at[0, index, step],
            sems.at[1, index, step],
            (self.c ^ (1 << order[step]), self.t),
        )

    def load(self, index):
        return pltpu.make_async_copy(
            self.n.whole[index].at[(slice(None),) * (self.bits - 1) + (self.bit(0),)],
            self.n.own[index],
            self.n.scatter_load_sems.at[index],
        )

    def start(self, index):
        if self.factors:
            left, right, needed = self.factors[index]
            wait_all(*needed)
            block_products(self.own(index), left, right, self.sizes[index][0], self.s)
        else:
            self.load(index).start()
        self.copy(index, 0).start()

    def add(self, index, step):
        order = self.order(index)
        if step == 0 and not self.factors:
            self.load(index).wait()
        self.copy(index, step).wait_recv()
        free = [b for b in range(self.bits - 1, 0, -1) if b not in order[: step + 1]]
        own, got = self.own(index), self.n.got[index * self.bits + step]
        line = self.sizes[index][0]

        def one(k, carry):
            picks = {b: (k >> (len(free) - 1 - i)) & 1 for i, b in enumerate(free)}
            here = self.spot({b: self.bit(b) for b in order[: step + 1]} | picks)
            total = own[here].astype(F32) + got[tuple(picks[b] for b in free)].astype(F32)
            if step == self.bits - 1:
                self.sum_of(index)[...] = total[:line]
            else:
                own[here] = total.astype(BF16)
            return carry

        if free:
            lax.fori_loop(0, 1 << len(free), one, 0)
        else:
            one(0, 0)
        if step < self.bits - 1:
            self.copy(index, step + 1).start()
        else:
            for other in self.beside:
                other[index].wait()
            self.store(index).start()

    def sum_of(self, index):
        return self.n.sums_v[index].at[0] if self.factors else self.n.sums_v[index]

    def store(self, index):
        return pltpu.make_async_copy(
            self.n.sums_v[index], self.n.sums[index], self.n.scatter_store_sems.at[index]
        )

    def tasks(self, every, bases):
        found = []
        for index in range(len(self.sizes)):
            found.append((bases[0] + index * every, lambda index=index: self.start(index)))
            for step in range(self.bits):
                at = bases[min(step + 1, len(bases) - 1)] + index * every
                at += 100 * max(0, step + 2 - len(bases))
                found.append((at, lambda index=index, step=step: self.add(index, step)))
        found.sort(key=lambda item: item[0])
        return found

    def finish(self):
        for index in range(len(self.sizes)):
            self.store(index).wait()
            for step in range(self.bits):
                self.copy(index, step).wait_send()


def scatter_scratch(s, sizes, computed, layers):
    bits = s.count.bit_length() - 1
    tails = [(line + -line % 16, width) for line, width in sizes]
    found = dict(
        sums_v=[VMEM(((layers,) if computed else ()) + size, F32) for size in sizes],
        got=[
            VMEM((2,) * (bits - 1 - step) + tail, BF16) for tail in tails for step in range(bits)
        ],
        scatter_sems=DMA((2, len(sizes), bits)),
        scatter_load_sems=DMA((len(sizes),)),
        scatter_store_sems=DMA((len(sizes),)),
    )
    if computed:
        return found | dict(whole_v=[VMEM((2,) * bits + tail, BF16) for tail in tails])
    return found | dict(own=[VMEM((2,) * (bits - 1) + tail, BF16) for tail in tails])


def block_view(array, s):
    bits = s.count.bit_length() - 1
    line = array.shape[0] // s.count
    view = array.reshape((2,) * bits + (line, array.shape[1]))
    if line % 16:
        view = jnp.pad(view, [(0, 0)] * bits + [(0, -line % 16), (0, 0)])
    return view


def factor_pairs(k):
    return [
        (k.a2, k.dup),
        (k.a2, k.dgate),
        (k.a1, k.dq),
        (k.hidden, k.dyb),
        (k.o, k.dhb),
        (k.a1, k.dk),
        (k.a1, k.dv),
    ]


def grad_sizes(s):
    return [
        (s.model // s.count, s.hidden),
        (s.model // s.count, s.hidden),
        (s.model // s.count, s.queries),
        (s.hidden // s.count, s.model),
        (s.queries // s.count, s.model),
        (s.model // s.count, s.keys),
        (s.model // s.count, s.keys),
    ]


def head_ins(k, w):
    return dict(
        hq=(k.dq, ANY),
        hk=(k.dk, ANY),
        hv=(k.dv, ANY),
        wq=(w.w_query, ANY),
        wk=(w.key_weight, ANY),
        wv=(w.value_weight, ANY),
        x=(k.x, ANY),
        attn_gain=(w.attn_gain, VMEM),
        grad=(k.dres, ANY),
    )


def head_scratch(k, s):
    return dict(
        hq_v=VMEM((s.rows, s.queries), BF16),
        hk_v=VMEM((s.rows, s.keys), BF16),
        hv_v=VMEM((s.rows, s.keys), BF16),
        wq_v=VMEM((s.model, s.queries), BF16),
        wk_v=VMEM((s.model, s.keys), BF16),
        wv_v=VMEM((s.model, s.keys), BF16),
        x_v=VMEM((s.rows, s.model), k.x.dtype),
        g_v=VMEM((s.rows, s.model), F32),
        upper=line_scratch(s.units, s.model),
        load_sems=DMA((32,)),
        store_sems=DMA((10, s.units)),
    )


def head_loads(n, loads, layer):
    early = (
        loads(n.hq, n.hq_v),
        loads(n.wq.at[layer], n.wq_v),
        loads(n.hk, n.hk_v),
        loads(n.wk.at[layer], n.wk_v),
        loads(n.hv, n.hv_v),
        loads(n.wv.at[layer], n.wv_v),
    )
    return early, (loads(n.x, n.x_v), loads(n.grad, n.g_v))


def head_inputs(n, i, upper):
    here = wide_rows(i)
    upper.push(
        i,
        dot_nt(n.hq_v[here], n.wq_v[...])
        + dot_nt(n.hk_v[here], n.wk_v[...])
        + dot_nt(n.hv_v[here], n.wv_v[...]),
    )


def head_norm(n, here, grad_in, layer):
    stream = n.x_v[here].astype(F32)
    inverse = rms_inverse(stream)
    unit = stream * inverse
    n.attn_sum[...] += column_sum(grad_in * unit)
    n.g_v[here] += norm_back(grad_in, unit, inverse, n.attn_gain[layer : layer + 1])


def backward_layer(layer, kept, w, tables, s):
    above, here_kept = kept[layer + 1], kept[layer]
    sizes = grad_sizes(s)

    def body(n):
        loads = Loads(n.load_sems)
        early, middle_loads = head_loads(n, loads, layer + 1)
        scatter = Scatter(n, s, sizes)
        feeds = (
            loads(n.wd.at[layer], n.wd_v),
            loads(n.gate, n.gate_v),
            loads(n.up, n.up_v),
            loads(n.wg.at[layer], n.wg_v),
            loads(n.wu.at[layer], n.wu_v),
        )
        lates = (
            loads(n.wo.at[layer], n.wo_v),
            loads(n.q, n.q_v),
            loads(n.kv, n.kv_v),
            loads(n.o, n.o_v),
            loads(n.inv, n.inv_v),
            loads(n.qraw, n.qraw_v),
            loads(n.kraw, n.kraw_v),
        )
        stores = Stores(n.store_sems)
        fed_back = (stores(n.dyb_v, n.dyb), stores(n.dgate_v, n.dgate), stores(n.dup_v, n.dup))
        turned = (stores(n.g_v, n.dres), stores(n.dhb_v, n.dhb), stores(n.dq_v, n.dq))
        keyed = (stores(n.dk_v, n.dk), stores(n.dv_v, n.dv))
        upper, lower = LineSum(n.upper), LineSum(n.lower)
        returns = Returns(n, s)
        greet(line_partners() + halo_partners(s.rows, s.count) + halving_partners(s.count))
        n.attn_sum[...] = jnp.zeros_like(n.attn_sum)
        wait_all(*early)

        def middle_copy(i):
            rows = wide_rows(i)
            return pltpu.make_async_copy(n.h.at[rows], n.x_v.at[rows], n.middle_sems.at[i])

        def inputs(i):
            head_inputs(n, i, upper)

        def pass_norm(i):
            pl.when(i == 0)(lambda: wait_all(*middle_loads, *feeds))
            here = wide_rows(i)
            head_norm(n, here, upper.take_wide(i), layer + 1)
            middle_copy(i).start()
            gate, up = n.gate_v[here].astype(F32), n.up_v[here].astype(F32)
            feed_back(n, i, gate, up, lower, fed_back)

        def attention(i):
            pl.when(i == 0)(lambda: wait_all(*lates))
            middle_copy(i).wait()
            attention_back(
                n, i, n.x_v[wide_rows(i)], n.kv_v, n.q_v, layer, lower, returns, turned, s
            )

        at = ARRIVED
        pipeline(
            s.units,
            lower.stages(at)
            + upper.stages(0)
            + [
                (at + ARRIVED, attention, WIDE // UNIT),
                (at, pass_norm, WIDE // UNIT),
                (0, inputs, WIDE // UNIT),
            ],
            [(0, lambda: back_start(n, returns))] + scatter.tasks(1, SCATTER_MIDDLE),
        )
        returns.send_rest()
        returns.receive()
        keys_back(n, layer, returns, keyed, s)
        returns.finish()
        scatter.finish()

        def finish(u):
            upper.finish(u)
            lower.finish(u)
            stores.finish(u)

        each_of(s.units, finish)

    whole = above.grads or [
        block_view(dot_tn(left, right).astype(BF16), s) for left, right in factor_pairs(above)
    ]
    held = dict(
        gate=here_kept.gate,
        up=here_kept.up,
        q=here_kept.q,
        kv=here_kept.kv,
        o=here_kept.o,
        inv=here_kept.inv,
        qraw=here_kept.qraw,
        kraw=here_kept.kraw,
    )
    return run_kernel(
        body,
        head_ins(above, w)
        | {x: (array, ANY) for x, array in held.items()}
        | dict(
            h=(here_kept.h, ANY),
            wd=(w.w_down, ANY),
            wg=(w.w_gate, ANY),
            wu=(w.w_up, ANY),
            wo=(w.w_out, ANY),
            ffn_gain=(w.ffn_gain, VMEM),
            qk_gain=(w.qk_gain, VMEM),
            cosine=(tables.cosine, VMEM),
            sine=(tables.sine, VMEM),
            lowest=(tables.lowest, VMEM),
            whole=[(array, ANY) for array in whole],
        ),
        outputs(attention_back_shapes(s))
        | attention_back_sums(s)
        | dict(
            attn_sum=(shaped(1, s.model, kind=F32), VMEM),
            sums=[(shaped(*size, kind=F32), ANY) for size in sizes],
        ),
        head_scratch(above, s)
        | weight_scratch(s)
        | {x + "_v": VMEM(array.shape, array.dtype) for x, array in held.items()}
        | buffers(attention_back_shapes(s))
        | attention_back_scratch(s)
        | scatter_scratch(s, sizes, False, 1)
        | dict(
            lower=line_scratch(s.units, s.model),
            middle_sems=DMA((s.rows // WIDE,)),
        ),
        20 + layer,
    )


def backward_end(kept, w, s):
    bottom = kept[0]
    sizes = grad_sizes(s)
    layers = len(kept)
    width = s.model // s.count
    bits = s.count.bit_length() - 1
    tp_bits = s.line.bit_length() - 1
    rounds = [(1 << b, 0) for b in range(bits)] + [(0, 1 << b) for b in range(tp_bits)]

    def body(n):
        c, t = place()
        loads = Loads(n.load_sems)
        early, lates = head_loads(n, loads, 0)
        a2, dup, dgate = loads(n.a2, n.a2_v), loads(n.dup, n.dup_v), loads(n.dgate, n.dgate_v)
        a1, hidden, dyb = loads(n.a1, n.a1_v), loads(n.hidden, n.hidden_v), loads(n.dyb, n.dyb_v)
        o, dhb = loads(n.o, n.o_v), loads(n.dhb, n.dhb_v)
        factors = [
            (n.a2_v, n.dup_v, (a2, dup)),
            (n.a2_v, n.dgate_v, (dgate,)),
            (n.a1_v, n.hq_v, (a1,)),
            (n.hidden_v, n.dyb_v, (hidden, dyb)),
            (n.o_v, n.dhb_v, (o, dhb)),
            (n.a1_v, n.hk_v, ()),
            (n.a1_v, n.hv_v, ()),
        ]
        scatter = Scatter(n, s, sizes, factors)
        stores = Stores(n.store_sems)
        out = stores(n.g_v, n.dres)
        upper = LineSum(n.upper)
        others = [(c >= 0, ((c + k) % s.count, t)) for k in range(1, s.count)]
        lines = [(c >= 0, (c, t ^ (1 << b))) for b in range(tp_bits)]
        greet(line_partners() + halving_partners(s.count) + others + lines)
        n.attn_sum[...] = jnp.zeros_like(n.attn_sum)
        n.acc[...] = jnp.zeros_like(n.acc)
        n.gains[...] = jnp.zeros_like(n.gains)
        for layer in range(layers):
            n.acc[0, 2 * layer : 2 * layer + 2] = n.qk_in[layer][...]
        wait_all(*early)
        scatter.beside = [
            [
                loads(n.done[(layer - 1) * len(sizes) + index], n.sums_v[index].at[layer])
                for index in range(len(sizes))
            ]
            for layer in range(1, layers)
        ]

        def head_copy(k):
            return remote(
                n.acc.at[k],
                n.other.at[k],
                n.small_sems.at[0, k],
                n.small_sems.at[1, k],
                (c ^ rounds[k][0], t ^ rounds[k][1]),
            )

        def head_step(k):
            if k > 0:
                head_copy(k - 1).wait_recv()
                n.acc[k] = n.acc[k - 1] + n.other[k - 1]
            if k < len(rounds):
                head_copy(k).start()

        def pass_norm(u):
            pl.when(u == 0)(lambda: wait_all(*lates))
            head_norm(n, unit_rows(u), upper.take(u), 0)
            send_out([u], out)

        tasks = scatter.tasks(SCATTER_EVERY, SCATTER_END)
        tasks += [(2 * k + 1, lambda k=k: head_step(k)) for k in range(len(rounds) + 1)]
        tasks.sort(key=lambda item: item[0])
        pipeline(
            s.units,
            upper.stages(0)
            + [
                (3 * HOP, pass_norm, 1),
                (0, lambda i: head_inputs(n, i, upper), WIDE // UNIT),
            ],
            tasks,
        )
        gains = [n.attn_sum] + n.attn_in + n.ffn_in
        for d in range(s.count):
            for row, gain in enumerate(gains):
                n.gains[d, row : row + 1] = gain[:, d * width : (d + 1) * width]

        def gain_copy(k):
            to = (c + k) % s.count
            return remote(
                n.gains.at[to],
                n.gains_got.at[k],
                n.gain_sems.at[0, k],
                n.gain_sems.at[1, k],
                (to, t),
            )

        for k in range(1, s.count):
            gain_copy(k).start()
        for layer in range(layers):
            n.qk_total[layer] = n.acc[len(rounds), 2 * layer : 2 * layer + 2]
        total = n.gains[c]
        for k in range(1, s.count):
            gain_copy(k).wait_recv()
            total = total + n.gains_got[k]
        n.attn_total[...] = total[:layers]
        n.ffn_total[...] = total[layers : 2 * layers]
        for k in range(1, s.count):
            gain_copy(k).wait_send()
        for k in range(len(rounds)):
            head_copy(k).wait_send()
        scatter.finish()

        def finish(u):
            upper.finish(u)
            stores.finish(u)

        each_of(s.units, finish)

    held = dict(
        a1=bottom.a1,
        a2=bottom.a2,
        o=bottom.o,
        hidden=bottom.hidden,
        dyb=bottom.dyb,
        dgate=bottom.dgate,
        dup=bottom.dup,
        dhb=bottom.dhb,
    )
    small = (len(rounds) + 1, 2 * layers + -2 * layers % 8, HEAD_SIZE)
    slabs = (s.count, 2 * layers + -2 * layers % 8, width)
    return run_kernel(
        body,
        head_ins(bottom, w)
        | {x: (array, ANY) for x, array in held.items()}
        | dict(
            qk_in=[(k.qk_sum, VMEM) for k in kept],
            attn_in=[(k.attn_sum, VMEM) for k in kept[1:]],
            ffn_in=[(k.ffn_sum, VMEM) for k in kept],
            done=[(array, ANY) for k in kept[1:] for array in k.sums],
        ),
        dict(
            dres=(shaped(s.rows, s.model, kind=F32), ANY),
            attn_total=(shaped(layers, width, kind=F32), VMEM),
            ffn_total=(shaped(layers, width, kind=F32), VMEM),
            qk_total=(shaped(layers, 2, HEAD_SIZE, kind=F32), VMEM),
            sums=[(shaped(layers, *size, kind=F32), ANY) for size in sizes],
        ),
        head_scratch(bottom, s)
        | {x + "_v": VMEM(array.shape, array.dtype) for x, array in held.items()}
        | scatter_scratch(s, sizes, True, layers)
        | dict(
            attn_sum=VMEM((1, s.model), F32),
            acc=VMEM(small, F32),
            other=VMEM(small, F32),
            gains=VMEM(slabs, F32),
            gains_got=VMEM(slabs, F32),
            small_sems=DMA((2, len(rounds))),
            gain_sems=DMA((2, s.count)),
        ),
        19,
    )


OUTPUT_AT = 17
def deliver(arrays):
    def body(n):
        copies = []
        for index, (source, target, held) in enumerate(zip(n.given, n.result, n.held)):
            copies.append(
                (
                    pltpu.make_async_copy(source, held, n.sems.at[0, index]),
                    pltpu.make_async_copy(held, target, n.sems.at[1, index]),
                )
            )
            copies[-1][0].start()
        for fetch, put in copies:
            fetch.wait()
            put.start()
        for fetch, put in copies:
            put.wait()

    return run_kernel(
        body,
        dict(given=[(array, ANY) for array in arrays]),
        dict(result=[(shaped(*array.shape, kind=array.dtype), ANY) for array in arrays]),
        dict(
            held=[VMEM(array.shape, array.dtype) for array in arrays],
            sems=DMA((2, len(arrays))),
        ),
        None,
    ).result


SCATTER_MIDDLE = (0, 3, 9, 16)
SCATTER_EVERY = 1
SCATTER_END = (0, 2, 7, 11)


def body(hidden_in, doc_lengths, cotangent, attn_gain, ffn_gain, qk_gain, w_query, *others):
    key_weight, value_weight, w_out, w_gate, w_up, w_down = others
    w = types.SimpleNamespace(
        attn_gain=attn_gain,
        ffn_gain=ffn_gain,
        qk_gain=qk_gain,
        w_query=w_query,
        key_weight=key_weight,
        value_weight=value_weight,
        w_out=w_out,
        w_gate=w_gate,
        w_up=w_up,
        w_down=w_down,
    )
    rows, model = hidden_in.shape
    layers, unused, queries = w_query.shape
    keys = key_weight.shape[2]
    s = types.SimpleNamespace(
        rows=rows,
        model=model,
        queries=queries,
        keys=keys,
        hidden=w_gate.shape[2],
        units=rows // UNIT,
        groups=keys // HEAD_SIZE,
        repeat=queries // keys,
        count=lax.axis_size(CTX),
        line=lax.axis_size(TP),
    )
    tables = make_tables(doc_lengths, rows)

    kept = []
    stream = hidden_in
    saved = None
    for layer in range(layers):
        if layer < layers - 1:
            result = forward_layer(layer, stream, saved, w, tables, s)
        else:
            result = turn_layer(layer, stream, saved, cotangent, w, tables, s)
        if saved:
            own = dict(a1=saved.a1, qraw=saved.qraw, kraw=saved.kraw, q=saved.q, kv=saved.kv)
        else:
            own = dict(
                a1=result.own_a1,
                qraw=result.own_qraw,
                kraw=result.own_kraw,
                q=result.own_q,
                kv=result.own_kv,
            )
        kept.append(types.SimpleNamespace(**(dict(grads=None) | vars(result) | own | dict(x=stream))))
        stream = result.y
        saved = result

    for layer in range(layers - 2, -1, -1):
        result = backward_layer(layer, kept, w, tables, s)
        kept[layer + 1].attn_sum = result.attn_sum
        kept[layer + 1].sums = result.sums
        vars(kept[layer]).update(
            dyb=result.dyb,
            dgate=result.dgate,
            dup=result.dup,
            dhb=result.dhb,
            dq=result.dq,
            dk=result.dk,
            dv=result.dv,
            dres=result.dres,
            ffn_sum=result.ffn_sum,
            qk_sum=result.qk_sum,
        )
    end = backward_end(kept, w, s)
    small = [end.attn_total, end.ffn_total, end.qk_total]
    stream, grad, *gains, up, gate, query, down, out, key, value = deliver(
        [stream, end.dres] + small + end.sums
    )
    return (
        stream,
        grad,
        *gains,
        query,
        key,
        value,
        out,
        gate,
        up,
        down,
    )


def solution(mesh):
    by_rows = P(CTX, None)
    by_columns = P(None, None, TP)
    by_hidden = P(None, TP, None)
    grad_columns = P(None, CTX, TP)
    grad_rows = P(None, (TP, CTX), None)
    return jax.shard_map(
        body,
        mesh=mesh,
        in_specs=(by_rows, P(), by_rows, P(), P(), P())
        + (by_columns,) * 3
        + (by_hidden,)
        + (by_columns,) * 2
        + (by_hidden,),
        out_specs=(by_rows, by_rows, P(None, CTX), P(None, CTX), P())
        + (grad_columns,) * 3
        + (grad_rows,)
        + (grad_columns,) * 2
        + (grad_rows,),
        check_vma=False,
    )
```

```python
import types

import jax
import jax.numpy as jnp
from jax import lax
from jax.experimental import pallas as pl
from jax.experimental.pallas import tpu as pltpu
from jax.sharding import PartitionSpec as P

HEAD_SIZE = 128
ATTENTION_WINDOW = 1024
EPS = 1e-06
THETA = 1000000.0

UNIT = 64
WIDE = 128
KEY_BLOCK = 384
HOP = 2
ARRIVED = 3 * HOP + WIDE // UNIT - 1
CTX = "ctx"
TP = "tp"
MESH = pl.DeviceIdType.MESH
F32 = jnp.float32
BF16 = jnp.bfloat16
SCALE = HEAD_SIZE ** (-0.5)
EXP2_SCALE = SCALE * 1.4426950408889634
ANY = pl.ANY
VMEM = pltpu.VMEM
DMA = pltpu.SemaphoreType.DMA


def dot_nn(left, right):
    return jnp.dot(left, right, preferred_element_type=F32)


def dot_nt(left, right):
    return lax.dot_general(left, right, (((1,), (1,)), ((), ())), preferred_element_type=F32)


def dot_tn(left, right):
    return lax.dot_general(left, right, (((0,), (0,)), ((), ())), preferred_element_type=F32)


def rms_inverse(value_rows):
    return lax.rsqrt(jnp.mean(value_rows * value_rows, axis=-1, keepdims=True) + EPS)


def rotate(value_rows, cosine, sine):
    return value_rows * cosine + pltpu.roll(value_rows, HEAD_SIZE // 2, 1) * sine


def unrotate(grad, cosine, sine):
    return grad * cosine + pltpu.roll(grad * sine, HEAD_SIZE // 2, 1)


def norm_back(grad, unit, inverse, gain):
    scaled = grad * gain
    inner = jnp.mean(scaled * unit, axis=-1, keepdims=True)
    return inverse * (scaled - unit * inner)


def column_sum(value_rows):
    return jnp.sum(value_rows, axis=0, keepdims=True)


def make_tables(lengths, rows):
    start = lax.axis_index(CTX) * rows
    spot = start + jnp.arange(rows, dtype=jnp.int32)
    order = jnp.arange(lengths.shape[0])
    ends = jnp.sum(jnp.where(order[None, :] <= order[:, None], lengths[None, :], 0), axis=1)
    passed = ends[None, :] <= spot[:, None]
    begin = jnp.sum(jnp.where(passed, lengths[None, :], 0), axis=1)
    lane = jnp.arange(HEAD_SIZE)
    half = HEAD_SIZE // 2
    freq = THETA ** (-((lane % half).astype(F32) * 2.0) / HEAD_SIZE)
    angle = (spot - begin).astype(F32)[:, None] * freq[None, :]
    lowest = jnp.maximum(begin, spot - (ATTENTION_WINDOW - 1)) - (start - ATTENTION_WINDOW)
    return types.SimpleNamespace(
        cosine=jnp.cos(angle),
        sine=jnp.sin(angle) * jnp.where(lane < half, -1.0, 1.0)[None, :],
        lowest=lowest[:, None],
    )


def halo_plan(rows):
    reach = -(-ATTENTION_WINDOW // rows)
    plan = []
    for hop in range(1, reach + 1):
        need = min(rows, ATTENTION_WINDOW - (hop - 1) * rows)
        plan.append((hop, need, ATTENTION_WINDOW - (hop - 1) * rows - need))
    return plan


def unit_rows(u):
    return pl.ds(pl.multiple_of(u * UNIT, UNIT), UNIT)


def wide_rows(w):
    return pl.ds(pl.multiple_of(w * WIDE, WIDE), WIDE)


def subs(w):
    return [w * (WIDE // UNIT) + i for i in range(WIDE // UNIT)]


def shaped(*shape, kind=BF16):
    return jax.ShapeDtypeStruct(shape, kind)


def listed(value):
    return list(value) if isinstance(value, list) else [value]


def run_kernel(body, ins, outs, scratch, collective_id):
    groups = [ins, outs, scratch]
    flat = [[x for value in group.values() for x in listed(value)] for group in groups]

    def named(values, chosen):
        values = list(values)
        found = {}
        for group in chosen:
            for name, value in group.items():
                if isinstance(value, list):
                    found[name] = [values.pop(0) for unused in value]
                else:
                    found[name] = values.pop(0)
        return types.SimpleNamespace(**found)

    results = pl.pallas_call(
        lambda *refs: body(named(refs, groups)),
        out_shape=[shape for shape, unused in flat[1]],
        in_specs=[pl.BlockSpec(memory_space=space) for unused, space in flat[0]],
        out_specs=[pl.BlockSpec(memory_space=space) for unused, space in flat[1]],
        scratch_shapes=flat[2],
        compiler_params=pltpu.CompilerParams(
            collective_id=collective_id,
            has_side_effects=collective_id is not None,
            vmem_limit_bytes=62 * 2**20,
        ),
    )(*[array for array, unused in flat[0]])
    return named(results, [outs])


def place():
    return lax.axis_index(CTX), lax.axis_index(TP)


def remote(source, target, send, receive, device):
    return pltpu.make_async_remote_copy(
        src_ref=source,
        dst_ref=target,
        send_sem=send,
        recv_sem=receive,
        device_id=device,
        device_id_type=MESH,
    )


def greet(partners):
    barrier = pltpu.get_barrier_semaphore()
    total = 0
    for exists, device in partners:
        total = total + jnp.where(exists, 1, 0)

        @pl.when(exists)
        def _():
            pl.semaphore_signal(barrier, inc=1, device_id=device, device_id_type=MESH)

    pl.semaphore_wait(barrier, total)


def line_partners():
    c, t = place()
    outer = (t == 0) | (t == 3)
    return [
        (outer, (c, jnp.where(t == 0, 1, 2))),
        (jnp.logical_not(outer), (c, jnp.where(t == 1, 0, 3))),
        (jnp.logical_not(outer), (c, jnp.clip(3 - t, 1, 2))),
    ]


def halo_partners(rows, count):
    c, t = place()
    partners = []
    for hop, unused, unused_too in halo_plan(rows):
        partners.append((c + hop < count, (jnp.minimum(c + hop, count - 1), t)))
        partners.append((c >= hop, (jnp.maximum(c - hop, 0), t)))
    return partners


class LineSum:
    def __init__(self, refs):
        self.part, self.total, self.inner, self.sems = refs
        self.c, self.t = place()
        self.outer = (self.t == 0) | (self.t == 3)
        self.is_inner = jnp.logical_not(self.outer)

    def copy(self, source, target, u, send, receive, to):
        return remote(
            source.at[u],
            target.at[u],
            self.sems.at[send, u],
            self.sems.at[receive, u],
            (self.c, to),
        )

    def inwards(self, u):
        return self.copy(self.part, self.total, u, 0, 1, jnp.where(self.t < 2, 1, 2))

    def across(self, u):
        return self.copy(self.part, self.inner, u, 0, 2, jnp.clip(3 - self.t, 1, 2))

    def outwards(self, u):
        return self.copy(self.total, self.total, u, 3, 4, jnp.where(self.t < 2, 0, 3))

    def hold(self, w, value):
        for i, u in enumerate(subs(w)):
            self.part[u] = value[i * UNIT : (i + 1) * UNIT].astype(BF16)

    def send(self, u):
        @pl.when(self.outer)
        def _():
            self.inwards(u).start()

    def push(self, w, value):
        self.hold(w, value)
        for u in subs(w):
            self.send(u)

    def meet(self, u):
        @pl.when(self.is_inner)
        def _():
            self.inwards(u).wait_recv()
            self.part[u] = (self.part[u].astype(F32) + self.total[u].astype(F32)).astype(BF16)
            self.across(u).start()

    def spread(self, u):
        @pl.when(self.is_inner)
        def _():
            self.across(u).wait_recv()
            self.total[u] = (self.part[u].astype(F32) + self.inner[u].astype(F32)).astype(BF16)
            self.outwards(u).start()

    def take(self, u):
        @pl.when(self.outer)
        def _():
            self.outwards(u).wait_recv()

        return self.total[u].astype(F32)

    def take_wide(self, w):
        return jnp.concatenate([self.take(u) for u in subs(w)], axis=0)

    def finish(self, u):
        @pl.when(self.outer)
        def _():
            self.inwards(u).wait_send()

        @pl.when(self.is_inner)
        def _():
            self.across(u).wait_send()
            self.outwards(u).wait_send()

    def stages(self, begin, hop=HOP):
        number = self.part.shape[0]
        return [(begin + 2 * hop, self.spread, 1, number), (begin + hop, self.meet, 1, number)]


def line_scratch(units, width):
    block = VMEM((units, UNIT, width), BF16)
    return [block, block, block, DMA((5, units))]


def pipeline(units, stages, tasks=()):
    stages = [stage if len(stage) > 3 else stage + (units,) for stage in stages]
    steps = max(number + delay + 1 - taken for delay, unused, taken, number in stages)

    def step(s, carry):
        for delay, function, taken, number in stages:
            ready = (s >= delay) & (s < number + delay)
            if taken > 1:
                ready = ready & ((s - delay) % taken == 0)

            @pl.when(ready)
            def _():
                function((s - delay) // taken if taken > 1 else s - delay)

        for at, task in tasks:
            if at < steps:

                @pl.when(s == at)
                def _():
                    task()

        return carry

    lax.fori_loop(0, steps, step, 0)
    for at, task in tasks:
        if at >= steps:
            task()


def each_of(number, function):
    def step(u, carry):
        function(u)
        return carry

    lax.fori_loop(0, number, step, 0)


class Loads:
    def __init__(self, sems):
        self.sems, self.number = sems, 0

    def __call__(self, source, target):
        copy = pltpu.make_async_copy(source, target, self.sems.at[self.number])
        copy.start()
        self.number += 1
        return copy


def wait_all(*copies):
    for copy in copies:
        copy.wait()


class Stores:
    def __init__(self, sems):
        self.sems, self.copies = sems, []

    def __call__(self, source, target):
        index = len(self.copies)

        def copy(u):
            rows = unit_rows(u)
            return pltpu.make_async_copy(source.at[rows], target.at[rows], self.sems.at[index, u])

        self.copies.append(copy)
        return copy

    def finish(self, u):
        for copy in self.copies:
            copy(u).wait()


def send_out(units, *copies):
    for u in units:
        for copy in copies:
            copy(u).start()


class Halo:
    def __init__(self, keys, sems, rows, count):
        self.keys, self.sems, self.rows, self.count = keys, sems, rows, count
        self.plan = halo_plan(rows)
        self.c, self.t = place()

    def copy(self, index, u, hop, need, offset):
        target = pl.multiple_of(offset + u * UNIT - (self.rows - need), UNIT)
        return remote(
            self.keys.at[pl.ds(pl.multiple_of(ATTENTION_WINDOW + u * UNIT, UNIT), UNIT)],
            self.keys.at[pl.ds(target, UNIT)],
            self.sems.at[2 * index, u],
            self.sems.at[2 * index + 1, u],
            (jnp.minimum(self.c + hop, self.count - 1), self.t),
        )

    def each(self, u, function, receives):
        for index, (hop, need, offset) in enumerate(self.plan):
            exists = self.c >= hop if receives else self.c + hop < self.count

            @pl.when(exists & (u >= (self.rows - need) // UNIT))
            def _():
                function(self.copy(index, u, hop, need, offset))

    def blank(self):
        width = self.keys.shape[1]
        for hop, need, offset in self.plan:

            @pl.when(self.c < hop)
            def _():
                self.keys[offset : offset + need] = jnp.zeros((need, width), BF16)

    def send(self, u):
        self.each(u, lambda copy: copy.start(), False)

    def finish(self, u):
        self.each(u, lambda copy: copy.wait_recv(), True)
        self.each(u, lambda copy: copy.wait_send(), False)


def project_heads(n, raw, out, out_rows, rows, which, layer):
    cosine, sine = n.cosine[rows], n.sine[rows]
    gain = n.qk_gain[layer, which : which + 1]
    for head in range(raw.shape[1] // HEAD_SIZE):
        part = raw[:, head_cols(head)]
        part = part * rms_inverse(part) * gain
        out[out_rows, head_cols(head)] = rotate(part, cosine, sine).astype(BF16)


def project_keys(n, first, number, stream, layer):
    rows = pl.ds(pl.multiple_of(first, number), number)
    own = pl.ds(pl.multiple_of(ATTENTION_WINDOW + first, number), number)
    normed = (stream * rms_inverse(stream) * n.attn_gain[layer : layer + 1]).astype(BF16)
    n.a1_v[rows] = normed
    key = dot_nn(normed, n.wk_v[...])
    n.kraw_v[rows] = key
    n.kv_v[own, key.shape[1] :] = dot_nn(normed, n.wv_v[...]).astype(BF16)
    project_heads(n, key, n.kv_v, own, rows, 1, layer)


def project_queries(n, first, number, layer):
    rows = pl.ds(pl.multiple_of(first, number), number)
    query = dot_nn(n.a1_v[rows], n.wq_v[...])
    n.qraw_v[rows] = query
    project_heads(n, query, n.q_v, rows, rows, 0, layer)


def project_shapes(s):
    return dict(
        a1=((s.rows, s.model), BF16),
        qraw=((s.rows, s.queries), F32),
        kraw=((s.rows, s.keys), F32),
        q=((s.rows, s.queries), BF16),
        kv=((ATTENTION_WINDOW + s.rows, 2 * s.keys), BF16),
    )


def outputs(shapes):
    return {x: (shaped(*shape, kind=kind), ANY) for x, (shape, kind) in shapes.items()}


def buffers(shapes):
    return {x + "_v": VMEM(shape, kind) for x, (shape, kind) in shapes.items()}


def project_ins(w, tables):
    return dict(
        attn_gain=(w.attn_gain, VMEM),
        qk_gain=(w.qk_gain, VMEM),
        cosine=(tables.cosine, VMEM),
        sine=(tables.sine, VMEM),
        wq=(w.w_query, ANY),
        wk=(w.key_weight, ANY),
        wv=(w.value_weight, ANY),
    )


def project_scratch(s):
    return buffers(project_shapes(s)) | dict(
        wq_v=VMEM((s.model, s.queries), BF16),
        wk_v=VMEM((s.model, s.keys), BF16),
        wv_v=VMEM((s.model, s.keys), BF16),
        halo_sems=DMA((2 * len(halo_plan(s.rows)), s.units)),
    )


def first_scratch(s):
    return dict(
        first_a1=VMEM((s.rows, s.model), BF16),
        first_qraw=VMEM((s.rows, s.queries), F32),
        first_kraw=VMEM((s.rows, s.keys), F32),
        first_wq=VMEM((s.model, s.queries), BF16),
        first_wk=VMEM((s.model, s.keys), BF16),
        first_wv=VMEM((s.model, s.keys), BF16),
        first_sems=DMA((2 * len(halo_plan(s.rows)), s.units)),
    )


def first_outs(s):
    return outputs({"own_" + x: shape for x, shape in project_shapes(s).items()})


def first_view(n):
    return types.SimpleNamespace(
        attn_gain=n.attn_gain,
        qk_gain=n.qk_gain,
        cosine=n.cosine,
        sine=n.sine,
        a1_v=n.first_a1,
        qraw_v=n.first_qraw,
        kraw_v=n.first_kraw,
        q_v=n.qin_v,
        kv_v=n.kvin_v,
        wq_v=n.first_wq,
        wk_v=n.first_wk,
        wv_v=n.first_wv,
    )


def key_block(i, block):
    return pl.ds(pl.multiple_of(i * WIDE + block * KEY_BLOCK, HEAD_SIZE), KEY_BLOCK)


def visible(i, lowest, block, repeat):
    shape = (WIDE, KEY_BLOCK)
    col = block * KEY_BLOCK + lax.broadcasted_iota(jnp.int32, shape, 1)
    seen = col >= lowest - i * WIDE
    if (block + 1) * KEY_BLOCK > ATTENTION_WINDOW:
        row = ATTENTION_WINDOW + lax.broadcasted_iota(jnp.int32, shape, 0)
        seen = seen & (col <= row)
    keep = jnp.where(seen, 1.0, 0.0)
    return jnp.concatenate([keep] * repeat, axis=0)


def key_blocks():
    return (ATTENTION_WINDOW + WIDE) // KEY_BLOCK


def stacked(value, group, repeat):
    first = group * repeat
    return jnp.concatenate(
        [value[:, (first + r) * HEAD_SIZE : (first + r + 1) * HEAD_SIZE] for r in range(repeat)],
        axis=0,
    )


def head_cols(index):
    return slice(index * HEAD_SIZE, (index + 1) * HEAD_SIZE)


def attend(n, i, s):
    rows = wide_rows(i)
    lowest = n.lowest[rows]
    lane = lax.broadcasted_iota(jnp.int32, (WIDE, HEAD_SIZE), 1)
    query_rows = n.qin_v[rows]
    queries = [stacked(query_rows, g, s.repeat) for g in range(s.groups)]
    mixed = [jnp.zeros((s.repeat * WIDE, HEAD_SIZE), F32) for unused in queries]
    total = [jnp.zeros((s.repeat * WIDE, 1), F32) for unused in queries]
    for block in range(key_blocks()):
        keys = key_block(i, block)
        keep = visible(i, lowest, block, s.repeat)
        for g in range(s.groups):
            scores = dot_nt(queries[g], n.kvin_v[keys, head_cols(g)])
            weights = jnp.exp2(scores * EXP2_SCALE) * keep
            total[g] = total[g] + jnp.sum(weights, axis=-1, keepdims=True)
            values = n.kvin_v[keys, head_cols(s.groups + g)]
            mixed[g] = mixed[g] + dot_nn(weights.astype(BF16), values)
    inverses = jnp.zeros((WIDE, HEAD_SIZE), F32)
    for g in range(s.groups):
        inverse = 1.0 / total[g]
        result = (mixed[g] * inverse).astype(BF16)
        for r in range(s.repeat):
            head = g * s.repeat + r
            part = slice(r * WIDE, (r + 1) * WIDE)
            n.o_v[rows, head_cols(head)] = result[part]
            inverses = jnp.where(lane == head, inverse[part], inverses)
    n.inv_v[rows] = inverses


def attend_back(n, i, grad_out, keys_ref, query_ref, s, first_done):
    rows = wide_rows(i)
    lowest = n.lowest[rows]
    query_rows, mixed_rows, inverses = query_ref[rows], n.o_v[rows], n.inv_v[rows]
    queries, grads, inners, scales, found = [], [], [], [], []
    for g in range(s.groups):
        queries.append(stacked(query_rows, g, s.repeat))
        grads.append(stacked(grad_out, g, s.repeat))
        mixed = stacked(mixed_rows, g, s.repeat)
        inners.append(
            jnp.sum(grads[g].astype(F32) * mixed.astype(F32), axis=-1, keepdims=True)
        )
        heads = [g * s.repeat + r for r in range(s.repeat)]
        scales.append(jnp.concatenate([inverses[:, h : h + 1] for h in heads], axis=0))
        found.append(jnp.zeros((s.repeat * WIDE, HEAD_SIZE), F32))
    for block in range(key_blocks()):
        keys = key_block(i, block)
        keep = visible(i, lowest, block, s.repeat)
        for g in range(s.groups):
            key_rows = keys_ref[keys, head_cols(g)]
            scores = dot_nt(queries[g], key_rows)
            probs = jnp.exp2(scores * EXP2_SCALE) * (keep * scales[g])
            grad_probs = dot_nt(grads[g], keys_ref[keys, head_cols(s.groups + g)])
            grad_scores = (probs * (grad_probs - inners[g])).astype(BF16)
            found[g] = found[g] + dot_nn(grad_scores, key_rows)
            n.dkv_v[keys, head_cols(g)] += dot_tn(grad_scores, queries[g])
            n.dkv_v[keys, head_cols(s.groups + g)] += dot_tn(probs.astype(BF16), grads[g])
        if block == 0:
            first_done()
    return [
        found[g][r * WIDE : (r + 1) * WIDE] for g in range(s.groups) for r in range(s.repeat)
    ]


def head_back(n, rows, grad, raw, which, layer):
    gain = n.qk_gain[layer, which : which + 1]
    turned = unrotate(grad, n.cosine[rows], n.sine[rows])
    inverse = rms_inverse(raw)
    unit = raw * inverse
    n.qk_sum[which : which + 1] += column_sum(turned * unit)
    return norm_back(turned, unit, inverse, gain).astype(BF16)


class Returns:
    def __init__(self, n, s):
        self.grads, self.low, self.back, self.sems = n.dkv_v, n.low_v, n.back_v, n.return_sems
        self.s, self.plan = s, halo_plan(s.rows)
        self.c, self.t = place()
        self.blocks = []
        for index, (hop, need, offset) in enumerate(self.plan):
            for b in range(need // WIDE):
                self.blocks.append((index, hop, offset + b * WIDE, b * WIDE))
        self.blocks.sort(key=lambda item: item[2])

    def copy(self, number):
        index, hop, source, target = self.blocks[number]
        return remote(
            self.low.at[pl.ds(source, WIDE)],
            self.back[index].at[pl.ds(target, WIDE)],
            self.sems.at[0, number],
            self.sems.at[1, number],
            (jnp.maximum(self.c - hop, 0), self.t),
        )

    def blank(self):
        for index, (hop, need, unused) in enumerate(self.plan):

            @pl.when(self.c + hop >= self.s.count)
            def _():
                self.back[index][...] = jnp.zeros((need, self.low.shape[1]), BF16)

    def send(self, number):
        rows = pl.ds(self.blocks[number][2], WIDE)

        @pl.when(self.c >= self.blocks[number][1])
        def _():
            self.low[rows] = self.grads[rows].astype(BF16)
            self.copy(number).start()

    def send_complete(self, i):
        for number, block in enumerate(self.blocks):
            if block[2] // WIDE < self.s.rows // WIDE - 1:

                @pl.when(i == block[2] // WIDE)
                def _():
                    self.send(number)

    def send_rest(self):
        for number, block in enumerate(self.blocks):
            if block[2] // WIDE >= self.s.rows // WIDE - 1:
                self.send(number)

    def receive(self):
        for number, block in enumerate(self.blocks):

            @pl.when(self.c + block[1] < self.s.count)
            def _():
                self.copy(number).wait_recv()

    def finish(self):
        for number, block in enumerate(self.blocks):

            @pl.when(self.c >= block[1])
            def _():
                self.copy(number).wait_send()


def attention_back_scratch(s):
    plan = halo_plan(s.rows)
    return dict(
        dkv_v=VMEM((ATTENTION_WINDOW + s.rows, 2 * s.keys), F32),
        low_v=VMEM((ATTENTION_WINDOW, 2 * s.keys), BF16),
        back_v=[VMEM((need, 2 * s.keys), BF16) for unused, need, unused_too in plan],
        total_v=VMEM((WIDE, 2 * s.keys), F32),
        return_sems=DMA((2, ATTENTION_WINDOW // WIDE)),
    )


def attention_back_shapes(s):
    return dict(
        dyb=((s.rows, s.model), BF16),
        dgate=((s.rows, s.hidden), BF16),
        dup=((s.rows, s.hidden), BF16),
        dhb=((s.rows, s.model), BF16),
        dq=((s.rows, s.queries), BF16),
        dk=((s.rows, s.keys), BF16),
        dv=((s.rows, s.keys), BF16),
    )


def attention_back_sums(s):
    return dict(
        dres=(shaped(s.rows, s.model, kind=F32), ANY),
        ffn_sum=(shaped(1, s.model, kind=F32), VMEM),
        qk_sum=(shaped(2, HEAD_SIZE, kind=F32), VMEM),
    )


def back_start(n, returns):
    returns.blank()
    n.dkv_v[...] = jnp.zeros_like(n.dkv_v)
    n.ffn_sum[...] = jnp.zeros_like(n.ffn_sum)
    n.qk_sum[...] = jnp.zeros_like(n.qk_sum)


def feed_back(n, i, gate, up, lower, made):
    here = wide_rows(i)
    low = n.g_v[here].astype(BF16)
    n.dyb_v[here] = low
    grad_hidden = dot_nt(low, n.wd_v[...])
    sigma = jax.nn.sigmoid(gate)
    dgate = (grad_hidden * up * (sigma * (1.0 + gate * (1.0 - sigma)))).astype(BF16)
    dup = (grad_hidden * gate * sigma).astype(BF16)
    n.dgate_v[here] = dgate
    n.dup_v[here] = dup
    lower.push(i, dot_nt(dgate, n.wg_v[...]) + dot_nt(dup, n.wu_v[...]))
    send_out(subs(i), *made)


def attention_back(n, i, middle, keys_ref, query_ref, layer, lower, returns, made, s):
    here = wide_rows(i)
    grad_in = lower.take_wide(i)
    inverse = rms_inverse(middle)
    unit = middle * inverse
    n.ffn_sum[...] += column_sum(grad_in * unit)
    total = n.g_v[here] + norm_back(grad_in, unit, inverse, n.ffn_gain[layer : layer + 1])
    n.g_v[here] = total
    low = total.astype(BF16)
    n.dhb_v[here] = low
    grad_out = dot_nt(low, n.wo_v[...]).astype(BF16)
    early = s.rows - WIDE + KEY_BLOCK >= ATTENTION_WINDOW
    send_rest = lambda: pl.when(i == s.rows // WIDE - 1)(returns.send_rest)
    pieces = attend_back(
        n, i, grad_out, keys_ref, query_ref, s, send_rest if early else lambda: None
    )
    returns.send_complete(i)
    if not early:
        send_rest()
    for head, piece in enumerate(pieces):
        n.dq_v[here, head_cols(head)] = head_back(
            n, here, piece * SCALE, n.qraw_v[here, head_cols(head)], 0, layer
        )
    send_out(subs(i), *made)


def keys_back(n, layer, returns, made, s):
    def each(i):
        here = wide_rows(i)
        own = pl.ds(pl.multiple_of(ATTENTION_WINDOW + i * WIDE, WIDE), WIDE)
        n.total_v[...] = n.dkv_v[own]
        for index, (hop, need, unused) in enumerate(returns.plan):
            skipped = s.rows - need

            @pl.when(i >= skipped // WIDE)
            def _():
                part = pl.ds(pl.multiple_of(i * WIDE - skipped, WIDE), WIDE)
                n.total_v[...] += n.back_v[index][part].astype(F32)

        for g in range(s.groups):
            n.dk_v[here, head_cols(g)] = head_back(
                n, here, n.total_v[:, head_cols(g)] * SCALE, n.kraw_v[here, head_cols(g)], 1, layer
            )
        n.dv_v[here] = n.total_v[:, s.keys :].astype(BF16)
        send_out(subs(i), *made)

    each_of(s.rows // WIDE, each)


def feed(n, i, middle, layer):
    here = wide_rows(i)
    normed = (middle * rms_inverse(middle) * n.ffn_gain[layer : layer + 1]).astype(BF16)
    n.a2_v[here] = normed
    gate = dot_nn(normed, n.wg_v[...])
    up = dot_nn(normed, n.wu_v[...])
    inside = (gate * jax.nn.sigmoid(gate) * up).astype(BF16)
    n.hidden_v[here] = inside
    return gate, up, dot_nn(inside, n.wd_v[...])


def layer_ins(stream, saved, w, tables):
    before = dict(qin=(saved.q, ANY), kvin=(saved.kv, ANY)) if saved else {}
    return before | dict(
        x=(stream, ANY),
        ffn_gain=(w.ffn_gain, VMEM),
        lowest=(tables.lowest, VMEM),
        wo=(w.w_out, ANY),
        wg=(w.w_gate, ANY),
        wu=(w.w_up, ANY),
        wd=(w.w_down, ANY),
    )


def weight_scratch(s):
    return dict(
        wo_v=VMEM((s.queries, s.model), BF16),
        wg_v=VMEM((s.model, s.hidden), BF16),
        wu_v=VMEM((s.model, s.hidden), BF16),
        wd_v=VMEM((s.hidden, s.model), BF16),
    )


def layer_scratch(stream, s, stores):
    return weight_scratch(s) | dict(
        x_v=VMEM((s.rows, s.model), stream.dtype),
        qin_v=VMEM((s.rows, s.queries), BF16),
        kvin_v=VMEM((ATTENTION_WINDOW + s.rows, 2 * s.keys), BF16),
        load_sems=DMA((20,)),
        store_sems=DMA((stores, s.units)),
        first=line_scratch(s.units, s.model),
        second=line_scratch(s.units, s.model),
    )


def layer_loads(n, loads, layer, projected):
    if projected:
        early = (loads(n.qin, n.qin_v), loads(n.kvin, n.kvin_v))
    else:
        early = (loads(n.x, n.x_v),)
    early += (loads(n.wo.at[layer], n.wo_v),)
    late = () if not projected else (loads(n.x, n.x_v),)
    late += (
        loads(n.wg.at[layer], n.wg_v),
        loads(n.wu.at[layer], n.wu_v),
        loads(n.wd.at[layer], n.wd_v),
    )
    return early, late


def kept_shapes(s):
    return dict(
        o=((s.rows, s.queries), BF16),
        a2=((s.rows, s.model), BF16),
        hidden=((s.rows, s.hidden), BF16),
    )


def forward_shapes(s):
    return kept_shapes(s) | dict(
        inv=((s.rows, HEAD_SIZE), F32),
        h=((s.rows, s.model), F32),
        gate=((s.rows, s.hidden), BF16),
        up=((s.rows, s.hidden), BF16),
        y=((s.rows, s.model), F32),
    )


def forward_layer(layer, stream, saved, w, tables, s):
    def body(n):
        loads = Loads(n.load_sems)
        if not saved:
            own_weights = (
                loads(n.wk.at[layer], n.first_wk),
                loads(n.wv.at[layer], n.first_wv),
                loads(n.wq.at[layer], n.first_wq),
            )
        early, late = layer_loads(n, loads, layer, saved is not None)
        above = (
            loads(n.wq.at[layer + 1], n.wq_v),
            loads(n.wk.at[layer + 1], n.wk_v),
            loads(n.wv.at[layer + 1], n.wv_v),
        )
        stores = Stores(n.store_sems)
        mixed = (stores(n.o_v, n.o), stores(n.inv_v, n.inv))
        fed = (
            stores(n.h_v, n.h),
            stores(n.a2_v, n.a2),
            stores(n.hidden_v, n.hidden),
            stores(n.gate_v, n.gate),
            stores(n.up_v, n.up),
        )
        closed = (
            stores(n.y_v, n.y),
            stores(n.a1_v, n.a1),
            stores(n.qraw_v, n.qraw),
            stores(n.kraw_v, n.kraw),
            stores(n.q_v, n.q),
        )
        first, second = LineSum(n.first), LineSum(n.second)
        halo = Halo(n.kv_v, n.halo_sems, s.rows, s.count)
        greet(line_partners() + halo_partners(s.rows, s.count))
        halo.blank()
        wait_all(*early)
        if not saved:
            wait_all(*own_weights)
            own = first_view(n)
            own_halo = Halo(n.kvin_v, n.first_sems, s.rows, s.count)
            own_halo.blank()

            def own_keys(i):
                project_keys(own, i * WIDE, WIDE, n.x_v[wide_rows(i)].astype(F32), layer)
                for u in subs(i):
                    own_halo.send(u)

            def own_queries(i):
                project_queries(own, i * WIDE, WIDE, layer)

            each_of(s.rows // WIDE, own_keys)
            each_of(s.rows // WIDE, own_queries)
            each_of(s.units, own_halo.finish)
            own_out = (
                loads(n.kvin_v, n.own_kv),
                loads(n.first_a1, n.own_a1),
                loads(n.first_qraw, n.own_qraw),
                loads(n.first_kraw, n.own_kraw),
                loads(n.qin_v, n.own_q),
            )

        def mix(i):
            attend(n, i, s)
            first.push(i, dot_nn(n.o_v[wide_rows(i)], n.wo_v[...]))
            send_out(subs(i), *mixed)

        def feed_wide(i):
            pl.when(i == 0)(lambda: wait_all(*late))
            here = wide_rows(i)
            middle = n.x_v[here].astype(F32) + first.take_wide(i)
            n.h_v[here] = middle
            gate, up, part = feed(n, i, middle, layer)
            second.push(i, part)
            n.gate_v[here] = gate.astype(BF16)
            n.up_v[here] = up.astype(BF16)
            send_out(subs(i), *fed)

        def close(u):
            pl.when(u == 0)(lambda: wait_all(*above))
            here = unit_rows(u)
            result = n.h_v[here] + second.take(u)
            n.y_v[here] = result
            project_keys(n, u * UNIT, UNIT, result, layer + 1)
            halo.send(u)
            project_queries(n, u * UNIT, UNIT, layer + 1)
            send_out([u], *closed)

        at = ARRIVED
        pipeline(
            s.units,
            second.stages(at)
            + first.stages(0)
            + [(at + 3 * HOP, close, 1), (at, feed_wide, WIDE // UNIT), (0, mix, WIDE // UNIT)],
        )
        each_of(s.units, halo.finish)
        keys = loads(n.kv_v, n.kv)

        def finish(u):
            first.finish(u)
            second.finish(u)
            stores.finish(u)

        each_of(s.units, finish)
        keys.wait()
        if not saved:
            wait_all(*own_out)

    return run_kernel(
        body,
        layer_ins(stream, saved, w, tables) | project_ins(w, tables),
        outputs(forward_shapes(s))
        | outputs(project_shapes(s))
        | ({} if saved else first_outs(s)),
        layer_scratch(stream, s, 12)
        | buffers(forward_shapes(s))
        | project_scratch(s)
        | ({} if saved else first_scratch(s)),
        2 + layer,
    )


def units_at_turn(s):
    return s.units - min(REST_WIDES, s.rows // WIDE // 2) * (WIDE // UNIT)


def turn_layer(layer, stream, saved, cotangent, w, tables, s):
    def body(n):
        loads = Loads(n.load_sems)
        early, late = layer_loads(n, loads, layer, True)
        late = late + (loads(n.grad, n.grad_v),)
        raws = (loads(n.qraw, n.qraw_v), loads(n.kraw, n.kraw_v))
        a1 = loads(n.a1, n.a1_v)
        stores = Stores(n.store_sems)
        closed = Stores(n.y_sems)
        put_result = closed(n.y_v, n.y)
        turned = (stores(n.g_v, n.dres), stores(n.dq_v, n.dq))
        keyed = (stores(n.dk_v, n.dk), stores(n.dv_v, n.dv))
        first, second, lower = LineSum(n.first), LineSum(n.second), LineSum(n.lower)
        returns = Returns(n, s)
        greet(line_partners() + halo_partners(s.rows, s.count))
        wait_all(*early)

        def mix(i):
            attend(n, i, s)
            first.push(i, dot_nn(n.o_v[wide_rows(i)], n.wo_v[...]))

        def feed_both(i):
            pl.when(i == 0)(lambda: wait_all(*late))
            here = wide_rows(i)
            middle = n.x_v[here] + first.take_wide(i)
            n.x_v[here] = middle
            n.g_v[here] = n.grad_v[here].astype(F32)
            gate, up, part = feed(n, i, middle, layer)
            feed_back(n, i, gate, up, lower, ())

            @pl.when(i < here_units * UNIT // WIDE)
            def _():
                second.hold(i, part)

            @pl.when(i >= here_units * UNIT // WIDE)
            def _():
                for k, u in enumerate(subs(i)):
                    n.rest_v[u - here_units] = part[k * UNIT : (k + 1) * UNIT].astype(BF16)

        def close(u):
            here = unit_rows(u)
            n.y_v[here] = (n.x_v[here] + second.take(u)).astype(BF16)
            send_out([u], put_result)

        rest_rows = pl.ds(here_units * UNIT, s.rows - here_units * UNIT)
        rest = (
            pltpu.make_async_copy(n.rest_v, n.rest, n.rest_sems.at[0]),
            pltpu.make_async_copy(n.x_v.at[rest_rows], n.rest_h, n.rest_sems.at[1]),
        )

        def put_rest():
            for copy in rest:
                copy.start()

        def attention(i):
            pl.when(i == 0)(lambda: wait_all(*raws))
            middle = n.x_v[wide_rows(i)]
            attention_back(
                n, i, middle, n.kvin_v, n.qin_v, layer, lower, returns, turned, s
            )

        at = ARRIVED
        def gradient(index):
            left, right = factors[index]
            block_products(n.grads_v[index], left, right, sizes[index][0], s)
            gradient_store(index).start()

        def gradient_store(index):
            return pltpu.make_async_copy(n.grads_v[index], n.grads[index], n.grad_sems.at[index])

        def end_keys():
            returns.receive()
            keys_back(n, layer, returns, keyed, s)
            a1.wait()

        factors = [
            (n.a2_v, n.dup_v),
            (n.a2_v, n.dgate_v),
            (n.a1_v, n.dq_v),
            (n.hidden_v, n.dyb_v),
            (n.o_v, n.dhb_v),
            (n.a1_v, n.dk_v),
            (n.a1_v, n.dv_v),
        ]
        after = at + ARRIVED + s.units
        tasks = [(1, lambda: back_start(n, returns)), (at + s.units, put_rest), (after + 4, end_keys)]
        for index, step in enumerate((1, 2, 5, 3, 4, 6, 6)):
            tasks.append((after + step, lambda index=index: gradient(index)))
        tasks.sort(key=lambda item: item[0])
        pipeline(
            s.units,
            lower.stages(at)
            + second.stages(OUTPUT_AT, HOP + 1)
            + first.stages(0)
            + [
                (OUTPUT_AT, second.send, 1, here_units),
                (OUTPUT_AT + 3 * HOP + 3, close, 1, here_units),
                (at + ARRIVED, attention, WIDE // UNIT),
                (at, feed_both, WIDE // UNIT),
                (0, mix, WIDE // UNIT),
            ],
            tasks,
        )
        returns.finish()
        for index in range(len(sizes)):
            gradient_store(index).wait()

        wait_all(*rest)

        def finish(u):
            first.finish(u)
            lower.finish(u)
            stores.finish(u)

        def finish_result(u):
            second.finish(u)
            closed.finish(u)

        each_of(s.units, finish)
        each_of(here_units, finish_result)

    sizes = grad_sizes(s)
    backs = attention_back_shapes(s)
    blocks = block_shapes(s, sizes)
    here_units = units_at_turn(s)
    rest_units = s.units - here_units
    return run_kernel(
        body,
        layer_ins(stream, saved, w, tables)
        | dict(
            grad=(cotangent, ANY),
            a1=(saved.a1, ANY),
            qraw=(saved.qraw, ANY),
            kraw=(saved.kraw, ANY),
            qk_gain=(w.qk_gain, VMEM),
            cosine=(tables.cosine, VMEM),
            sine=(tables.sine, VMEM),
        ),
        outputs({x: backs[x] for x in dict(dq=0, dk=0, dv=0)})
        | attention_back_sums(s)
        | dict(
            y=(shaped(here_units * UNIT, s.model), ANY),
            rest=(shaped(rest_units, UNIT, s.model), ANY),
            rest_h=(shaped(rest_units * UNIT, s.model, kind=F32), ANY),
            grads=[(shaped(*block), ANY) for block in blocks],
        ),
        layer_scratch(stream, s, 5)
        | buffers(kept_shapes(s))
        | buffers(backs)
        | attention_back_scratch(s)
        | dict(
            y_v=VMEM((here_units * UNIT, s.model), BF16),
            y_sems=DMA((1, here_units)),
            rest_v=VMEM((rest_units, UNIT, s.model), BF16),
            rest_sems=DMA((2,)),
            second=line_scratch(here_units, s.model),
            a1_v=VMEM((s.rows, s.model), BF16),
            grads_v=[VMEM(block, BF16) for block in blocks],
            grad_sems=DMA((len(sizes),)),
            inv_v=VMEM((s.rows, HEAD_SIZE), F32),
            grad_v=VMEM((s.rows, s.model), BF16),
            g_v=VMEM((s.rows, s.model), F32),
            qraw_v=VMEM((s.rows, s.queries), F32),
            kraw_v=VMEM((s.rows, s.keys), F32),
            lower=line_scratch(s.units, s.model),
        ),
        2 + layer,
    )


def halving_partners(count):
    c, t = place()
    return [(c >= 0, (c ^ (1 << b), t)) for b in range(count.bit_length() - 1)]


def block_products(target, left, right, line, s):
    bits = s.count.bit_length() - 1
    half = s.count // 2
    for part in range(2):
        product = dot_tn(left[:, part * half * line : (part + 1) * half * line], right[...])
        for k in range(half):
            block = part * half + k
            at = tuple((block >> b) & 1 for b in range(bits - 1, -1, -1))
            target[at + (slice(0, line),)] = product[k * line : (k + 1) * line].astype(BF16)


def block_shapes(s, sizes):
    bits = s.count.bit_length() - 1
    return [(2,) * bits + (line + -line % 16, width) for line, width in sizes]


class Scatter:
    def __init__(self, n, s, sizes, factors=None):
        self.n, self.s, self.sizes, self.factors = n, s, sizes, factors
        self.bits = s.count.bit_length() - 1
        self.c, self.t = place()
        self.beside = []

    def bit(self, b):
        return (self.c >> b) & 1

    def order(self, index):
        rest = list(range(1, self.bits))
        return [0] + (rest if index % 2 == 0 else rest[::-1])

    def spot(self, picks):
        low = 0 if self.factors else 1
        return tuple(picks.get(b, slice(None)) for b in range(self.bits - 1, low - 1, -1))

    def own(self, index):
        return (self.n.whole_v if self.factors else self.n.own)[index]

    def copy(self, index, step):
        order = self.order(index)
        picks = {b: self.bit(b) for b in order[:step]}
        picks[order[step]] = 1 - self.bit(order[step])
        if step == 0 and not self.factors:
            source = self.n.whole[index].at[
                (slice(None),) * (self.bits - 1) + (1 - self.bit(0),)
            ]
        else:
            source = self.own(index).at[self.spot(picks)]
        sems = self.n.scatter_sems
        return remote(
            source,
            self.n.got[index * self.bits + step],
            sems.at[0, index, step],
            sems.at[1, index, step],
            (self.c ^ (1 << order[step]), self.t),
        )

    def load(self, index):
        return pltpu.make_async_copy(
            self.n.whole[index].at[(slice(None),) * (self.bits - 1) + (self.bit(0),)],
            self.n.own[index],
            self.n.scatter_load_sems.at[index],
        )

    def start(self, index):
        if self.factors:
            left, right, needed = self.factors[index]
            wait_all(*needed)
            block_products(self.own(index), left, right, self.sizes[index][0], self.s)
        else:
            self.load(index).start()
        self.copy(index, 0).start()

    def add(self, index, step):
        order = self.order(index)
        if step == 0 and not self.factors:
            self.load(index).wait()
        self.copy(index, step).wait_recv()
        free = [b for b in range(self.bits - 1, 0, -1) if b not in order[: step + 1]]
        own, got = self.own(index), self.n.got[index * self.bits + step]
        line = self.sizes[index][0]

        def one(k, carry):
            picks = {b: (k >> (len(free) - 1 - i)) & 1 for i, b in enumerate(free)}
            here = self.spot({b: self.bit(b) for b in order[: step + 1]} | picks)
            total = own[here].astype(F32) + got[tuple(picks[b] for b in free)].astype(F32)
            if step == self.bits - 1:
                self.sum_of(index)[...] = total[:line]
            else:
                own[here] = total.astype(BF16)
            return carry

        if free:
            lax.fori_loop(0, 1 << len(free), one, 0)
        else:
            one(0, 0)
        if step < self.bits - 1:
            self.copy(index, step + 1).start()
        else:
            for other in self.beside:
                other[index].wait()
            self.store(index).start()

    def sum_of(self, index):
        return self.n.sums_v[index].at[0] if self.factors else self.n.sums_v[index]

    def store(self, index):
        return pltpu.make_async_copy(
            self.n.sums_v[index], self.n.sums[index], self.n.scatter_store_sems.at[index]
        )

    def tasks(self, every, bases):
        found = []
        for index in range(len(self.sizes)):
            found.append((bases[0] + index * every, lambda index=index: self.start(index)))
            for step in range(self.bits):
                at = bases[min(step + 1, len(bases) - 1)] + index * every
                at += 100 * max(0, step + 2 - len(bases))
                found.append((at, lambda index=index, step=step: self.add(index, step)))
        found.sort(key=lambda item: item[0])
        return found

    def finish(self):
        for index in range(len(self.sizes)):
            self.store(index).wait()
            for step in range(self.bits):
                self.copy(index, step).wait_send()


def scatter_scratch(s, sizes, computed, layers):
    bits = s.count.bit_length() - 1
    tails = [(line + -line % 16, width) for line, width in sizes]
    found = dict(
        sums_v=[VMEM(((layers,) if computed else ()) + size, F32) for size in sizes],
        got=[
            VMEM((2,) * (bits - 1 - step) + tail, BF16) for tail in tails for step in range(bits)
        ],
        scatter_sems=DMA((2, len(sizes), bits)),
        scatter_load_sems=DMA((len(sizes),)),
        scatter_store_sems=DMA((len(sizes),)),
    )
    if computed:
        return found | dict(whole_v=[VMEM((2,) * bits + tail, BF16) for tail in tails])
    return found | dict(own=[VMEM((2,) * (bits - 1) + tail, BF16) for tail in tails])


def block_view(array, s):
    bits = s.count.bit_length() - 1
    line = array.shape[0] // s.count
    view = array.reshape((2,) * bits + (line, array.shape[1]))
    if line % 16:
        view = jnp.pad(view, [(0, 0)] * bits + [(0, -line % 16), (0, 0)])
    return view


def factor_pairs(k):
    return [
        (k.a2, k.dup),
        (k.a2, k.dgate),
        (k.a1, k.dq),
        (k.hidden, k.dyb),
        (k.o, k.dhb),
        (k.a1, k.dk),
        (k.a1, k.dv),
    ]


def grad_sizes(s):
    return [
        (s.model // s.count, s.hidden),
        (s.model // s.count, s.hidden),
        (s.model // s.count, s.queries),
        (s.hidden // s.count, s.model),
        (s.queries // s.count, s.model),
        (s.model // s.count, s.keys),
        (s.model // s.count, s.keys),
    ]


def head_ins(k, w):
    return dict(
        hq=(k.dq, ANY),
        hk=(k.dk, ANY),
        hv=(k.dv, ANY),
        wq=(w.w_query, ANY),
        wk=(w.key_weight, ANY),
        wv=(w.value_weight, ANY),
        x=(k.x, ANY),
        attn_gain=(w.attn_gain, VMEM),
        grad=(k.dres, ANY),
    )


def head_scratch(k, s):
    return dict(
        hq_v=VMEM((s.rows, s.queries), BF16),
        hk_v=VMEM((s.rows, s.keys), BF16),
        hv_v=VMEM((s.rows, s.keys), BF16),
        wq_v=VMEM((s.model, s.queries), BF16),
        wk_v=VMEM((s.model, s.keys), BF16),
        wv_v=VMEM((s.model, s.keys), BF16),
        x_v=VMEM((s.rows, s.model), k.x.dtype),
        g_v=VMEM((s.rows, s.model), F32),
        upper=line_scratch(s.units, s.model),
        load_sems=DMA((32,)),
        store_sems=DMA((10, s.units)),
    )


def head_loads(n, loads, layer):
    early = (
        loads(n.hq, n.hq_v),
        loads(n.wq.at[layer], n.wq_v),
        loads(n.hk, n.hk_v),
        loads(n.wk.at[layer], n.wk_v),
        loads(n.hv, n.hv_v),
        loads(n.wv.at[layer], n.wv_v),
    )
    return early, (loads(n.x, n.x_v), loads(n.grad, n.g_v))


def head_inputs(n, i, upper):
    here = wide_rows(i)
    upper.push(
        i,
        dot_nt(n.hq_v[here], n.wq_v[...])
        + dot_nt(n.hk_v[here], n.wk_v[...])
        + dot_nt(n.hv_v[here], n.wv_v[...]),
    )


def head_norm(n, here, grad_in, layer):
    stream = n.x_v[here].astype(F32)
    inverse = rms_inverse(stream)
    unit = stream * inverse
    n.attn_sum[...] += column_sum(grad_in * unit)
    n.g_v[here] += norm_back(grad_in, unit, inverse, n.attn_gain[layer : layer + 1])


def backward_layer(layer, kept, w, tables, s):
    above, here_kept = kept[layer + 1], kept[layer]
    sizes = grad_sizes(s)
    rest_units = s.units - units_at_turn(s) if layer + 2 == len(kept) else 0
    backs = attention_back_shapes(s)
    extra_ins, extra_outs, extra_scratch = {}, {}, {}
    if rest_units:
        extra_ins = dict(rest=(above.rest, ANY), rest_h=(above.rest_h, ANY))
        extra_outs = dict(y=(shaped(rest_units * UNIT, s.model), ANY))
        extra_scratch = dict(
            second=line_scratch(rest_units, s.model),
            y_sems=DMA((1, rest_units)),
            rest_sems=DMA((1,)),
        )

    def body(n):
        loads = Loads(n.load_sems)
        early, middle_loads = head_loads(n, loads, layer + 1)
        scatter = Scatter(n, s, sizes)
        n.dgate_v, n.dup_v = n.gate_v, n.up_v
        feeds = (
            loads(n.wd.at[layer], n.wd_v),
            loads(n.gate, n.gate_v),
            loads(n.up, n.up_v),
            loads(n.wg.at[layer], n.wg_v),
            loads(n.wu.at[layer], n.wu_v),
        )
        lates = (
            loads(n.wo.at[layer], n.wo_v),
            loads(n.q, n.q_v),
            loads(n.kv, n.kv_v),
            loads(n.o, n.o_v),
            loads(n.inv, n.inv_v),
            loads(n.qraw, n.qraw_v),
            loads(n.kraw, n.kraw_v),
        )
        stores = Stores(n.store_sems)
        fed_back = (stores(n.dyb_v, n.dyb), stores(n.dgate_v, n.dgate), stores(n.dup_v, n.dup))
        turned = (stores(n.g_v, n.dres), stores(n.dhb_v, n.dhb), stores(n.dq_v, n.dq))
        keyed = (stores(n.dk_v, n.dk), stores(n.dv_v, n.dv))
        upper, lower = LineSum(n.upper), LineSum(n.lower)
        returns = Returns(n, s)
        greet(line_partners() + halo_partners(s.rows, s.count) + halving_partners(s.count))
        n.attn_sum[...] = jnp.zeros_like(n.attn_sum)
        wait_all(*early)

        if rest_units:
            second = LineSum(n.second)
            rest = loads(n.rest, second.part)
            rest_h = pltpu.make_async_copy(
                n.rest_h, n.x_v.at[pl.ds(0, rest_units * UNIT)], n.rest_sems.at[0]
            )

            def result_copy(u):
                return pltpu.make_async_copy(
                    second.inner.at[u], n.y.at[unit_rows(u)], n.y_sems.at[0, u]
                )

            def send_result(u):
                pl.when(u == 0)(rest.wait)
                second.send(u)

            def close(u):
                pl.when(u == 0)(rest_h.wait)
                total = n.x_v[unit_rows(u)].astype(F32) + second.take(u)
                second.inner[u] = total.astype(BF16)
                result_copy(u).start()

        def middle_copy(i):
            rows = wide_rows(i)
            return pltpu.make_async_copy(n.h.at[rows], n.x_v.at[rows], n.middle_sems.at[i])

        def inputs(i):
            head_inputs(n, i, upper)

        def pass_norm(i):
            pl.when(i == 0)(lambda: wait_all(*middle_loads, *feeds))
            here = wide_rows(i)
            head_norm(n, here, upper.take_wide(i), layer + 1)
            middle_copy(i).start()
            gate, up = n.gate_v[here].astype(F32), n.up_v[here].astype(F32)
            feed_back(n, i, gate, up, lower, fed_back)

        def attention(i):
            pl.when(i == 0)(lambda: wait_all(*lates))
            middle_copy(i).wait()
            attention_back(
                n, i, n.x_v[wide_rows(i)], n.kv_v, n.q_v, layer, lower, returns, turned, s
            )

        at = ARRIVED
        after = at + ARRIVED + s.units

        def end_keys():
            returns.receive()
            keys_back(n, layer, returns, keyed, s)

        tasks = [(0, lambda: back_start(n, returns)), (after + 2, end_keys)]
        tasks += scatter.tasks(1, SCATTER_MIDDLE)
        stages = lower.stages(at) + upper.stages(0)
        if rest_units:
            passed = at + ARRIVED + -(-rest_units * UNIT // WIDE) * (WIDE // UNIT) - 1
            tasks.append((passed, rest_h.start))
            stages += second.stages(REST_AT, REST_HOP) + [
                (REST_AT, send_result, 1, rest_units),
                (max(REST_AT + 3 * REST_HOP, passed + 1), close, 1, rest_units),
            ]
        tasks.sort(key=lambda item: item[0])
        pipeline(
            s.units,
            stages
            + [
                (at + ARRIVED, attention, WIDE // UNIT),
                (at, pass_norm, WIDE // UNIT),
                (0, inputs, WIDE // UNIT),
            ],
            tasks,
        )
        returns.finish()
        scatter.finish()
        if rest_units:

            def finish_result(u):
                second.finish(u)
                result_copy(u).wait()

            each_of(rest_units, finish_result)

        def finish(u):
            upper.finish(u)
            lower.finish(u)
            stores.finish(u)

        each_of(s.units, finish)

    whole = above.grads or [
        block_view(dot_tn(left, right).astype(BF16), s) for left, right in factor_pairs(above)
    ]
    held = dict(
        gate=here_kept.gate,
        up=here_kept.up,
        q=here_kept.q,
        kv=here_kept.kv,
        o=here_kept.o,
        inv=here_kept.inv,
        qraw=here_kept.qraw,
        kraw=here_kept.kraw,
    )
    return run_kernel(
        body,
        head_ins(above, w)
        | {x: (array, ANY) for x, array in held.items()}
        | dict(
            h=(here_kept.h, ANY),
            wd=(w.w_down, ANY),
            wg=(w.w_gate, ANY),
            wu=(w.w_up, ANY),
            wo=(w.w_out, ANY),
            ffn_gain=(w.ffn_gain, VMEM),
            qk_gain=(w.qk_gain, VMEM),
            cosine=(tables.cosine, VMEM),
            sine=(tables.sine, VMEM),
            lowest=(tables.lowest, VMEM),
            whole=[(array, ANY) for array in whole],
        )
        | extra_ins,
        outputs(attention_back_shapes(s))
        | attention_back_sums(s)
        | dict(
            attn_sum=(shaped(1, s.model, kind=F32), VMEM),
            sums=[(shaped(*size, kind=F32), ANY) for size in sizes],
        )
        | extra_outs,
        head_scratch(above, s)
        | extra_scratch
        | weight_scratch(s)
        | {x + "_v": VMEM(array.shape, array.dtype) for x, array in held.items()}
        | buffers({x: b for x, b in backs.items() if x not in dict(dgate=0, dup=0)})
        | attention_back_scratch(s)
        | scatter_scratch(s, sizes, False, 1)
        | dict(
            lower=line_scratch(s.units, s.model),
            middle_sems=DMA((s.rows // WIDE,)),
        ),
        20 + layer,
    )


def backward_end(kept, w, s):
    bottom = kept[0]
    sizes = grad_sizes(s)
    layers = len(kept)
    width = s.model // s.count
    bits = s.count.bit_length() - 1
    tp_bits = s.line.bit_length() - 1
    rounds = [(1 << b, 0) for b in range(bits)] + [(0, 1 << b) for b in range(tp_bits)]

    def body(n):
        c, t = place()
        loads = Loads(n.load_sems)
        early, lates = head_loads(n, loads, 0)
        a2, dup, dgate = loads(n.a2, n.a2_v), loads(n.dup, n.dup_v), loads(n.dgate, n.dgate_v)
        a1, hidden, dyb = loads(n.a1, n.a1_v), loads(n.hidden, n.hidden_v), loads(n.dyb, n.dyb_v)
        o, dhb = loads(n.o, n.o_v), loads(n.dhb, n.dhb_v)
        factors = [
            (n.a2_v, n.dup_v, (a2, dup)),
            (n.a2_v, n.dgate_v, (dgate,)),
            (n.a1_v, n.hq_v, (a1,)),
            (n.hidden_v, n.dyb_v, (hidden, dyb)),
            (n.o_v, n.dhb_v, (o, dhb)),
            (n.a1_v, n.hk_v, ()),
            (n.a1_v, n.hv_v, ()),
        ]
        scatter = Scatter(n, s, sizes, factors)
        stores = Stores(n.store_sems)
        out = stores(n.g_v, n.dres)
        upper = LineSum(n.upper)
        others = [(c >= 0, ((c + k) % s.count, t)) for k in range(1, s.count)]
        lines = [(c >= 0, (c, t ^ (1 << b))) for b in range(tp_bits)]
        greet(line_partners() + halving_partners(s.count) + others + lines)
        n.attn_sum[...] = jnp.zeros_like(n.attn_sum)
        n.acc[...] = jnp.zeros_like(n.acc)
        n.gains[...] = jnp.zeros_like(n.gains)
        for layer in range(layers):
            n.acc[0, 2 * layer : 2 * layer + 2] = n.qk_in[layer][...]
        wait_all(*early)
        scatter.beside = [
            [
                loads(n.done[(layer - 1) * len(sizes) + index], n.sums_v[index].at[layer])
                for index in range(len(sizes))
            ]
            for layer in range(1, layers)
        ]

        def head_copy(k):
            return remote(
                n.acc.at[k],
                n.other.at[k],
                n.small_sems.at[0, k],
                n.small_sems.at[1, k],
                (c ^ rounds[k][0], t ^ rounds[k][1]),
            )

        def head_step(k):
            if k > 0:
                head_copy(k - 1).wait_recv()
                n.acc[k] = n.acc[k - 1] + n.other[k - 1]
            if k < len(rounds):
                head_copy(k).start()

        def pass_norm(u):
            pl.when(u == 0)(lambda: wait_all(*lates))
            head_norm(n, unit_rows(u), upper.take(u), 0)
            send_out([u], out)

        tasks = scatter.tasks(SCATTER_EVERY, SCATTER_END)
        tasks += [(2 * k + 1, lambda k=k: head_step(k)) for k in range(len(rounds) + 1)]
        tasks.sort(key=lambda item: item[0])
        pipeline(
            s.units,
            upper.stages(0)
            + [
                (3 * HOP, pass_norm, 1),
                (0, lambda i: head_inputs(n, i, upper), WIDE // UNIT),
            ],
            tasks,
        )
        gains = [n.attn_sum] + n.attn_in + n.ffn_in
        for d in range(s.count):
            for row, gain in enumerate(gains):
                n.gains[d, row : row + 1] = gain[:, d * width : (d + 1) * width]

        def gain_copy(k):
            to = (c + k) % s.count
            return remote(
                n.gains.at[to],
                n.gains_got.at[k],
                n.gain_sems.at[0, k],
                n.gain_sems.at[1, k],
                (to, t),
            )

        for k in range(1, s.count):
            gain_copy(k).start()
        for layer in range(layers):
            n.qk_total[layer] = n.acc[len(rounds), 2 * layer : 2 * layer + 2]
        total = n.gains[c]
        for k in range(1, s.count):
            gain_copy(k).wait_recv()
            total = total + n.gains_got[k]
        n.attn_total[...] = total[:layers]
        n.ffn_total[...] = total[layers : 2 * layers]
        for k in range(1, s.count):
            gain_copy(k).wait_send()
        for k in range(len(rounds)):
            head_copy(k).wait_send()
        scatter.finish()

        def finish(u):
            upper.finish(u)
            stores.finish(u)

        each_of(s.units, finish)

    held = dict(
        a1=bottom.a1,
        a2=bottom.a2,
        o=bottom.o,
        hidden=bottom.hidden,
        dyb=bottom.dyb,
        dgate=bottom.dgate,
        dup=bottom.dup,
        dhb=bottom.dhb,
    )
    small = (len(rounds) + 1, 2 * layers + -2 * layers % 8, HEAD_SIZE)
    slabs = (s.count, 2 * layers + -2 * layers % 8, width)
    return run_kernel(
        body,
        head_ins(bottom, w)
        | {x: (array, ANY) for x, array in held.items()}
        | dict(
            qk_in=[(k.qk_sum, VMEM) for k in kept],
            attn_in=[(k.attn_sum, VMEM) for k in kept[1:]],
            ffn_in=[(k.ffn_sum, VMEM) for k in kept],
            done=[(array, ANY) for k in kept[1:] for array in k.sums],
        ),
        dict(
            dres=(shaped(s.rows, s.model, kind=F32), ANY),
            attn_total=(shaped(layers, width, kind=F32), VMEM),
            ffn_total=(shaped(layers, width, kind=F32), VMEM),
            qk_total=(shaped(layers, 2, HEAD_SIZE, kind=F32), VMEM),
            sums=[(shaped(layers, *size, kind=F32), ANY) for size in sizes],
        ),
        head_scratch(bottom, s)
        | {x + "_v": VMEM(array.shape, array.dtype) for x, array in held.items()}
        | scatter_scratch(s, sizes, True, layers)
        | dict(
            attn_sum=VMEM((1, s.model), F32),
            acc=VMEM(small, F32),
            other=VMEM(small, F32),
            gains=VMEM(slabs, F32),
            gains_got=VMEM(slabs, F32),
            small_sems=DMA((2, len(rounds))),
            gain_sems=DMA((2, s.count)),
        ),
        19,
    )


def deliver(results):
    pieces = [piece for result in results for piece in result]
    spots = [
        (index, sum(other.shape[0] for other in result[:k]), result[k].shape[0])
        for index, result in enumerate(results)
        for k in range(len(result))
    ]

    def body(n):
        copies = []
        for k, (index, first, rows) in enumerate(spots):
            target = n.result[index].at[pl.ds(first, rows)]
            copies.append(
                (
                    pltpu.make_async_copy(n.given[k], n.held[k], n.sems.at[0, k]),
                    pltpu.make_async_copy(n.held[k], target, n.sems.at[1, k]),
                )
            )
            copies[-1][0].start()
        for fetch, put in copies:
            fetch.wait()
            put.start()
        for fetch, put in copies:
            put.wait()

    shapes = [
        (sum(piece.shape[0] for piece in result),) + result[0].shape[1:] for result in results
    ]
    return run_kernel(
        body,
        dict(given=[(piece, ANY) for piece in pieces]),
        dict(
            result=[
                (shaped(*shape, kind=result[0].dtype), ANY)
                for shape, result in zip(shapes, results)
            ]
        ),
        dict(
            held=[VMEM(piece.shape, piece.dtype) for piece in pieces],
            sems=DMA((2, len(pieces))),
        ),
        None,
    ).result


OUTPUT_AT = 17
REST_AT = 19
REST_WIDES = 2
REST_HOP = 3
SCATTER_MIDDLE = (0, 3, 9, 16)
SCATTER_EVERY = 1
SCATTER_END = (0, 2, 7, 11)


def body(hidden_in, doc_lengths, cotangent, attn_gain, ffn_gain, qk_gain, w_query, *others):
    key_weight, value_weight, w_out, w_gate, w_up, w_down = others
    w = types.SimpleNamespace(
        attn_gain=attn_gain,
        ffn_gain=ffn_gain,
        qk_gain=qk_gain,
        w_query=w_query,
        key_weight=key_weight,
        value_weight=value_weight,
        w_out=w_out,
        w_gate=w_gate,
        w_up=w_up,
        w_down=w_down,
    )
    rows, model = hidden_in.shape
    layers, unused, queries = w_query.shape
    keys = key_weight.shape[2]
    s = types.SimpleNamespace(
        rows=rows,
        model=model,
        queries=queries,
        keys=keys,
        hidden=w_gate.shape[2],
        units=rows // UNIT,
        groups=keys // HEAD_SIZE,
        repeat=queries // keys,
        count=lax.axis_size(CTX),
        line=lax.axis_size(TP),
    )
    tables = make_tables(doc_lengths, rows)

    kept = []
    stream = hidden_in
    saved = None
    for layer in range(layers):
        if layer < layers - 1:
            result = forward_layer(layer, stream, saved, w, tables, s)
        else:
            result = turn_layer(layer, stream, saved, cotangent, w, tables, s)
        if saved:
            own = dict(a1=saved.a1, qraw=saved.qraw, kraw=saved.kraw, q=saved.q, kv=saved.kv)
        else:
            own = dict(
                a1=result.own_a1,
                qraw=result.own_qraw,
                kraw=result.own_kraw,
                q=result.own_q,
                kv=result.own_kv,
            )
        kept.append(types.SimpleNamespace(**(dict(grads=None) | vars(result) | own | dict(x=stream))))
        stream = result.y
        saved = result
    streams = [stream]

    for layer in range(layers - 2, -1, -1):
        result = backward_layer(layer, kept, w, tables, s)
        if layer == layers - 2:
            streams.append(result.y)
        kept[layer + 1].attn_sum = result.attn_sum
        kept[layer + 1].sums = result.sums
        vars(kept[layer]).update(
            dyb=result.dyb,
            dgate=result.dgate,
            dup=result.dup,
            dhb=result.dhb,
            dq=result.dq,
            dk=result.dk,
            dv=result.dv,
            dres=result.dres,
            ffn_sum=result.ffn_sum,
            qk_sum=result.qk_sum,
        )
    end = backward_end(kept, w, s)
    small = [end.attn_total, end.ffn_total, end.qk_total]
    stream, grad, *gains, up, gate, query, down, out, key, value = deliver(
        [streams] + [[array] for array in [end.dres] + small + end.sums]
    )
    return (
        stream,
        grad,
        *gains,
        query,
        key,
        value,
        out,
        gate,
        up,
        down,
    )


def solution(mesh):
    by_rows = P(CTX, None)
    by_columns = P(None, None, TP)
    by_hidden = P(None, TP, None)
    grad_columns = P(None, CTX, TP)
    grad_rows = P(None, (TP, CTX), None)
    return jax.shard_map(
        body,
        mesh=mesh,
        in_specs=(by_rows, P(), by_rows, P(), P(), P())
        + (by_columns,) * 3
        + (by_hidden,)
        + (by_columns,) * 2
        + (by_hidden,),
        out_specs=(by_rows, by_rows, P(None, CTX), P(None, CTX), P())
        + (grad_columns,) * 3
        + (grad_rows,)
        + (grad_columns,) * 2
        + (grad_rows,),
        check_vma=False,
    )
```

```python
import types

import jax
import jax.numpy as jnp
from jax import lax
from jax.experimental import pallas as pl
from jax.experimental.pallas import tpu as pltpu
from jax.sharding import PartitionSpec as P

HEAD_SIZE = 128
ATTENTION_WINDOW = 1024
EPS = 1e-06
THETA = 1000000.0

UNIT = 64
WIDE = 128
KEY_BLOCK = 384
HOP = 2
ARRIVED = 3 * HOP + WIDE // UNIT - 1
CTX = "ctx"
TP = "tp"
MESH = pl.DeviceIdType.MESH
F32 = jnp.float32
BF16 = jnp.bfloat16
SCALE = HEAD_SIZE ** (-0.5)
EXP2_SCALE = SCALE * 1.4426950408889634
ANY = pl.ANY
VMEM = pltpu.VMEM
DMA = pltpu.SemaphoreType.DMA


def dot_nn(left, right):
    return jnp.dot(left, right, preferred_element_type=F32)


def dot_nt(left, right):
    return lax.dot_general(left, right, (((1,), (1,)), ((), ())), preferred_element_type=F32)


def dot_tn(left, right):
    return lax.dot_general(left, right, (((0,), (0,)), ((), ())), preferred_element_type=F32)


def rms_inverse(value_rows):
    return lax.rsqrt(jnp.mean(value_rows * value_rows, axis=-1, keepdims=True) + EPS)


def rotate(value_rows, cosine, sine):
    return value_rows * cosine + pltpu.roll(value_rows, HEAD_SIZE // 2, 1) * sine


def unrotate(grad, cosine, sine):
    return grad * cosine + pltpu.roll(grad * sine, HEAD_SIZE // 2, 1)


def norm_back(grad, unit, inverse, gain):
    scaled = grad * gain
    inner = jnp.mean(scaled * unit, axis=-1, keepdims=True)
    return inverse * (scaled - unit * inner)


def column_sum(value_rows):
    return jnp.sum(value_rows, axis=0, keepdims=True)


def rotation_frequencies():
    half = jnp.arange(HEAD_SIZE // 2, dtype=F32)
    freq = THETA ** (-(half * 2.0) / HEAD_SIZE)
    return jnp.concatenate([freq, freq])[None, :]


def fill_tables(n, i, rows):
    here = wide_rows(i)
    start = lax.axis_index(CTX) * rows
    shape = (WIDE, HEAD_SIZE)
    spot = start + i * WIDE + lax.broadcasted_iota(jnp.int32, shape, 0)
    begin, end = jnp.zeros(shape, jnp.int32), 0
    for doc in range(n.lengths.shape[0]):
        end = end + n.lengths[doc]
        begin = begin + jnp.where(spot >= end, n.lengths[doc], 0)
    angle = (spot - begin).astype(F32) * n.frequencies[...]
    lane = lax.broadcasted_iota(jnp.int32, shape, 1)
    n.cosine[here] = jnp.cos(angle)
    n.sine[here] = jnp.sin(angle) * jnp.where(lane < HEAD_SIZE // 2, -1.0, 1.0)
    lowest = jnp.maximum(begin, spot - (ATTENTION_WINDOW - 1)) - (start - ATTENTION_WINDOW)
    n.lowest[here] = lowest[:, :1]


def halo_plan(rows):
    reach = -(-ATTENTION_WINDOW // rows)
    plan = []
    for hop in range(1, reach + 1):
        need = min(rows, ATTENTION_WINDOW - (hop - 1) * rows)
        plan.append((hop, need, ATTENTION_WINDOW - (hop - 1) * rows - need))
    return plan


def unit_rows(u):
    return pl.ds(pl.multiple_of(u * UNIT, UNIT), UNIT)


def wide_rows(w):
    return pl.ds(pl.multiple_of(w * WIDE, WIDE), WIDE)


def subs(w):
    return [w * (WIDE // UNIT) + i for i in range(WIDE // UNIT)]


def shaped(*shape, kind=BF16):
    return jax.ShapeDtypeStruct(shape, kind)


def listed(value):
    return list(value) if isinstance(value, list) else [value]


def run_kernel(body, ins, outs, scratch, collective_id):
    groups = [ins, outs, scratch]
    flat = [[x for value in group.values() for x in listed(value)] for group in groups]

    def named(values, chosen):
        values = list(values)
        found = {}
        for group in chosen:
            for name, value in group.items():
                if isinstance(value, list):
                    found[name] = [values.pop(0) for unused in value]
                else:
                    found[name] = values.pop(0)
        return types.SimpleNamespace(**found)

    results = pl.pallas_call(
        lambda *refs: body(named(refs, groups)),
        out_shape=[shape for shape, unused in flat[1]],
        in_specs=[pl.BlockSpec(memory_space=space) for unused, space in flat[0]],
        out_specs=[pl.BlockSpec(memory_space=space) for unused, space in flat[1]],
        scratch_shapes=flat[2],
        compiler_params=pltpu.CompilerParams(
            collective_id=collective_id,
            has_side_effects=collective_id is not None,
            vmem_limit_bytes=62 * 2**20,
        ),
    )(*[array for array, unused in flat[0]])
    return named(results, [outs])


def place():
    return lax.axis_index(CTX), lax.axis_index(TP)


def remote(source, target, send, receive, device):
    return pltpu.make_async_remote_copy(
        src_ref=source,
        dst_ref=target,
        send_sem=send,
        recv_sem=receive,
        device_id=device,
        device_id_type=MESH,
    )


def greet(partners, meanwhile=lambda: None):
    barrier = pltpu.get_barrier_semaphore()
    total = 0
    for exists, device in partners:
        total = total + jnp.where(exists, 1, 0)

        @pl.when(exists)
        def _():
            pl.semaphore_signal(barrier, inc=1, device_id=device, device_id_type=MESH)

    meanwhile()
    pl.semaphore_wait(barrier, total)


def line_partners():
    c, t = place()
    outer = (t == 0) | (t == 3)
    return [
        (outer, (c, jnp.where(t == 0, 1, 2))),
        (jnp.logical_not(outer), (c, jnp.where(t == 1, 0, 3))),
        (jnp.logical_not(outer), (c, jnp.clip(3 - t, 1, 2))),
    ]


def halo_partners(rows, count):
    c, t = place()
    partners = []
    for hop, unused, unused_too in halo_plan(rows):
        partners.append((c + hop < count, (jnp.minimum(c + hop, count - 1), t)))
        partners.append((c >= hop, (jnp.maximum(c - hop, 0), t)))
    return partners


class LineSum:
    def __init__(self, refs):
        self.part, self.total, self.inner, self.sems = refs
        self.c, self.t = place()
        self.outer = (self.t == 0) | (self.t == 3)
        self.is_inner = jnp.logical_not(self.outer)

    def copy(self, source, target, u, send, receive, to):
        return remote(
            source.at[u],
            target.at[u],
            self.sems.at[send, u],
            self.sems.at[receive, u],
            (self.c, to),
        )

    def inwards(self, u):
        return self.copy(self.part, self.total, u, 0, 1, jnp.where(self.t < 2, 1, 2))

    def across(self, u):
        return self.copy(self.part, self.inner, u, 0, 2, jnp.clip(3 - self.t, 1, 2))

    def outwards(self, u):
        return self.copy(self.total, self.total, u, 3, 4, jnp.where(self.t < 2, 0, 3))

    def hold(self, w, value):
        for i, u in enumerate(subs(w)):
            self.part[u] = value[i * UNIT : (i + 1) * UNIT].astype(BF16)

    def send(self, u):
        @pl.when(self.outer)
        def _():
            self.inwards(u).start()

    def push(self, w, value):
        self.hold(w, value)
        for u in subs(w):
            self.send(u)

    def meet(self, u):
        @pl.when(self.is_inner)
        def _():
            self.inwards(u).wait_recv()
            self.part[u] = (self.part[u].astype(F32) + self.total[u].astype(F32)).astype(BF16)
            self.across(u).start()

    def spread(self, u):
        @pl.when(self.is_inner)
        def _():
            self.across(u).wait_recv()
            self.total[u] = (self.part[u].astype(F32) + self.inner[u].astype(F32)).astype(BF16)
            self.outwards(u).start()

    def take(self, u):
        @pl.when(self.outer)
        def _():
            self.outwards(u).wait_recv()

        return self.total[u].astype(F32)

    def take_wide(self, w):
        return jnp.concatenate([self.take(u) for u in subs(w)], axis=0)

    def finish(self, u):
        @pl.when(self.outer)
        def _():
            self.inwards(u).wait_send()

        @pl.when(self.is_inner)
        def _():
            self.across(u).wait_send()
            self.outwards(u).wait_send()

    def stages(self, begin, hop=HOP):
        number = self.part.shape[0]
        return [(begin + 2 * hop, self.spread, 1, number), (begin + hop, self.meet, 1, number)]


def line_scratch(units, width):
    block = VMEM((units, UNIT, width), BF16)
    return [block, block, block, DMA((5, units))]


def pipeline(units, stages, tasks=()):
    stages = [stage if len(stage) > 3 else stage + (units,) for stage in stages]
    steps = max(number + delay + 1 - taken for delay, unused, taken, number in stages)

    def step(s, carry):
        for delay, function, taken, number in stages:
            ready = (s >= delay) & (s < number + delay)
            if taken > 1:
                ready = ready & ((s - delay) % taken == 0)

            @pl.when(ready)
            def _():
                function((s - delay) // taken if taken > 1 else s - delay)

        for at, task in tasks:
            if at < steps:

                @pl.when(s == at)
                def _():
                    task()

        return carry

    lax.fori_loop(0, steps, step, 0)
    for at, task in tasks:
        if at >= steps:
            task()


def each_of(number, function):
    def step(u, carry):
        function(u)
        return carry

    lax.fori_loop(0, number, step, 0)


class Loads:
    def __init__(self, sems):
        self.sems, self.number = sems, 0

    def __call__(self, source, target):
        copy = pltpu.make_async_copy(source, target, self.sems.at[self.number])
        copy.start()
        self.number += 1
        return copy


def wait_all(*copies):
    for copy in copies:
        copy.wait()


class Stores:
    def __init__(self, sems):
        self.sems, self.copies = sems, []

    def __call__(self, source, target):
        index = len(self.copies)

        def copy(u):
            rows = unit_rows(u)
            return pltpu.make_async_copy(source.at[rows], target.at[rows], self.sems.at[index, u])

        self.copies.append(copy)
        return copy

    def finish(self, u):
        for copy in self.copies:
            copy(u).wait()


def send_out(units, *copies):
    for u in units:
        for copy in copies:
            copy(u).start()


class Halo:
    def __init__(self, keys, sems, rows, count):
        self.keys, self.sems, self.rows, self.count = keys, sems, rows, count
        self.plan = halo_plan(rows)
        self.c, self.t = place()

    def copy(self, index, u, hop, need, offset):
        target = pl.multiple_of(offset + u * UNIT - (self.rows - need), UNIT)
        return remote(
            self.keys.at[pl.ds(pl.multiple_of(ATTENTION_WINDOW + u * UNIT, UNIT), UNIT)],
            self.keys.at[pl.ds(target, UNIT)],
            self.sems.at[2 * index, u],
            self.sems.at[2 * index + 1, u],
            (jnp.minimum(self.c + hop, self.count - 1), self.t),
        )

    def each(self, u, function, receives):
        for index, (hop, need, offset) in enumerate(self.plan):
            exists = self.c >= hop if receives else self.c + hop < self.count

            @pl.when(exists & (u >= (self.rows - need) // UNIT))
            def _():
                function(self.copy(index, u, hop, need, offset))

    def blank(self):
        width = self.keys.shape[1]
        for hop, need, offset in self.plan:

            @pl.when(self.c < hop)
            def _():
                self.keys[offset : offset + need] = jnp.zeros((need, width), BF16)

    def send(self, u):
        self.each(u, lambda copy: copy.start(), False)

    def finish(self, u):
        self.each(u, lambda copy: copy.wait_recv(), True)
        self.each(u, lambda copy: copy.wait_send(), False)


def project_heads(n, raw, out, out_rows, rows, which, layer):
    cosine, sine = n.cosine[rows], n.sine[rows]
    gain = n.qk_gain[layer, which : which + 1]
    for head in range(raw.shape[1] // HEAD_SIZE):
        part = raw[:, head_cols(head)]
        part = part * rms_inverse(part) * gain
        out[out_rows, head_cols(head)] = rotate(part, cosine, sine).astype(BF16)


def project_keys(n, first, number, stream, layer):
    rows = pl.ds(pl.multiple_of(first, number), number)
    own = pl.ds(pl.multiple_of(ATTENTION_WINDOW + first, number), number)
    normed = (stream * rms_inverse(stream) * n.attn_gain[layer : layer + 1]).astype(BF16)
    n.a1_v[rows] = normed
    key = dot_nn(normed, n.wk_v[...])
    n.kraw_v[rows] = key
    n.kv_v[own, key.shape[1] :] = dot_nn(normed, n.wv_v[...]).astype(BF16)
    project_heads(n, key, n.kv_v, own, rows, 1, layer)


def project_queries(n, first, number, layer):
    rows = pl.ds(pl.multiple_of(first, number), number)
    query = dot_nn(n.a1_v[rows], n.wq_v[...])
    n.qraw_v[rows] = query
    project_heads(n, query, n.q_v, rows, rows, 0, layer)


def project_shapes(s):
    return dict(
        a1=((s.rows, s.model), BF16),
        qraw=((s.rows, s.queries), F32),
        kraw=((s.rows, s.keys), F32),
        q=((s.rows, s.queries), BF16),
        kv=((ATTENTION_WINDOW + s.rows, 2 * s.keys), BF16),
    )


def outputs(shapes):
    return {x: (shaped(*shape, kind=kind), ANY) for x, (shape, kind) in shapes.items()}


def buffers(shapes):
    return {x + "_v": VMEM(shape, kind) for x, (shape, kind) in shapes.items()}


def project_ins(w, tables):
    turns = dict(cosine=(tables.cosine, VMEM), sine=(tables.sine, VMEM)) if tables else {}
    return turns | dict(
        attn_gain=(w.attn_gain, VMEM),
        qk_gain=(w.qk_gain, VMEM),
        wq=(w.w_query, ANY),
        wk=(w.key_weight, ANY),
        wv=(w.value_weight, ANY),
    )


def project_scratch(s):
    return buffers(project_shapes(s)) | dict(
        wq_v=VMEM((s.model, s.queries), BF16),
        wk_v=VMEM((s.model, s.keys), BF16),
        wv_v=VMEM((s.model, s.keys), BF16),
        halo_sems=DMA((2 * len(halo_plan(s.rows)), s.units)),
    )


def first_scratch(s):
    return dict(
        first_a1=VMEM((s.rows, s.model), BF16),
        first_qraw=VMEM((s.rows, s.queries), F32),
        first_kraw=VMEM((s.rows, s.keys), F32),
        first_wq=VMEM((s.model, s.queries), BF16),
        first_wk=VMEM((s.model, s.keys), BF16),
        first_wv=VMEM((s.model, s.keys), BF16),
        first_sems=DMA((2 * len(halo_plan(s.rows)), s.units)),
    )


def first_outs(s):
    return outputs({"own_" + x: shape for x, shape in project_shapes(s).items()}) | dict(
        cosine=(shaped(s.rows, HEAD_SIZE, kind=F32), VMEM),
        sine=(shaped(s.rows, HEAD_SIZE, kind=F32), VMEM),
        lowest=(shaped(s.rows, 1, kind=jnp.int32), VMEM),
    )


def first_view(n):
    return types.SimpleNamespace(
        attn_gain=n.attn_gain,
        qk_gain=n.qk_gain,
        cosine=n.cosine,
        sine=n.sine,
        a1_v=n.first_a1,
        qraw_v=n.first_qraw,
        kraw_v=n.first_kraw,
        q_v=n.qin_v,
        kv_v=n.kvin_v,
        wq_v=n.first_wq,
        wk_v=n.first_wk,
        wv_v=n.first_wv,
    )


def key_block(i, block):
    return pl.ds(pl.multiple_of(i * WIDE + block * KEY_BLOCK, HEAD_SIZE), KEY_BLOCK)


def visible(i, lowest, block, repeat):
    shape = (WIDE, KEY_BLOCK)
    col = block * KEY_BLOCK + lax.broadcasted_iota(jnp.int32, shape, 1)
    seen = col >= lowest - i * WIDE
    if (block + 1) * KEY_BLOCK > ATTENTION_WINDOW:
        row = ATTENTION_WINDOW + lax.broadcasted_iota(jnp.int32, shape, 0)
        seen = seen & (col <= row)
    keep = jnp.where(seen, 1.0, 0.0)
    return jnp.concatenate([keep] * repeat, axis=0)


def key_blocks():
    return (ATTENTION_WINDOW + WIDE) // KEY_BLOCK


def stacked(value, group, repeat):
    first = group * repeat
    return jnp.concatenate(
        [value[:, (first + r) * HEAD_SIZE : (first + r + 1) * HEAD_SIZE] for r in range(repeat)],
        axis=0,
    )


def head_cols(index):
    return slice(index * HEAD_SIZE, (index + 1) * HEAD_SIZE)


def attend(n, i, s):
    rows = wide_rows(i)
    lowest = n.lowest[rows]
    lane = lax.broadcasted_iota(jnp.int32, (WIDE, HEAD_SIZE), 1)
    query_rows = n.qin_v[rows]
    queries = [stacked(query_rows, g, s.repeat) for g in range(s.groups)]
    mixed = [jnp.zeros((s.repeat * WIDE, HEAD_SIZE), F32) for unused in queries]
    total = [jnp.zeros((s.repeat * WIDE, 1), F32) for unused in queries]
    for block in range(key_blocks()):
        keys = key_block(i, block)
        keep = visible(i, lowest, block, s.repeat)
        for g in range(s.groups):
            scores = dot_nt(queries[g], n.kvin_v[keys, head_cols(g)])
            weights = jnp.exp2(scores * EXP2_SCALE) * keep
            total[g] = total[g] + jnp.sum(weights, axis=-1, keepdims=True)
            values = n.kvin_v[keys, head_cols(s.groups + g)]
            mixed[g] = mixed[g] + dot_nn(weights.astype(BF16), values)
    inverses = jnp.zeros((WIDE, HEAD_SIZE), F32)
    for g in range(s.groups):
        inverse = 1.0 / total[g]
        result = (mixed[g] * inverse).astype(BF16)
        for r in range(s.repeat):
            head = g * s.repeat + r
            part = slice(r * WIDE, (r + 1) * WIDE)
            n.o_v[rows, head_cols(head)] = result[part]
            inverses = jnp.where(lane == head, inverse[part], inverses)
    n.inv_v[rows] = inverses


def attend_back(n, i, grad_out, keys_ref, query_ref, s, first_done):
    rows = wide_rows(i)
    lowest = n.lowest[rows]
    query_rows, mixed_rows, inverses = query_ref[rows], n.o_v[rows], n.inv_v[rows]
    queries, grads, inners, scales, found = [], [], [], [], []
    for g in range(s.groups):
        queries.append(stacked(query_rows, g, s.repeat))
        grads.append(stacked(grad_out, g, s.repeat))
        mixed = stacked(mixed_rows, g, s.repeat)
        inners.append(
            jnp.sum(grads[g].astype(F32) * mixed.astype(F32), axis=-1, keepdims=True)
        )
        heads = [g * s.repeat + r for r in range(s.repeat)]
        scales.append(jnp.concatenate([inverses[:, h : h + 1] for h in heads], axis=0))
        found.append(jnp.zeros((s.repeat * WIDE, HEAD_SIZE), F32))
    for block in range(key_blocks()):
        keys = key_block(i, block)
        keep = visible(i, lowest, block, s.repeat)
        for g in range(s.groups):
            key_rows = keys_ref[keys, head_cols(g)]
            scores = dot_nt(queries[g], key_rows)
            probs = jnp.exp2(scores * EXP2_SCALE) * (keep * scales[g])
            grad_probs = dot_nt(grads[g], keys_ref[keys, head_cols(s.groups + g)])
            grad_scores = (probs * (grad_probs - inners[g])).astype(BF16)
            found[g] = found[g] + dot_nn(grad_scores, key_rows)
            n.dkv_v[keys, head_cols(g)] += dot_tn(grad_scores, queries[g])
            n.dkv_v[keys, head_cols(s.groups + g)] += dot_tn(probs.astype(BF16), grads[g])
        if block == 0:
            first_done()
    return [
        found[g][r * WIDE : (r + 1) * WIDE] for g in range(s.groups) for r in range(s.repeat)
    ]


def head_back(n, rows, grad, raw, which, layer):
    gain = n.qk_gain[layer, which : which + 1]
    turned = unrotate(grad, n.cosine[rows], n.sine[rows])
    inverse = rms_inverse(raw)
    unit = raw * inverse
    n.qk_sum[which : which + 1] += column_sum(turned * unit)
    return norm_back(turned, unit, inverse, gain).astype(BF16)


class Returns:
    def __init__(self, n, s):
        self.grads, self.low, self.back, self.sems = n.dkv_v, n.low_v, n.back_v, n.return_sems
        self.s, self.plan = s, halo_plan(s.rows)
        self.c, self.t = place()
        self.blocks = []
        for index, (hop, need, offset) in enumerate(self.plan):
            for b in range(need // WIDE):
                self.blocks.append((index, hop, offset + b * WIDE, b * WIDE))
        self.blocks.sort(key=lambda item: item[2])

    def copy(self, number):
        index, hop, source, target = self.blocks[number]
        return remote(
            self.low.at[pl.ds(source, WIDE)],
            self.back[index].at[pl.ds(target, WIDE)],
            self.sems.at[0, number],
            self.sems.at[1, number],
            (jnp.maximum(self.c - hop, 0), self.t),
        )

    def blank(self):
        for index, (hop, need, unused) in enumerate(self.plan):

            @pl.when(self.c + hop >= self.s.count)
            def _():
                self.back[index][...] = jnp.zeros((need, self.low.shape[1]), BF16)

    def send(self, number):
        rows = pl.ds(self.blocks[number][2], WIDE)

        @pl.when(self.c >= self.blocks[number][1])
        def _():
            self.low[rows] = self.grads[rows].astype(BF16)
            self.copy(number).start()

    def send_complete(self, i):
        for number, block in enumerate(self.blocks):
            if block[2] // WIDE < self.s.rows // WIDE - 1:

                @pl.when(i == block[2] // WIDE)
                def _():
                    self.send(number)

    def send_rest(self):
        for number, block in enumerate(self.blocks):
            if block[2] // WIDE >= self.s.rows // WIDE - 1:
                self.send(number)

    def receive(self):
        for number, block in enumerate(self.blocks):

            @pl.when(self.c + block[1] < self.s.count)
            def _():
                self.copy(number).wait_recv()

    def finish(self):
        for number, block in enumerate(self.blocks):

            @pl.when(self.c >= block[1])
            def _():
                self.copy(number).wait_send()


def attention_back_scratch(s):
    plan = halo_plan(s.rows)
    return dict(
        dkv_v=VMEM((ATTENTION_WINDOW + s.rows, 2 * s.keys), F32),
        low_v=VMEM((ATTENTION_WINDOW, 2 * s.keys), BF16),
        back_v=[VMEM((need, 2 * s.keys), BF16) for unused, need, unused_too in plan],
        total_v=VMEM((WIDE, 2 * s.keys), F32),
        return_sems=DMA((2, ATTENTION_WINDOW // WIDE)),
    )


def attention_back_shapes(s):
    return dict(
        dyb=((s.rows, s.model), BF16),
        dgate=((s.rows, s.hidden), BF16),
        dup=((s.rows, s.hidden), BF16),
        dhb=((s.rows, s.model), BF16),
        dq=((s.rows, s.queries), BF16),
        dk=((s.rows, s.keys), BF16),
        dv=((s.rows, s.keys), BF16),
    )


def attention_back_sums(s):
    return dict(
        dres=(shaped(s.rows, s.model, kind=F32), ANY),
        ffn_sum=(shaped(1, s.model, kind=F32), VMEM),
        qk_sum=(shaped(2, HEAD_SIZE, kind=F32), VMEM),
    )


def back_start(n, returns):
    returns.blank()
    n.dkv_v[...] = jnp.zeros_like(n.dkv_v)
    n.ffn_sum[...] = jnp.zeros_like(n.ffn_sum)
    n.qk_sum[...] = jnp.zeros_like(n.qk_sum)


def feed_back(n, i, gate, up, lower, made):
    here = wide_rows(i)
    low = n.g_v[here].astype(BF16)
    n.dyb_v[here] = low
    grad_hidden = dot_nt(low, n.wd_v[...])
    sigma = jax.nn.sigmoid(gate)
    dgate = (grad_hidden * up * (sigma * (1.0 + gate * (1.0 - sigma)))).astype(BF16)
    dup = (grad_hidden * gate * sigma).astype(BF16)
    n.dgate_v[here] = dgate
    n.dup_v[here] = dup
    lower.push(i, dot_nt(dgate, n.wg_v[...]) + dot_nt(dup, n.wu_v[...]))
    send_out(subs(i), *made)


def attention_back(n, i, middle, keys_ref, query_ref, layer, lower, returns, made, s):
    here = wide_rows(i)
    grad_in = lower.take_wide(i)
    inverse = rms_inverse(middle)
    unit = middle * inverse
    n.ffn_sum[...] += column_sum(grad_in * unit)
    total = n.g_v[here] + norm_back(grad_in, unit, inverse, n.ffn_gain[layer : layer + 1])
    n.g_v[here] = total
    low = total.astype(BF16)
    n.dhb_v[here] = low
    grad_out = dot_nt(low, n.wo_v[...]).astype(BF16)
    early = s.rows - WIDE + KEY_BLOCK >= ATTENTION_WINDOW
    send_rest = lambda: pl.when(i == s.rows // WIDE - 1)(returns.send_rest)
    pieces = attend_back(
        n, i, grad_out, keys_ref, query_ref, s, send_rest if early else lambda: None
    )
    returns.send_complete(i)
    if not early:
        send_rest()
    for head, piece in enumerate(pieces):
        n.dq_v[here, head_cols(head)] = head_back(
            n, here, piece * SCALE, n.qraw_v[here, head_cols(head)], 0, layer
        )
    send_out(subs(i), *made)


def keys_back(n, layer, returns, made, s):
    def each(i):
        here = wide_rows(i)
        own = pl.ds(pl.multiple_of(ATTENTION_WINDOW + i * WIDE, WIDE), WIDE)
        n.total_v[...] = n.dkv_v[own]
        for index, (hop, need, unused) in enumerate(returns.plan):
            skipped = s.rows - need

            @pl.when(i >= skipped // WIDE)
            def _():
                part = pl.ds(pl.multiple_of(i * WIDE - skipped, WIDE), WIDE)
                n.total_v[...] += n.back_v[index][part].astype(F32)

        for g in range(s.groups):
            n.dk_v[here, head_cols(g)] = head_back(
                n, here, n.total_v[:, head_cols(g)] * SCALE, n.kraw_v[here, head_cols(g)], 1, layer
            )
        n.dv_v[here] = n.total_v[:, s.keys :].astype(BF16)
        send_out(subs(i), *made)

    each_of(s.rows // WIDE, each)


def feed(n, i, middle, layer):
    here = wide_rows(i)
    normed = (middle * rms_inverse(middle) * n.ffn_gain[layer : layer + 1]).astype(BF16)
    n.a2_v[here] = normed
    gate = dot_nn(normed, n.wg_v[...])
    up = dot_nn(normed, n.wu_v[...])
    inside = (gate * jax.nn.sigmoid(gate) * up).astype(BF16)
    n.hidden_v[here] = inside
    return gate, up, dot_nn(inside, n.wd_v[...])


def layer_ins(stream, saved, w, tables):
    before = {}
    if saved:
        before = dict(
            qin=(saved.q, ANY), kvin=(saved.kv, ANY), lowest=(tables.lowest, VMEM)
        )
    return before | dict(
        x=(stream, ANY),
        ffn_gain=(w.ffn_gain, VMEM),
        wo=(w.w_out, ANY),
        wg=(w.w_gate, ANY),
        wu=(w.w_up, ANY),
        wd=(w.w_down, ANY),
    )


def weight_scratch(s):
    return dict(
        wo_v=VMEM((s.queries, s.model), BF16),
        wg_v=VMEM((s.model, s.hidden), BF16),
        wu_v=VMEM((s.model, s.hidden), BF16),
        wd_v=VMEM((s.hidden, s.model), BF16),
    )


def layer_scratch(stream, s, stores):
    return weight_scratch(s) | dict(
        x_v=VMEM((s.rows, s.model), stream.dtype),
        qin_v=VMEM((s.rows, s.queries), BF16),
        kvin_v=VMEM((ATTENTION_WINDOW + s.rows, 2 * s.keys), BF16),
        load_sems=DMA((20,)),
        store_sems=DMA((stores, s.units)),
        first=line_scratch(s.units, s.model),
        second=line_scratch(s.units, s.model),
    )


def layer_loads(n, loads, layer, projected):
    if projected:
        early = (loads(n.qin, n.qin_v), loads(n.kvin, n.kvin_v))
    else:
        early = (loads(n.x, n.x_v),)
    early += (loads(n.wo.at[layer], n.wo_v),)
    late = () if not projected else (loads(n.x, n.x_v),)
    late += (
        loads(n.wg.at[layer], n.wg_v),
        loads(n.wu.at[layer], n.wu_v),
        loads(n.wd.at[layer], n.wd_v),
    )
    return early, late


def kept_shapes(s):
    return dict(
        o=((s.rows, s.queries), BF16),
        a2=((s.rows, s.model), BF16),
        hidden=((s.rows, s.hidden), BF16),
    )


def forward_shapes(s):
    return kept_shapes(s) | dict(
        inv=((s.rows, HEAD_SIZE), F32),
        h=((s.rows, s.model), F32),
        gate=((s.rows, s.hidden), BF16),
        up=((s.rows, s.hidden), BF16),
        y=((s.rows, s.model), F32),
    )


def forward_layer(layer, stream, saved, w, tables, s, lengths):
    def body(n):
        loads = Loads(n.load_sems)
        if not saved:
            own_weights = (
                loads(n.wk.at[layer], n.first_wk),
                loads(n.wv.at[layer], n.first_wv),
                loads(n.wq.at[layer], n.first_wq),
            )
        early, late = layer_loads(n, loads, layer, saved is not None)
        above = (
            loads(n.wq.at[layer + 1], n.wq_v),
            loads(n.wk.at[layer + 1], n.wk_v),
            loads(n.wv.at[layer + 1], n.wv_v),
        )
        stores = Stores(n.store_sems)
        mixed = (stores(n.o_v, n.o), stores(n.inv_v, n.inv))
        fed = (
            stores(n.h_v, n.h),
            stores(n.a2_v, n.a2),
            stores(n.hidden_v, n.hidden),
            stores(n.gate_v, n.gate),
            stores(n.up_v, n.up),
        )
        closed = (
            stores(n.y_v, n.y),
            stores(n.a1_v, n.a1),
            stores(n.qraw_v, n.qraw),
            stores(n.kraw_v, n.kraw),
            stores(n.q_v, n.q),
        )
        first, second = LineSum(n.first), LineSum(n.second)
        halo = Halo(n.kv_v, n.halo_sems, s.rows, s.count)

        def meanwhile():
            halo.blank()
            if not saved:
                each_of(s.rows // WIDE, lambda i: fill_tables(n, i, s.rows))

        greet(line_partners() + halo_partners(s.rows, s.count), meanwhile)
        wait_all(*early)
        if not saved:
            wait_all(*own_weights)
            own = first_view(n)
            own_halo = Halo(n.kvin_v, n.first_sems, s.rows, s.count)
            own_halo.blank()

            def own_keys(i):
                project_keys(own, i * WIDE, WIDE, n.x_v[wide_rows(i)].astype(F32), layer)
                for u in subs(i):
                    own_halo.send(u)

            def own_queries(i):
                project_queries(own, i * WIDE, WIDE, layer)

            each_of(s.rows // WIDE, own_keys)
            each_of(s.rows // WIDE, own_queries)
            each_of(s.units, own_halo.finish)
            own_out = (
                loads(n.kvin_v, n.own_kv),
                loads(n.first_a1, n.own_a1),
                loads(n.first_qraw, n.own_qraw),
                loads(n.first_kraw, n.own_kraw),
                loads(n.qin_v, n.own_q),
            )

        def mix(i):
            attend(n, i, s)
            first.push(i, dot_nn(n.o_v[wide_rows(i)], n.wo_v[...]))
            send_out(subs(i), *mixed)

        def feed_wide(i):
            pl.when(i == 0)(lambda: wait_all(*late))
            here = wide_rows(i)
            middle = n.x_v[here].astype(F32) + first.take_wide(i)
            n.h_v[here] = middle
            gate, up, part = feed(n, i, middle, layer)
            second.push(i, part)
            n.gate_v[here] = gate.astype(BF16)
            n.up_v[here] = up.astype(BF16)
            send_out(subs(i), *fed)

        def close(u):
            pl.when(u == 0)(lambda: wait_all(*above))
            here = unit_rows(u)
            result = n.h_v[here] + second.take(u)
            n.y_v[here] = result
            project_keys(n, u * UNIT, UNIT, result, layer + 1)
            halo.send(u)
            project_queries(n, u * UNIT, UNIT, layer + 1)
            send_out([u], *closed)

        at = ARRIVED
        pipeline(
            s.units,
            second.stages(at)
            + first.stages(0)
            + [(at + 3 * HOP, close, 1), (at, feed_wide, WIDE // UNIT), (0, mix, WIDE // UNIT)],
        )
        each_of(s.units, halo.finish)
        keys = loads(n.kv_v, n.kv)

        def finish(u):
            first.finish(u)
            second.finish(u)
            stores.finish(u)

        each_of(s.units, finish)
        keys.wait()
        if not saved:
            wait_all(*own_out)

    return run_kernel(
        body,
        layer_ins(stream, saved, w, tables)
        | project_ins(w, tables)
        | (
            {}
            if saved
            else dict(
                lengths=(lengths, pltpu.SMEM),
                frequencies=(rotation_frequencies(), VMEM),
            )
        ),
        outputs(forward_shapes(s))
        | outputs(project_shapes(s))
        | ({} if saved else first_outs(s)),
        layer_scratch(stream, s, 12)
        | buffers(forward_shapes(s))
        | project_scratch(s)
        | ({} if saved else first_scratch(s)),
        2 + layer,
    )


def units_at_turn(s):
    return s.units - min(REST_WIDES, s.rows // WIDE // 2) * (WIDE // UNIT)


def turn_layer(layer, stream, saved, cotangent, w, tables, s):
    def body(n):
        loads = Loads(n.load_sems)
        early, late = layer_loads(n, loads, layer, True)
        late = late + (loads(n.grad, n.grad_v),)
        raws = (loads(n.qraw, n.qraw_v), loads(n.kraw, n.kraw_v))
        a1 = loads(n.a1, n.a1_v)
        stores = Stores(n.store_sems)
        closed = Stores(n.y_sems)
        put_result = closed(n.y_v, n.y)
        turned = (stores(n.g_v, n.dres), stores(n.dq_v, n.dq))
        keyed = (stores(n.dk_v, n.dk), stores(n.dv_v, n.dv))
        first, second, lower = LineSum(n.first), LineSum(n.second), LineSum(n.lower)
        returns = Returns(n, s)
        greet(line_partners() + halo_partners(s.rows, s.count))
        wait_all(*early)

        def mix(i):
            attend(n, i, s)
            first.push(i, dot_nn(n.o_v[wide_rows(i)], n.wo_v[...]))

        def feed_both(i):
            pl.when(i == 0)(lambda: wait_all(*late))
            here = wide_rows(i)
            middle = n.x_v[here] + first.take_wide(i)
            n.x_v[here] = middle
            n.g_v[here] = n.grad_v[here].astype(F32)
            gate, up, part = feed(n, i, middle, layer)
            feed_back(n, i, gate, up, lower, ())

            @pl.when(i < here_units * UNIT // WIDE)
            def _():
                second.hold(i, part)

            @pl.when(i >= here_units * UNIT // WIDE)
            def _():
                for k, u in enumerate(subs(i)):
                    n.rest_v[u - here_units] = part[k * UNIT : (k + 1) * UNIT].astype(BF16)

        def close(u):
            here = unit_rows(u)
            n.y_v[here] = (n.x_v[here] + second.take(u)).astype(BF16)
            send_out([u], put_result)

        rest_rows = pl.ds(here_units * UNIT, s.rows - here_units * UNIT)
        rest = (
            pltpu.make_async_copy(n.rest_v, n.rest, n.rest_sems.at[0]),
            pltpu.make_async_copy(n.x_v.at[rest_rows], n.rest_h, n.rest_sems.at[1]),
        )

        def put_rest():
            for copy in rest:
                copy.start()

        def attention(i):
            pl.when(i == 0)(lambda: wait_all(*raws))
            middle = n.x_v[wide_rows(i)]
            attention_back(
                n, i, middle, n.kvin_v, n.qin_v, layer, lower, returns, turned, s
            )

        at = ARRIVED
        def gradient(index):
            left, right = factors[index]
            block_products(n.grads_v[index], left, right, sizes[index][0], s)
            gradient_store(index).start()

        def gradient_store(index):
            return pltpu.make_async_copy(n.grads_v[index], n.grads[index], n.grad_sems.at[index])

        def end_keys():
            returns.receive()
            keys_back(n, layer, returns, keyed, s)
            a1.wait()

        factors = [
            (n.a2_v, n.dup_v),
            (n.a2_v, n.dgate_v),
            (n.a1_v, n.dq_v),
            (n.hidden_v, n.dyb_v),
            (n.o_v, n.dhb_v),
            (n.a1_v, n.dk_v),
            (n.a1_v, n.dv_v),
        ]
        after = at + ARRIVED + s.units
        tasks = [(1, lambda: back_start(n, returns)), (at + s.units, put_rest), (after + 4, end_keys)]
        for index, step in enumerate((1, 2, 5, 3, 4, 6, 6)):
            tasks.append((after + step, lambda index=index: gradient(index)))
        tasks.sort(key=lambda item: item[0])
        pipeline(
            s.units,
            lower.stages(at)
            + second.stages(OUTPUT_AT, HOP + 1)
            + first.stages(0)
            + [
                (OUTPUT_AT, second.send, 1, here_units),
                (OUTPUT_AT + 3 * HOP + 3, close, 1, here_units),
                (at + ARRIVED, attention, WIDE // UNIT),
                (at, feed_both, WIDE // UNIT),
                (0, mix, WIDE // UNIT),
            ],
            tasks,
        )
        returns.finish()
        for index in range(len(sizes)):
            gradient_store(index).wait()

        wait_all(*rest)

        def finish(u):
            first.finish(u)
            lower.finish(u)
            stores.finish(u)

        def finish_result(u):
            second.finish(u)
            closed.finish(u)

        each_of(s.units, finish)
        each_of(here_units, finish_result)

    sizes = grad_sizes(s)
    backs = attention_back_shapes(s)
    blocks = block_shapes(s, sizes)
    here_units = units_at_turn(s)
    rest_units = s.units - here_units
    return run_kernel(
        body,
        layer_ins(stream, saved, w, tables)
        | dict(
            grad=(cotangent, ANY),
            a1=(saved.a1, ANY),
            qraw=(saved.qraw, ANY),
            kraw=(saved.kraw, ANY),
            qk_gain=(w.qk_gain, VMEM),
            cosine=(tables.cosine, VMEM),
            sine=(tables.sine, VMEM),
        ),
        outputs({x: backs[x] for x in dict(dq=0, dk=0, dv=0)})
        | attention_back_sums(s)
        | dict(
            y=(shaped(here_units * UNIT, s.model), ANY),
            rest=(shaped(rest_units, UNIT, s.model), ANY),
            rest_h=(shaped(rest_units * UNIT, s.model, kind=F32), ANY),
            grads=[(shaped(*block), ANY) for block in blocks],
        ),
        layer_scratch(stream, s, 5)
        | buffers(kept_shapes(s))
        | buffers(backs)
        | attention_back_scratch(s)
        | dict(
            y_v=VMEM((here_units * UNIT, s.model), BF16),
            y_sems=DMA((1, here_units)),
            rest_v=VMEM((rest_units, UNIT, s.model), BF16),
            rest_sems=DMA((2,)),
            second=line_scratch(here_units, s.model),
            a1_v=VMEM((s.rows, s.model), BF16),
            grads_v=[VMEM(block, BF16) for block in blocks],
            grad_sems=DMA((len(sizes),)),
            inv_v=VMEM((s.rows, HEAD_SIZE), F32),
            grad_v=VMEM((s.rows, s.model), BF16),
            g_v=VMEM((s.rows, s.model), F32),
            qraw_v=VMEM((s.rows, s.queries), F32),
            kraw_v=VMEM((s.rows, s.keys), F32),
            lower=line_scratch(s.units, s.model),
        ),
        2 + layer,
    )


def halving_partners(count):
    c, t = place()
    return [(c >= 0, (c ^ (1 << b), t)) for b in range(count.bit_length() - 1)]


def block_products(target, left, right, line, s):
    bits = s.count.bit_length() - 1
    half = s.count // 2
    for part in range(2):
        product = dot_tn(left[:, part * half * line : (part + 1) * half * line], right[...])
        for k in range(half):
            block = part * half + k
            at = tuple((block >> b) & 1 for b in range(bits - 1, -1, -1))
            target[at + (slice(0, line),)] = product[k * line : (k + 1) * line].astype(BF16)


def block_shapes(s, sizes):
    bits = s.count.bit_length() - 1
    return [(2,) * bits + (line + -line % 16, width) for line, width in sizes]


class Scatter:
    def __init__(self, n, s, sizes, factors=None):
        self.n, self.s, self.sizes, self.factors = n, s, sizes, factors
        self.bits = s.count.bit_length() - 1
        self.c, self.t = place()
        self.beside = []

    def bit(self, b):
        return (self.c >> b) & 1

    def order(self, index):
        rest = list(range(1, self.bits))
        return [0] + (rest if index % 2 == 0 else rest[::-1])

    def spot(self, picks):
        low = 0 if self.factors else 1
        return tuple(picks.get(b, slice(None)) for b in range(self.bits - 1, low - 1, -1))

    def own(self, index):
        return (self.n.whole_v if self.factors else self.n.own)[index]

    def copy(self, index, step):
        order = self.order(index)
        picks = {b: self.bit(b) for b in order[:step]}
        picks[order[step]] = 1 - self.bit(order[step])
        if step == 0 and not self.factors:
            source = self.n.whole[index].at[
                (slice(None),) * (self.bits - 1) + (1 - self.bit(0),)
            ]
        else:
            source = self.own(index).at[self.spot(picks)]
        sems = self.n.scatter_sems
        return remote(
            source,
            self.n.got[index * self.bits + step],
            sems.at[0, index, step],
            sems.at[1, index, step],
            (self.c ^ (1 << order[step]), self.t),
        )

    def load(self, index):
        return pltpu.make_async_copy(
            self.n.whole[index].at[(slice(None),) * (self.bits - 1) + (self.bit(0),)],
            self.n.own[index],
            self.n.scatter_load_sems.at[index],
        )

    def start(self, index):
        if self.factors:
            left, right, needed = self.factors[index]
            wait_all(*needed)
            block_products(self.own(index), left, right, self.sizes[index][0], self.s)
        else:
            self.load(index).start()
        self.copy(index, 0).start()

    def add(self, index, step):
        order = self.order(index)
        if step == 0 and not self.factors:
            self.load(index).wait()
        self.copy(index, step).wait_recv()
        free = [b for b in range(self.bits - 1, 0, -1) if b not in order[: step + 1]]
        own, got = self.own(index), self.n.got[index * self.bits + step]
        line = self.sizes[index][0]

        def one(k, carry):
            picks = {b: (k >> (len(free) - 1 - i)) & 1 for i, b in enumerate(free)}
            here = self.spot({b: self.bit(b) for b in order[: step + 1]} | picks)
            total = own[here].astype(F32) + got[tuple(picks[b] for b in free)].astype(F32)
            if step == self.bits - 1:
                self.sum_of(index)[...] = total[:line]
            else:
                own[here] = total.astype(BF16)
            return carry

        if free:
            lax.fori_loop(0, 1 << len(free), one, 0)
        else:
            one(0, 0)
        if step < self.bits - 1:
            self.copy(index, step + 1).start()
        else:
            for other in self.beside:
                other[index].wait()
            self.store(index).start()

    def sum_of(self, index):
        return self.n.sums_v[index].at[0] if self.factors else self.n.sums_v[index]

    def store(self, index):
        return pltpu.make_async_copy(
            self.n.sums_v[index], self.n.sums[index], self.n.scatter_store_sems.at[index]
        )

    def tasks(self, every, bases):
        found = []
        for index in range(len(self.sizes)):
            found.append((bases[0] + index * every, lambda index=index: self.start(index)))
            for step in range(self.bits):
                at = bases[min(step + 1, len(bases) - 1)] + index * every
                at += 100 * max(0, step + 2 - len(bases))
                found.append((at, lambda index=index, step=step: self.add(index, step)))
        found.sort(key=lambda item: item[0])
        return found

    def finish(self):
        for index in range(len(self.sizes)):
            self.store(index).wait()
            for step in range(self.bits):
                self.copy(index, step).wait_send()


def scatter_scratch(s, sizes, computed, layers):
    bits = s.count.bit_length() - 1
    tails = [(line + -line % 16, width) for line, width in sizes]
    found = dict(
        sums_v=[VMEM(((layers,) if computed else ()) + size, F32) for size in sizes],
        got=[
            VMEM((2,) * (bits - 1 - step) + tail, BF16) for tail in tails for step in range(bits)
        ],
        scatter_sems=DMA((2, len(sizes), bits)),
        scatter_load_sems=DMA((len(sizes),)),
        scatter_store_sems=DMA((len(sizes),)),
    )
    if computed:
        return found | dict(whole_v=[VMEM((2,) * bits + tail, BF16) for tail in tails])
    return found | dict(own=[VMEM((2,) * (bits - 1) + tail, BF16) for tail in tails])


def block_view(array, s):
    bits = s.count.bit_length() - 1
    line = array.shape[0] // s.count
    view = array.reshape((2,) * bits + (line, array.shape[1]))
    if line % 16:
        view = jnp.pad(view, [(0, 0)] * bits + [(0, -line % 16), (0, 0)])
    return view


def factor_pairs(k):
    return [
        (k.a2, k.dup),
        (k.a2, k.dgate),
        (k.a1, k.dq),
        (k.hidden, k.dyb),
        (k.o, k.dhb),
        (k.a1, k.dk),
        (k.a1, k.dv),
    ]


def grad_sizes(s):
    return [
        (s.model // s.count, s.hidden),
        (s.model // s.count, s.hidden),
        (s.model // s.count, s.queries),
        (s.hidden // s.count, s.model),
        (s.queries // s.count, s.model),
        (s.model // s.count, s.keys),
        (s.model // s.count, s.keys),
    ]


def head_ins(k, w):
    return dict(
        hq=(k.dq, ANY),
        hk=(k.dk, ANY),
        hv=(k.dv, ANY),
        wq=(w.w_query, ANY),
        wk=(w.key_weight, ANY),
        wv=(w.value_weight, ANY),
        x=(k.x, ANY),
        attn_gain=(w.attn_gain, VMEM),
        grad=(k.dres, ANY),
    )


def head_scratch(k, s):
    return dict(
        hq_v=VMEM((s.rows, s.queries), BF16),
        hk_v=VMEM((s.rows, s.keys), BF16),
        hv_v=VMEM((s.rows, s.keys), BF16),
        wq_v=VMEM((s.model, s.queries), BF16),
        wk_v=VMEM((s.model, s.keys), BF16),
        wv_v=VMEM((s.model, s.keys), BF16),
        x_v=VMEM((s.rows, s.model), k.x.dtype),
        g_v=VMEM((s.rows, s.model), F32),
        upper=line_scratch(s.units, s.model),
        load_sems=DMA((32,)),
        store_sems=DMA((10, s.units)),
    )


def head_loads(n, loads, layer):
    early = (
        loads(n.hq, n.hq_v),
        loads(n.wq.at[layer], n.wq_v),
        loads(n.hk, n.hk_v),
        loads(n.wk.at[layer], n.wk_v),
        loads(n.hv, n.hv_v),
        loads(n.wv.at[layer], n.wv_v),
    )
    return early, (loads(n.x, n.x_v), loads(n.grad, n.g_v))


def head_inputs(n, i, upper):
    here = wide_rows(i)
    upper.push(
        i,
        dot_nt(n.hq_v[here], n.wq_v[...])
        + dot_nt(n.hk_v[here], n.wk_v[...])
        + dot_nt(n.hv_v[here], n.wv_v[...]),
    )


def head_norm(n, here, grad_in, layer):
    stream = n.x_v[here].astype(F32)
    inverse = rms_inverse(stream)
    unit = stream * inverse
    n.attn_sum[...] += column_sum(grad_in * unit)
    n.g_v[here] += norm_back(grad_in, unit, inverse, n.attn_gain[layer : layer + 1])


def backward_layer(layer, kept, w, tables, s):
    above, here_kept = kept[layer + 1], kept[layer]
    sizes = grad_sizes(s)
    rest_units = s.units - units_at_turn(s) if layer + 2 == len(kept) else 0
    backs = attention_back_shapes(s)
    extra_ins, extra_outs, extra_scratch = {}, {}, {}
    if rest_units:
        extra_ins = dict(rest=(above.rest, ANY), rest_h=(above.rest_h, ANY))
        extra_outs = dict(y=(shaped(rest_units * UNIT, s.model), ANY))
        extra_scratch = dict(
            second=line_scratch(rest_units, s.model),
            y_sems=DMA((1, rest_units)),
            rest_sems=DMA((1,)),
        )

    def body(n):
        loads = Loads(n.load_sems)
        early, middle_loads = head_loads(n, loads, layer + 1)
        scatter = Scatter(n, s, sizes)
        n.dgate_v, n.dup_v = n.gate_v, n.up_v
        feeds = (
            loads(n.wd.at[layer], n.wd_v),
            loads(n.gate, n.gate_v),
            loads(n.up, n.up_v),
            loads(n.wg.at[layer], n.wg_v),
            loads(n.wu.at[layer], n.wu_v),
        )
        lates = (
            loads(n.wo.at[layer], n.wo_v),
            loads(n.q, n.q_v),
            loads(n.kv, n.kv_v),
            loads(n.o, n.o_v),
            loads(n.inv, n.inv_v),
            loads(n.qraw, n.qraw_v),
            loads(n.kraw, n.kraw_v),
        )
        stores = Stores(n.store_sems)
        fed_back = (stores(n.dyb_v, n.dyb), stores(n.dgate_v, n.dgate), stores(n.dup_v, n.dup))
        turned = (stores(n.g_v, n.dres), stores(n.dhb_v, n.dhb), stores(n.dq_v, n.dq))
        keyed = (stores(n.dk_v, n.dk), stores(n.dv_v, n.dv))
        upper, lower = LineSum(n.upper), LineSum(n.lower)
        returns = Returns(n, s)
        greet(line_partners() + halo_partners(s.rows, s.count) + halving_partners(s.count))
        n.attn_sum[...] = jnp.zeros_like(n.attn_sum)
        wait_all(*early)

        if rest_units:
            second = LineSum(n.second)
            rest = loads(n.rest, second.part)
            rest_h = pltpu.make_async_copy(
                n.rest_h, n.x_v.at[pl.ds(0, rest_units * UNIT)], n.rest_sems.at[0]
            )

            def result_copy(u):
                return pltpu.make_async_copy(
                    second.inner.at[u], n.y.at[unit_rows(u)], n.y_sems.at[0, u]
                )

            def send_result(u):
                pl.when(u == 0)(rest.wait)
                second.send(u)

            def close(u):
                pl.when(u == 0)(rest_h.wait)
                total = n.x_v[unit_rows(u)].astype(F32) + second.take(u)
                second.inner[u] = total.astype(BF16)
                result_copy(u).start()

        def middle_copy(i):
            rows = wide_rows(i)
            return pltpu.make_async_copy(n.h.at[rows], n.x_v.at[rows], n.middle_sems.at[i])

        def inputs(i):
            head_inputs(n, i, upper)

        def pass_norm(i):
            pl.when(i == 0)(lambda: wait_all(*middle_loads, *feeds))
            here = wide_rows(i)
            head_norm(n, here, upper.take_wide(i), layer + 1)
            middle_copy(i).start()
            gate, up = n.gate_v[here].astype(F32), n.up_v[here].astype(F32)
            feed_back(n, i, gate, up, lower, fed_back)

        def attention(i):
            pl.when(i == 0)(lambda: wait_all(*lates))
            middle_copy(i).wait()
            attention_back(
                n, i, n.x_v[wide_rows(i)], n.kv_v, n.q_v, layer, lower, returns, turned, s
            )

        at = ARRIVED
        after = at + ARRIVED + s.units

        def end_keys():
            returns.receive()
            keys_back(n, layer, returns, keyed, s)

        tasks = [(0, lambda: back_start(n, returns)), (after + 2, end_keys)]
        tasks += scatter.tasks(1, SCATTER_MIDDLE)
        stages = lower.stages(at) + upper.stages(0)
        if rest_units:
            passed = at + ARRIVED + -(-rest_units * UNIT // WIDE) * (WIDE // UNIT) - 1
            tasks.append((passed, rest_h.start))
            stages += second.stages(REST_AT, REST_HOP) + [
                (REST_AT, send_result, 1, rest_units),
                (max(REST_AT + 3 * REST_HOP, passed + 1), close, 1, rest_units),
            ]
        tasks.sort(key=lambda item: item[0])
        pipeline(
            s.units,
            stages
            + [
                (at + ARRIVED, attention, WIDE // UNIT),
                (at, pass_norm, WIDE // UNIT),
                (0, inputs, WIDE // UNIT),
            ],
            tasks,
        )
        returns.finish()
        scatter.finish()
        if rest_units:

            def finish_result(u):
                second.finish(u)
                result_copy(u).wait()

            each_of(rest_units, finish_result)

        def finish(u):
            upper.finish(u)
            lower.finish(u)
            stores.finish(u)

        each_of(s.units, finish)

    whole = above.grads or [
        block_view(dot_tn(left, right).astype(BF16), s) for left, right in factor_pairs(above)
    ]
    held = dict(
        gate=here_kept.gate,
        up=here_kept.up,
        q=here_kept.q,
        kv=here_kept.kv,
        o=here_kept.o,
        inv=here_kept.inv,
        qraw=here_kept.qraw,
        kraw=here_kept.kraw,
    )
    return run_kernel(
        body,
        head_ins(above, w)
        | {x: (array, ANY) for x, array in held.items()}
        | dict(
            h=(here_kept.h, ANY),
            wd=(w.w_down, ANY),
            wg=(w.w_gate, ANY),
            wu=(w.w_up, ANY),
            wo=(w.w_out, ANY),
            ffn_gain=(w.ffn_gain, VMEM),
            qk_gain=(w.qk_gain, VMEM),
            cosine=(tables.cosine, VMEM),
            sine=(tables.sine, VMEM),
            lowest=(tables.lowest, VMEM),
            whole=[(array, ANY) for array in whole],
        )
        | extra_ins,
        outputs(attention_back_shapes(s))
        | attention_back_sums(s)
        | dict(
            attn_sum=(shaped(1, s.model, kind=F32), VMEM),
            sums=[(shaped(*size, kind=F32), ANY) for size in sizes],
        )
        | extra_outs,
        head_scratch(above, s)
        | extra_scratch
        | weight_scratch(s)
        | {x + "_v": VMEM(array.shape, array.dtype) for x, array in held.items()}
        | buffers({x: b for x, b in backs.items() if x not in dict(dgate=0, dup=0)})
        | attention_back_scratch(s)
        | scatter_scratch(s, sizes, False, 1)
        | dict(
            lower=line_scratch(s.units, s.model),
            middle_sems=DMA((s.rows // WIDE,)),
        ),
        20 + layer,
    )


def backward_end(kept, w, s):
    bottom = kept[0]
    sizes = grad_sizes(s)
    layers = len(kept)
    width = s.model // s.count
    bits = s.count.bit_length() - 1
    tp_bits = s.line.bit_length() - 1
    rounds = [(1 << b, 0) for b in range(bits)] + [(0, 1 << b) for b in range(tp_bits)]

    def body(n):
        c, t = place()
        loads = Loads(n.load_sems)
        early, lates = head_loads(n, loads, 0)
        a2, dup, dgate = loads(n.a2, n.a2_v), loads(n.dup, n.dup_v), loads(n.dgate, n.dgate_v)
        a1, hidden, dyb = loads(n.a1, n.a1_v), loads(n.hidden, n.hidden_v), loads(n.dyb, n.dyb_v)
        o, dhb = loads(n.o, n.o_v), loads(n.dhb, n.dhb_v)
        factors = [
            (n.a2_v, n.dup_v, (a2, dup)),
            (n.a2_v, n.dgate_v, (dgate,)),
            (n.a1_v, n.hq_v, (a1,)),
            (n.hidden_v, n.dyb_v, (hidden, dyb)),
            (n.o_v, n.dhb_v, (o, dhb)),
            (n.a1_v, n.hk_v, ()),
            (n.a1_v, n.hv_v, ()),
        ]
        scatter = Scatter(n, s, sizes, factors)
        stores = Stores(n.store_sems)
        out = stores(n.g_v, n.dres)
        upper = LineSum(n.upper)
        others = [(c >= 0, ((c + k) % s.count, t)) for k in range(1, s.count)]
        lines = [(c >= 0, (c, t ^ (1 << b))) for b in range(tp_bits)]
        greet(line_partners() + halving_partners(s.count) + others + lines)
        n.attn_sum[...] = jnp.zeros_like(n.attn_sum)
        n.acc[...] = jnp.zeros_like(n.acc)
        n.gains[...] = jnp.zeros_like(n.gains)
        for layer in range(layers):
            n.acc[0, 2 * layer : 2 * layer + 2] = n.qk_in[layer][...]
        wait_all(*early)
        scatter.beside = [
            [
                loads(n.done[(layer - 1) * len(sizes) + index], n.sums_v[index].at[layer])
                for index in range(len(sizes))
            ]
            for layer in range(1, layers)
        ]

        def head_copy(k):
            return remote(
                n.acc.at[k],
                n.other.at[k],
                n.small_sems.at[0, k],
                n.small_sems.at[1, k],
                (c ^ rounds[k][0], t ^ rounds[k][1]),
            )

        def head_step(k):
            if k > 0:
                head_copy(k - 1).wait_recv()
                n.acc[k] = n.acc[k - 1] + n.other[k - 1]
            if k < len(rounds):
                head_copy(k).start()

        def pass_norm(u):
            pl.when(u == 0)(lambda: wait_all(*lates))
            head_norm(n, unit_rows(u), upper.take(u), 0)
            send_out([u], out)

        tasks = scatter.tasks(SCATTER_EVERY, SCATTER_END)
        tasks += [(2 * k + 1, lambda k=k: head_step(k)) for k in range(len(rounds) + 1)]
        tasks.sort(key=lambda item: item[0])
        pipeline(
            s.units,
            upper.stages(0)
            + [
                (3 * HOP, pass_norm, 1),
                (0, lambda i: head_inputs(n, i, upper), WIDE // UNIT),
            ],
            tasks,
        )
        gains = [n.attn_sum] + n.attn_in + n.ffn_in
        for d in range(s.count):
            for row, gain in enumerate(gains):
                n.gains[d, row : row + 1] = gain[:, d * width : (d + 1) * width]

        def gain_copy(k):
            to = (c + k) % s.count
            return remote(
                n.gains.at[to],
                n.gains_got.at[k],
                n.gain_sems.at[0, k],
                n.gain_sems.at[1, k],
                (to, t),
            )

        for k in range(1, s.count):
            gain_copy(k).start()
        for layer in range(layers):
            n.qk_total[layer] = n.acc[len(rounds), 2 * layer : 2 * layer + 2]
        total = n.gains[c]
        for k in range(1, s.count):
            gain_copy(k).wait_recv()
            total = total + n.gains_got[k]
        n.attn_total[...] = total[:layers]
        n.ffn_total[...] = total[layers : 2 * layers]
        for k in range(1, s.count):
            gain_copy(k).wait_send()
        for k in range(len(rounds)):
            head_copy(k).wait_send()
        scatter.finish()

        def finish(u):
            upper.finish(u)
            stores.finish(u)

        each_of(s.units, finish)

    held = dict(
        a1=bottom.a1,
        a2=bottom.a2,
        o=bottom.o,
        hidden=bottom.hidden,
        dyb=bottom.dyb,
        dgate=bottom.dgate,
        dup=bottom.dup,
        dhb=bottom.dhb,
    )
    small = (len(rounds) + 1, 2 * layers + -2 * layers % 8, HEAD_SIZE)
    slabs = (s.count, 2 * layers + -2 * layers % 8, width)
    return run_kernel(
        body,
        head_ins(bottom, w)
        | {x: (array, ANY) for x, array in held.items()}
        | dict(
            qk_in=[(k.qk_sum, VMEM) for k in kept],
            attn_in=[(k.attn_sum, VMEM) for k in kept[1:]],
            ffn_in=[(k.ffn_sum, VMEM) for k in kept],
            done=[(array, ANY) for k in kept[1:] for array in k.sums],
        ),
        dict(
            dres=(shaped(s.rows, s.model, kind=F32), ANY),
            attn_total=(shaped(layers, width, kind=F32), VMEM),
            ffn_total=(shaped(layers, width, kind=F32), VMEM),
            qk_total=(shaped(layers, 2, HEAD_SIZE, kind=F32), VMEM),
            sums=[(shaped(layers, *size, kind=F32), ANY) for size in sizes],
        ),
        head_scratch(bottom, s)
        | {x + "_v": VMEM(array.shape, array.dtype) for x, array in held.items()}
        | scatter_scratch(s, sizes, True, layers)
        | dict(
            attn_sum=VMEM((1, s.model), F32),
            acc=VMEM(small, F32),
            other=VMEM(small, F32),
            gains=VMEM(slabs, F32),
            gains_got=VMEM(slabs, F32),
            small_sems=DMA((2, len(rounds))),
            gain_sems=DMA((2, s.count)),
        ),
        19,
    )


def deliver(results):
    pieces = [piece for result in results for piece in result]
    spots = [
        (index, sum(other.shape[0] for other in result[:k]), result[k].shape[0])
        for index, result in enumerate(results)
        for k in range(len(result))
    ]

    def body(n):
        copies = []
        for k, (index, first, rows) in enumerate(spots):
            target = n.result[index].at[pl.ds(first, rows)]
            copies.append(
                (
                    pltpu.make_async_copy(n.given[k], n.held[k], n.sems.at[0, k]),
                    pltpu.make_async_copy(n.held[k], target, n.sems.at[1, k]),
                )
            )
            copies[-1][0].start()
        for fetch, put in copies:
            fetch.wait()
            put.start()
        for fetch, put in copies:
            put.wait()

    shapes = [
        (sum(piece.shape[0] for piece in result),) + result[0].shape[1:] for result in results
    ]
    return run_kernel(
        body,
        dict(given=[(piece, ANY) for piece in pieces]),
        dict(
            result=[
                (shaped(*shape, kind=result[0].dtype), ANY)
                for shape, result in zip(shapes, results)
            ]
        ),
        dict(
            held=[VMEM(piece.shape, piece.dtype) for piece in pieces],
            sems=DMA((2, len(pieces))),
        ),
        None,
    ).result


OUTPUT_AT = 17
REST_AT = 19
REST_WIDES = 2
REST_HOP = 3
SCATTER_MIDDLE = (0, 3, 9, 16)
SCATTER_EVERY = 1
SCATTER_END = (0, 2, 7, 11)


def body(hidden_in, doc_lengths, cotangent, attn_gain, ffn_gain, qk_gain, w_query, *others):
    key_weight, value_weight, w_out, w_gate, w_up, w_down = others
    w = types.SimpleNamespace(
        attn_gain=attn_gain,
        ffn_gain=ffn_gain,
        qk_gain=qk_gain,
        w_query=w_query,
        key_weight=key_weight,
        value_weight=value_weight,
        w_out=w_out,
        w_gate=w_gate,
        w_up=w_up,
        w_down=w_down,
    )
    rows, model = hidden_in.shape
    layers, unused, queries = w_query.shape
    keys = key_weight.shape[2]
    s = types.SimpleNamespace(
        rows=rows,
        model=model,
        queries=queries,
        keys=keys,
        hidden=w_gate.shape[2],
        units=rows // UNIT,
        groups=keys // HEAD_SIZE,
        repeat=queries // keys,
        count=lax.axis_size(CTX),
        line=lax.axis_size(TP),
    )
    tables = None

    kept = []
    stream = hidden_in
    saved = None
    for layer in range(layers):
        if layer < layers - 1:
            result = forward_layer(layer, stream, saved, w, tables, s, doc_lengths)
        else:
            result = turn_layer(layer, stream, saved, cotangent, w, tables, s)
        if saved:
            own = dict(a1=saved.a1, qraw=saved.qraw, kraw=saved.kraw, q=saved.q, kv=saved.kv)
        else:
            own = dict(
                a1=result.own_a1,
                qraw=result.own_qraw,
                kraw=result.own_kraw,
                q=result.own_q,
                kv=result.own_kv,
            )
            tables = types.SimpleNamespace(
                cosine=result.cosine, sine=result.sine, lowest=result.lowest
            )
        kept.append(types.SimpleNamespace(**(dict(grads=None) | vars(result) | own | dict(x=stream))))
        stream = result.y
        saved = result
    streams = [stream]

    for layer in range(layers - 2, -1, -1):
        result = backward_layer(layer, kept, w, tables, s)
        if layer == layers - 2:
            streams.append(result.y)
        kept[layer + 1].attn_sum = result.attn_sum
        kept[layer + 1].sums = result.sums
        vars(kept[layer]).update(
            dyb=result.dyb,
            dgate=result.dgate,
            dup=result.dup,
            dhb=result.dhb,
            dq=result.dq,
            dk=result.dk,
            dv=result.dv,
            dres=result.dres,
            ffn_sum=result.ffn_sum,
            qk_sum=result.qk_sum,
        )
    end = backward_end(kept, w, s)
    small = [end.attn_total, end.ffn_total, end.qk_total]
    stream, grad, *gains, up, gate, query, down, out, key, value = deliver(
        [streams] + [[array] for array in [end.dres] + small + end.sums]
    )
    return (
        stream,
        grad,
        *gains,
        query,
        key,
        value,
        out,
        gate,
        up,
        down,
    )


def solution(mesh):
    by_rows = P(CTX, None)
    by_columns = P(None, None, TP)
    by_hidden = P(None, TP, None)
    grad_columns = P(None, CTX, TP)
    grad_rows = P(None, (TP, CTX), None)
    return jax.shard_map(
        body,
        mesh=mesh,
        in_specs=(by_rows, P(), by_rows, P(), P(), P())
        + (by_columns,) * 3
        + (by_hidden,)
        + (by_columns,) * 2
        + (by_hidden,),
        out_specs=(by_rows, by_rows, P(None, CTX), P(None, CTX), P())
        + (grad_columns,) * 3
        + (grad_rows,)
        + (grad_columns,) * 2
        + (grad_rows,),
        check_vma=False,
    )
```

```python
import types

import jax
import jax.numpy as jnp
from jax import lax
from jax.experimental import pallas as pl
from jax.experimental.pallas import tpu as pltpu
from jax.sharding import PartitionSpec as P

HEAD_SIZE = 128
ATTENTION_WINDOW = 1024
EPS = 1e-06
THETA = 1000000.0

UNIT = 64
WIDE = 128
KEY_BLOCK = 384
HOP = 2
ARRIVED = 3 * HOP + WIDE // UNIT - 1
CTX = "ctx"
TP = "tp"
MESH = pl.DeviceIdType.MESH
F32 = jnp.float32
BF16 = jnp.bfloat16
SCALE = HEAD_SIZE ** (-0.5)
EXP2_SCALE = SCALE * 1.4426950408889634
ANY = pl.ANY
VMEM = pltpu.VMEM
DMA = pltpu.SemaphoreType.DMA


def dot_nn(left, right):
    return jnp.dot(left, right, preferred_element_type=F32)


def dot_nt(left, right):
    return lax.dot_general(left, right, (((1,), (1,)), ((), ())), preferred_element_type=F32)


def dot_tn(left, right):
    return lax.dot_general(left, right, (((0,), (0,)), ((), ())), preferred_element_type=F32)


def rms_inverse(value_rows):
    return lax.rsqrt(jnp.mean(value_rows * value_rows, axis=-1, keepdims=True) + EPS)


def rotate(value_rows, cosine, sine):
    return value_rows * cosine + pltpu.roll(value_rows, HEAD_SIZE // 2, 1) * sine


def unrotate(grad, cosine, sine):
    return grad * cosine + pltpu.roll(grad * sine, HEAD_SIZE // 2, 1)


def norm_back(grad, unit, inverse, gain):
    scaled = grad * gain
    inner = jnp.mean(scaled * unit, axis=-1, keepdims=True)
    return inverse * (scaled - unit * inner)


def column_sum(value_rows):
    return jnp.sum(value_rows, axis=0, keepdims=True)


def rotation_frequencies():
    half = jnp.arange(HEAD_SIZE // 2, dtype=F32)
    freq = THETA ** (-(half * 2.0) / HEAD_SIZE)
    return jnp.concatenate([freq, freq])[None, :]


def fill_tables(n, i, rows):
    here = wide_rows(i)
    start = lax.axis_index(CTX) * rows
    shape = (WIDE, HEAD_SIZE)
    spot = start + i * WIDE + lax.broadcasted_iota(jnp.int32, shape, 0)
    begin, end = jnp.zeros(shape, jnp.int32), 0
    for doc in range(n.lengths.shape[0]):
        end = end + n.lengths[doc]
        begin = begin + jnp.where(spot >= end, n.lengths[doc], 0)
    angle = (spot - begin).astype(F32) * n.frequencies[...]
    lane = lax.broadcasted_iota(jnp.int32, shape, 1)
    n.cosine[here] = jnp.cos(angle)
    n.sine[here] = jnp.sin(angle) * jnp.where(lane < HEAD_SIZE // 2, -1.0, 1.0)
    lowest = jnp.maximum(begin, spot - (ATTENTION_WINDOW - 1)) - (start - ATTENTION_WINDOW)
    n.lowest[here] = lowest[:, :1]


def halo_plan(rows):
    reach = -(-ATTENTION_WINDOW // rows)
    plan = []
    for hop in range(1, reach + 1):
        need = min(rows, ATTENTION_WINDOW - (hop - 1) * rows)
        plan.append((hop, need, ATTENTION_WINDOW - (hop - 1) * rows - need))
    return plan


def unit_rows(u):
    return pl.ds(pl.multiple_of(u * UNIT, UNIT), UNIT)


def wide_rows(w):
    return pl.ds(pl.multiple_of(w * WIDE, WIDE), WIDE)


def subs(w):
    return [w * (WIDE // UNIT) + i for i in range(WIDE // UNIT)]


def shaped(*shape, kind=BF16):
    return jax.ShapeDtypeStruct(shape, kind)


def listed(value):
    return list(value) if isinstance(value, list) else [value]


def run_kernel(body, ins, outs, scratch, collective_id):
    groups = [ins, outs, scratch]
    flat = [[x for value in group.values() for x in listed(value)] for group in groups]

    def named(values, chosen):
        values = list(values)
        found = {}
        for group in chosen:
            for name, value in group.items():
                if isinstance(value, list):
                    found[name] = [values.pop(0) for unused in value]
                else:
                    found[name] = values.pop(0)
        return types.SimpleNamespace(**found)

    results = pl.pallas_call(
        lambda *refs: body(named(refs, groups)),
        out_shape=[shape for shape, unused in flat[1]],
        in_specs=[pl.BlockSpec(memory_space=space) for unused, space in flat[0]],
        out_specs=[pl.BlockSpec(memory_space=space) for unused, space in flat[1]],
        scratch_shapes=flat[2],
        compiler_params=pltpu.CompilerParams(
            collective_id=collective_id,
            has_side_effects=collective_id is not None,
            vmem_limit_bytes=62 * 2**20,
        ),
    )(*[array for array, unused in flat[0]])
    return named(results, [outs])


def place():
    return lax.axis_index(CTX), lax.axis_index(TP)


def remote(source, target, send, receive, device):
    return pltpu.make_async_remote_copy(
        src_ref=source,
        dst_ref=target,
        send_sem=send,
        recv_sem=receive,
        device_id=device,
        device_id_type=MESH,
    )


def greet(partners, meanwhile=lambda: None):
    barrier = pltpu.get_barrier_semaphore()
    total = 0
    for exists, device in partners:
        total = total + jnp.where(exists, 1, 0)

        @pl.when(exists)
        def _():
            pl.semaphore_signal(barrier, inc=1, device_id=device, device_id_type=MESH)

    meanwhile()
    pl.semaphore_wait(barrier, total)


def line_partners():
    c, t = place()
    outer = (t == 0) | (t == 3)
    return [
        (outer, (c, jnp.where(t == 0, 1, 2))),
        (jnp.logical_not(outer), (c, jnp.where(t == 1, 0, 3))),
        (jnp.logical_not(outer), (c, jnp.clip(3 - t, 1, 2))),
    ]


def halo_partners(rows, count):
    c, t = place()
    partners = []
    for hop, unused, unused_too in halo_plan(rows):
        partners.append((c + hop < count, (jnp.minimum(c + hop, count - 1), t)))
        partners.append((c >= hop, (jnp.maximum(c - hop, 0), t)))
    return partners


class LineSum:
    def __init__(self, refs):
        self.part, self.total, self.inner, self.sems = refs
        self.c, self.t = place()
        self.outer = (self.t == 0) | (self.t == 3)
        self.is_inner = jnp.logical_not(self.outer)

    def copy(self, source, target, u, send, receive, to):
        return remote(
            source.at[u],
            target.at[u],
            self.sems.at[send, u],
            self.sems.at[receive, u],
            (self.c, to),
        )

    def inwards(self, u):
        return self.copy(self.part, self.total, u, 0, 1, jnp.where(self.t < 2, 1, 2))

    def across(self, u):
        return self.copy(self.part, self.inner, u, 0, 2, jnp.clip(3 - self.t, 1, 2))

    def outwards(self, u):
        return self.copy(self.total, self.total, u, 3, 4, jnp.where(self.t < 2, 0, 3))

    def hold(self, w, value):
        for i, u in enumerate(subs(w)):
            self.part[u] = value[i * UNIT : (i + 1) * UNIT].astype(BF16)

    def send(self, u):
        @pl.when(self.outer)
        def _():
            self.inwards(u).start()

    def push(self, w, value):
        self.hold(w, value)
        for u in subs(w):
            self.send(u)

    def meet(self, u):
        @pl.when(self.is_inner)
        def _():
            self.inwards(u).wait_recv()
            self.part[u] = (self.part[u].astype(F32) + self.total[u].astype(F32)).astype(BF16)
            self.across(u).start()

    def spread(self, u):
        @pl.when(self.is_inner)
        def _():
            self.across(u).wait_recv()
            self.total[u] = (self.part[u].astype(F32) + self.inner[u].astype(F32)).astype(BF16)
            self.outwards(u).start()

    def take(self, u):
        @pl.when(self.outer)
        def _():
            self.outwards(u).wait_recv()

        return self.total[u].astype(F32)

    def take_wide(self, w):
        return jnp.concatenate([self.take(u) for u in subs(w)], axis=0)

    def finish(self, u):
        @pl.when(self.outer)
        def _():
            self.inwards(u).wait_send()

        @pl.when(self.is_inner)
        def _():
            self.across(u).wait_send()
            self.outwards(u).wait_send()

    def stages(self, begin, hop=HOP):
        number = self.part.shape[0]
        return [(begin + 2 * hop, self.spread, 1, number), (begin + hop, self.meet, 1, number)]


def line_scratch(units, width):
    block = VMEM((units, UNIT, width), BF16)
    return [block, block, block, DMA((5, units))]


def pipeline(units, stages, tasks=()):
    stages = [stage if len(stage) > 3 else stage + (units,) for stage in stages]
    steps = max(number + delay + 1 - taken for delay, unused, taken, number in stages)

    def step(s, carry):
        for delay, function, taken, number in stages:
            ready = (s >= delay) & (s < number + delay)
            if taken > 1:
                ready = ready & ((s - delay) % taken == 0)

            @pl.when(ready)
            def _():
                function((s - delay) // taken if taken > 1 else s - delay)

        for at, task in tasks:
            if at < steps:

                @pl.when(s == at)
                def _():
                    task()

        return carry

    lax.fori_loop(0, steps, step, 0)
    for at, task in tasks:
        if at >= steps:
            task()


def each_of(number, function):
    def step(u, carry):
        function(u)
        return carry

    lax.fori_loop(0, number, step, 0)


class Loads:
    def __init__(self, sems):
        self.sems, self.number = sems, 0

    def __call__(self, source, target):
        copy = pltpu.make_async_copy(source, target, self.sems.at[self.number])
        copy.start()
        self.number += 1
        return copy


def wait_all(*copies):
    for copy in copies:
        copy.wait()


class Stores:
    def __init__(self, sems):
        self.sems, self.copies = sems, []

    def __call__(self, source, target):
        index = len(self.copies)

        def copy(u):
            rows = unit_rows(u)
            return pltpu.make_async_copy(source.at[rows], target.at[rows], self.sems.at[index, u])

        self.copies.append(copy)
        return copy

    def finish(self, u):
        for copy in self.copies:
            copy(u).wait()


def send_out(units, *copies):
    for u in units:
        for copy in copies:
            copy(u).start()


class Halo:
    def __init__(self, keys, sems, rows, count):
        self.keys, self.sems, self.rows, self.count = keys, sems, rows, count
        self.plan = halo_plan(rows)
        self.c, self.t = place()

    def copy(self, index, u, hop, need, offset):
        target = pl.multiple_of(offset + u * UNIT - (self.rows - need), UNIT)
        return remote(
            self.keys.at[pl.ds(pl.multiple_of(ATTENTION_WINDOW + u * UNIT, UNIT), UNIT)],
            self.keys.at[pl.ds(target, UNIT)],
            self.sems.at[2 * index, u],
            self.sems.at[2 * index + 1, u],
            (jnp.minimum(self.c + hop, self.count - 1), self.t),
        )

    def each(self, u, function, receives):
        for index, (hop, need, offset) in enumerate(self.plan):
            exists = self.c >= hop if receives else self.c + hop < self.count

            @pl.when(exists & (u >= (self.rows - need) // UNIT))
            def _():
                function(self.copy(index, u, hop, need, offset))

    def blank(self):
        width = self.keys.shape[1]
        for hop, need, offset in self.plan:

            @pl.when(self.c < hop)
            def _():
                self.keys[offset : offset + need] = jnp.zeros((need, width), BF16)

    def send(self, u):
        self.each(u, lambda copy: copy.start(), False)

    def finish(self, u):
        self.each(u, lambda copy: copy.wait_recv(), True)
        self.each(u, lambda copy: copy.wait_send(), False)


def project_heads(n, raw, out, out_rows, rows, which, layer):
    cosine, sine = n.cosine[rows], n.sine[rows]
    gain = n.qk_gain[layer, which : which + 1]
    for head in range(raw.shape[1] // HEAD_SIZE):
        part = raw[:, head_cols(head)]
        part = part * rms_inverse(part) * gain
        out[out_rows, head_cols(head)] = rotate(part, cosine, sine).astype(BF16)


def project_keys(n, first, number, stream, layer):
    rows = pl.ds(pl.multiple_of(first, number), number)
    own = pl.ds(pl.multiple_of(ATTENTION_WINDOW + first, number), number)
    normed = (stream * rms_inverse(stream) * n.attn_gain[layer : layer + 1]).astype(BF16)
    n.a1_v[rows] = normed
    key = dot_nn(normed, n.wk_v[...])
    n.kraw_v[rows] = key
    n.kv_v[own, key.shape[1] :] = dot_nn(normed, n.wv_v[...]).astype(BF16)
    project_heads(n, key, n.kv_v, own, rows, 1, layer)


def project_queries(n, first, number, layer):
    rows = pl.ds(pl.multiple_of(first, number), number)
    query = dot_nn(n.a1_v[rows], n.wq_v[...])
    n.qraw_v[rows] = query
    project_heads(n, query, n.q_v, rows, rows, 0, layer)


def project_shapes(s):
    return dict(
        a1=((s.rows, s.model), BF16),
        qraw=((s.rows, s.queries), F32),
        kraw=((s.rows, s.keys), F32),
        q=((s.rows, s.queries), BF16),
        kv=((ATTENTION_WINDOW + s.rows, 2 * s.keys), BF16),
    )


def outputs(shapes):
    return {x: (shaped(*shape, kind=kind), ANY) for x, (shape, kind) in shapes.items()}


def buffers(shapes):
    return {x + "_v": VMEM(shape, kind) for x, (shape, kind) in shapes.items()}


def project_ins(w, tables):
    turns = dict(cosine=(tables.cosine, VMEM), sine=(tables.sine, VMEM)) if tables else {}
    return turns | dict(
        attn_gain=(w.attn_gain, VMEM),
        qk_gain=(w.qk_gain, VMEM),
        wq=(w.w_query, ANY),
        wk=(w.key_weight, ANY),
        wv=(w.value_weight, ANY),
    )


def project_scratch(s):
    return buffers(project_shapes(s)) | dict(
        wq_v=VMEM((s.model, s.queries), BF16),
        wk_v=VMEM((s.model, s.keys), BF16),
        wv_v=VMEM((s.model, s.keys), BF16),
        halo_sems=DMA((2 * len(halo_plan(s.rows)), s.units)),
    )


def first_scratch(s):
    return dict(
        first_a1=VMEM((s.rows, s.model), BF16),
        first_qraw=VMEM((s.rows, s.queries), F32),
        first_kraw=VMEM((s.rows, s.keys), F32),
        first_wq=VMEM((s.model, s.queries), BF16),
        first_wk=VMEM((s.model, s.keys), BF16),
        first_wv=VMEM((s.model, s.keys), BF16),
        first_sems=DMA((2 * len(halo_plan(s.rows)), s.units)),
    )


def first_outs(s):
    return outputs({"own_" + x: shape for x, shape in project_shapes(s).items()}) | dict(
        cosine=(shaped(s.rows, HEAD_SIZE, kind=F32), VMEM),
        sine=(shaped(s.rows, HEAD_SIZE, kind=F32), VMEM),
        lowest=(shaped(s.rows, 1, kind=jnp.int32), VMEM),
    )


def first_view(n):
    return types.SimpleNamespace(
        attn_gain=n.attn_gain,
        qk_gain=n.qk_gain,
        cosine=n.cosine,
        sine=n.sine,
        a1_v=n.first_a1,
        qraw_v=n.first_qraw,
        kraw_v=n.first_kraw,
        q_v=n.qin_v,
        kv_v=n.kvin_v,
        wq_v=n.first_wq,
        wk_v=n.first_wk,
        wv_v=n.first_wv,
    )


def key_block(i, block):
    return pl.ds(pl.multiple_of(i * WIDE + block * KEY_BLOCK, HEAD_SIZE), KEY_BLOCK)


def visible(i, lowest, block, repeat):
    shape = (WIDE, KEY_BLOCK)
    col = block * KEY_BLOCK + lax.broadcasted_iota(jnp.int32, shape, 1)
    seen = col >= lowest - i * WIDE
    if (block + 1) * KEY_BLOCK > ATTENTION_WINDOW:
        row = ATTENTION_WINDOW + lax.broadcasted_iota(jnp.int32, shape, 0)
        seen = seen & (col <= row)
    keep = jnp.where(seen, 1.0, 0.0)
    return jnp.concatenate([keep] * repeat, axis=0)


def key_blocks():
    return (ATTENTION_WINDOW + WIDE) // KEY_BLOCK


def stacked(value, group, repeat):
    first = group * repeat
    return jnp.concatenate(
        [value[:, (first + r) * HEAD_SIZE : (first + r + 1) * HEAD_SIZE] for r in range(repeat)],
        axis=0,
    )


def head_cols(index):
    return slice(index * HEAD_SIZE, (index + 1) * HEAD_SIZE)


def attend(n, i, s):
    rows = wide_rows(i)
    lowest = n.lowest[rows]
    lane = lax.broadcasted_iota(jnp.int32, (WIDE, HEAD_SIZE), 1)
    query_rows = n.qin_v[rows]
    queries = [stacked(query_rows, g, s.repeat) for g in range(s.groups)]
    mixed = [jnp.zeros((s.repeat * WIDE, HEAD_SIZE), F32) for unused in queries]
    total = [jnp.zeros((s.repeat * WIDE, 1), F32) for unused in queries]
    for block in range(key_blocks()):
        keys = key_block(i, block)
        keep = visible(i, lowest, block, s.repeat)
        for g in range(s.groups):
            scores = dot_nt(queries[g], n.kvin_v[keys, head_cols(g)])
            weights = jnp.exp2(scores * EXP2_SCALE) * keep
            total[g] = total[g] + jnp.sum(weights, axis=-1, keepdims=True)
            values = n.kvin_v[keys, head_cols(s.groups + g)]
            mixed[g] = mixed[g] + dot_nn(weights.astype(BF16), values)
    inverses = jnp.zeros((WIDE, HEAD_SIZE), F32)
    for g in range(s.groups):
        inverse = 1.0 / total[g]
        result = (mixed[g] * inverse).astype(BF16)
        for r in range(s.repeat):
            head = g * s.repeat + r
            part = slice(r * WIDE, (r + 1) * WIDE)
            n.o_v[rows, head_cols(head)] = result[part]
            inverses = jnp.where(lane == head, inverse[part], inverses)
    n.inv_v[rows] = inverses


def attend_back(n, i, grad_out, keys_ref, query_ref, s, first_done):
    rows = wide_rows(i)
    lowest = n.lowest[rows]
    query_rows, mixed_rows, inverses = query_ref[rows], n.o_v[rows], n.inv_v[rows]
    queries, grads, inners, scales, found = [], [], [], [], []
    for g in range(s.groups):
        queries.append(stacked(query_rows, g, s.repeat))
        grads.append(stacked(grad_out, g, s.repeat))
        mixed = stacked(mixed_rows, g, s.repeat)
        inners.append(
            jnp.sum(grads[g].astype(F32) * mixed.astype(F32), axis=-1, keepdims=True)
        )
        heads = [g * s.repeat + r for r in range(s.repeat)]
        scales.append(jnp.concatenate([inverses[:, h : h + 1] for h in heads], axis=0))
        found.append(jnp.zeros((s.repeat * WIDE, HEAD_SIZE), F32))
    for block in range(key_blocks()):
        keys = key_block(i, block)
        keep = visible(i, lowest, block, s.repeat)
        for g in range(s.groups):
            key_rows = keys_ref[keys, head_cols(g)]
            scores = dot_nt(queries[g], key_rows)
            probs = jnp.exp2(scores * EXP2_SCALE) * (keep * scales[g])
            grad_probs = dot_nt(grads[g], keys_ref[keys, head_cols(s.groups + g)])
            grad_scores = (probs * (grad_probs - inners[g])).astype(BF16)
            found[g] = found[g] + dot_nn(grad_scores, key_rows)
            n.dkv_v[keys, head_cols(g)] += dot_tn(grad_scores, queries[g])
            n.dkv_v[keys, head_cols(s.groups + g)] += dot_tn(probs.astype(BF16), grads[g])
        if block == 0:
            first_done()
    return [
        found[g][r * WIDE : (r + 1) * WIDE] for g in range(s.groups) for r in range(s.repeat)
    ]


def head_back(n, rows, grad, raw, which, layer):
    gain = n.qk_gain[layer, which : which + 1]
    turned = unrotate(grad, n.cosine[rows], n.sine[rows])
    inverse = rms_inverse(raw)
    unit = raw * inverse
    n.qk_sum[which : which + 1] += column_sum(turned * unit)
    return norm_back(turned, unit, inverse, gain).astype(BF16)


class Returns:
    def __init__(self, n, s):
        self.grads, self.low, self.back, self.sems = n.dkv_v, n.low_v, n.back_v, n.return_sems
        self.s, self.plan = s, halo_plan(s.rows)
        self.c, self.t = place()
        self.blocks = []
        for index, (hop, need, offset) in enumerate(self.plan):
            for b in range(need // WIDE):
                self.blocks.append((index, hop, offset + b * WIDE, b * WIDE))
        self.blocks.sort(key=lambda item: item[2])

    def copy(self, number):
        index, hop, source, target = self.blocks[number]
        return remote(
            self.low.at[pl.ds(source, WIDE)],
            self.back[index].at[pl.ds(target, WIDE)],
            self.sems.at[0, number],
            self.sems.at[1, number],
            (jnp.maximum(self.c - hop, 0), self.t),
        )

    def blank(self):
        for index, (hop, need, unused) in enumerate(self.plan):

            @pl.when(self.c + hop >= self.s.count)
            def _():
                self.back[index][...] = jnp.zeros((need, self.low.shape[1]), BF16)

    def send(self, number):
        rows = pl.ds(self.blocks[number][2], WIDE)

        @pl.when(self.c >= self.blocks[number][1])
        def _():
            self.low[rows] = self.grads[rows].astype(BF16)
            self.copy(number).start()

    def send_complete(self, i):
        for number, block in enumerate(self.blocks):
            if block[2] // WIDE < self.s.rows // WIDE - 1:

                @pl.when(i == block[2] // WIDE)
                def _():
                    self.send(number)

    def send_rest(self):
        for number, block in enumerate(self.blocks):
            if block[2] // WIDE >= self.s.rows // WIDE - 1:
                self.send(number)

    def receive(self):
        for number, block in enumerate(self.blocks):

            @pl.when(self.c + block[1] < self.s.count)
            def _():
                self.copy(number).wait_recv()

    def finish(self):
        for number, block in enumerate(self.blocks):

            @pl.when(self.c >= block[1])
            def _():
                self.copy(number).wait_send()


def attention_back_scratch(s):
    plan = halo_plan(s.rows)
    return dict(
        dkv_v=VMEM((ATTENTION_WINDOW + s.rows, 2 * s.keys), F32),
        low_v=VMEM((ATTENTION_WINDOW, 2 * s.keys), BF16),
        back_v=[VMEM((need, 2 * s.keys), BF16) for unused, need, unused_too in plan],
        total_v=VMEM((WIDE, 2 * s.keys), F32),
        return_sems=DMA((2, ATTENTION_WINDOW // WIDE)),
    )


def attention_back_shapes(s):
    return dict(
        dyb=((s.rows, s.model), BF16),
        dgate=((s.rows, s.hidden), BF16),
        dup=((s.rows, s.hidden), BF16),
        dhb=((s.rows, s.model), BF16),
        dq=((s.rows, s.queries), BF16),
        dk=((s.rows, s.keys), BF16),
        dv=((s.rows, s.keys), BF16),
    )


def attention_back_sums(s):
    return dict(
        dres=(shaped(s.rows, s.model, kind=F32), ANY),
        ffn_sum=(shaped(1, s.model, kind=F32), VMEM),
        qk_sum=(shaped(2, HEAD_SIZE, kind=F32), VMEM),
    )


def back_start(n, returns):
    returns.blank()
    n.dkv_v[...] = jnp.zeros_like(n.dkv_v)
    n.ffn_sum[...] = jnp.zeros_like(n.ffn_sum)
    n.qk_sum[...] = jnp.zeros_like(n.qk_sum)


def feed_back(n, i, gate, up, lower, made):
    here = wide_rows(i)
    low = n.g_v[here].astype(BF16)
    n.dyb_v[here] = low
    grad_hidden = dot_nt(low, n.wd_v[...])
    sigma = jax.nn.sigmoid(gate)
    dgate = (grad_hidden * up * (sigma * (1.0 + gate * (1.0 - sigma)))).astype(BF16)
    dup = (grad_hidden * gate * sigma).astype(BF16)
    n.dgate_v[here] = dgate
    n.dup_v[here] = dup
    lower.push(i, dot_nt(dgate, n.wg_v[...]) + dot_nt(dup, n.wu_v[...]))
    send_out(subs(i), *made)


def attention_back(n, i, middle, keys_ref, query_ref, layer, lower, returns, made, s):
    here = wide_rows(i)
    grad_in = lower.take_wide(i)
    inverse = rms_inverse(middle)
    unit = middle * inverse
    n.ffn_sum[...] += column_sum(grad_in * unit)
    total = n.g_v[here] + norm_back(grad_in, unit, inverse, n.ffn_gain[layer : layer + 1])
    n.g_v[here] = total
    low = total.astype(BF16)
    n.dhb_v[here] = low
    grad_out = dot_nt(low, n.wo_v[...]).astype(BF16)
    early = s.rows - WIDE + KEY_BLOCK >= ATTENTION_WINDOW
    send_rest = lambda: pl.when(i == s.rows // WIDE - 1)(returns.send_rest)
    pieces = attend_back(
        n, i, grad_out, keys_ref, query_ref, s, send_rest if early else lambda: None
    )
    returns.send_complete(i)
    if not early:
        send_rest()
    for head, piece in enumerate(pieces):
        n.dq_v[here, head_cols(head)] = head_back(
            n, here, piece * SCALE, n.qraw_v[here, head_cols(head)], 0, layer
        )
    send_out(subs(i), *made)


def keys_back(n, layer, returns, made, s):
    def each(i):
        here = wide_rows(i)
        own = pl.ds(pl.multiple_of(ATTENTION_WINDOW + i * WIDE, WIDE), WIDE)
        n.total_v[...] = n.dkv_v[own]
        for index, (hop, need, unused) in enumerate(returns.plan):
            skipped = s.rows - need

            @pl.when(i >= skipped // WIDE)
            def _():
                part = pl.ds(pl.multiple_of(i * WIDE - skipped, WIDE), WIDE)
                n.total_v[...] += n.back_v[index][part].astype(F32)

        for g in range(s.groups):
            n.dk_v[here, head_cols(g)] = head_back(
                n, here, n.total_v[:, head_cols(g)] * SCALE, n.kraw_v[here, head_cols(g)], 1, layer
            )
        n.dv_v[here] = n.total_v[:, s.keys :].astype(BF16)
        send_out(subs(i), *made)

    each_of(s.rows // WIDE, each)


def feed(n, i, middle, layer):
    here = wide_rows(i)
    normed = (middle * rms_inverse(middle) * n.ffn_gain[layer : layer + 1]).astype(BF16)
    n.a2_v[here] = normed
    gate = dot_nn(normed, n.wg_v[...])
    up = dot_nn(normed, n.wu_v[...])
    inside = (gate * jax.nn.sigmoid(gate) * up).astype(BF16)
    n.hidden_v[here] = inside
    return gate, up, dot_nn(inside, n.wd_v[...])


def layer_ins(stream, saved, w, tables):
    before = {}
    if saved:
        before = dict(
            qin=(saved.q, ANY), kvin=(saved.kv, ANY), lowest=(tables.lowest, VMEM)
        )
    return before | dict(
        x=(stream, ANY),
        ffn_gain=(w.ffn_gain, VMEM),
        wo=(w.w_out, ANY),
        wg=(w.w_gate, ANY),
        wu=(w.w_up, ANY),
        wd=(w.w_down, ANY),
    )


def weight_scratch(s):
    return dict(
        wo_v=VMEM((s.queries, s.model), BF16),
        wg_v=VMEM((s.model, s.hidden), BF16),
        wu_v=VMEM((s.model, s.hidden), BF16),
        wd_v=VMEM((s.hidden, s.model), BF16),
    )


def layer_scratch(stream, s, stores):
    return weight_scratch(s) | dict(
        x_v=VMEM((s.rows, s.model), stream.dtype),
        qin_v=VMEM((s.rows, s.queries), BF16),
        kvin_v=VMEM((ATTENTION_WINDOW + s.rows, 2 * s.keys), BF16),
        load_sems=DMA((20,)),
        store_sems=DMA((stores, s.units)),
        first=line_scratch(s.units, s.model),
        second=line_scratch(s.units, s.model),
    )


def layer_loads(n, loads, layer, projected):
    if projected:
        early = (loads(n.qin, n.qin_v), loads(n.kvin, n.kvin_v))
    else:
        early = (loads(n.x, n.x_v),)
    early += (loads(n.wo.at[layer], n.wo_v),)
    late = () if not projected else (loads(n.x, n.x_v),)
    late += (
        loads(n.wg.at[layer], n.wg_v),
        loads(n.wu.at[layer], n.wu_v),
        loads(n.wd.at[layer], n.wd_v),
    )
    return early, late


def kept_shapes(s):
    return dict(
        o=((s.rows, s.queries), BF16),
        a2=((s.rows, s.model), BF16),
        hidden=((s.rows, s.hidden), BF16),
    )


def forward_shapes(s):
    return kept_shapes(s) | dict(
        inv=((s.rows, HEAD_SIZE), F32),
        h=((s.rows, s.model), F32),
        gate=((s.rows, s.hidden), BF16),
        up=((s.rows, s.hidden), BF16),
        y=((s.rows, s.model), F32),
    )


def forward_layer(layer, stream, saved, w, tables, s, lengths):
    def body(n):
        loads = Loads(n.load_sems)
        if not saved:
            own_weights = (
                loads(n.wk.at[layer], n.first_wk),
                loads(n.wv.at[layer], n.first_wv),
                loads(n.wq.at[layer], n.first_wq),
            )
        early, late = layer_loads(n, loads, layer, saved is not None)
        above = (
            loads(n.wq.at[layer + 1], n.wq_v),
            loads(n.wk.at[layer + 1], n.wk_v),
            loads(n.wv.at[layer + 1], n.wv_v),
        )
        stores = Stores(n.store_sems)
        mixed = (stores(n.o_v, n.o), stores(n.inv_v, n.inv))
        fed = (
            stores(n.h_v, n.h),
            stores(n.a2_v, n.a2),
            stores(n.hidden_v, n.hidden),
            stores(n.gate_v, n.gate),
            stores(n.up_v, n.up),
        )
        closed = (
            stores(n.y_v, n.y),
            stores(n.a1_v, n.a1),
            stores(n.qraw_v, n.qraw),
            stores(n.kraw_v, n.kraw),
            stores(n.q_v, n.q),
        )
        first, second = LineSum(n.first), LineSum(n.second)
        halo = Halo(n.kv_v, n.halo_sems, s.rows, s.count)

        def meanwhile():
            halo.blank()
            if not saved:
                each_of(s.rows // WIDE, lambda i: fill_tables(n, i, s.rows))

        greet(line_partners() + halo_partners(s.rows, s.count), meanwhile)
        wait_all(*early)
        if not saved:
            wait_all(*own_weights)
            own = first_view(n)
            own_halo = Halo(n.kvin_v, n.first_sems, s.rows, s.count)
            own_halo.blank()

            def own_keys(i):
                project_keys(own, i * WIDE, WIDE, n.x_v[wide_rows(i)].astype(F32), layer)
                for u in subs(i):
                    own_halo.send(u)

            def own_queries(i):
                project_queries(own, i * WIDE, WIDE, layer)

            each_of(s.rows // WIDE, own_keys)
            each_of(s.rows // WIDE, own_queries)
            each_of(s.units, own_halo.finish)
            own_out = (
                loads(n.kvin_v, n.own_kv),
                loads(n.first_a1, n.own_a1),
                loads(n.first_qraw, n.own_qraw),
                loads(n.first_kraw, n.own_kraw),
                loads(n.qin_v, n.own_q),
            )

        def mix(i):
            attend(n, i, s)
            first.push(i, dot_nn(n.o_v[wide_rows(i)], n.wo_v[...]))
            send_out(subs(i), *mixed)

        def feed_wide(i):
            pl.when(i == 0)(lambda: wait_all(*late))
            here = wide_rows(i)
            middle = n.x_v[here].astype(F32) + first.take_wide(i)
            n.h_v[here] = middle
            gate, up, part = feed(n, i, middle, layer)
            second.push(i, part)
            n.gate_v[here] = gate.astype(BF16)
            n.up_v[here] = up.astype(BF16)
            send_out(subs(i), *fed)

        def close(u):
            pl.when(u == 0)(lambda: wait_all(*above))
            here = unit_rows(u)
            result = n.h_v[here] + second.take(u)
            n.y_v[here] = result
            project_keys(n, u * UNIT, UNIT, result, layer + 1)
            halo.send(u)
            project_queries(n, u * UNIT, UNIT, layer + 1)
            send_out([u], *closed)

        at = ARRIVED
        pipeline(
            s.units,
            second.stages(at)
            + first.stages(0)
            + [(at + 3 * HOP, close, 1), (at, feed_wide, WIDE // UNIT), (0, mix, WIDE // UNIT)],
        )
        each_of(s.units, halo.finish)
        keys = loads(n.kv_v, n.kv)

        def finish(u):
            first.finish(u)
            second.finish(u)
            stores.finish(u)

        each_of(s.units, finish)
        keys.wait()
        if not saved:
            wait_all(*own_out)

    return run_kernel(
        body,
        layer_ins(stream, saved, w, tables)
        | project_ins(w, tables)
        | (
            {}
            if saved
            else dict(
                lengths=(lengths, pltpu.SMEM),
                frequencies=(rotation_frequencies(), VMEM),
            )
        ),
        outputs(forward_shapes(s))
        | outputs(project_shapes(s))
        | ({} if saved else first_outs(s)),
        layer_scratch(stream, s, 12)
        | buffers(forward_shapes(s))
        | project_scratch(s)
        | ({} if saved else first_scratch(s)),
        2 + layer,
    )


def units_at_turn(s):
    return s.units - min(REST_WIDES, s.rows // WIDE // 2) * (WIDE // UNIT)


def turn_layer(layer, stream, saved, cotangent, w, tables, s):
    def body(n):
        loads = Loads(n.load_sems)
        early, late = layer_loads(n, loads, layer, True)
        late = late + (loads(n.grad, n.grad_v),)
        raws = (loads(n.qraw, n.qraw_v), loads(n.kraw, n.kraw_v))
        a1 = loads(n.a1, n.a1_v)
        stores = Stores(n.store_sems)
        closed = Stores(n.y_sems)
        put_result = closed(n.y_v, n.y)
        turned = (stores(n.g_v, n.dres), stores(n.dq_v, n.dq))
        keyed = (stores(n.dk_v, n.dk), stores(n.dv_v, n.dv))
        first, second, lower = LineSum(n.first), LineSum(n.second), LineSum(n.lower)
        returns = Returns(n, s)
        greet(line_partners() + halo_partners(s.rows, s.count))
        wait_all(*early)

        def mix(i):
            attend(n, i, s)
            first.push(i, dot_nn(n.o_v[wide_rows(i)], n.wo_v[...]))

        def feed_both(i):
            pl.when(i == 0)(lambda: wait_all(*late))
            here = wide_rows(i)
            middle = n.x_v[here] + first.take_wide(i)
            n.x_v[here] = middle
            n.g_v[here] = n.grad_v[here].astype(F32)
            gate, up, part = feed(n, i, middle, layer)
            feed_back(n, i, gate, up, lower, ())

            @pl.when(i < here_units * UNIT // WIDE)
            def _():
                second.hold(i, part)

            @pl.when(i >= here_units * UNIT // WIDE)
            def _():
                for k, u in enumerate(subs(i)):
                    n.rest_v[u - here_units] = part[k * UNIT : (k + 1) * UNIT].astype(BF16)

        def close(u):
            here = unit_rows(u)
            n.y_v[here] = (n.x_v[here] + second.take(u)).astype(BF16)
            send_out([u], put_result)

        rest_rows = pl.ds(here_units * UNIT, s.rows - here_units * UNIT)
        rest = (
            pltpu.make_async_copy(n.rest_v, n.rest, n.rest_sems.at[0]),
            pltpu.make_async_copy(n.x_v.at[rest_rows], n.rest_h, n.rest_sems.at[1]),
        )

        def put_rest():
            for copy in rest:
                copy.start()

        def attention(i):
            pl.when(i == 0)(lambda: wait_all(*raws))
            middle = n.x_v[wide_rows(i)]
            attention_back(
                n, i, middle, n.kvin_v, n.qin_v, layer, lower, returns, turned, s
            )

        at = ARRIVED
        def gradient(index):
            left, right = factors[index]
            block_products(n.grads_v[index], left, right, sizes[index][0], s)
            gradient_store(index).start()

        def gradient_store(index):
            return pltpu.make_async_copy(n.grads_v[index], n.grads[index], n.grad_sems.at[index])

        def end_keys():
            returns.receive()
            keys_back(n, layer, returns, keyed, s)
            a1.wait()

        factors = [
            (n.a2_v, n.dup_v),
            (n.a2_v, n.dgate_v),
            (n.a1_v, n.dq_v),
            (n.hidden_v, n.dyb_v),
            (n.o_v, n.dhb_v),
            (n.a1_v, n.dk_v),
            (n.a1_v, n.dv_v),
        ]
        after = at + ARRIVED + s.units
        tasks = [(1, lambda: back_start(n, returns)), (at + s.units, put_rest), (after + 4, end_keys)]
        for index, step in enumerate((1, 2, 5, 3, 4, 6, 6)):
            tasks.append((after + step, lambda index=index: gradient(index)))
        tasks.sort(key=lambda item: item[0])
        pipeline(
            s.units,
            lower.stages(at)
            + second.stages(OUTPUT_AT, HOP + 1)
            + first.stages(0)
            + [
                (OUTPUT_AT, second.send, 1, here_units),
                (OUTPUT_AT + 3 * HOP + 3, close, 1, here_units),
                (at + ARRIVED, attention, WIDE // UNIT),
                (at, feed_both, WIDE // UNIT),
                (0, mix, WIDE // UNIT),
            ],
            tasks,
        )
        returns.finish()
        for index in range(len(sizes)):
            gradient_store(index).wait()

        wait_all(*rest)

        def finish(u):
            first.finish(u)
            lower.finish(u)
            stores.finish(u)

        def finish_result(u):
            second.finish(u)
            closed.finish(u)

        each_of(s.units, finish)
        each_of(here_units, finish_result)

    sizes = grad_sizes(s)
    backs = attention_back_shapes(s)
    blocks = block_shapes(s, sizes)
    here_units = units_at_turn(s)
    rest_units = s.units - here_units
    return run_kernel(
        body,
        layer_ins(stream, saved, w, tables)
        | dict(
            grad=(cotangent, ANY),
            a1=(saved.a1, ANY),
            qraw=(saved.qraw, ANY),
            kraw=(saved.kraw, ANY),
            qk_gain=(w.qk_gain, VMEM),
            cosine=(tables.cosine, VMEM),
            sine=(tables.sine, VMEM),
        ),
        outputs({x: backs[x] for x in dict(dq=0, dk=0, dv=0)})
        | attention_back_sums(s)
        | dict(
            y=(shaped(here_units * UNIT, s.model), ANY),
            rest=(shaped(rest_units, UNIT, s.model), ANY),
            rest_h=(shaped(rest_units * UNIT, s.model, kind=F32), ANY),
            grads=[(shaped(*block), ANY) for block in blocks],
        ),
        layer_scratch(stream, s, 5)
        | buffers(kept_shapes(s))
        | buffers(backs)
        | attention_back_scratch(s)
        | dict(
            y_v=VMEM((here_units * UNIT, s.model), BF16),
            y_sems=DMA((1, here_units)),
            rest_v=VMEM((rest_units, UNIT, s.model), BF16),
            rest_sems=DMA((2,)),
            second=line_scratch(here_units, s.model),
            a1_v=VMEM((s.rows, s.model), BF16),
            grads_v=[VMEM(block, BF16) for block in blocks],
            grad_sems=DMA((len(sizes),)),
            inv_v=VMEM((s.rows, HEAD_SIZE), F32),
            grad_v=VMEM((s.rows, s.model), BF16),
            g_v=VMEM((s.rows, s.model), F32),
            qraw_v=VMEM((s.rows, s.queries), F32),
            kraw_v=VMEM((s.rows, s.keys), F32),
            lower=line_scratch(s.units, s.model),
        ),
        2 + layer,
    )


def halving_partners(count):
    c, t = place()
    return [(c >= 0, (c ^ (1 << b), t)) for b in range(count.bit_length() - 1)]


def block_products(target, left, right, line, s):
    bits = s.count.bit_length() - 1
    half = s.count // 2
    for part in range(2):
        product = dot_tn(left[:, part * half * line : (part + 1) * half * line], right[...])
        for k in range(half):
            block = part * half + k
            at = tuple((block >> b) & 1 for b in range(bits - 1, -1, -1))
            target[at + (slice(0, line),)] = product[k * line : (k + 1) * line].astype(BF16)


def block_shapes(s, sizes):
    bits = s.count.bit_length() - 1
    return [(2,) * bits + (line + -line % 16, width) for line, width in sizes]


class Scatter:
    def __init__(self, n, s, sizes, factors=None):
        self.n, self.s, self.sizes, self.factors = n, s, sizes, factors
        self.bits = s.count.bit_length() - 1
        self.c, self.t = place()
        self.beside = []

    def bit(self, b):
        return (self.c >> b) & 1

    def order(self, index):
        rest = list(range(1, self.bits))
        return [0] + (rest if index % 2 == 0 else rest[::-1])

    def spot(self, picks):
        low = 0 if self.factors else 1
        return tuple(picks.get(b, slice(None)) for b in range(self.bits - 1, low - 1, -1))

    def own(self, index):
        return (self.n.whole_v if self.factors else self.n.own)[index]

    def copy(self, index, step):
        order = self.order(index)
        picks = {b: self.bit(b) for b in order[:step]}
        picks[order[step]] = 1 - self.bit(order[step])
        if step == 0 and not self.factors:
            source = self.n.whole[index].at[
                (slice(None),) * (self.bits - 1) + (1 - self.bit(0),)
            ]
        else:
            source = self.own(index).at[self.spot(picks)]
        sems = self.n.scatter_sems
        return remote(
            source,
            self.n.got[index * self.bits + step],
            sems.at[0, index, step],
            sems.at[1, index, step],
            (self.c ^ (1 << order[step]), self.t),
        )

    def load(self, index):
        return pltpu.make_async_copy(
            self.n.whole[index].at[(slice(None),) * (self.bits - 1) + (self.bit(0),)],
            self.n.own[index],
            self.n.scatter_load_sems.at[index],
        )

    def start(self, index):
        if self.factors:
            left, right, needed = self.factors[index]
            wait_all(*needed)
            block_products(self.own(index), left, right, self.sizes[index][0], self.s)
        else:
            self.load(index).start()
        self.copy(index, 0).start()

    def add(self, index, step):
        order = self.order(index)
        if step == 0 and not self.factors:
            self.load(index).wait()
        self.copy(index, step).wait_recv()
        free = [b for b in range(self.bits - 1, 0, -1) if b not in order[: step + 1]]
        own, got = self.own(index), self.n.got[index * self.bits + step]
        line = self.sizes[index][0]

        def one(k, carry):
            picks = {b: (k >> (len(free) - 1 - i)) & 1 for i, b in enumerate(free)}
            here = self.spot({b: self.bit(b) for b in order[: step + 1]} | picks)
            total = own[here].astype(F32) + got[tuple(picks[b] for b in free)].astype(F32)
            if step == self.bits - 1:
                self.sum_of(index)[...] = total[:line]
            else:
                own[here] = total.astype(BF16)
            return carry

        if free:
            lax.fori_loop(0, 1 << len(free), one, 0)
        else:
            one(0, 0)
        if step < self.bits - 1:
            self.copy(index, step + 1).start()
        else:
            for other in self.beside:
                other[index].wait()
            self.store(index).start()

    def sum_of(self, index):
        return self.n.sums_v[index].at[0] if self.factors else self.n.sums_v[index]

    def store(self, index):
        return pltpu.make_async_copy(
            self.n.sums_v[index], self.n.sums[index], self.n.scatter_store_sems.at[index]
        )

    def tasks(self, every, bases):
        found = []
        for index in range(len(self.sizes)):
            found.append((bases[0] + index * every, lambda index=index: self.start(index)))
            for step in range(self.bits):
                at = bases[min(step + 1, len(bases) - 1)] + index * every
                at += 100 * max(0, step + 2 - len(bases))
                found.append((at, lambda index=index, step=step: self.add(index, step)))
        found.sort(key=lambda item: item[0])
        return found

    def finish(self):
        for index in range(len(self.sizes)):
            self.store(index).wait()
            for step in range(self.bits):
                self.copy(index, step).wait_send()


def scatter_scratch(s, sizes, computed, layers):
    bits = s.count.bit_length() - 1
    tails = [(line + -line % 16, width) for line, width in sizes]
    found = dict(
        sums_v=[VMEM(((layers,) if computed else ()) + size, F32) for size in sizes],
        got=[
            VMEM((2,) * (bits - 1 - step) + tail, BF16) for tail in tails for step in range(bits)
        ],
        scatter_sems=DMA((2, len(sizes), bits)),
        scatter_load_sems=DMA((len(sizes),)),
        scatter_store_sems=DMA((len(sizes),)),
    )
    if computed:
        return found | dict(whole_v=[VMEM((2,) * bits + tail, BF16) for tail in tails])
    return found | dict(own=[VMEM((2,) * (bits - 1) + tail, BF16) for tail in tails])


def block_view(array, s):
    bits = s.count.bit_length() - 1
    line = array.shape[0] // s.count
    view = array.reshape((2,) * bits + (line, array.shape[1]))
    if line % 16:
        view = jnp.pad(view, [(0, 0)] * bits + [(0, -line % 16), (0, 0)])
    return view


def factor_pairs(k):
    return [
        (k.a2, k.dup),
        (k.a2, k.dgate),
        (k.a1, k.dq),
        (k.hidden, k.dyb),
        (k.o, k.dhb),
        (k.a1, k.dk),
        (k.a1, k.dv),
    ]


def grad_sizes(s):
    return [
        (s.model // s.count, s.hidden),
        (s.model // s.count, s.hidden),
        (s.model // s.count, s.queries),
        (s.hidden // s.count, s.model),
        (s.queries // s.count, s.model),
        (s.model // s.count, s.keys),
        (s.model // s.count, s.keys),
    ]


def head_ins(k, w):
    return dict(
        hq=(k.dq, ANY),
        hk=(k.dk, ANY),
        hv=(k.dv, ANY),
        wq=(w.w_query, ANY),
        wk=(w.key_weight, ANY),
        wv=(w.value_weight, ANY),
        x=(k.x, ANY),
        attn_gain=(w.attn_gain, VMEM),
        grad=(k.dres, ANY),
    )


def head_scratch(k, s):
    return dict(
        hq_v=VMEM((s.rows, s.queries), BF16),
        hk_v=VMEM((s.rows, s.keys), BF16),
        hv_v=VMEM((s.rows, s.keys), BF16),
        wq_v=VMEM((s.model, s.queries), BF16),
        wk_v=VMEM((s.model, s.keys), BF16),
        wv_v=VMEM((s.model, s.keys), BF16),
        x_v=VMEM((s.rows, s.model), k.x.dtype),
        g_v=VMEM((s.rows, s.model), F32),
        upper=line_scratch(s.units, s.model),
        load_sems=DMA((32,)),
        store_sems=DMA((10, s.units)),
    )


def head_loads(n, loads, layer):
    early = (
        loads(n.hq, n.hq_v),
        loads(n.wq.at[layer], n.wq_v),
        loads(n.hk, n.hk_v),
        loads(n.wk.at[layer], n.wk_v),
        loads(n.hv, n.hv_v),
        loads(n.wv.at[layer], n.wv_v),
    )
    return early, (loads(n.x, n.x_v), loads(n.grad, n.g_v))


def head_inputs(n, i, upper):
    here = wide_rows(i)
    upper.push(
        i,
        dot_nt(n.hq_v[here], n.wq_v[...])
        + dot_nt(n.hk_v[here], n.wk_v[...])
        + dot_nt(n.hv_v[here], n.wv_v[...]),
    )


def head_norm(n, here, grad_in, layer):
    stream = n.x_v[here].astype(F32)
    inverse = rms_inverse(stream)
    unit = stream * inverse
    n.attn_sum[...] += column_sum(grad_in * unit)
    n.g_v[here] += norm_back(grad_in, unit, inverse, n.attn_gain[layer : layer + 1])


def backward_layer(layer, kept, w, tables, s):
    above, here_kept = kept[layer + 1], kept[layer]
    sizes = grad_sizes(s)
    rest_units = s.units - units_at_turn(s) if layer + 2 == len(kept) else 0
    backs = attention_back_shapes(s)
    extra_ins, extra_outs, extra_scratch = {}, {}, {}
    if rest_units:
        extra_ins = dict(rest=(above.rest, ANY), rest_h=(above.rest_h, ANY))
        extra_outs = dict(y=(shaped(rest_units * UNIT, s.model), ANY))
        extra_scratch = dict(
            second=line_scratch(rest_units, s.model),
            y_sems=DMA((1, rest_units)),
            rest_sems=DMA((1,)),
        )

    def body(n):
        loads = Loads(n.load_sems)
        early, middle_loads = head_loads(n, loads, layer + 1)
        scatter = Scatter(n, s, sizes)
        n.dgate_v, n.dup_v = n.gate_v, n.up_v
        feeds = (
            loads(n.wd.at[layer], n.wd_v),
            loads(n.gate, n.gate_v),
            loads(n.up, n.up_v),
            loads(n.wg.at[layer], n.wg_v),
            loads(n.wu.at[layer], n.wu_v),
        )
        lates = (
            loads(n.wo.at[layer], n.wo_v),
            loads(n.q, n.q_v),
            loads(n.kv, n.kv_v),
            loads(n.o, n.o_v),
            loads(n.inv, n.inv_v),
            loads(n.qraw, n.qraw_v),
            loads(n.kraw, n.kraw_v),
        )
        stores = Stores(n.store_sems)
        fed_back = (stores(n.dyb_v, n.dyb), stores(n.dgate_v, n.dgate), stores(n.dup_v, n.dup))
        turned = (stores(n.g_v, n.dres), stores(n.dhb_v, n.dhb), stores(n.dq_v, n.dq))
        keyed = (stores(n.dk_v, n.dk), stores(n.dv_v, n.dv))
        upper, lower = LineSum(n.upper), LineSum(n.lower)
        returns = Returns(n, s)
        greet(line_partners() + halo_partners(s.rows, s.count) + halving_partners(s.count))
        n.attn_sum[...] = jnp.zeros_like(n.attn_sum)
        wait_all(*early)

        if rest_units:
            second = LineSum(n.second)
            rest = loads(n.rest, second.part)
            rest_h = pltpu.make_async_copy(
                n.rest_h, n.x_v.at[pl.ds(0, rest_units * UNIT)], n.rest_sems.at[0]
            )

            def result_copy(u):
                return pltpu.make_async_copy(
                    second.inner.at[u], n.y.at[unit_rows(u)], n.y_sems.at[0, u]
                )

            def send_result(u):
                pl.when(u == 0)(rest.wait)
                second.send(u)

            def close(u):
                pl.when(u == 0)(rest_h.wait)
                total = n.x_v[unit_rows(u)].astype(F32) + second.take(u)
                second.inner[u] = total.astype(BF16)
                result_copy(u).start()

        def middle_copy(i):
            rows = wide_rows(i)
            return pltpu.make_async_copy(n.h.at[rows], n.x_v.at[rows], n.middle_sems.at[i])

        def inputs(i):
            head_inputs(n, i, upper)

        def pass_norm(i):
            pl.when(i == 0)(lambda: wait_all(*middle_loads, *feeds))
            here = wide_rows(i)
            head_norm(n, here, upper.take_wide(i), layer + 1)
            middle_copy(i).start()
            gate, up = n.gate_v[here].astype(F32), n.up_v[here].astype(F32)
            feed_back(n, i, gate, up, lower, fed_back)

        def attention(i):
            pl.when(i == 0)(lambda: wait_all(*lates))
            middle_copy(i).wait()
            attention_back(
                n, i, n.x_v[wide_rows(i)], n.kv_v, n.q_v, layer, lower, returns, turned, s
            )

        at = ARRIVED
        after = at + ARRIVED + s.units

        def end_keys():
            returns.receive()
            keys_back(n, layer, returns, keyed, s)

        tasks = [(0, lambda: back_start(n, returns)), (after + 2, end_keys)]
        tasks += scatter.tasks(1, SCATTER_MIDDLE)
        stages = lower.stages(at) + upper.stages(0)
        if rest_units:
            passed = at + ARRIVED + -(-rest_units * UNIT // WIDE) * (WIDE // UNIT) - 1
            tasks.append((passed, rest_h.start))
            stages += second.stages(REST_AT, REST_HOP) + [
                (REST_AT, send_result, 1, rest_units),
                (max(REST_AT + 3 * REST_HOP, passed + 1), close, 1, rest_units),
            ]
        tasks.sort(key=lambda item: item[0])
        pipeline(
            s.units,
            stages
            + [
                (at + ARRIVED, attention, WIDE // UNIT),
                (at, pass_norm, WIDE // UNIT),
                (0, inputs, WIDE // UNIT),
            ],
            tasks,
        )
        returns.finish()
        scatter.finish()
        if rest_units:

            def finish_result(u):
                second.finish(u)
                result_copy(u).wait()

            each_of(rest_units, finish_result)

        def finish(u):
            upper.finish(u)
            lower.finish(u)
            stores.finish(u)

        each_of(s.units, finish)

    whole = above.grads or [
        block_view(dot_tn(left, right).astype(BF16), s) for left, right in factor_pairs(above)
    ]
    held = dict(
        gate=here_kept.gate,
        up=here_kept.up,
        q=here_kept.q,
        kv=here_kept.kv,
        o=here_kept.o,
        inv=here_kept.inv,
        qraw=here_kept.qraw,
        kraw=here_kept.kraw,
    )
    return run_kernel(
        body,
        head_ins(above, w)
        | {x: (array, ANY) for x, array in held.items()}
        | dict(
            h=(here_kept.h, ANY),
            wd=(w.w_down, ANY),
            wg=(w.w_gate, ANY),
            wu=(w.w_up, ANY),
            wo=(w.w_out, ANY),
            ffn_gain=(w.ffn_gain, VMEM),
            qk_gain=(w.qk_gain, VMEM),
            cosine=(tables.cosine, VMEM),
            sine=(tables.sine, VMEM),
            lowest=(tables.lowest, VMEM),
            whole=[(array, ANY) for array in whole],
        )
        | extra_ins,
        outputs(attention_back_shapes(s))
        | attention_back_sums(s)
        | dict(
            attn_sum=(shaped(1, s.model, kind=F32), VMEM),
            sums=[(shaped(*size, kind=F32), ANY) for size in sizes],
        )
        | extra_outs,
        head_scratch(above, s)
        | extra_scratch
        | weight_scratch(s)
        | {x + "_v": VMEM(array.shape, array.dtype) for x, array in held.items()}
        | buffers({x: b for x, b in backs.items() if x not in dict(dgate=0, dup=0)})
        | attention_back_scratch(s)
        | scatter_scratch(s, sizes, False, 1)
        | dict(
            lower=line_scratch(s.units, s.model),
            middle_sems=DMA((s.rows // WIDE,)),
        ),
        20 + layer,
    )


def backward_end(kept, w, s):
    bottom = kept[0]
    sizes = grad_sizes(s)
    layers = len(kept)
    width = s.model // s.count
    bits = s.count.bit_length() - 1
    tp_bits = s.line.bit_length() - 1
    rounds = [(1 << b, 0) for b in range(bits)] + [(0, 1 << b) for b in range(tp_bits)]

    def body(n):
        c, t = place()
        loads = Loads(n.load_sems)
        early, lates = head_loads(n, loads, 0)
        a2, dup, dgate = loads(n.a2, n.a2_v), loads(n.dup, n.dup_v), loads(n.dgate, n.dgate_v)
        a1, hidden, dyb = loads(n.a1, n.a1_v), loads(n.hidden, n.hidden_v), loads(n.dyb, n.dyb_v)
        o, dhb = loads(n.o, n.o_v), loads(n.dhb, n.dhb_v)
        factors = [
            (n.a2_v, n.dup_v, (a2, dup)),
            (n.a2_v, n.dgate_v, (dgate,)),
            (n.a1_v, n.hq_v, (a1,)),
            (n.hidden_v, n.dyb_v, (hidden, dyb)),
            (n.o_v, n.dhb_v, (o, dhb)),
            (n.a1_v, n.hk_v, ()),
            (n.a1_v, n.hv_v, ()),
        ]
        scatter = Scatter(n, s, sizes, factors)
        stores = Stores(n.store_sems)
        out = stores(n.g_v, n.dres)
        upper = LineSum(n.upper)
        others = [(c >= 0, ((c + k) % s.count, t)) for k in range(1, s.count)]
        lines = [(c >= 0, (c, t ^ (1 << b))) for b in range(tp_bits)]
        greet(line_partners() + halving_partners(s.count) + others + lines)
        n.attn_sum[...] = jnp.zeros_like(n.attn_sum)
        n.acc[...] = jnp.zeros_like(n.acc)
        n.gains[...] = jnp.zeros_like(n.gains)
        for layer in range(layers):
            n.acc[0, 2 * layer : 2 * layer + 2] = n.qk_in[layer][...]
        wait_all(*early)
        scatter.beside = [
            [
                loads(n.done[(layer - 1) * len(sizes) + index], n.sums_v[index].at[layer])
                for index in range(len(sizes))
            ]
            for layer in range(1, layers)
        ]

        def head_copy(k):
            return remote(
                n.acc.at[k],
                n.other.at[k],
                n.small_sems.at[0, k],
                n.small_sems.at[1, k],
                (c ^ rounds[k][0], t ^ rounds[k][1]),
            )

        def head_step(k):
            if k > 0:
                head_copy(k - 1).wait_recv()
                n.acc[k] = n.acc[k - 1] + n.other[k - 1]
            if k < len(rounds):
                head_copy(k).start()

        def pass_norm(u):
            pl.when(u == 0)(lambda: wait_all(*lates))
            head_norm(n, unit_rows(u), upper.take(u), 0)
            send_out([u], out)

        tasks = scatter.tasks(SCATTER_EVERY, SCATTER_END)
        tasks += [(2 * k + 1, lambda k=k: head_step(k)) for k in range(len(rounds) + 1)]
        tasks.sort(key=lambda item: item[0])
        pipeline(
            s.units,
            upper.stages(0)
            + [
                (3 * HOP, pass_norm, 1),
                (0, lambda i: head_inputs(n, i, upper), WIDE // UNIT),
            ],
            tasks,
        )
        gains = [n.attn_sum] + n.attn_in + n.ffn_in
        for d in range(s.count):
            for row, gain in enumerate(gains):
                n.gains[d, row : row + 1] = gain[:, d * width : (d + 1) * width]

        def gain_copy(k):
            to = (c + k) % s.count
            return remote(
                n.gains.at[to],
                n.gains_got.at[k],
                n.gain_sems.at[0, k],
                n.gain_sems.at[1, k],
                (to, t),
            )

        for k in range(1, s.count):
            gain_copy(k).start()
        for layer in range(layers):
            n.qk_total[layer] = n.acc[len(rounds), 2 * layer : 2 * layer + 2]
        total = n.gains[c]
        for k in range(1, s.count):
            gain_copy(k).wait_recv()
            total = total + n.gains_got[k]
        n.attn_total[...] = total[:layers]
        n.ffn_total[...] = total[layers : 2 * layers]
        for k in range(1, s.count):
            gain_copy(k).wait_send()
        for k in range(len(rounds)):
            head_copy(k).wait_send()
        scatter.finish()

        def finish(u):
            upper.finish(u)
            stores.finish(u)

        each_of(s.units, finish)

    held = dict(
        a1=bottom.a1,
        a2=bottom.a2,
        o=bottom.o,
        hidden=bottom.hidden,
        dyb=bottom.dyb,
        dgate=bottom.dgate,
        dup=bottom.dup,
        dhb=bottom.dhb,
    )
    small = (len(rounds) + 1, 2 * layers + -2 * layers % 8, HEAD_SIZE)
    slabs = (s.count, 2 * layers + -2 * layers % 8, width)
    return run_kernel(
        body,
        head_ins(bottom, w)
        | {x: (array, ANY) for x, array in held.items()}
        | dict(
            qk_in=[(k.qk_sum, VMEM) for k in kept],
            attn_in=[(k.attn_sum, VMEM) for k in kept[1:]],
            ffn_in=[(k.ffn_sum, VMEM) for k in kept],
            done=[(array, ANY) for k in kept[1:] for array in k.sums],
        ),
        dict(
            dres=(shaped(s.rows, s.model, kind=F32), ANY),
            attn_total=(shaped(layers, width, kind=F32), VMEM),
            ffn_total=(shaped(layers, width, kind=F32), VMEM),
            qk_total=(shaped(layers, 2, HEAD_SIZE, kind=F32), VMEM),
            sums=[(shaped(layers, *size, kind=F32), ANY) for size in sizes],
        ),
        head_scratch(bottom, s)
        | {x + "_v": VMEM(array.shape, array.dtype) for x, array in held.items()}
        | scatter_scratch(s, sizes, True, layers)
        | dict(
            attn_sum=VMEM((1, s.model), F32),
            acc=VMEM(small, F32),
            other=VMEM(small, F32),
            gains=VMEM(slabs, F32),
            gains_got=VMEM(slabs, F32),
            small_sems=DMA((2, len(rounds))),
            gain_sems=DMA((2, s.count)),
        ),
        19,
    )


def deliver(results):
    pieces = [piece for result in results for piece in result]
    spots = [
        (index, sum(other.shape[0] for other in result[:k]), result[k].shape[0])
        for index, result in enumerate(results)
        for k in range(len(result))
    ]

    def body(n):
        copies = []
        for k, (index, first, rows) in enumerate(spots):
            target = n.result[index].at[pl.ds(first, rows)]
            copies.append(
                (
                    pltpu.make_async_copy(n.given[k], n.held[k], n.sems.at[0, k]),
                    pltpu.make_async_copy(n.held[k], target, n.sems.at[1, k]),
                )
            )
            copies[-1][0].start()
        for fetch, put in copies:
            fetch.wait()
            put.start()
        for fetch, put in copies:
            put.wait()

    shapes = [
        (sum(piece.shape[0] for piece in result),) + result[0].shape[1:] for result in results
    ]
    return run_kernel(
        body,
        dict(given=[(piece, ANY) for piece in pieces]),
        dict(
            result=[
                (shaped(*shape, kind=result[0].dtype), ANY)
                for shape, result in zip(shapes, results)
            ]
        ),
        dict(
            held=[VMEM(piece.shape, piece.dtype) for piece in pieces],
            sems=DMA((2, len(pieces))),
        ),
        None,
    ).result


OUTPUT_AT = 17
REST_AT = 19
REST_WIDES = 2
REST_HOP = 3
SCATTER_MIDDLE = (3, 7, 13, 19)
SCATTER_EVERY = 1
SCATTER_END = (0, 2, 7, 11)


def body(hidden_in, doc_lengths, cotangent, attn_gain, ffn_gain, qk_gain, w_query, *others):
    key_weight, value_weight, w_out, w_gate, w_up, w_down = others
    w = types.SimpleNamespace(
        attn_gain=attn_gain,
        ffn_gain=ffn_gain,
        qk_gain=qk_gain,
        w_query=w_query,
        key_weight=key_weight,
        value_weight=value_weight,
        w_out=w_out,
        w_gate=w_gate,
        w_up=w_up,
        w_down=w_down,
    )
    rows, model = hidden_in.shape
    layers, unused, queries = w_query.shape
    keys = key_weight.shape[2]
    s = types.SimpleNamespace(
        rows=rows,
        model=model,
        queries=queries,
        keys=keys,
        hidden=w_gate.shape[2],
        units=rows // UNIT,
        groups=keys // HEAD_SIZE,
        repeat=queries // keys,
        count=lax.axis_size(CTX),
        line=lax.axis_size(TP),
    )
    tables = None

    kept = []
    stream = hidden_in
    saved = None
    for layer in range(layers):
        if layer < layers - 1:
            result = forward_layer(layer, stream, saved, w, tables, s, doc_lengths)
        else:
            result = turn_layer(layer, stream, saved, cotangent, w, tables, s)
        if saved:
            own = dict(a1=saved.a1, qraw=saved.qraw, kraw=saved.kraw, q=saved.q, kv=saved.kv)
        else:
            own = dict(
                a1=result.own_a1,
                qraw=result.own_qraw,
                kraw=result.own_kraw,
                q=result.own_q,
                kv=result.own_kv,
            )
            tables = types.SimpleNamespace(
                cosine=result.cosine, sine=result.sine, lowest=result.lowest
            )
        kept.append(types.SimpleNamespace(**(dict(grads=None) | vars(result) | own | dict(x=stream))))
        stream = result.y
        saved = result
    streams = [stream]

    for layer in range(layers - 2, -1, -1):
        result = backward_layer(layer, kept, w, tables, s)
        if layer == layers - 2:
            streams.append(result.y)
        kept[layer + 1].attn_sum = result.attn_sum
        kept[layer + 1].sums = result.sums
        vars(kept[layer]).update(
            dyb=result.dyb,
            dgate=result.dgate,
            dup=result.dup,
            dhb=result.dhb,
            dq=result.dq,
            dk=result.dk,
            dv=result.dv,
            dres=result.dres,
            ffn_sum=result.ffn_sum,
            qk_sum=result.qk_sum,
        )
    end = backward_end(kept, w, s)
    small = [end.attn_total, end.ffn_total, end.qk_total]
    stream, grad, *gains, up, gate, query, down, out, key, value = deliver(
        [streams] + [[array] for array in [end.dres] + small + end.sums]
    )
    return (
        stream,
        grad,
        *gains,
        query,
        key,
        value,
        out,
        gate,
        up,
        down,
    )


def solution(mesh):
    by_rows = P(CTX, None)
    by_columns = P(None, None, TP)
    by_hidden = P(None, TP, None)
    grad_columns = P(None, CTX, TP)
    grad_rows = P(None, (TP, CTX), None)
    return jax.shard_map(
        body,
        mesh=mesh,
        in_specs=(by_rows, P(), by_rows, P(), P(), P())
        + (by_columns,) * 3
        + (by_hidden,)
        + (by_columns,) * 2
        + (by_hidden,),
        out_specs=(by_rows, by_rows, P(None, CTX), P(None, CTX), P())
        + (grad_columns,) * 3
        + (grad_rows,)
        + (grad_columns,) * 2
        + (grad_rows,),
        check_vma=False,
    )
```

```python
import types

import jax
import jax.numpy as jnp
from jax import lax
from jax.experimental import pallas as pl
from jax.experimental.pallas import tpu as pltpu
from jax.sharding import PartitionSpec as P

HEAD_SIZE = 128
ATTENTION_WINDOW = 1024
EPS = 1e-06
THETA = 1000000.0

UNIT = 64
WIDE = 128
KEY_BLOCK = 384
HOP = 2
ARRIVED = 3 * HOP + WIDE // UNIT - 1
CTX = "ctx"
TP = "tp"
MESH = pl.DeviceIdType.MESH
F32 = jnp.float32
BF16 = jnp.bfloat16
SCALE = HEAD_SIZE ** (-0.5)
EXP2_SCALE = SCALE * 1.4426950408889634
ANY = pl.ANY
VMEM = pltpu.VMEM
DMA = pltpu.SemaphoreType.DMA


def dot_nn(left, right):
    return jnp.dot(left, right, preferred_element_type=F32)


def dot_nt(left, right):
    return lax.dot_general(left, right, (((1,), (1,)), ((), ())), preferred_element_type=F32)


def dot_tn(left, right):
    return lax.dot_general(left, right, (((0,), (0,)), ((), ())), preferred_element_type=F32)


def rms_inverse(value_rows):
    return lax.rsqrt(jnp.mean(value_rows * value_rows, axis=-1, keepdims=True) + EPS)


def rotate(value_rows, cosine, sine):
    return value_rows * cosine + pltpu.roll(value_rows, HEAD_SIZE // 2, 1) * sine


def unrotate(grad, cosine, sine):
    return grad * cosine + pltpu.roll(grad * sine, HEAD_SIZE // 2, 1)


def norm_back(grad, unit, inverse, gain):
    scaled = grad * gain
    inner = jnp.mean(scaled * unit, axis=-1, keepdims=True)
    return inverse * (scaled - unit * inner)


def column_sum(value_rows):
    return jnp.sum(value_rows, axis=0, keepdims=True)


def rotation_frequencies():
    half = jnp.arange(HEAD_SIZE // 2, dtype=F32)
    freq = THETA ** (-(half * 2.0) / HEAD_SIZE)
    return jnp.concatenate([freq, freq])[None, :]


def fill_tables(n, i, rows):
    here = wide_rows(i)
    start = lax.axis_index(CTX) * rows
    shape = (WIDE, HEAD_SIZE)
    spot = start + i * WIDE + lax.broadcasted_iota(jnp.int32, shape, 0)
    begin, end = jnp.zeros(shape, jnp.int32), 0
    for doc in range(n.lengths.shape[0]):
        end = end + n.lengths[doc]
        begin = begin + jnp.where(spot >= end, n.lengths[doc], 0)
    angle = (spot - begin).astype(F32) * n.frequencies[...]
    lane = lax.broadcasted_iota(jnp.int32, shape, 1)
    n.cosine[here] = jnp.cos(angle)
    n.sine[here] = jnp.sin(angle) * jnp.where(lane < HEAD_SIZE // 2, -1.0, 1.0)
    lowest = jnp.maximum(begin, spot - (ATTENTION_WINDOW - 1)) - (start - ATTENTION_WINDOW)
    n.lowest[here] = lowest[:, :1]


def halo_plan(rows):
    reach = -(-ATTENTION_WINDOW // rows)
    plan = []
    for hop in range(1, reach + 1):
        need = min(rows, ATTENTION_WINDOW - (hop - 1) * rows)
        plan.append((hop, need, ATTENTION_WINDOW - (hop - 1) * rows - need))
    return plan


def unit_rows(u):
    return pl.ds(pl.multiple_of(u * UNIT, UNIT), UNIT)


def wide_rows(w):
    return pl.ds(pl.multiple_of(w * WIDE, WIDE), WIDE)


def subs(w):
    return [w * (WIDE // UNIT) + i for i in range(WIDE // UNIT)]


def shaped(*shape, kind=BF16):
    return jax.ShapeDtypeStruct(shape, kind)


def listed(value):
    return list(value) if isinstance(value, list) else [value]


def run_kernel(body, ins, outs, scratch, collective_id):
    groups = [ins, outs, scratch]
    flat = [[x for value in group.values() for x in listed(value)] for group in groups]

    def named(values, chosen):
        values = list(values)
        found = {}
        for group in chosen:
            for name, value in group.items():
                if isinstance(value, list):
                    found[name] = [values.pop(0) for unused in value]
                else:
                    found[name] = values.pop(0)
        return types.SimpleNamespace(**found)

    results = pl.pallas_call(
        lambda *refs: body(named(refs, groups)),
        out_shape=[shape for shape, unused in flat[1]],
        in_specs=[pl.BlockSpec(memory_space=space) for unused, space in flat[0]],
        out_specs=[pl.BlockSpec(memory_space=space) for unused, space in flat[1]],
        scratch_shapes=flat[2],
        compiler_params=pltpu.CompilerParams(
            collective_id=collective_id,
            has_side_effects=collective_id is not None,
            vmem_limit_bytes=62 * 2**20,
        ),
    )(*[array for array, unused in flat[0]])
    return named(results, [outs])


def place():
    return lax.axis_index(CTX), lax.axis_index(TP)


def remote(source, target, send, receive, device):
    return pltpu.make_async_remote_copy(
        src_ref=source,
        dst_ref=target,
        send_sem=send,
        recv_sem=receive,
        device_id=device,
        device_id_type=MESH,
    )


def greet(partners, meanwhile=lambda: None):
    barrier = pltpu.get_barrier_semaphore()
    total = 0
    for exists, device in partners:
        total = total + jnp.where(exists, 1, 0)

        @pl.when(exists)
        def _():
            pl.semaphore_signal(barrier, inc=1, device_id=device, device_id_type=MESH)

    meanwhile()
    pl.semaphore_wait(barrier, total)


def line_partners():
    c, t = place()
    outer = (t == 0) | (t == 3)
    return [
        (outer, (c, jnp.where(t == 0, 1, 2))),
        (jnp.logical_not(outer), (c, jnp.where(t == 1, 0, 3))),
        (jnp.logical_not(outer), (c, jnp.clip(3 - t, 1, 2))),
    ]


def halo_partners(rows, count):
    c, t = place()
    partners = []
    for hop, unused, unused_too in halo_plan(rows):
        partners.append((c + hop < count, (jnp.minimum(c + hop, count - 1), t)))
        partners.append((c >= hop, (jnp.maximum(c - hop, 0), t)))
    return partners


class LineSum:
    def __init__(self, refs):
        self.part, self.total, self.inner, self.sems = refs
        self.c, self.t = place()
        self.outer = (self.t == 0) | (self.t == 3)
        self.is_inner = jnp.logical_not(self.outer)

    def copy(self, source, target, u, send, receive, to):
        return remote(
            source.at[u],
            target.at[u],
            self.sems.at[send, u],
            self.sems.at[receive, u],
            (self.c, to),
        )

    def inwards(self, u):
        return self.copy(self.part, self.total, u, 0, 1, jnp.where(self.t < 2, 1, 2))

    def across(self, u):
        return self.copy(self.part, self.inner, u, 0, 2, jnp.clip(3 - self.t, 1, 2))

    def outwards(self, u):
        return self.copy(self.total, self.total, u, 3, 4, jnp.where(self.t < 2, 0, 3))

    def hold(self, w, value):
        for i, u in enumerate(subs(w)):
            self.part[u] = value[i * UNIT : (i + 1) * UNIT].astype(BF16)

    def send(self, u):
        @pl.when(self.outer)
        def _():
            self.inwards(u).start()

    def push(self, w, value):
        self.hold(w, value)
        for u in subs(w):
            self.send(u)

    def meet(self, u):
        @pl.when(self.is_inner)
        def _():
            self.inwards(u).wait_recv()
            self.part[u] = (self.part[u].astype(F32) + self.total[u].astype(F32)).astype(BF16)
            self.across(u).start()

    def spread(self, u):
        @pl.when(self.is_inner)
        def _():
            self.across(u).wait_recv()
            self.total[u] = (self.part[u].astype(F32) + self.inner[u].astype(F32)).astype(BF16)
            self.outwards(u).start()

    def take(self, u):
        @pl.when(self.outer)
        def _():
            self.outwards(u).wait_recv()

        return self.total[u].astype(F32)

    def take_wide(self, w):
        return jnp.concatenate([self.take(u) for u in subs(w)], axis=0)

    def finish(self, u):
        @pl.when(self.outer)
        def _():
            self.inwards(u).wait_send()

        @pl.when(self.is_inner)
        def _():
            self.across(u).wait_send()
            self.outwards(u).wait_send()

    def stages(self, begin, hop=HOP):
        number = self.part.shape[0]
        return [(begin + 2 * hop, self.spread, 1, number), (begin + hop, self.meet, 1, number)]


def line_scratch(units, width):
    block = VMEM((units, UNIT, width), BF16)
    return [block, block, block, DMA((5, units))]


def pipeline(units, stages, tasks=()):
    stages = [stage if len(stage) > 3 else stage + (units,) for stage in stages]
    steps = max(number + delay + 1 - taken for delay, unused, taken, number in stages)

    def step(s, carry):
        for delay, function, taken, number in stages:
            ready = (s >= delay) & (s < number + delay)
            if taken > 1:
                ready = ready & ((s - delay) % taken == 0)

            @pl.when(ready)
            def _():
                function((s - delay) // taken if taken > 1 else s - delay)

        for at, task in tasks:
            if at < steps:

                @pl.when(s == at)
                def _():
                    task()

        return carry

    lax.fori_loop(0, steps, step, 0)
    for at, task in tasks:
        if at >= steps:
            task()


def each_of(number, function):
    def step(u, carry):
        function(u)
        return carry

    lax.fori_loop(0, number, step, 0)


class Loads:
    def __init__(self, sems):
        self.sems, self.number = sems, 0

    def __call__(self, source, target):
        copy = pltpu.make_async_copy(source, target, self.sems.at[self.number])
        copy.start()
        self.number += 1
        return copy


def wait_all(*copies):
    for copy in copies:
        copy.wait()


class Stores:
    def __init__(self, sems):
        self.sems, self.copies = sems, []

    def __call__(self, source, target):
        index = len(self.copies)

        def copy(u):
            rows = unit_rows(u)
            return pltpu.make_async_copy(source.at[rows], target.at[rows], self.sems.at[index, u])

        self.copies.append(copy)
        return copy

    def finish(self, u):
        for copy in self.copies:
            copy(u).wait()


def send_out(units, *copies):
    for u in units:
        for copy in copies:
            copy(u).start()


class Halo:
    def __init__(self, keys, sems, rows, count, relayed=False):
        self.keys, self.sems, self.rows, self.count = keys, sems, rows, count
        self.plan = halo_plan(rows)
        self.c, self.t = place()
        self.relayed = relayed and len(self.plan) == 2
        self.even = self.c % 2 == 0

    def relays(self, u):
        return self.even & (self.c >= 2) & (u >= (self.rows - self.plan[1][1]) // UNIT)

    def relay_copy(self, u):
        offset, skipped = self.plan[1][2], self.rows - self.plan[1][1]
        source = pl.multiple_of(self.plan[0][2] + u * UNIT, UNIT)
        target = pl.multiple_of(offset + u * UNIT - skipped, UNIT)
        return remote(
            self.keys.at[pl.ds(source, UNIT)],
            self.keys.at[pl.ds(target, UNIT)],
            self.sems.at[2, u - skipped // UNIT],
            self.sems.at[3, u],
            (jnp.minimum(self.c + 1, self.count - 1), self.t),
        )

    def relay(self, u):
        @pl.when(self.relays(u))
        def _():
            self.copy(0, u, *self.plan[0]).wait_recv()
            self.relay_copy(u).start()

    def copy(self, index, u, hop, need, offset):
        target = pl.multiple_of(offset + u * UNIT - (self.rows - need), UNIT)
        return remote(
            self.keys.at[pl.ds(pl.multiple_of(ATTENTION_WINDOW + u * UNIT, UNIT), UNIT)],
            self.keys.at[pl.ds(target, UNIT)],
            self.sems.at[2 * index, u],
            self.sems.at[2 * index + 1, u],
            (jnp.minimum(self.c + hop, self.count - 1), self.t),
        )

    def each(self, u, function, receives):
        for index, (hop, need, offset) in enumerate(self.plan):
            exists = self.c >= hop if receives else self.c + hop < self.count
            if self.relayed and receives and index == 0:
                exists = exists & jnp.logical_not(self.relays(u))
            if self.relayed and not receives and index == 1:
                exists = exists & self.even

            @pl.when(exists & (u >= (self.rows - need) // UNIT))
            def _():
                function(self.copy(index, u, hop, need, offset))

    def blank(self):
        width = self.keys.shape[1]
        for hop, need, offset in self.plan:

            @pl.when(self.c < hop)
            def _():
                self.keys[offset : offset + need] = jnp.zeros((need, width), BF16)

    def send(self, u):
        self.each(u, lambda copy: copy.start(), False)

    def finish(self, u):
        self.each(u, lambda copy: copy.wait_recv(), True)
        self.each(u, lambda copy: copy.wait_send(), False)
        if self.relayed:
            pl.when(self.relays(u))(lambda: self.relay_copy(u).wait_send())


def project_heads(n, raw, out, out_rows, rows, which, layer):
    cosine, sine = n.cosine[rows], n.sine[rows]
    gain = n.qk_gain[layer, which : which + 1]
    for head in range(raw.shape[1] // HEAD_SIZE):
        part = raw[:, head_cols(head)]
        part = part * rms_inverse(part) * gain
        out[out_rows, head_cols(head)] = rotate(part, cosine, sine).astype(BF16)


def project_keys(n, first, number, stream, layer):
    rows = pl.ds(pl.multiple_of(first, number), number)
    own = pl.ds(pl.multiple_of(ATTENTION_WINDOW + first, number), number)
    normed = (stream * rms_inverse(stream) * n.attn_gain[layer : layer + 1]).astype(BF16)
    n.a1_v[rows] = normed
    key = dot_nn(normed, n.wk_v[...])
    n.kraw_v[rows] = key
    n.kv_v[own, key.shape[1] :] = dot_nn(normed, n.wv_v[...]).astype(BF16)
    project_heads(n, key, n.kv_v, own, rows, 1, layer)


def project_queries(n, first, number, layer):
    rows = pl.ds(pl.multiple_of(first, number), number)
    query = dot_nn(n.a1_v[rows], n.wq_v[...])
    n.qraw_v[rows] = query
    project_heads(n, query, n.q_v, rows, rows, 0, layer)


def project_shapes(s):
    return dict(
        a1=((s.rows, s.model), BF16),
        qraw=((s.rows, s.queries), F32),
        kraw=((s.rows, s.keys), F32),
        q=((s.rows, s.queries), BF16),
        kv=((ATTENTION_WINDOW + s.rows, 2 * s.keys), BF16),
    )


def outputs(shapes):
    return {x: (shaped(*shape, kind=kind), ANY) for x, (shape, kind) in shapes.items()}


def buffers(shapes):
    return {x + "_v": VMEM(shape, kind) for x, (shape, kind) in shapes.items()}


def project_ins(w, tables):
    turns = dict(cosine=(tables.cosine, VMEM), sine=(tables.sine, VMEM)) if tables else {}
    return turns | dict(
        attn_gain=(w.attn_gain, VMEM),
        qk_gain=(w.qk_gain, VMEM),
        wq=(w.w_query, ANY),
        wk=(w.key_weight, ANY),
        wv=(w.value_weight, ANY),
    )


def project_scratch(s):
    return buffers(project_shapes(s)) | dict(
        wq_v=VMEM((s.model, s.queries), BF16),
        wk_v=VMEM((s.model, s.keys), BF16),
        wv_v=VMEM((s.model, s.keys), BF16),
        halo_sems=DMA((2 * len(halo_plan(s.rows)), s.units)),
    )


def first_scratch(s):
    return dict(
        first_a1=VMEM((s.rows, s.model), BF16),
        first_qraw=VMEM((s.rows, s.queries), F32),
        first_kraw=VMEM((s.rows, s.keys), F32),
        first_wq=VMEM((s.model, s.queries), BF16),
        first_wk=VMEM((s.model, s.keys), BF16),
        first_wv=VMEM((s.model, s.keys), BF16),
        first_sems=DMA((2 * len(halo_plan(s.rows)), s.units)),
    )


def first_outs(s):
    return outputs({"own_" + x: shape for x, shape in project_shapes(s).items()}) | dict(
        cosine=(shaped(s.rows, HEAD_SIZE, kind=F32), VMEM),
        sine=(shaped(s.rows, HEAD_SIZE, kind=F32), VMEM),
        lowest=(shaped(s.rows, 1, kind=jnp.int32), VMEM),
    )


def first_view(n):
    return types.SimpleNamespace(
        attn_gain=n.attn_gain,
        qk_gain=n.qk_gain,
        cosine=n.cosine,
        sine=n.sine,
        a1_v=n.first_a1,
        qraw_v=n.first_qraw,
        kraw_v=n.first_kraw,
        q_v=n.qin_v,
        kv_v=n.kvin_v,
        wq_v=n.first_wq,
        wk_v=n.first_wk,
        wv_v=n.first_wv,
    )


def key_block(i, block):
    return pl.ds(pl.multiple_of(i * WIDE + block * KEY_BLOCK, HEAD_SIZE), KEY_BLOCK)


def visible(i, lowest, block, repeat):
    shape = (WIDE, KEY_BLOCK)
    col = block * KEY_BLOCK + lax.broadcasted_iota(jnp.int32, shape, 1)
    seen = col >= lowest - i * WIDE
    if (block + 1) * KEY_BLOCK > ATTENTION_WINDOW:
        row = ATTENTION_WINDOW + lax.broadcasted_iota(jnp.int32, shape, 0)
        seen = seen & (col <= row)
    keep = jnp.where(seen, 1.0, 0.0)
    return jnp.concatenate([keep] * repeat, axis=0)


def key_blocks():
    return (ATTENTION_WINDOW + WIDE) // KEY_BLOCK


def stacked(value, group, repeat):
    first = group * repeat
    return jnp.concatenate(
        [value[:, (first + r) * HEAD_SIZE : (first + r + 1) * HEAD_SIZE] for r in range(repeat)],
        axis=0,
    )


def head_cols(index):
    return slice(index * HEAD_SIZE, (index + 1) * HEAD_SIZE)


def attend(n, i, s):
    rows = wide_rows(i)
    lowest = n.lowest[rows]
    lane = lax.broadcasted_iota(jnp.int32, (WIDE, HEAD_SIZE), 1)
    query_rows = n.qin_v[rows]
    queries = [stacked(query_rows, g, s.repeat) for g in range(s.groups)]
    mixed = [jnp.zeros((s.repeat * WIDE, HEAD_SIZE), F32) for unused in queries]
    total = [jnp.zeros((s.repeat * WIDE, 1), F32) for unused in queries]
    for block in range(key_blocks()):
        keys = key_block(i, block)
        keep = visible(i, lowest, block, s.repeat)
        for g in range(s.groups):
            scores = dot_nt(queries[g], n.kvin_v[keys, head_cols(g)])
            weights = jnp.exp2(scores * EXP2_SCALE) * keep
            total[g] = total[g] + jnp.sum(weights, axis=-1, keepdims=True)
            values = n.kvin_v[keys, head_cols(s.groups + g)]
            mixed[g] = mixed[g] + dot_nn(weights.astype(BF16), values)
    inverses = jnp.zeros((WIDE, HEAD_SIZE), F32)
    for g in range(s.groups):
        inverse = 1.0 / total[g]
        result = (mixed[g] * inverse).astype(BF16)
        for r in range(s.repeat):
            head = g * s.repeat + r
            part = slice(r * WIDE, (r + 1) * WIDE)
            n.o_v[rows, head_cols(head)] = result[part]
            inverses = jnp.where(lane == head, inverse[part], inverses)
    n.inv_v[rows] = inverses


def attend_back(n, i, grad_out, keys_ref, query_ref, s, first_done):
    rows = wide_rows(i)
    lowest = n.lowest[rows]
    query_rows, mixed_rows, inverses = query_ref[rows], n.o_v[rows], n.inv_v[rows]
    queries, grads, inners, scales, found = [], [], [], [], []
    for g in range(s.groups):
        queries.append(stacked(query_rows, g, s.repeat))
        grads.append(stacked(grad_out, g, s.repeat))
        mixed = stacked(mixed_rows, g, s.repeat)
        inners.append(
            jnp.sum(grads[g].astype(F32) * mixed.astype(F32), axis=-1, keepdims=True)
        )
        heads = [g * s.repeat + r for r in range(s.repeat)]
        scales.append(jnp.concatenate([inverses[:, h : h + 1] for h in heads], axis=0))
        found.append(jnp.zeros((s.repeat * WIDE, HEAD_SIZE), F32))
    for block in range(key_blocks()):
        keys = key_block(i, block)
        keep = visible(i, lowest, block, s.repeat)
        for g in range(s.groups):
            key_rows = keys_ref[keys, head_cols(g)]
            scores = dot_nt(queries[g], key_rows)
            probs = jnp.exp2(scores * EXP2_SCALE) * (keep * scales[g])
            grad_probs = dot_nt(grads[g], keys_ref[keys, head_cols(s.groups + g)])
            grad_scores = (probs * (grad_probs - inners[g])).astype(BF16)
            found[g] = found[g] + dot_nn(grad_scores, key_rows)
            n.dkv_v[keys, head_cols(g)] += dot_tn(grad_scores, queries[g])
            n.dkv_v[keys, head_cols(s.groups + g)] += dot_tn(probs.astype(BF16), grads[g])
        if block == 0:
            first_done()
    return [
        found[g][r * WIDE : (r + 1) * WIDE] for g in range(s.groups) for r in range(s.repeat)
    ]


def head_back(n, rows, grad, raw, which, layer):
    gain = n.qk_gain[layer, which : which + 1]
    turned = unrotate(grad, n.cosine[rows], n.sine[rows])
    inverse = rms_inverse(raw)
    unit = raw * inverse
    n.qk_sum[which : which + 1] += column_sum(turned * unit)
    return norm_back(turned, unit, inverse, gain).astype(BF16)


class Returns:
    def __init__(self, n, s):
        self.grads, self.low, self.back, self.sems = n.dkv_v, n.low_v, n.back_v, n.return_sems
        self.s, self.plan = s, halo_plan(s.rows)
        self.c, self.t = place()
        self.blocks = []
        for index, (hop, need, offset) in enumerate(self.plan):
            for b in range(need // WIDE):
                self.blocks.append((index, hop, offset + b * WIDE, b * WIDE))
        self.blocks.sort(key=lambda item: item[2])

    def copy(self, number):
        index, hop, source, target = self.blocks[number]
        return remote(
            self.low.at[pl.ds(source, WIDE)],
            self.back[index].at[pl.ds(target, WIDE)],
            self.sems.at[0, number],
            self.sems.at[1, number],
            (jnp.maximum(self.c - hop, 0), self.t),
        )

    def blank(self):
        for index, (hop, need, unused) in enumerate(self.plan):

            @pl.when(self.c + hop >= self.s.count)
            def _():
                self.back[index][...] = jnp.zeros((need, self.low.shape[1]), BF16)

    def send(self, number):
        rows = pl.ds(self.blocks[number][2], WIDE)

        @pl.when(self.c >= self.blocks[number][1])
        def _():
            self.low[rows] = self.grads[rows].astype(BF16)
            self.copy(number).start()

    def send_complete(self, i):
        for number, block in enumerate(self.blocks):
            if block[2] // WIDE < self.s.rows // WIDE - 1:

                @pl.when(i == block[2] // WIDE)
                def _():
                    self.send(number)

    def send_rest(self):
        for number, block in enumerate(self.blocks):
            if block[2] // WIDE >= self.s.rows // WIDE - 1:
                self.send(number)

    def receive(self):
        for number, block in enumerate(self.blocks):

            @pl.when(self.c + block[1] < self.s.count)
            def _():
                self.copy(number).wait_recv()

    def finish(self):
        for number, block in enumerate(self.blocks):

            @pl.when(self.c >= block[1])
            def _():
                self.copy(number).wait_send()


def attention_back_scratch(s):
    plan = halo_plan(s.rows)
    return dict(
        dkv_v=VMEM((ATTENTION_WINDOW + s.rows, 2 * s.keys), F32),
        low_v=VMEM((ATTENTION_WINDOW, 2 * s.keys), BF16),
        back_v=[VMEM((need, 2 * s.keys), BF16) for unused, need, unused_too in plan],
        total_v=VMEM((WIDE, 2 * s.keys), F32),
        return_sems=DMA((2, ATTENTION_WINDOW // WIDE)),
    )


def attention_back_shapes(s):
    return dict(
        dyb=((s.rows, s.model), BF16),
        dgate=((s.rows, s.hidden), BF16),
        dup=((s.rows, s.hidden), BF16),
        dhb=((s.rows, s.model), BF16),
        dq=((s.rows, s.queries), BF16),
        dk=((s.rows, s.keys), BF16),
        dv=((s.rows, s.keys), BF16),
    )


def attention_back_sums(s):
    return dict(
        dres=(shaped(s.rows, s.model, kind=F32), ANY),
        ffn_sum=(shaped(1, s.model, kind=F32), VMEM),
        qk_sum=(shaped(2, HEAD_SIZE, kind=F32), VMEM),
    )


def back_start(n, returns):
    returns.blank()
    n.dkv_v[...] = jnp.zeros_like(n.dkv_v)
    n.ffn_sum[...] = jnp.zeros_like(n.ffn_sum)
    n.qk_sum[...] = jnp.zeros_like(n.qk_sum)


def feed_back(n, i, gate, up, lower, made):
    here = wide_rows(i)
    low = n.g_v[here].astype(BF16)
    n.dyb_v[here] = low
    grad_hidden = dot_nt(low, n.wd_v[...])
    sigma = jax.nn.sigmoid(gate)
    dgate = (grad_hidden * up * (sigma * (1.0 + gate * (1.0 - sigma)))).astype(BF16)
    dup = (grad_hidden * gate * sigma).astype(BF16)
    n.dgate_v[here] = dgate
    n.dup_v[here] = dup
    lower.push(i, dot_nt(dgate, n.wg_v[...]) + dot_nt(dup, n.wu_v[...]))
    send_out(subs(i), *made)


def attention_back(n, i, middle, keys_ref, query_ref, layer, lower, returns, made, s):
    here = wide_rows(i)
    grad_in = lower.take_wide(i)
    inverse = rms_inverse(middle)
    unit = middle * inverse
    n.ffn_sum[...] += column_sum(grad_in * unit)
    total = n.g_v[here] + norm_back(grad_in, unit, inverse, n.ffn_gain[layer : layer + 1])
    n.g_v[here] = total
    low = total.astype(BF16)
    n.dhb_v[here] = low
    grad_out = dot_nt(low, n.wo_v[...]).astype(BF16)
    early = s.rows - WIDE + KEY_BLOCK >= ATTENTION_WINDOW
    send_rest = lambda: pl.when(i == s.rows // WIDE - 1)(returns.send_rest)
    pieces = attend_back(
        n, i, grad_out, keys_ref, query_ref, s, send_rest if early else lambda: None
    )
    returns.send_complete(i)
    if not early:
        send_rest()
    for head, piece in enumerate(pieces):
        n.dq_v[here, head_cols(head)] = head_back(
            n, here, piece * SCALE, n.qraw_v[here, head_cols(head)], 0, layer
        )
    send_out(subs(i), *made)


def keys_back(n, layer, returns, made, s):
    def each(i):
        here = wide_rows(i)
        own = pl.ds(pl.multiple_of(ATTENTION_WINDOW + i * WIDE, WIDE), WIDE)
        n.total_v[...] = n.dkv_v[own]
        for index, (hop, need, unused) in enumerate(returns.plan):
            skipped = s.rows - need

            @pl.when(i >= skipped // WIDE)
            def _():
                part = pl.ds(pl.multiple_of(i * WIDE - skipped, WIDE), WIDE)
                n.total_v[...] += n.back_v[index][part].astype(F32)

        for g in range(s.groups):
            n.dk_v[here, head_cols(g)] = head_back(
                n, here, n.total_v[:, head_cols(g)] * SCALE, n.kraw_v[here, head_cols(g)], 1, layer
            )
        n.dv_v[here] = n.total_v[:, s.keys :].astype(BF16)
        send_out(subs(i), *made)

    each_of(s.rows // WIDE, each)


def feed(n, i, middle, layer):
    here = wide_rows(i)
    normed = (middle * rms_inverse(middle) * n.ffn_gain[layer : layer + 1]).astype(BF16)
    n.a2_v[here] = normed
    gate = dot_nn(normed, n.wg_v[...])
    up = dot_nn(normed, n.wu_v[...])
    inside = (gate * jax.nn.sigmoid(gate) * up).astype(BF16)
    n.hidden_v[here] = inside
    return gate, up, dot_nn(inside, n.wd_v[...])


def layer_ins(stream, saved, w, tables):
    before = {}
    if saved:
        before = dict(
            qin=(saved.q, ANY), kvin=(saved.kv, ANY), lowest=(tables.lowest, VMEM)
        )
    return before | dict(
        x=(stream, ANY),
        ffn_gain=(w.ffn_gain, VMEM),
        wo=(w.w_out, ANY),
        wg=(w.w_gate, ANY),
        wu=(w.w_up, ANY),
        wd=(w.w_down, ANY),
    )


def weight_scratch(s):
    return dict(
        wo_v=VMEM((s.queries, s.model), BF16),
        wg_v=VMEM((s.model, s.hidden), BF16),
        wu_v=VMEM((s.model, s.hidden), BF16),
        wd_v=VMEM((s.hidden, s.model), BF16),
    )


def layer_scratch(stream, s, stores):
    return weight_scratch(s) | dict(
        x_v=VMEM((s.rows, s.model), stream.dtype),
        qin_v=VMEM((s.rows, s.queries), BF16),
        kvin_v=VMEM((ATTENTION_WINDOW + s.rows, 2 * s.keys), BF16),
        load_sems=DMA((20,)),
        store_sems=DMA((stores, s.units)),
        first=line_scratch(s.units, s.model),
        second=line_scratch(s.units, s.model),
    )


def layer_loads(n, loads, layer, projected):
    if projected:
        early = (loads(n.qin, n.qin_v), loads(n.kvin, n.kvin_v))
    else:
        early = (loads(n.x, n.x_v),)
    early += (loads(n.wo.at[layer], n.wo_v),)
    late = () if not projected else (loads(n.x, n.x_v),)
    late += (
        loads(n.wg.at[layer], n.wg_v),
        loads(n.wu.at[layer], n.wu_v),
        loads(n.wd.at[layer], n.wd_v),
    )
    return early, late


def kept_shapes(s):
    return dict(
        o=((s.rows, s.queries), BF16),
        a2=((s.rows, s.model), BF16),
        hidden=((s.rows, s.hidden), BF16),
    )


def forward_shapes(s):
    return kept_shapes(s) | dict(
        inv=((s.rows, HEAD_SIZE), F32),
        h=((s.rows, s.model), F32),
        gate=((s.rows, s.hidden), BF16),
        up=((s.rows, s.hidden), BF16),
        y=((s.rows, s.model), F32),
    )


def forward_layer(layer, stream, saved, w, tables, s, lengths):
    def body(n):
        loads = Loads(n.load_sems)
        if not saved:
            own_weights = (
                loads(n.wk.at[layer], n.first_wk),
                loads(n.wv.at[layer], n.first_wv),
                loads(n.wq.at[layer], n.first_wq),
            )
        early, late = layer_loads(n, loads, layer, saved is not None)
        above = (
            loads(n.wq.at[layer + 1], n.wq_v),
            loads(n.wk.at[layer + 1], n.wk_v),
            loads(n.wv.at[layer + 1], n.wv_v),
        )
        stores = Stores(n.store_sems)
        mixed = (stores(n.o_v, n.o), stores(n.inv_v, n.inv))
        fed = (
            stores(n.h_v, n.h),
            stores(n.a2_v, n.a2),
            stores(n.hidden_v, n.hidden),
            stores(n.gate_v, n.gate),
            stores(n.up_v, n.up),
        )
        closed = (
            stores(n.y_v, n.y),
            stores(n.a1_v, n.a1),
            stores(n.qraw_v, n.qraw),
            stores(n.kraw_v, n.kraw),
            stores(n.q_v, n.q),
        )
        first, second = LineSum(n.first), LineSum(n.second)
        halo = Halo(n.kv_v, n.halo_sems, s.rows, s.count)

        def meanwhile():
            halo.blank()
            if not saved:
                each_of(s.rows // WIDE, lambda i: fill_tables(n, i, s.rows))

        greet(line_partners() + halo_partners(s.rows, s.count), meanwhile)
        wait_all(*early)
        if not saved:
            wait_all(*own_weights)
            own = first_view(n)
            own_halo = Halo(n.kvin_v, n.first_sems, s.rows, s.count, True)
            own_halo.blank()

            def own_keys(i):
                project_keys(own, i * WIDE, WIDE, n.x_v[wide_rows(i)].astype(F32), layer)
                for u in subs(i):
                    own_halo.send(u)

            def own_queries(i):
                project_queries(own, i * WIDE, WIDE, layer)

            each_of(s.rows // WIDE, own_keys)
            each_of(s.rows // WIDE, own_queries)
            if own_halo.relayed:
                each_of(s.units, own_halo.relay)
            each_of(s.units, own_halo.finish)
            own_out = (
                loads(n.kvin_v, n.own_kv),
                loads(n.first_a1, n.own_a1),
                loads(n.first_qraw, n.own_qraw),
                loads(n.first_kraw, n.own_kraw),
                loads(n.qin_v, n.own_q),
            )

        def mix(i):
            attend(n, i, s)
            first.push(i, dot_nn(n.o_v[wide_rows(i)], n.wo_v[...]))
            send_out(subs(i), *mixed)

        def feed_wide(i):
            pl.when(i == 0)(lambda: wait_all(*late))
            here = wide_rows(i)
            middle = n.x_v[here].astype(F32) + first.take_wide(i)
            n.h_v[here] = middle
            gate, up, part = feed(n, i, middle, layer)
            second.push(i, part)
            n.gate_v[here] = gate.astype(BF16)
            n.up_v[here] = up.astype(BF16)
            send_out(subs(i), *fed)

        def close(u):
            pl.when(u == 0)(lambda: wait_all(*above))
            here = unit_rows(u)
            result = n.h_v[here] + second.take(u)
            n.y_v[here] = result
            project_keys(n, u * UNIT, UNIT, result, layer + 1)
            halo.send(u)
            project_queries(n, u * UNIT, UNIT, layer + 1)
            send_out([u], *closed)

        at = ARRIVED
        pipeline(
            s.units,
            second.stages(at)
            + first.stages(0)
            + [(at + 3 * HOP, close, 1), (at, feed_wide, WIDE // UNIT), (0, mix, WIDE // UNIT)],
        )
        each_of(s.units, halo.finish)
        keys = loads(n.kv_v, n.kv)

        def finish(u):
            first.finish(u)
            second.finish(u)
            stores.finish(u)

        each_of(s.units, finish)
        keys.wait()
        if not saved:
            wait_all(*own_out)

    return run_kernel(
        body,
        layer_ins(stream, saved, w, tables)
        | project_ins(w, tables)
        | (
            {}
            if saved
            else dict(
                lengths=(lengths, pltpu.SMEM),
                frequencies=(rotation_frequencies(), VMEM),
            )
        ),
        outputs(forward_shapes(s))
        | outputs(project_shapes(s))
        | ({} if saved else first_outs(s)),
        layer_scratch(stream, s, 12)
        | buffers(forward_shapes(s))
        | project_scratch(s)
        | ({} if saved else first_scratch(s)),
        2 + layer,
    )


def units_at_turn(s):
    return s.units - min(REST_WIDES, s.rows // WIDE // 2) * (WIDE // UNIT)


def turn_layer(layer, stream, saved, cotangent, w, tables, s):
    def body(n):
        loads = Loads(n.load_sems)
        early, late = layer_loads(n, loads, layer, True)
        late = late + (loads(n.grad, n.grad_v),)
        raws = (loads(n.qraw, n.qraw_v), loads(n.kraw, n.kraw_v))
        a1 = loads(n.a1, n.a1_v)
        stores = Stores(n.store_sems)
        closed = Stores(n.y_sems)
        put_result = closed(n.y_v, n.y)
        turned = (stores(n.g_v, n.dres), stores(n.dq_v, n.dq))
        keyed = (stores(n.dk_v, n.dk), stores(n.dv_v, n.dv))
        first, second, lower = LineSum(n.first), LineSum(n.second), LineSum(n.lower)
        returns = Returns(n, s)
        greet(line_partners() + halo_partners(s.rows, s.count))
        wait_all(*early)

        def mix(i):
            attend(n, i, s)
            first.push(i, dot_nn(n.o_v[wide_rows(i)], n.wo_v[...]))

        def feed_both(i):
            pl.when(i == 0)(lambda: wait_all(*late))
            here = wide_rows(i)
            middle = n.x_v[here] + first.take_wide(i)
            n.x_v[here] = middle
            n.g_v[here] = n.grad_v[here].astype(F32)
            gate, up, part = feed(n, i, middle, layer)
            feed_back(n, i, gate, up, lower, ())

            @pl.when(i < here_units * UNIT // WIDE)
            def _():
                second.hold(i, part)

            @pl.when(i >= here_units * UNIT // WIDE)
            def _():
                for k, u in enumerate(subs(i)):
                    n.rest_v[u - here_units] = part[k * UNIT : (k + 1) * UNIT].astype(BF16)

        def close(u):
            here = unit_rows(u)
            n.y_v[here] = (n.x_v[here] + second.take(u)).astype(BF16)
            send_out([u], put_result)

        rest_rows = pl.ds(here_units * UNIT, s.rows - here_units * UNIT)
        rest = (
            pltpu.make_async_copy(n.rest_v, n.rest, n.rest_sems.at[0]),
            pltpu.make_async_copy(n.x_v.at[rest_rows], n.rest_h, n.rest_sems.at[1]),
        )

        def put_rest():
            for copy in rest:
                copy.start()

        def attention(i):
            pl.when(i == 0)(lambda: wait_all(*raws))
            middle = n.x_v[wide_rows(i)]
            attention_back(
                n, i, middle, n.kvin_v, n.qin_v, layer, lower, returns, turned, s
            )

        at = ARRIVED
        def gradient(index):
            left, right = factors[index]
            block_products(n.grads_v[index], left, right, sizes[index][0], s)
            gradient_store(index).start()

        def gradient_store(index):
            return pltpu.make_async_copy(n.grads_v[index], n.grads[index], n.grad_sems.at[index])

        def end_keys():
            returns.receive()
            keys_back(n, layer, returns, keyed, s)
            a1.wait()

        factors = [
            (n.a2_v, n.dup_v),
            (n.a2_v, n.dgate_v),
            (n.a1_v, n.dq_v),
            (n.hidden_v, n.dyb_v),
            (n.o_v, n.dhb_v),
            (n.a1_v, n.dk_v),
            (n.a1_v, n.dv_v),
        ]
        after = at + ARRIVED + s.units
        tasks = [(1, lambda: back_start(n, returns)), (at + s.units, put_rest), (after + 4, end_keys)]
        for index, step in enumerate((1, 2, 5, 3, 4, 6, 6)):
            tasks.append((after + step, lambda index=index: gradient(index)))
        tasks.sort(key=lambda item: item[0])
        pipeline(
            s.units,
            lower.stages(at)
            + second.stages(OUTPUT_AT, HOP + 1)
            + first.stages(0)
            + [
                (OUTPUT_AT, second.send, 1, here_units),
                (OUTPUT_AT + 3 * HOP + 3, close, 1, here_units),
                (at + ARRIVED, attention, WIDE // UNIT),
                (at, feed_both, WIDE // UNIT),
                (0, mix, WIDE // UNIT),
            ],
            tasks,
        )
        returns.finish()
        for index in range(len(sizes)):
            gradient_store(index).wait()

        wait_all(*rest)

        def finish(u):
            first.finish(u)
            lower.finish(u)
            stores.finish(u)

        def finish_result(u):
            second.finish(u)
            closed.finish(u)

        each_of(s.units, finish)
        each_of(here_units, finish_result)

    sizes = grad_sizes(s)
    backs = attention_back_shapes(s)
    blocks = block_shapes(s, sizes)
    here_units = units_at_turn(s)
    rest_units = s.units - here_units
    return run_kernel(
        body,
        layer_ins(stream, saved, w, tables)
        | dict(
            grad=(cotangent, ANY),
            a1=(saved.a1, ANY),
            qraw=(saved.qraw, ANY),
            kraw=(saved.kraw, ANY),
            qk_gain=(w.qk_gain, VMEM),
            cosine=(tables.cosine, VMEM),
            sine=(tables.sine, VMEM),
        ),
        outputs({x: backs[x] for x in dict(dq=0, dk=0, dv=0)})
        | attention_back_sums(s)
        | dict(
            y=(shaped(here_units * UNIT, s.model), ANY),
            rest=(shaped(rest_units, UNIT, s.model), ANY),
            rest_h=(shaped(rest_units * UNIT, s.model, kind=F32), ANY),
            grads=[(shaped(*block), ANY) for block in blocks],
        ),
        layer_scratch(stream, s, 5)
        | buffers(kept_shapes(s))
        | buffers(backs)
        | attention_back_scratch(s)
        | dict(
            y_v=VMEM((here_units * UNIT, s.model), BF16),
            y_sems=DMA((1, here_units)),
            rest_v=VMEM((rest_units, UNIT, s.model), BF16),
            rest_sems=DMA((2,)),
            second=line_scratch(here_units, s.model),
            a1_v=VMEM((s.rows, s.model), BF16),
            grads_v=[VMEM(block, BF16) for block in blocks],
            grad_sems=DMA((len(sizes),)),
            inv_v=VMEM((s.rows, HEAD_SIZE), F32),
            grad_v=VMEM((s.rows, s.model), BF16),
            g_v=VMEM((s.rows, s.model), F32),
            qraw_v=VMEM((s.rows, s.queries), F32),
            kraw_v=VMEM((s.rows, s.keys), F32),
            lower=line_scratch(s.units, s.model),
        ),
        2 + layer,
    )


def halving_partners(count):
    c, t = place()
    return [(c >= 0, (c ^ (1 << b), t)) for b in range(count.bit_length() - 1)]


def block_products(target, left, right, line, s):
    bits = s.count.bit_length() - 1
    half = s.count // 2
    for part in range(2):
        product = dot_tn(left[:, part * half * line : (part + 1) * half * line], right[...])
        for k in range(half):
            block = part * half + k
            at = tuple((block >> b) & 1 for b in range(bits - 1, -1, -1))
            target[at + (slice(0, line),)] = product[k * line : (k + 1) * line].astype(BF16)


def block_shapes(s, sizes):
    bits = s.count.bit_length() - 1
    return [(2,) * bits + (line + -line % 16, width) for line, width in sizes]


class Scatter:
    def __init__(self, n, s, sizes, factors=None):
        self.n, self.s, self.sizes, self.factors = n, s, sizes, factors
        self.bits = s.count.bit_length() - 1
        self.c, self.t = place()
        self.beside = []

    def bit(self, b):
        return (self.c >> b) & 1

    def order(self, index):
        rest = list(range(1, self.bits))
        return [0] + (rest if index % 2 == 0 else rest[::-1])

    def spot(self, picks):
        low = 0 if self.factors else 1
        return tuple(picks.get(b, slice(None)) for b in range(self.bits - 1, low - 1, -1))

    def own(self, index):
        return (self.n.whole_v if self.factors else self.n.own)[index]

    def copy(self, index, step):
        order = self.order(index)
        picks = {b: self.bit(b) for b in order[:step]}
        picks[order[step]] = 1 - self.bit(order[step])
        if step == 0 and not self.factors:
            source = self.n.whole[index].at[
                (slice(None),) * (self.bits - 1) + (1 - self.bit(0),)
            ]
        else:
            source = self.own(index).at[self.spot(picks)]
        sems = self.n.scatter_sems
        return remote(
            source,
            self.n.got[index * self.bits + step],
            sems.at[0, index, step],
            sems.at[1, index, step],
            (self.c ^ (1 << order[step]), self.t),
        )

    def load(self, index):
        return pltpu.make_async_copy(
            self.n.whole[index].at[(slice(None),) * (self.bits - 1) + (self.bit(0),)],
            self.n.own[index],
            self.n.scatter_load_sems.at[index],
        )

    def start(self, index):
        if self.factors:
            left, right, needed = self.factors[index]
            wait_all(*needed)
            block_products(self.own(index), left, right, self.sizes[index][0], self.s)
        else:
            self.load(index).start()
        self.copy(index, 0).start()

    def add(self, index, step):
        order = self.order(index)
        if step == 0 and not self.factors:
            self.load(index).wait()
        self.copy(index, step).wait_recv()
        free = [b for b in range(self.bits - 1, 0, -1) if b not in order[: step + 1]]
        own, got = self.own(index), self.n.got[index * self.bits + step]
        line = self.sizes[index][0]

        def one(k, carry):
            picks = {b: (k >> (len(free) - 1 - i)) & 1 for i, b in enumerate(free)}
            here = self.spot({b: self.bit(b) for b in order[: step + 1]} | picks)
            total = own[here].astype(F32) + got[tuple(picks[b] for b in free)].astype(F32)
            if step == self.bits - 1:
                self.sum_of(index)[...] = total[:line]
            else:
                own[here] = total.astype(BF16)
            return carry

        if free:
            lax.fori_loop(0, 1 << len(free), one, 0)
        else:
            one(0, 0)
        if step < self.bits - 1:
            self.copy(index, step + 1).start()
        else:
            for other in self.beside:
                other[index].wait()
            self.store(index).start()

    def sum_of(self, index):
        return self.n.sums_v[index].at[0] if self.factors else self.n.sums_v[index]

    def store(self, index):
        return pltpu.make_async_copy(
            self.n.sums_v[index], self.n.sums[index], self.n.scatter_store_sems.at[index]
        )

    def tasks(self, every, bases):
        found = []
        for index in range(len(self.sizes)):
            found.append((bases[0] + index * every, lambda index=index: self.start(index)))
            for step in range(self.bits):
                at = bases[min(step + 1, len(bases) - 1)] + index * every
                at += 100 * max(0, step + 2 - len(bases))
                found.append((at, lambda index=index, step=step: self.add(index, step)))
        found.sort(key=lambda item: item[0])
        return found

    def finish(self):
        for index in range(len(self.sizes)):
            self.store(index).wait()
            for step in range(self.bits):
                self.copy(index, step).wait_send()


def scatter_scratch(s, sizes, computed, layers):
    bits = s.count.bit_length() - 1
    tails = [(line + -line % 16, width) for line, width in sizes]
    found = dict(
        sums_v=[VMEM(((layers,) if computed else ()) + size, F32) for size in sizes],
        got=[
            VMEM((2,) * (bits - 1 - step) + tail, BF16) for tail in tails for step in range(bits)
        ],
        scatter_sems=DMA((2, len(sizes), bits)),
        scatter_load_sems=DMA((len(sizes),)),
        scatter_store_sems=DMA((len(sizes),)),
    )
    if computed:
        return found | dict(whole_v=[VMEM((2,) * bits + tail, BF16) for tail in tails])
    return found | dict(own=[VMEM((2,) * (bits - 1) + tail, BF16) for tail in tails])


def block_view(array, s):
    bits = s.count.bit_length() - 1
    line = array.shape[0] // s.count
    view = array.reshape((2,) * bits + (line, array.shape[1]))
    if line % 16:
        view = jnp.pad(view, [(0, 0)] * bits + [(0, -line % 16), (0, 0)])
    return view


def factor_pairs(k):
    return [
        (k.a2, k.dup),
        (k.a2, k.dgate),
        (k.a1, k.dq),
        (k.hidden, k.dyb),
        (k.o, k.dhb),
        (k.a1, k.dk),
        (k.a1, k.dv),
    ]


def grad_sizes(s):
    return [
        (s.model // s.count, s.hidden),
        (s.model // s.count, s.hidden),
        (s.model // s.count, s.queries),
        (s.hidden // s.count, s.model),
        (s.queries // s.count, s.model),
        (s.model // s.count, s.keys),
        (s.model // s.count, s.keys),
    ]


def head_ins(k, w):
    return dict(
        hq=(k.dq, ANY),
        hk=(k.dk, ANY),
        hv=(k.dv, ANY),
        wq=(w.w_query, ANY),
        wk=(w.key_weight, ANY),
        wv=(w.value_weight, ANY),
        x=(k.x, ANY),
        attn_gain=(w.attn_gain, VMEM),
        grad=(k.dres, ANY),
    )


def head_scratch(k, s):
    return dict(
        hq_v=VMEM((s.rows, s.queries), BF16),
        hk_v=VMEM((s.rows, s.keys), BF16),
        hv_v=VMEM((s.rows, s.keys), BF16),
        wq_v=VMEM((s.model, s.queries), BF16),
        wk_v=VMEM((s.model, s.keys), BF16),
        wv_v=VMEM((s.model, s.keys), BF16),
        x_v=VMEM((s.rows, s.model), k.x.dtype),
        g_v=VMEM((s.rows, s.model), F32),
        upper=line_scratch(s.units, s.model),
        load_sems=DMA((32,)),
        store_sems=DMA((10, s.units)),
    )


def head_loads(n, loads, layer):
    early = (
        loads(n.hq, n.hq_v),
        loads(n.wq.at[layer], n.wq_v),
        loads(n.hk, n.hk_v),
        loads(n.wk.at[layer], n.wk_v),
        loads(n.hv, n.hv_v),
        loads(n.wv.at[layer], n.wv_v),
    )
    return early, (loads(n.x, n.x_v), loads(n.grad, n.g_v))


def head_inputs(n, i, upper):
    here = wide_rows(i)
    upper.push(
        i,
        dot_nt(n.hq_v[here], n.wq_v[...])
        + dot_nt(n.hk_v[here], n.wk_v[...])
        + dot_nt(n.hv_v[here], n.wv_v[...]),
    )


def head_norm(n, here, grad_in, layer):
    stream = n.x_v[here].astype(F32)
    inverse = rms_inverse(stream)
    unit = stream * inverse
    n.attn_sum[...] += column_sum(grad_in * unit)
    n.g_v[here] += norm_back(grad_in, unit, inverse, n.attn_gain[layer : layer + 1])


def backward_layer(layer, kept, w, tables, s):
    above, here_kept = kept[layer + 1], kept[layer]
    sizes = grad_sizes(s)
    rest_units = s.units - units_at_turn(s) if layer + 2 == len(kept) else 0
    backs = attention_back_shapes(s)
    extra_ins, extra_outs, extra_scratch = {}, {}, {}
    if rest_units:
        extra_ins = dict(rest=(above.rest, ANY), rest_h=(above.rest_h, ANY))
        extra_outs = dict(y=(shaped(rest_units * UNIT, s.model), ANY))
        extra_scratch = dict(
            second=line_scratch(rest_units, s.model),
            y_sems=DMA((1, rest_units)),
            rest_sems=DMA((1,)),
        )

    def body(n):
        loads = Loads(n.load_sems)
        early, middle_loads = head_loads(n, loads, layer + 1)
        scatter = Scatter(n, s, sizes)
        n.dgate_v, n.dup_v = n.gate_v, n.up_v
        feeds = (
            loads(n.wd.at[layer], n.wd_v),
            loads(n.gate, n.gate_v),
            loads(n.up, n.up_v),
            loads(n.wg.at[layer], n.wg_v),
            loads(n.wu.at[layer], n.wu_v),
        )
        lates = (
            loads(n.wo.at[layer], n.wo_v),
            loads(n.q, n.q_v),
            loads(n.kv, n.kv_v),
            loads(n.o, n.o_v),
            loads(n.inv, n.inv_v),
            loads(n.qraw, n.qraw_v),
            loads(n.kraw, n.kraw_v),
        )
        stores = Stores(n.store_sems)
        fed_back = (stores(n.dyb_v, n.dyb), stores(n.dgate_v, n.dgate), stores(n.dup_v, n.dup))
        turned = (stores(n.g_v, n.dres), stores(n.dhb_v, n.dhb), stores(n.dq_v, n.dq))
        keyed = (stores(n.dk_v, n.dk), stores(n.dv_v, n.dv))
        upper, lower = LineSum(n.upper), LineSum(n.lower)
        returns = Returns(n, s)
        greet(line_partners() + halo_partners(s.rows, s.count) + halving_partners(s.count))
        n.attn_sum[...] = jnp.zeros_like(n.attn_sum)
        wait_all(*early)

        if rest_units:
            second = LineSum(n.second)
            rest = loads(n.rest, second.part)
            rest_h = pltpu.make_async_copy(
                n.rest_h, n.x_v.at[pl.ds(0, rest_units * UNIT)], n.rest_sems.at[0]
            )

            def result_copy(u):
                return pltpu.make_async_copy(
                    second.inner.at[u], n.y.at[unit_rows(u)], n.y_sems.at[0, u]
                )

            def send_result(u):
                pl.when(u == 0)(rest.wait)
                second.send(u)

            def close(u):
                pl.when(u == 0)(rest_h.wait)
                total = n.x_v[unit_rows(u)].astype(F32) + second.take(u)
                second.inner[u] = total.astype(BF16)
                result_copy(u).start()

        def middle_copy(i):
            rows = wide_rows(i)
            return pltpu.make_async_copy(n.h.at[rows], n.x_v.at[rows], n.middle_sems.at[i])

        def inputs(i):
            head_inputs(n, i, upper)

        def pass_norm(i):
            pl.when(i == 0)(lambda: wait_all(*middle_loads, *feeds))
            here = wide_rows(i)
            head_norm(n, here, upper.take_wide(i), layer + 1)
            middle_copy(i).start()
            gate, up = n.gate_v[here].astype(F32), n.up_v[here].astype(F32)
            feed_back(n, i, gate, up, lower, fed_back)

        def attention(i):
            pl.when(i == 0)(lambda: wait_all(*lates))
            middle_copy(i).wait()
            attention_back(
                n, i, n.x_v[wide_rows(i)], n.kv_v, n.q_v, layer, lower, returns, turned, s
            )

        at = ARRIVED
        after = at + ARRIVED + s.units

        def end_keys():
            returns.receive()
            keys_back(n, layer, returns, keyed, s)

        tasks = [(0, lambda: back_start(n, returns)), (after + 2, end_keys)]
        tasks += scatter.tasks(1, SCATTER_MIDDLE)
        stages = lower.stages(at) + upper.stages(0)
        if rest_units:
            passed = at + ARRIVED + -(-rest_units * UNIT // WIDE) * (WIDE // UNIT) - 1
            tasks.append((passed, rest_h.start))
            stages += second.stages(REST_AT, REST_HOP) + [
                (REST_AT, send_result, 1, rest_units),
                (max(REST_AT + 3 * REST_HOP, passed + 1), close, 1, rest_units),
            ]
        tasks.sort(key=lambda item: item[0])
        pipeline(
            s.units,
            stages
            + [
                (at + ARRIVED, attention, WIDE // UNIT),
                (at, pass_norm, WIDE // UNIT),
                (0, inputs, WIDE // UNIT),
            ],
            tasks,
        )
        returns.finish()
        scatter.finish()
        if rest_units:

            def finish_result(u):
                second.finish(u)
                result_copy(u).wait()

            each_of(rest_units, finish_result)

        def finish(u):
            upper.finish(u)
            lower.finish(u)
            stores.finish(u)

        each_of(s.units, finish)

    whole = above.grads or [
        block_view(dot_tn(left, right).astype(BF16), s) for left, right in factor_pairs(above)
    ]
    held = dict(
        gate=here_kept.gate,
        up=here_kept.up,
        q=here_kept.q,
        kv=here_kept.kv,
        o=here_kept.o,
        inv=here_kept.inv,
        qraw=here_kept.qraw,
        kraw=here_kept.kraw,
    )
    return run_kernel(
        body,
        head_ins(above, w)
        | {x: (array, ANY) for x, array in held.items()}
        | dict(
            h=(here_kept.h, ANY),
            wd=(w.w_down, ANY),
            wg=(w.w_gate, ANY),
            wu=(w.w_up, ANY),
            wo=(w.w_out, ANY),
            ffn_gain=(w.ffn_gain, VMEM),
            qk_gain=(w.qk_gain, VMEM),
            cosine=(tables.cosine, VMEM),
            sine=(tables.sine, VMEM),
            lowest=(tables.lowest, VMEM),
            whole=[(array, ANY) for array in whole],
        )
        | extra_ins,
        outputs(attention_back_shapes(s))
        | attention_back_sums(s)
        | dict(
            attn_sum=(shaped(1, s.model, kind=F32), VMEM),
            sums=[(shaped(*size, kind=F32), ANY) for size in sizes],
        )
        | extra_outs,
        head_scratch(above, s)
        | extra_scratch
        | weight_scratch(s)
        | {x + "_v": VMEM(array.shape, array.dtype) for x, array in held.items()}
        | buffers({x: b for x, b in backs.items() if x not in dict(dgate=0, dup=0)})
        | attention_back_scratch(s)
        | scatter_scratch(s, sizes, False, 1)
        | dict(
            lower=line_scratch(s.units, s.model),
            middle_sems=DMA((s.rows // WIDE,)),
        ),
        20 + layer,
    )


def backward_end(kept, w, s):
    bottom = kept[0]
    sizes = grad_sizes(s)
    layers = len(kept)
    width = s.model // s.count
    bits = s.count.bit_length() - 1
    tp_bits = s.line.bit_length() - 1
    rounds = [(1 << b, 0) for b in range(bits)] + [(0, 1 << b) for b in range(tp_bits)]

    def body(n):
        c, t = place()
        loads = Loads(n.load_sems)
        early, lates = head_loads(n, loads, 0)
        a2, dup, dgate = loads(n.a2, n.a2_v), loads(n.dup, n.dup_v), loads(n.dgate, n.dgate_v)
        a1, hidden, dyb = loads(n.a1, n.a1_v), loads(n.hidden, n.hidden_v), loads(n.dyb, n.dyb_v)
        o, dhb = loads(n.o, n.o_v), loads(n.dhb, n.dhb_v)
        factors = [
            (n.a2_v, n.dup_v, (a2, dup)),
            (n.a2_v, n.dgate_v, (dgate,)),
            (n.a1_v, n.hq_v, (a1,)),
            (n.hidden_v, n.dyb_v, (hidden, dyb)),
            (n.o_v, n.dhb_v, (o, dhb)),
            (n.a1_v, n.hk_v, ()),
            (n.a1_v, n.hv_v, ()),
        ]
        scatter = Scatter(n, s, sizes, factors)
        stores = Stores(n.store_sems)
        out = stores(n.g_v, n.dres)
        upper = LineSum(n.upper)
        others = [(c >= 0, ((c + k) % s.count, t)) for k in range(1, s.count)]
        lines = [(c >= 0, (c, t ^ (1 << b))) for b in range(tp_bits)]
        greet(line_partners() + halving_partners(s.count) + others + lines)
        n.attn_sum[...] = jnp.zeros_like(n.attn_sum)
        n.acc[...] = jnp.zeros_like(n.acc)
        n.gains[...] = jnp.zeros_like(n.gains)
        for layer in range(layers):
            n.acc[0, 2 * layer : 2 * layer + 2] = n.qk_in[layer][...]
        wait_all(*early)
        scatter.beside = [
            [
                loads(n.done[(layer - 1) * len(sizes) + index], n.sums_v[index].at[layer])
                for index in range(len(sizes))
            ]
            for layer in range(1, layers)
        ]

        def head_copy(k):
            return remote(
                n.acc.at[k],
                n.other.at[k],
                n.small_sems.at[0, k],
                n.small_sems.at[1, k],
                (c ^ rounds[k][0], t ^ rounds[k][1]),
            )

        def head_step(k):
            if k > 0:
                head_copy(k - 1).wait_recv()
                n.acc[k] = n.acc[k - 1] + n.other[k - 1]
            if k < len(rounds):
                head_copy(k).start()

        def pass_norm(u):
            pl.when(u == 0)(lambda: wait_all(*lates))
            head_norm(n, unit_rows(u), upper.take(u), 0)
            send_out([u], out)

        tasks = scatter.tasks(SCATTER_EVERY, SCATTER_END)
        tasks += [(2 * k + 1, lambda k=k: head_step(k)) for k in range(len(rounds) + 1)]
        tasks.sort(key=lambda item: item[0])
        pipeline(
            s.units,
            upper.stages(0)
            + [
                (3 * HOP, pass_norm, 1),
                (0, lambda i: head_inputs(n, i, upper), WIDE // UNIT),
            ],
            tasks,
        )
        gains = [n.attn_sum] + n.attn_in + n.ffn_in
        for d in range(s.count):
            for row, gain in enumerate(gains):
                n.gains[d, row : row + 1] = gain[:, d * width : (d + 1) * width]

        def gain_copy(k):
            to = (c + k) % s.count
            return remote(
                n.gains.at[to],
                n.gains_got.at[k],
                n.gain_sems.at[0, k],
                n.gain_sems.at[1, k],
                (to, t),
            )

        for k in range(1, s.count):
            gain_copy(k).start()
        for layer in range(layers):
            n.qk_total[layer] = n.acc[len(rounds), 2 * layer : 2 * layer + 2]
        total = n.gains[c]
        for k in range(1, s.count):
            gain_copy(k).wait_recv()
            total = total + n.gains_got[k]
        n.attn_total[...] = total[:layers]
        n.ffn_total[...] = total[layers : 2 * layers]
        for k in range(1, s.count):
            gain_copy(k).wait_send()
        for k in range(len(rounds)):
            head_copy(k).wait_send()
        scatter.finish()

        def finish(u):
            upper.finish(u)
            stores.finish(u)

        each_of(s.units, finish)

    held = dict(
        a1=bottom.a1,
        a2=bottom.a2,
        o=bottom.o,
        hidden=bottom.hidden,
        dyb=bottom.dyb,
        dgate=bottom.dgate,
        dup=bottom.dup,
        dhb=bottom.dhb,
    )
    small = (len(rounds) + 1, 2 * layers + -2 * layers % 8, HEAD_SIZE)
    slabs = (s.count, 2 * layers + -2 * layers % 8, width)
    return run_kernel(
        body,
        head_ins(bottom, w)
        | {x: (array, ANY) for x, array in held.items()}
        | dict(
            qk_in=[(k.qk_sum, VMEM) for k in kept],
            attn_in=[(k.attn_sum, VMEM) for k in kept[1:]],
            ffn_in=[(k.ffn_sum, VMEM) for k in kept],
            done=[(array, ANY) for k in kept[1:] for array in k.sums],
        ),
        dict(
            dres=(shaped(s.rows, s.model, kind=F32), ANY),
            attn_total=(shaped(layers, width, kind=F32), VMEM),
            ffn_total=(shaped(layers, width, kind=F32), VMEM),
            qk_total=(shaped(layers, 2, HEAD_SIZE, kind=F32), VMEM),
            sums=[(shaped(layers, *size, kind=F32), ANY) for size in sizes],
        ),
        head_scratch(bottom, s)
        | {x + "_v": VMEM(array.shape, array.dtype) for x, array in held.items()}
        | scatter_scratch(s, sizes, True, layers)
        | dict(
            attn_sum=VMEM((1, s.model), F32),
            acc=VMEM(small, F32),
            other=VMEM(small, F32),
            gains=VMEM(slabs, F32),
            gains_got=VMEM(slabs, F32),
            small_sems=DMA((2, len(rounds))),
            gain_sems=DMA((2, s.count)),
        ),
        19,
    )


def deliver(results):
    pieces = [piece for result in results for piece in result]
    spots = [
        (index, sum(other.shape[0] for other in result[:k]), result[k].shape[0])
        for index, result in enumerate(results)
        for k in range(len(result))
    ]

    def body(n):
        copies = []
        for k, (index, first, rows) in enumerate(spots):
            target = n.result[index].at[pl.ds(first, rows)]
            copies.append(
                (
                    pltpu.make_async_copy(n.given[k], n.held[k], n.sems.at[0, k]),
                    pltpu.make_async_copy(n.held[k], target, n.sems.at[1, k]),
                )
            )
            copies[-1][0].start()
        for fetch, put in copies:
            fetch.wait()
            put.start()
        for fetch, put in copies:
            put.wait()

    shapes = [
        (sum(piece.shape[0] for piece in result),) + result[0].shape[1:] for result in results
    ]
    return run_kernel(
        body,
        dict(given=[(piece, ANY) for piece in pieces]),
        dict(
            result=[
                (shaped(*shape, kind=result[0].dtype), ANY)
                for shape, result in zip(shapes, results)
            ]
        ),
        dict(
            held=[VMEM(piece.shape, piece.dtype) for piece in pieces],
            sems=DMA((2, len(pieces))),
        ),
        None,
    ).result


OUTPUT_AT = 17
REST_AT = 19
REST_WIDES = 2
REST_HOP = 3
SCATTER_MIDDLE = (0, 3, 9, 16)
SCATTER_EVERY = 1
SCATTER_END = (0, 2, 7, 11)


def body(hidden_in, doc_lengths, cotangent, attn_gain, ffn_gain, qk_gain, w_query, *others):
    key_weight, value_weight, w_out, w_gate, w_up, w_down = others
    w = types.SimpleNamespace(
        attn_gain=attn_gain,
        ffn_gain=ffn_gain,
        qk_gain=qk_gain,
        w_query=w_query,
        key_weight=key_weight,
        value_weight=value_weight,
        w_out=w_out,
        w_gate=w_gate,
        w_up=w_up,
        w_down=w_down,
    )
    rows, model = hidden_in.shape
    layers, unused, queries = w_query.shape
    keys = key_weight.shape[2]
    s = types.SimpleNamespace(
        rows=rows,
        model=model,
        queries=queries,
        keys=keys,
        hidden=w_gate.shape[2],
        units=rows // UNIT,
        groups=keys // HEAD_SIZE,
        repeat=queries // keys,
        count=lax.axis_size(CTX),
        line=lax.axis_size(TP),
    )
    tables = None

    kept = []
    stream = hidden_in
    saved = None
    for layer in range(layers):
        if layer < layers - 1:
            result = forward_layer(layer, stream, saved, w, tables, s, doc_lengths)
        else:
            result = turn_layer(layer, stream, saved, cotangent, w, tables, s)
        if saved:
            own = dict(a1=saved.a1, qraw=saved.qraw, kraw=saved.kraw, q=saved.q, kv=saved.kv)
        else:
            own = dict(
                a1=result.own_a1,
                qraw=result.own_qraw,
                kraw=result.own_kraw,
                q=result.own_q,
                kv=result.own_kv,
            )
            tables = types.SimpleNamespace(
                cosine=result.cosine, sine=result.sine, lowest=result.lowest
            )
        kept.append(types.SimpleNamespace(**(dict(grads=None) | vars(result) | own | dict(x=stream))))
        stream = result.y
        saved = result
    streams = [stream]

    for layer in range(layers - 2, -1, -1):
        result = backward_layer(layer, kept, w, tables, s)
        if layer == layers - 2:
            streams.append(result.y)
        kept[layer + 1].attn_sum = result.attn_sum
        kept[layer + 1].sums = result.sums
        vars(kept[layer]).update(
            dyb=result.dyb,
            dgate=result.dgate,
            dup=result.dup,
            dhb=result.dhb,
            dq=result.dq,
            dk=result.dk,
            dv=result.dv,
            dres=result.dres,
            ffn_sum=result.ffn_sum,
            qk_sum=result.qk_sum,
        )
    end = backward_end(kept, w, s)
    small = [end.attn_total, end.ffn_total, end.qk_total]
    stream, grad, *gains, up, gate, query, down, out, key, value = deliver(
        [streams] + [[array] for array in [end.dres] + small + end.sums]
    )
    return (
        stream,
        grad,
        *gains,
        query,
        key,
        value,
        out,
        gate,
        up,
        down,
    )


def solution(mesh):
    by_rows = P(CTX, None)
    by_columns = P(None, None, TP)
    by_hidden = P(None, TP, None)
    grad_columns = P(None, CTX, TP)
    grad_rows = P(None, (TP, CTX), None)
    return jax.shard_map(
        body,
        mesh=mesh,
        in_specs=(by_rows, P(), by_rows, P(), P(), P())
        + (by_columns,) * 3
        + (by_hidden,)
        + (by_columns,) * 2
        + (by_hidden,),
        out_specs=(by_rows, by_rows, P(None, CTX), P(None, CTX), P())
        + (grad_columns,) * 3
        + (grad_rows,)
        + (grad_columns,) * 2
        + (grad_rows,),
        check_vma=False,
    )
```
